512 devices in a mesh: gx: 64 (over x, z_lo, core), gy: 8 (over z_hi, y).
Axes of the slice: x: 4, y: 4, z: 16 (z_hi: 2, z_lo: 8; z = z_hi * 8 + z_lo), core: 2. Of those that a mesh axis runs over, the one named last changes fastest.
Arguments:
- model_state: float32 [4, 64, 256, 1024], P(None, None, 'gx', 'gy'), may hold values from -6 to 6
- density: float32 [64], replicated, may hold values from 0.3 to 1.2
- layer_in: bfloat16 [256, 256], replicated, may hold values from -0.375 to 0.375
- layer_bias: float32 [256], replicated, may hold values from -4 to 4
- layer_out: bfloat16 [256, 128], replicated, may hold values from -0.375 to 0.375
- mode_forward: float32 [64, 64], replicated, may hold values from -0.75 to 0.75
- mode_back: float32 [64, 64], replicated, may hold values from -0.75 to 0.75
- mode_rate: float32 [64], replicated, may hold values from 0.002 to 0.025
Outputs:
- new_state: float32 [4, 64, 256, 1024], P(None, None, 'gx', 'gy')
The draws below stay inside these ranges and needn't reach their ends.
All inputs are finite; a program needn't handle non-finite values.
Results may differ from the reference program's by a relative error of at most 0.0003.
Values sent between devices are 32-bit elements; how exact they have to be, the bound alone decides.
No kernel may reach another device: no remote copies, remote signals or barrier semaphores. Data moves between devices by JAX's collectives and lax.ppermute only.
A program may use at most 64 MiB of HBM per device.

```python
import math
import jax
import jax.numpy as jnp
from jax import lax

L = 64
H = 256
NX = 256
NY = 1024


def block_levels(key, dims, pieces, low, top_value):
    loudness = 1.0
    for position, parts in pieces:
        draws = jax.random.uniform(jax.random.fold_in(jax.random.fold_in(key, 6), position), (parts,), jnp.float32, low / len(pieces), top_value / len(pieces))
        loudness = loudness * jnp.repeat(jnp.exp(draws), dims[position] // parts).reshape((-1,) + (1,) * (len(dims) - 1 - position))
    return loudness


def noise(key, extent, width, reach, shards=(), held_as=jnp.bfloat16):
    entries = width * jax.random.normal(key, extent, jnp.float32)
    if shards:
        entries = entries * block_levels(key, extent, shards, -0.22, 0.18)
    return jnp.clip(entries, -reach, reach).astype(held_as)


def setup_inputs(seed: int = 0) -> dict:
    keys = jax.random.split(jax.random.key(seed), 9)
    model_state = noise(keys[0], (4, L, NX, NY), 1.0, 6.0, ((2, 64), (3, 8)), jnp.float32)
    density = jnp.clip(jnp.exp(jax.random.uniform(keys[1], (L,), jnp.float32, math.log(0.3), math.log(1.2))), 0.3, 1.2)
    layer_in = noise(keys[2], (4 * L, H), (4 * L) ** -0.5, 0.375)
    layer_bias = noise(keys[3], (H,), 1.0, 4.0, (), jnp.float32)
    layer_out = noise(keys[4], (H, 2 * L), H ** -0.5, 0.375)
    mode_forward = noise(keys[5], (L, L), L ** -0.5, 0.75, (), jnp.float32)
    mode_back = noise(keys[6], (L, L), L ** -0.5, 0.75, (), jnp.float32)
    mode_rate = jnp.clip(jnp.exp(jax.random.uniform(keys[7], (L,), jnp.float32, math.log(0.002), math.log(0.025))), 0.002, 0.025)
    return dict(model_state=model_state, density=density, layer_in=layer_in, layer_bias=layer_bias, layer_out=layer_out, mode_forward=mode_forward, mode_back=mode_back, mode_rate=mode_rate)


HIGH = lax.Precision.HIGHEST
TIME_STEP = 0.2
BUOYANCY = 0.5


def centered(values, axis_pos):
    return 0.5 * (jnp.roll(values, -1, axis_pos) - jnp.roll(values, 1, axis_pos))


def vertical(values):
    zero_layer = jnp.zeros_like(values[:1])
    upper = jnp.concatenate([values[1:], zero_layer], 0)
    lower = jnp.concatenate([zero_layer, values[:-1]], 0)
    return 0.5 * (upper - lower)


def advect(scalar_field, eastward, northward, upward):
    return -(eastward * centered(scalar_field, 1) + northward * centered(scalar_field, 2) + upward * vertical(scalar_field))


def reference(model_state, density, layer_in, layer_bias, layer_out, mode_forward, mode_back, mode_rate):
    eastward = model_state[0]
    northward = model_state[1]
    upward = model_state[2]
    potential = model_state[3]
    levels, cells_east, cells_north = potential.shape
    contract_first = (((0,), (0,)), ((), ()))

    def column_physics(x_position):
        column_slab = lax.dynamic_index_in_dim(model_state, x_position, 2, keepdims=False)
        features = column_slab.reshape(4 * levels, cells_north).astype(jnp.bfloat16)
        before = lax.dot_general(layer_in, features, contract_first, preferred_element_type=jnp.float32) + layer_bias[:, None]
        hidden = jax.nn.silu(before).astype(jnp.bfloat16)
        forcing_slab = lax.dot_general(layer_out, hidden, contract_first, preferred_element_type=jnp.float32)
        return forcing_slab.reshape(2, levels, cells_north)

    forcing = jnp.moveaxis(lax.map(column_physics, jnp.arange(cells_east, dtype=jnp.int32)), 0, 2)
    east_star = eastward + TIME_STEP * advect(eastward, eastward, northward, upward)
    north_star = northward + TIME_STEP * advect(northward, eastward, northward, upward)
    up_star = upward + TIME_STEP * (advect(upward, eastward, northward, upward) + BUOYANCY * potential + forcing[1])
    potential_new = potential + TIME_STEP * (advect(potential, eastward, northward, upward) + forcing[0])
    profile = density[:, None, None]
    divergence = centered(east_star, 1) + centered(north_star, 2) + vertical(profile * up_star) / profile
    modal = jnp.einsum("ml,lxy->mxy", mode_forward, divergence, precision=HIGH)
    spectrum = jnp.fft.fft2(modal, axes=(1, 2))
    symbol_east = jnp.sin(jnp.arange(cells_east, dtype=jnp.float32) * (2.0 * math.pi / cells_east))
    symbol_north = jnp.sin(jnp.arange(cells_north, dtype=jnp.float32) * (2.0 * math.pi / cells_north))
    denominator = mode_rate[:, None, None] + (symbol_east * symbol_east)[None, :, None] + (symbol_north * symbol_north)[None, None, :]
    pressure_modal = jnp.real(jnp.fft.ifft2(-spectrum / denominator, axes=(1, 2)))
    pressure = jnp.einsum("ml,lxy->mxy", mode_back, pressure_modal, precision=HIGH)
    slope_east = jnp.einsum("ml,lxy->mxy", mode_back, centered(pressure_modal, 1), precision=HIGH)
    slope_north = jnp.einsum("ml,lxy->mxy", mode_back, centered(pressure_modal, 2), precision=HIGH)
    return jnp.stack([east_star - slope_east, north_star - slope_north, up_star - vertical(pressure), potential_new])
```

```python
import math

import jax
import jax.numpy as jnp
import ml_dtypes
import numpy as np
from jax import lax
from jax.experimental import pallas as pl
from jax.experimental.pallas import tpu as pltpu
from jax.sharding import PartitionSpec as P

F32 = jnp.float32
BF16 = jnp.bfloat16
LEVELS = 64
ROWS = 4
LANES = 128
LOW = 16
HIGH = 32


def split_table(table):
    high = table.astype(np.float32).astype(ml_dtypes.bfloat16)
    low = (table - high.astype(np.float64)).astype(np.float32).astype(ml_dtypes.bfloat16)
    return high, low


def east_tables(total, blocks):
    rows = total // blocks
    x = (np.arange(rows)[:, None] + rows * np.arange(blocks)[None, :]).reshape(-1)
    k = np.arange(total)
    angle = 2.0 * math.pi * ((k[:, None] * x[None, :]) % total) / total
    basis = np.where((k <= total // 2)[:, None], np.cos(angle), np.sin(angle))
    scale = np.where((k == 0) | (k == total // 2), 1.0, math.sqrt(2.0)) / math.sqrt(total)
    basis = basis * scale[:, None]
    square = np.sin(2.0 * math.pi * k / total) ** 2
    square[total // 2] = 0.0
    return basis, square.astype(np.float32)


def lane_of(shape):
    return lax.broadcasted_iota(jnp.int32, shape, len(shape) - 1)


def row_of(shape):
    return lax.broadcasted_iota(jnp.int32, shape, 0)


def turn(values, shift, axis):
    size = values.shape[axis]
    return pltpu.roll(values, shift % size, axis) if shift % size else values


def parts(values):
    high = values.astype(BF16)
    return high, (values - high.astype(F32)).astype(BF16)


def dot3(left, right):
    dot = lambda a, b: jnp.dot(a, b, preferred_element_type=F32)
    return dot(left[0], right[0]) + (dot(left[0], right[1]) + dot(left[1], right[0]))


def level_difference(values):
    row = row_of(values.shape)
    last = values.shape[0] - 1
    upper = jnp.where(row < last, turn(values, -1, 0), 0.0)
    lower = jnp.where(row > 0, turn(values, 1, 0), 0.0)
    return upper - lower


def north_difference(values, low=0.0, high=0.0):
    lane = lane_of(values.shape)
    after = jnp.where(lane < LANES - 1, turn(values, -1, 1), high)
    before = jnp.where(lane > 0, turn(values, 1, 1), low)
    return after - before


def plane(ref, field, x):
    return ref[pl.ds(field * LEVELS * ROWS + x, LEVELS, stride=ROWS), :]


def edges_kernel(place, state, x_even, x_odd, y_even, y_odd):
    even_x = place[0] % 2 == 0
    even_y = place[1] % 2 == 0
    for slot, (field, depth) in enumerate(((0, 0), (1, 0), (2, 0), (3, 0), (0, 1))):
        low = plane(state, field, depth)
        high = plane(state, field, ROWS - 1 - depth)
        span = pl.ds(slot * LEVELS, LEVELS)
        x_even[span, :] = jnp.where(even_x, high, low)
        x_odd[span, :] = jnp.where(even_x, low, high)
    lane = lane_of((LEVELS, LANES))
    gathered = jnp.zeros((LEVELS, LANES), F32)
    for field in range(4):
        for x in range(ROWS):
            values = plane(state, field, x)
            slot = field * ROWS + x
            gathered = jnp.where(lane == slot, turn(values, slot, 1), gathered)
            gathered = jnp.where(lane == 16 + slot, turn(values, 17 + slot, 1), gathered)
    flat = jnp.transpose(jnp.concatenate([gathered, jnp.zeros_like(gathered)], axis=0))
    low, high = flat[0:16], flat[16:32]
    y_even[...] = jnp.where(even_y, high, low)
    y_odd[...] = jnp.where(even_y, low, high)


def inner_kernel(state, layer_in, bias, layer_out, star):
    fields = [[plane(state, f, x) for x in range(ROWS)] for f in range(4)]
    columns = jnp.concatenate(
        [jnp.concatenate([fields[f][x] for f in range(4)], axis=0).astype(BF16) for x in range(ROWS)],
        axis=1,
    )
    before = jnp.dot(layer_in[...], columns, preferred_element_type=F32) + bias[...]
    hidden = (before * (1.0 / (1.0 + jnp.exp(-before)))).astype(BF16)
    forcing = jnp.dot(layer_out[...], hidden, preferred_element_type=F32)
    for x in range(ROWS):
        u, v, w, th = (fields[f][x] for f in range(4))
        span = slice(x * LANES, (x + 1) * LANES)
        heating, lift = forcing[:LEVELS, span], forcing[LEVELS:, span]
        for f in range(4):
            here = fields[f][x]
            change = v * north_difference(here) + w * level_difference(here)
            if x == 0:
                change = change + u * fields[f][1]
            elif x == ROWS - 1:
                change = change - u * fields[f][x - 1]
            else:
                change = change + u * (fields[f][x + 1] - fields[f][x - 1])
            value = here - 0.1 * change
            if f == 2:
                value = value + 0.2 * (0.5 * th + lift)
            if f == 3:
                value = value + 0.2 * heating
            star[pl.ds((f * ROWS + x) * LEVELS, LEVELS), :] = value


def outer_kernel(
    place, state, inner, x_even, x_odd, y_even, y_odd, level_up, level_down, forward, star, message
):
    even_x = place[0] % 2 == 0
    even_y = place[1] % 2 == 0
    shape = (LEVELS, LANES)
    lane = lane_of(shape)

    def beyond(slot):
        first = x_even[pl.ds(slot * LEVELS, LEVELS), :]
        second = x_odd[pl.ds(slot * LEVELS, LEVELS), :]
        return jnp.where(even_x, second, first), jnp.where(even_x, first, second)

    low_y = jnp.where(even_y, y_odd[...], y_even[...])
    high_y = jnp.where(even_y, y_even[...], y_odd[...])
    columns = jnp.transpose(jnp.concatenate([low_y, high_y, jnp.zeros((96, LANES), F32)], axis=0))
    columns = columns[:LEVELS]
    outer_x = [beyond(slot) for slot in range(5)]

    whole = [[None] * ROWS for _ in range(4)]
    side_u = [None] * ROWS
    for x in range(ROWS):
        u, v = plane(state, 0, x), plane(state, 1, x)
        for f in range(4):
            slot = f * ROWS + x
            side = jnp.where(lane == 0, turn(columns, -slot, 1), 0.0)
            side = jnp.where(lane == LANES - 1, -turn(columns, LANES - 1 - 16 - slot, 1), side)
            side = 0.1 * v * side
            if f == 0:
                side_u[x] = side
            value = inner[pl.ds(slot * LEVELS, LEVELS), :] + side
            if x == 0:
                value = value + 0.1 * u * outer_x[f][0]
            if x == ROWS - 1:
                value = value - 0.1 * u * outer_x[f][1]
            whole[f][x] = value
            star[pl.ds(slot * LEVELS, LEVELS), :] = value

    def east_star(which, neighbour):
        u, v, w = (outer_x[f][which] for f in range(3))
        second = outer_x[4][which]
        along = (neighbour - second) if which == 0 else (second - neighbour)
        return u - 0.1 * (u * along + v * north_difference(u) + w * level_difference(u))

    padded = [east_star(0, plane(state, 0, 0))] + whole[0] + [east_star(1, plane(state, 0, ROWS - 1))]
    divergence = []
    extra = jnp.where(lane == 0, -0.5 * side_u[ROWS - 1], 0.0)
    extra = jnp.where(lane == LANES - 1, -0.5 * side_u[ROWS - 1], extra)
    extra = jnp.where(lane == 1, 0.5 * turn(side_u[0], 1, 1), extra)
    extra = jnp.where(lane == LANES - 2, 0.5 * turn(side_u[0], -1, 1), extra)
    up, down = level_up[...], level_down[...]
    for x in range(ROWS):
        v, w = whole[1][x], whole[2][x]
        upright = up * turn(w, -1, 0) - down * turn(w, 1, 0)
        divergence.append(0.5 * (padded[x + 2] - padded[x]) + 0.5 * north_difference(v) + upright)
        extra = jnp.where(lane == LOW + x, 0.5 * turn(v, LOW + x, 1), extra)
        extra = jnp.where(lane == HIGH + x, -0.5 * turn(v, HIGH + x + 1, 1), extra)
    modal = dot3(parts(forward[...]), parts(jnp.concatenate(divergence + [extra], axis=1)))
    for r in range(ROWS + 1):
        message[pl.ds(r, LEVELS, stride=ROWS + 1), :] = modal[:, r * LANES : (r + 1) * LANES]


def decay(rate, square):
    lam = rate + square
    root = jnp.sqrt(lam * (1.0 + lam))
    inverse = 1.0 + 2.0 * lam + 2.0 * root
    return root, inverse, 1.0 / inverse


def squarings(rho, count):
    powers = [rho]
    for _ in range(count):
        powers.append(powers[-1] * powers[-1])
    return powers


def lane_powers(powers, exponent):
    product = None
    for bit in range(6):
        factor = jnp.where((exponent & (1 << bit)) != 0, powers[bit], 1.0)
        product = factor if product is None else product * factor
    return product


def solve_kernel(place, rates, received, basis_high, basis_low, square, local, moments):
    blocks = received.shape[0] // (ROWS + 1)
    size = blocks * ROWS
    lane = lane_of((blocks, LANES))
    rows = [received[pl.ds(r, blocks, stride=ROWS + 1), :] for r in range(ROWS + 1)]
    extra = rows[ROWS]
    ends = (lane == 0) | (lane == LANES - 1)
    rows[0] = rows[0] + jnp.where(ends, turn(extra, 1, 0), 0.0)
    inward = jnp.where(lane == 0, turn(extra, -1, 1), turn(extra, 1, 1))
    rows[ROWS - 1] = rows[ROWS - 1] + jnp.where(ends, turn(inward, -1, 0), 0.0)
    outside = []
    for r in range(ROWS):
        value = jnp.where((lane == 0), turn(extra, -(HIGH + r), 1), 0.0)
        value = jnp.where((lane == 1), turn(extra, 1 - (LOW + r), 1), value)
        value = jnp.where((lane == 2), turn(extra, 2 - (HIGH + r), 1), value)
        outside.append(jnp.where((lane == 3), turn(extra, 3 - (LOW + r), 1), value))
    right = jnp.concatenate(
        [jnp.concatenate(rows[:ROWS], axis=0), jnp.concatenate(outside, axis=0)], axis=1
    )
    spectral = dot3((basis_high[...], basis_low[...]), parts(right))
    source, ext = spectral[:, :LANES], spectral[:, LANES:]

    rate = rates[place[0]]
    _, _, rho = decay(rate, square[...])
    powers = squarings(rho, 6)
    lane = lane_of((size, LANES))
    ahead, behind = source, source
    for bit in range(6):
        shift = 2 << bit
        ahead = ahead + powers[bit] * jnp.where(lane >= shift, turn(ahead, shift, 1), 0.0)
        behind = behind + powers[bit] * jnp.where(lane < LANES - shift, turn(behind, -shift, 1), 0.0)
    half = lane >> 1
    rising = lane_powers(powers, half)
    falling = lane_powers(powers, 63 - half)
    odd = (lane & 1) != 0
    first = jnp.broadcast_to(ext[:, 0:1], (size, LANES))
    second = jnp.broadcast_to(ext[:, 1:2], (size, LANES))
    border = rho * jnp.where(odd, rising * second, falling * first)
    local[...] = ahead + behind - source + border
    weight = jnp.where((lane == 1) | (lane == 2), powers[6] * rho, 1.0)
    column = jnp.where(lane < 2, turn(rho * ahead, 2, 1), turn(rho * behind, 2, 1)) + ext * weight
    column = jnp.where(lane < 4, column, 0.0)
    across = jnp.transpose(column)[:8]
    for j in range(8):
        moments[pl.ds(j * 8, 8), :] = across


def back_kernel(place, rates, local, moments, basis_high, basis_low, square, square_row, message):
    size = local.shape[0]
    blocks = size // ROWS
    rate = rates[place[0]]
    mine = place[1]
    root, inverse, rho = decay(rate, square_row[...])
    r64 = squarings(rho, 6)[6]
    r128 = r64 * r64
    r256 = r128 * r128
    row = row_of((8, size))
    carry = jnp.zeros((8, size), F32)
    for j in range(8):
        from_low = (mine - j - 1) & 7
        from_high = (j - mine - 1) & 7
        exponent = jnp.where(row < 2, from_low, from_high)
        weight = jnp.where((exponent & 1) != 0, r64, 1.0)
        weight = weight * jnp.where((exponent & 2) != 0, r128, 1.0)
        weight = weight * jnp.where((exponent & 4) != 0, r256, 1.0)
        carry = carry + weight * moments[pl.ds(j * 8, 8), :]
    carry = carry / (1.0 - r256 * r256)
    own = moments[pl.ds(pl.multiple_of(mine * 8, 8), 8), :]
    scale = -1.0 / root[0:1]
    after = scale * (own[0:1] + carry[0:1] * r64[0:1] + carry[2:3] * inverse[0:1])
    before = scale * (own[3:4] + carry[3:4] * r64[0:1] + carry[1:2] * inverse[0:1])
    stacked = jnp.concatenate([carry[0:4], after, before, jnp.zeros((LANES - 6, size), F32)], axis=0)
    columns = jnp.transpose(stacked)

    root, _, rho = decay(rate, square[...])
    powers = squarings(rho, 5)
    lane = lane_of((size, LANES))
    half = lane >> 1
    odd = (lane & 1) != 0
    spread = lambda i: jnp.broadcast_to(columns[:, i : i + 1], (size, LANES))
    total = local[...] + lane_powers(powers, half) * jnp.where(odd, spread(1), spread(0))
    total = total + lane_powers(powers, 63 - half) * jnp.where(odd, spread(3), spread(2))
    total = -total / root
    ext = jnp.where((lane == 4) | (lane == 5), columns, 0.0)
    pressure = dot3(
        (basis_high[...], basis_low[...]), parts(jnp.concatenate([total, ext], axis=1))
    )
    lane = lane_of((blocks, LANES))
    inside = [pressure[r * blocks : (r + 1) * blocks, :LANES] for r in range(ROWS)]
    left = turn(inside[ROWS - 1], 1, 0)
    right = turn(inside[0], -1, 0)
    extra = jnp.where((lane == 0) | (lane == LANES - 1), left, 0.0)
    extra = jnp.where(lane == 1, turn(right, 1, 1), extra)
    extra = jnp.where(lane == LANES - 2, turn(right, -1, 1), extra)
    for r in range(ROWS):
        outside = pressure[r * blocks : (r + 1) * blocks, LANES:]
        extra = jnp.where(lane == HIGH + r, turn(outside, HIGH + r - 4, 1), extra)
        extra = jnp.where(lane == LOW + r, turn(outside, LOW + r - 5, 1), extra)
        message[pl.ds(r, blocks, stride=ROWS + 1), :] = inside[r]
    message[pl.ds(ROWS, blocks, stride=ROWS + 1), :] = extra


def final_kernel(received, sent, star, back, rate, out):
    lane = lane_of((LEVELS, LANES))
    p = [received[pl.ds(r, LEVELS, stride=ROWS + 1), :] for r in range(ROWS)]
    extra = received[pl.ds(ROWS, LEVELS, stride=ROWS + 1), :]
    low = [turn(extra, -(LOW + r), 1) for r in range(ROWS)]
    high = [turn(extra, LANES - 1 - (HIGH + r), 1) for r in range(ROWS)]
    four_rate = 4.0 * rate[...]

    def next_row(r, opposite):
        here = p[r]
        divergence = sent[pl.ds(r, LEVELS, stride=ROWS + 1), :]
        plus = jnp.where(lane < LANES - 2, turn(here, -2, 1), turn(high[r], -1, 1))
        minus = jnp.where(lane > 1, turn(here, 2, 1), turn(low[r], 1, 1))
        return (
            2.0 * here
            - opposite
            + four_rate * here
            + (2.0 * here - plus - minus)
            + 4.0 * divergence
        )

    ends = (lane == 0) | (lane == LANES - 1)
    before = jnp.where(ends, extra, next_row(1, p[3]))
    inward = jnp.where(lane == 0, turn(extra, -1, 1), turn(extra, 1, 1))
    after = jnp.where(ends, inward, next_row(2, p[0]))
    padded = [before] + p + [after]
    slopes = [0.5 * (padded[x + 2] - padded[x]) for x in range(ROWS)]
    slopes += [0.5 * north_difference(p[x], low[x], high[x]) for x in range(ROWS)]
    matrix = back[...]
    slope = dot3(parts(matrix), parts(jnp.concatenate(slopes, axis=1)))
    lift = dot3(parts(0.5 * level_difference(matrix)), parts(jnp.concatenate(p, axis=1)))
    for x in range(ROWS):
        take = lambda values, i: values[:, i * LANES : (i + 1) * LANES]
        for f, change in ((0, take(slope, x)), (1, take(slope, ROWS + x)), (2, take(lift, x)), (3, None)):
            value = star[pl.ds((f * ROWS + x) * LEVELS, LEVELS), :]
            if change is not None:
                value = value - change
            out[pl.ds(f * LEVELS * ROWS + x, LEVELS, stride=ROWS), :] = value


def call(kernel, shapes, smem, args, name):
    vmem = pl.BlockSpec(memory_space=pltpu.VMEM)
    scalar = pl.BlockSpec(memory_space=pltpu.SMEM)
    return pl.pallas_call(
        kernel,
        out_shape=[jax.ShapeDtypeStruct(s, F32) for s in shapes],
        in_specs=[scalar] * smem + [vmem] * (len(args) - smem),
        out_specs=[vmem] * len(shapes),
        compiler_params=pltpu.CompilerParams(vmem_limit_bytes=32 * 1024 * 1024),
        name=name,
    )(*args)


def swap(values, axis, odd):
    count = lax.axis_size(axis)
    pairs = []
    for i in range(odd, count + odd, 2):
        pairs += [(i % count, (i + 1) % count), ((i + 1) % count, i % count)]
    return lax.ppermute(values, axis, pairs)


def exchange(values, axis, groups, rows):
    shaped = values.reshape(groups, 1, rows * values.shape[1])
    return lax.all_to_all(shaped, axis, 0, 0, tiled=True).reshape(values.shape)


def on_device(
    model_state, density, layer_in, layer_bias, layer_out, mode_forward, mode_back, mode_rate
):
    blocks = lax.axis_size("gx")
    total_east = blocks * ROWS
    place = jnp.stack([lax.axis_index("gx"), lax.axis_index("gy")]).astype(jnp.int32)
    state = model_state.reshape(4 * LEVELS * ROWS, LANES)
    basis, square = east_tables(total_east, blocks)
    forward_high, forward_low = split_table(basis)
    back_high, back_low = split_table(np.ascontiguousarray(basis.T))
    square_wide = np.ascontiguousarray(np.broadcast_to(square[:, None], (total_east, LANES)))
    square_row = np.ascontiguousarray(np.broadcast_to(square[None, :], (8, total_east)))

    x_even, x_odd, y_even, y_odd = call(
        edges_kernel,
        [(5 * LEVELS, LANES)] * 2 + [(16, LANES)] * 2,
        1,
        [place, state],
        "edges",
    )
    got_y_odd = swap(y_odd, "gy", 1)
    got_x_odd = swap(x_odd, "gx", 1)
    got_y_even = swap(y_even, "gy", 0)
    got_x_even = swap(x_even, "gx", 0)
    (inner,) = call(
        inner_kernel,
        [(16 * LEVELS, LANES)],
        0,
        [state, layer_in.T, layer_bias[:, None], layer_out.T],
        "inner",
    )
    zero = jnp.zeros((1,), F32)
    level_up = jnp.concatenate([0.5 * density[1:] / density[:-1], zero])
    level_down = jnp.concatenate([zero, 0.5 * density[:-1] / density[1:]])
    star, message = call(
        outer_kernel,
        [(16 * LEVELS, LANES), (blocks * (ROWS + 1), LANES)],
        1,
        [
            place,
            state,
            inner,
            got_x_even,
            got_x_odd,
            got_y_even,
            got_y_odd,
            level_up[:, None],
            level_down[:, None],
            mode_forward,
        ],
        "outer",
    )
    modal = exchange(message, "gx", blocks, ROWS + 1)
    local, moments = call(
        solve_kernel,
        [(total_east, LANES), (64, total_east)],
        2,
        [place, mode_rate, modal, forward_high, forward_low, square_wide],
        "solve",
    )
    moments = lax.all_to_all(
        moments.reshape(8, 8, total_east), "gy", 0, 0, tiled=True
    ).reshape(64, total_east)
    (reply,) = call(
        back_kernel,
        [(total_east * (ROWS + 1) // ROWS, LANES)],
        2,
        [place, mode_rate, local, moments, back_high, back_low, square_wide, square_row],
        "back",
    )
    pressure = exchange(reply, "gx", blocks, ROWS + 1)
    (out,) = call(
        final_kernel,
        [(4 * LEVELS * ROWS, LANES)],
        0,
        [pressure, message, star, mode_back, mode_rate[:, None]],
        "final",
    )
    return out.reshape(model_state.shape)


def solution(mesh):
    return jax.shard_map(
        on_device,
        mesh=mesh,
        in_specs=(P(None, None, "gx", "gy"), P(), P(), P(), P(), P(), P(), P()),
        out_specs=P(None, None, "gx", "gy"),
        check_vma=False,
    )
```

```python
import math

import jax
import jax.numpy as jnp
import ml_dtypes
import numpy as np
from jax import lax
from jax.experimental import pallas as pl
from jax.experimental.pallas import tpu as pltpu
from jax.sharding import PartitionSpec as P

F32 = jnp.float32
BF16 = jnp.bfloat16
LEVELS = 64
ROWS = 4
LANES = 128
LOW = 16
HIGH = 32


def split_table(table):
    high = table.astype(np.float32).astype(ml_dtypes.bfloat16)
    low = (table - high.astype(np.float64)).astype(np.float32).astype(ml_dtypes.bfloat16)
    return high, low


def east_tables(total, blocks):
    rows = total // blocks
    x = (np.arange(rows)[:, None] + rows * np.arange(blocks)[None, :]).reshape(-1)
    k = np.arange(total)
    angle = 2.0 * math.pi * ((k[:, None] * x[None, :]) % total) / total
    basis = np.where((k <= total // 2)[:, None], np.cos(angle), np.sin(angle))
    scale = np.where((k == 0) | (k == total // 2), 1.0, math.sqrt(2.0)) / math.sqrt(total)
    basis = basis * scale[:, None]
    square = np.sin(math.pi * k / total) ** 2
    return basis, square.astype(np.float32)


def lane_of(shape):
    return lax.broadcasted_iota(jnp.int32, shape, len(shape) - 1)


def row_of(shape):
    return lax.broadcasted_iota(jnp.int32, shape, 0)


def turn(values, shift, axis):
    size = values.shape[axis]
    return pltpu.roll(values, shift % size, axis) if shift % size else values


def parts(values):
    high = values.astype(BF16)
    return high, (values - high.astype(F32)).astype(BF16)


def dot3(left, right):
    dot = lambda a, b: jnp.dot(a, b, preferred_element_type=F32)
    return dot(left[0], right[0]) + (dot(left[0], right[1]) + dot(left[1], right[0]))


def level_difference(values):
    row = row_of(values.shape)
    last = values.shape[0] - 1
    upper = jnp.where(row < last, turn(values, -1, 0), 0.0)
    lower = jnp.where(row > 0, turn(values, 1, 0), 0.0)
    return upper - lower


def north_difference(values, low=0.0, high=0.0):
    lane = lane_of(values.shape)
    after = jnp.where(lane < LANES - 1, turn(values, -1, 1), high)
    before = jnp.where(lane > 0, turn(values, 1, 1), low)
    return after - before


def plane(ref, field, x):
    return ref[pl.ds(field * LEVELS * ROWS + x, LEVELS, stride=ROWS), :]


def edges_kernel(place, state, x_even, x_odd, y_even, y_odd):
    even_x = place[0] % 2 == 0
    even_y = place[1] % 2 == 0
    for slot, (field, depth) in enumerate(((0, 0), (1, 0), (2, 0), (3, 0), (0, 1))):
        low = plane(state, field, depth)
        high = plane(state, field, ROWS - 1 - depth)
        span = pl.ds(slot * LEVELS, LEVELS)
        x_even[span, :] = jnp.where(even_x, high, low)
        x_odd[span, :] = jnp.where(even_x, low, high)
    lane = lane_of((LEVELS, LANES))
    gathered = jnp.zeros((LEVELS, LANES), F32)
    for field in range(4):
        for x in range(ROWS):
            values = plane(state, field, x)
            slot = field * ROWS + x
            gathered = jnp.where(lane == slot, turn(values, slot, 1), gathered)
            gathered = jnp.where(lane == 16 + slot, turn(values, 17 + slot, 1), gathered)
    flat = jnp.transpose(jnp.concatenate([gathered, jnp.zeros_like(gathered)], axis=0))
    low, high = flat[0:16], flat[16:32]
    y_even[...] = jnp.where(even_y, high, low)
    y_odd[...] = jnp.where(even_y, low, high)


def inner_kernel(state, layer_in, bias, layer_out, star):
    fields = [[plane(state, f, x) for x in range(ROWS)] for f in range(4)]
    columns = jnp.concatenate(
        [jnp.concatenate([fields[f][x] for f in range(4)], axis=0).astype(BF16) for x in range(ROWS)],
        axis=1,
    )
    before = jnp.dot(layer_in[...], columns, preferred_element_type=F32) + bias[...]
    hidden = (before * (1.0 / (1.0 + jnp.exp(-before)))).astype(BF16)
    forcing = jnp.dot(layer_out[...], hidden, preferred_element_type=F32)
    for x in range(ROWS):
        u, v, w, th = (fields[f][x] for f in range(4))
        span = slice(x * LANES, (x + 1) * LANES)
        heating, lift = forcing[:LEVELS, span], forcing[LEVELS:, span]
        for f in range(4):
            here = fields[f][x]
            change = v * north_difference(here) + w * level_difference(here)
            if x == 0:
                change = change + u * fields[f][1]
            elif x == ROWS - 1:
                change = change - u * fields[f][x - 1]
            else:
                change = change + u * (fields[f][x + 1] - fields[f][x - 1])
            value = here - 0.1 * change
            if f == 2:
                value = value + 0.2 * (0.5 * th + lift)
            if f == 3:
                value = value + 0.2 * heating
            star[pl.ds((f * ROWS + x) * LEVELS, LEVELS), :] = value


def outer_kernel(
    place, state, inner, x_even, x_odd, y_even, y_odd, level_up, level_down, forward, star, message
):
    even_x = place[0] % 2 == 0
    even_y = place[1] % 2 == 0
    shape = (LEVELS, LANES)
    lane = lane_of(shape)

    def beyond(slot):
        first = x_even[pl.ds(slot * LEVELS, LEVELS), :]
        second = x_odd[pl.ds(slot * LEVELS, LEVELS), :]
        return jnp.where(even_x, second, first), jnp.where(even_x, first, second)

    low_y = jnp.where(even_y, y_odd[...], y_even[...])
    high_y = jnp.where(even_y, y_even[...], y_odd[...])
    columns = jnp.transpose(jnp.concatenate([low_y, high_y, jnp.zeros((96, LANES), F32)], axis=0))
    columns = columns[:LEVELS]
    outer_x = [beyond(slot) for slot in range(5)]

    whole = [[None] * ROWS for _ in range(4)]
    side_u = [None] * ROWS
    for x in range(ROWS):
        u, v = plane(state, 0, x), plane(state, 1, x)
        for f in range(4):
            slot = f * ROWS + x
            side = jnp.where(lane == 0, turn(columns, -slot, 1), 0.0)
            side = jnp.where(lane == LANES - 1, -turn(columns, LANES - 1 - 16 - slot, 1), side)
            side = 0.1 * v * side
            if f == 0:
                side_u[x] = side
            value = inner[pl.ds(slot * LEVELS, LEVELS), :] + side
            if x == 0:
                value = value + 0.1 * u * outer_x[f][0]
            if x == ROWS - 1:
                value = value - 0.1 * u * outer_x[f][1]
            whole[f][x] = value
            star[pl.ds(slot * LEVELS, LEVELS), :] = value

    def east_star(which, neighbour):
        u, v, w = (outer_x[f][which] for f in range(3))
        second = outer_x[4][which]
        along = (neighbour - second) if which == 0 else (second - neighbour)
        return u - 0.1 * (u * along + v * north_difference(u) + w * level_difference(u))

    padded = [east_star(0, plane(state, 0, 0))] + whole[0] + [east_star(1, plane(state, 0, ROWS - 1))]
    divergence = []
    extra = [-0.5 * side_u[ROWS - 1], 0.5 * side_u[0]]
    up, down = level_up[...], level_down[...]
    for x in range(ROWS):
        v, w = whole[1][x], whole[2][x]
        upright = up * turn(w, -1, 0) - down * turn(w, 1, 0)
        divergence.append(0.5 * (padded[x + 2] - padded[x]) + 0.5 * north_difference(v) + upright)
        low, high = LOW + x // 2, HIGH + x // 2
        value = jnp.where(lane == low, 0.5 * turn(v, low, 1), extra[x % 2])
        extra[x % 2] = jnp.where(lane == high, -0.5 * turn(v, high + 1, 1), value)
    pieces = [divergence[0], divergence[2], extra[0], divergence[1], divergence[3], extra[1]]
    modal = dot3(parts(forward[...]), parts(jnp.concatenate(pieces, axis=1)))
    for i in range(6):
        message[pl.ds(i, LEVELS, stride=6), :] = modal[:, i * LANES : (i + 1) * LANES]


def decay(rate, square):
    lam = rate + square
    root = jnp.sqrt(lam * (1.0 + lam))
    inverse = 1.0 + 2.0 * lam + 2.0 * root
    return root, inverse, 1.0 / inverse


def squarings(rho, count):
    powers = [rho]
    for _ in range(count):
        powers.append(powers[-1] * powers[-1])
    return powers


def lane_powers(powers, exponent):
    product = None
    for bit in range(6):
        factor = jnp.where((exponent & (1 << bit)) != 0, powers[bit], 1.0)
        product = factor if product is None else product * factor
    return product


def solve_kernel(place, rates, received, basis_high, basis_low, square, local, moments):
    blocks = received.shape[0] // 6
    half_size = blocks * 2
    size = half_size * 2
    lane = lane_of((blocks, LANES))
    ends = (lane == 0) | (lane == LANES - 1)
    even = place[1] < 4
    inside, outside = [], [None, None]
    for h in range(2):
        first, second, extra = (received[pl.ds(3 * h + j, blocks, stride=6), :] for j in range(3))
        first = first + jnp.where(ends & even, turn(extra, 1, 0), 0.0)
        second = second + jnp.where(ends & ~even, turn(extra, -1, 0), 0.0)
        inside.append(jnp.concatenate([first, second], axis=0))
        for r in range(2):
            value = jnp.zeros_like(extra) if outside[r] is None else outside[r]
            for i in range(4):
                at = 4 * h + i
                value = jnp.where(lane == at, turn(extra, at - (HIGH, LOW)[i % 2] - r, 1), value)
            outside[r] = value
    right = jnp.concatenate(inside + [jnp.concatenate(outside, axis=0)], axis=1)
    spectral = dot3((basis_high[...], basis_low[...]), parts(right))
    source = jnp.concatenate([spectral[:, :LANES], spectral[:, LANES : 2 * LANES]], axis=0)
    ext = spectral[:, 2 * LANES :]
    ext = jnp.concatenate([ext, turn(ext, -4, 1)], axis=0)

    rate = rates[place[0]]
    _, _, rho = decay(rate, square[...])
    powers = squarings(rho, 6)
    lane = lane_of((size, LANES))
    ahead, behind = source, source
    for bit in range(6):
        shift = 2 << bit
        ahead = ahead + powers[bit] * jnp.where(lane >= shift, turn(ahead, shift, 1), 0.0)
        behind = behind + powers[bit] * jnp.where(lane < LANES - shift, turn(behind, -shift, 1), 0.0)
    half = lane >> 1
    rising = lane_powers(powers, half)
    falling = lane_powers(powers, 63 - half)
    odd = (lane & 1) != 0
    first = jnp.broadcast_to(ext[:, 0:1], (size, LANES))
    second = jnp.broadcast_to(ext[:, 1:2], (size, LANES))
    border = rho * jnp.where(odd, rising * second, falling * first)
    local[...] = ahead + behind - source + border
    weight = jnp.where((lane == 1) | (lane == 2), powers[6] * rho, 1.0)
    column = jnp.where(lane < 2, turn(rho * ahead, 2, 1), turn(rho * behind, 2, 1)) + ext * weight
    column = jnp.where(lane < 4, column, 0.0)
    across = jnp.transpose(column)[:8]
    for j in range(4):
        moments[pl.ds(j * 8, 8), :] = across


def back_kernel(place, rates, local, moments, basis_high, basis_low, square, square_row, message):
    size = local.shape[0]
    half_size = size // 2
    blocks = half_size // 2
    rate = rates[place[0]]
    even = place[1] < 4
    mine = place[1] & 3
    root, inverse, rho = decay(rate, square_row[...])
    r64 = squarings(rho, 6)[6]
    r128 = r64 * r64
    r256 = r128 * r128
    row = row_of((8, size))
    carry = jnp.zeros((8, size), F32)
    for j in range(4):
        theirs = moments[pl.ds(j * 8, 8), :]
        for offset, values in ((-1, theirs), (3, turn(theirs, half_size, 1))):
            exponent = jnp.where(row < 2, (mine - j + offset) & 7, (j - mine + offset) & 7)
            weight = jnp.where((exponent & 1) != 0, r64, 1.0)
            weight = weight * jnp.where((exponent & 2) != 0, r128, 1.0)
            weight = weight * jnp.where((exponent & 4) != 0, r256, 1.0)
            carry = carry + weight * values
    carry = carry / (1.0 - r256 * r256)
    own = moments[pl.ds(pl.multiple_of(mine * 8, 8), 8), :]
    scale = -1.0 / root[0:1]
    after = scale * (own[0:1] + carry[0:1] * r64[0:1] + carry[2:3] * inverse[0:1])
    before = scale * (own[3:4] + carry[3:4] * r64[0:1] + carry[1:2] * inverse[0:1])
    stacked = jnp.concatenate([carry[0:4], after, before, jnp.zeros((LANES - 6, size), F32)], axis=0)
    columns = jnp.transpose(stacked)

    root, _, rho = decay(rate, square[...])
    powers = squarings(rho, 5)
    lane = lane_of((size, LANES))
    half = lane >> 1
    odd = (lane & 1) != 0
    spread = lambda i: jnp.broadcast_to(columns[:, i : i + 1], (size, LANES))
    total = local[...] + lane_powers(powers, half) * jnp.where(odd, spread(1), spread(0))
    total = total + lane_powers(powers, 63 - half) * jnp.where(odd, spread(3), spread(2))
    total = -total / root
    ext = jnp.where((lane == 4) | (lane == 5), columns, 0.0)
    ext = ext[:half_size] + turn(ext[half_size:], 2, 1)
    pressure = dot3(
        (basis_high[...], basis_low[...]),
        parts(jnp.concatenate([total[:half_size], total[half_size:], ext], axis=1)),
    )
    lane = lane_of((blocks, LANES))
    ends = (lane == 0) | (lane == LANES - 1)
    outside = [pressure[r * blocks : (r + 1) * blocks, 2 * LANES :] for r in range(2)]
    for h in range(2):
        span = slice(h * LANES, (h + 1) * LANES)
        first, second = pressure[:blocks, span], pressure[blocks:, span]
        extra = jnp.where(ends, jnp.where(even, turn(first, -1, 0), turn(second, 1, 0)), 0.0)
        for r in range(2):
            extra = jnp.where(lane == HIGH + r, turn(outside[r], HIGH + r - 4 - 2 * h, 1), extra)
            extra = jnp.where(lane == LOW + r, turn(outside[r], LOW + r - 5 - 2 * h, 1), extra)
        for j, value in enumerate((first, second, extra)):
            message[pl.ds(3 * h + j, blocks, stride=6), :] = value


def final_kernel(received, sent, star, back, rate, out):
    lane = lane_of((LEVELS, LANES))
    row_at = lambda ref, r: ref[pl.ds(3 * (r % 2) + r // 2, LEVELS, stride=6), :]
    p = [row_at(received, r) for r in range(ROWS)]
    extra = [row_at(received, 4), row_at(received, 5)]
    low = [turn(extra[r % 2], -(LOW + r // 2), 1) for r in range(ROWS)]
    high = [turn(extra[r % 2], LANES - 1 - (HIGH + r // 2), 1) for r in range(ROWS)]
    four_rate = 4.0 * rate[...]

    def next_row(r, opposite):
        here = p[r]
        divergence = row_at(sent, r)
        plus = jnp.where(lane < LANES - 2, turn(here, -2, 1), turn(high[r], -1, 1))
        minus = jnp.where(lane > 1, turn(here, 2, 1), turn(low[r], 1, 1))
        return (
            2.0 * here
            - opposite
            + four_rate * here
            + (2.0 * here - plus - minus)
            + 4.0 * divergence
        )

    ends = (lane == 0) | (lane == LANES - 1)
    before = jnp.where(ends, extra[1], next_row(1, p[3]))
    after = jnp.where(ends, extra[0], next_row(2, p[0]))
    padded = [before] + p + [after]
    slopes = [0.5 * (padded[x + 2] - padded[x]) for x in range(ROWS)]
    slopes += [0.5 * north_difference(p[x], low[x], high[x]) for x in range(ROWS)]
    matrix = back[...]
    slope = dot3(parts(matrix), parts(jnp.concatenate(slopes, axis=1)))
    lift = dot3(parts(0.5 * level_difference(matrix)), parts(jnp.concatenate(p, axis=1)))
    for x in range(ROWS):
        take = lambda values, i: values[:, i * LANES : (i + 1) * LANES]
        for f, change in ((0, take(slope, x)), (1, take(slope, ROWS + x)), (2, take(lift, x)), (3, None)):
            value = star[pl.ds((f * ROWS + x) * LEVELS, LEVELS), :]
            if change is not None:
                value = value - change
            out[pl.ds(f * LEVELS * ROWS + x, LEVELS, stride=ROWS), :] = value


def call(kernel, shapes, smem, args, name):
    vmem = pl.BlockSpec(memory_space=pltpu.VMEM)
    scalar = pl.BlockSpec(memory_space=pltpu.SMEM)
    return pl.pallas_call(
        kernel,
        out_shape=[jax.ShapeDtypeStruct(s, F32) for s in shapes],
        in_specs=[scalar] * smem + [vmem] * (len(args) - smem),
        out_specs=[vmem] * len(shapes),
        compiler_params=pltpu.CompilerParams(vmem_limit_bytes=32 * 1024 * 1024),
        name=name,
    )(*args)


def swap(values, axis, odd):
    count = lax.axis_size(axis)
    pairs = []
    for i in range(odd, count + odd, 2):
        pairs += [(i % count, (i + 1) % count), ((i + 1) % count, i % count)]
    return lax.ppermute(values, axis, pairs)


def exchange(values):
    count_x, count_y = lax.axis_size("gx"), lax.axis_size("gy")
    near = count_y // 2
    groups = [[i * count_y + h * near + y for i in range(count_x) for h in range(2)] for y in range(near)]
    shaped = values.reshape(2 * count_x, 1, values.size // (2 * count_x))
    moved = lax.all_to_all(
        shaped, ("gx", "gy"), 0, 0, tiled=True, axis_index_groups=groups
    )
    return moved.reshape(values.shape)


def on_device(
    model_state, density, layer_in, layer_bias, layer_out, mode_forward, mode_back, mode_rate
):
    blocks = lax.axis_size("gx")
    total_east = blocks * ROWS
    place = jnp.stack([lax.axis_index("gx"), lax.axis_index("gy")]).astype(jnp.int32)
    state = model_state.reshape(4 * LEVELS * ROWS, LANES)
    basis, square = east_tables(total_east // 2, blocks)
    square = np.concatenate([square, square])
    forward_high, forward_low = split_table(basis)
    back_high, back_low = split_table(np.ascontiguousarray(basis.T))
    square_wide = np.ascontiguousarray(np.broadcast_to(square[:, None], (total_east, LANES)))
    square_row = np.ascontiguousarray(np.broadcast_to(square[None, :], (8, total_east)))

    x_even, x_odd, y_even, y_odd = call(
        edges_kernel,
        [(5 * LEVELS, LANES)] * 2 + [(16, LANES)] * 2,
        1,
        [place, state],
        "edges",
    )
    got_y_odd = swap(y_odd, "gy", 1)
    got_x_odd = swap(x_odd, "gx", 1)
    got_y_even = swap(y_even, "gy", 0)
    got_x_even = swap(x_even, "gx", 0)
    (inner,) = call(
        inner_kernel,
        [(16 * LEVELS, LANES)],
        0,
        [state, layer_in.T, layer_bias[:, None], layer_out.T],
        "inner",
    )
    zero = jnp.zeros((1,), F32)
    level_up = jnp.concatenate([0.5 * density[1:] / density[:-1], zero])
    level_down = jnp.concatenate([zero, 0.5 * density[:-1] / density[1:]])
    star, message = call(
        outer_kernel,
        [(16 * LEVELS, LANES), (blocks * 6, LANES)],
        1,
        [
            place,
            state,
            inner,
            got_x_even,
            got_x_odd,
            got_y_even,
            got_y_odd,
            level_up[:, None],
            level_down[:, None],
            mode_forward,
        ],
        "outer",
    )
    modal = exchange(message)
    local, moments = call(
        solve_kernel,
        [(total_east, LANES), (32, total_east)],
        2,
        [place, mode_rate, modal, forward_high, forward_low, square_wide],
        "solve",
    )
    moments = lax.all_to_all(
        moments.reshape(4, 8, total_east),
        "gy",
        0,
        0,
        tiled=True,
        axis_index_groups=[[0, 1, 2, 3], [4, 5, 6, 7]],
    ).reshape(32, total_east)
    (reply,) = call(
        back_kernel,
        [(blocks * 6, LANES)],
        2,
        [place, mode_rate, local, moments, back_high, back_low, square_wide, square_row],
        "back",
    )
    pressure = exchange(reply)
    (out,) = call(
        final_kernel,
        [(4 * LEVELS * ROWS, LANES)],
        0,
        [pressure, message, star, mode_back, mode_rate[:, None]],
        "final",
    )
    return out.reshape(model_state.shape)


def solution(mesh):
    return jax.shard_map(
        on_device,
        mesh=mesh,
        in_specs=(P(None, None, "gx", "gy"), P(), P(), P(), P(), P(), P(), P()),
        out_specs=P(None, None, "gx", "gy"),
        check_vma=False,
    )
```

```python
import math

import jax
import jax.numpy as jnp
import ml_dtypes
import numpy as np
from jax import lax
from jax.experimental import pallas as pl
from jax.experimental.pallas import tpu as pltpu
from jax.sharding import PartitionSpec as P

F32 = jnp.float32
BF16 = jnp.bfloat16
LEVELS = 64
ROWS = 4
LANES = 128
LOW = 16
HIGH = 32


def split_table(table):
    high = table.astype(np.float32).astype(ml_dtypes.bfloat16)
    low = (table - high.astype(np.float64)).astype(np.float32).astype(ml_dtypes.bfloat16)
    return high, low


def east_tables(total, blocks):
    rows = total // blocks
    x = (np.arange(rows)[:, None] + rows * np.arange(blocks)[None, :]).reshape(-1)
    k = np.arange(total)
    angle = 2.0 * math.pi * ((k[:, None] * x[None, :]) % total) / total
    basis = np.where((k <= total // 2)[:, None], np.cos(angle), np.sin(angle))
    scale = np.where((k == 0) | (k == total // 2), 1.0, math.sqrt(2.0)) / math.sqrt(total)
    basis = basis * scale[:, None]
    square = np.sin(math.pi * k / total) ** 2
    return basis, square.astype(np.float32)


def lane_of(shape):
    return lax.broadcasted_iota(jnp.int32, shape, len(shape) - 1)


def row_of(shape):
    return lax.broadcasted_iota(jnp.int32, shape, 0)


def turn(values, shift, axis):
    size = values.shape[axis]
    return pltpu.roll(values, shift % size, axis) if shift % size else values


def parts(values):
    high = values.astype(BF16)
    return high, (values - high.astype(F32)).astype(BF16)


def dot3(left, right):
    dot = lambda a, b: jnp.dot(a, b, preferred_element_type=F32)
    return dot(left[0], right[0]) + (dot(left[0], right[1]) + dot(left[1], right[0]))


def level_difference(values):
    row = row_of(values.shape)
    last = values.shape[0] - 1
    upper = jnp.where(row < last, turn(values, -1, 0), 0.0)
    lower = jnp.where(row > 0, turn(values, 1, 0), 0.0)
    return upper - lower


def north_difference(values, low=0.0, high=0.0):
    lane = lane_of(values.shape)
    after = jnp.where(lane < LANES - 1, turn(values, -1, 1), high)
    before = jnp.where(lane > 0, turn(values, 1, 1), low)
    return after - before


def plane(ref, field, x):
    return ref[pl.ds(field * LEVELS * ROWS + x, LEVELS, stride=ROWS), :]


def far_both(gx, gy):
    return ((gx % 16 == 0) | (gx % 16 == 15)) & ((gy % 4 == 0) | (gy % 4 == 3))


def edges_kernel(place, state, x_even, x_odd, y_even, y_odd):
    even_x = place[0] % 2 == 0
    even_y = place[1] % 2 == 0
    for slot, (field, depth) in enumerate(((0, 0), (1, 0), (2, 0), (3, 0), (0, 1))):
        low = plane(state, field, depth)
        high = plane(state, field, ROWS - 1 - depth)
        span = pl.ds(slot * LEVELS, LEVELS)
        x_even[span, :] = jnp.where(even_x, high, low)
        x_odd[span, :] = jnp.where(even_x, low, high)
    lane = lane_of((LEVELS, LANES))
    gathered = jnp.zeros((LEVELS, LANES), F32)
    for field in range(4):
        for x in range(ROWS):
            values = plane(state, field, x)
            slot = field * ROWS + x
            gathered = jnp.where(lane == slot, turn(values, slot, 1), gathered)
            gathered = jnp.where(lane == 16 + slot, turn(values, 17 + slot, 1), gathered)
    flat = jnp.transpose(jnp.concatenate([gathered, jnp.zeros_like(gathered)], axis=0))
    low, high = flat[0:16], flat[16:32]
    y_even[...] = jnp.where(even_y, high, low)
    y_odd[...] = jnp.where(even_y, low, high)
    x_even[pl.ds(5 * LEVELS, 16), :] = jnp.where(even_y, low, high)


def inner_kernel(state, layer_in, bias, layer_out, star):
    fields = [[plane(state, f, x) for x in range(ROWS)] for f in range(4)]
    columns = jnp.concatenate(
        [jnp.concatenate([fields[f][x] for f in range(4)], axis=0).astype(BF16) for x in range(ROWS)],
        axis=1,
    )
    before = jnp.dot(layer_in[...], columns, preferred_element_type=F32) + bias[...]
    hidden = (before * (1.0 / (1.0 + jnp.exp(-before)))).astype(BF16)
    forcing = jnp.dot(layer_out[...], hidden, preferred_element_type=F32)
    for x in range(ROWS):
        u, v, w, th = (fields[f][x] for f in range(4))
        span = slice(x * LANES, (x + 1) * LANES)
        heating, lift = forcing[:LEVELS, span], forcing[LEVELS:, span]
        for f in range(4):
            here = fields[f][x]
            change = v * north_difference(here) + w * level_difference(here)
            if x == 0:
                change = change + u * fields[f][1]
            elif x == ROWS - 1:
                change = change - u * fields[f][x - 1]
            else:
                change = change + u * (fields[f][x + 1] - fields[f][x - 1])
            value = here - 0.1 * change
            if f == 2:
                value = value + 0.2 * (0.5 * th + lift)
            if f == 3:
                value = value + 0.2 * heating
            star[pl.ds((f * ROWS + x) * LEVELS, LEVELS), :] = value


def outer_kernel(
    place,
    state,
    inner,
    x_even,
    x_odd,
    y_even,
    y_odd,
    relayed,
    level_up,
    level_down,
    forward,
    star,
    message,
):
    even_x = place[0] % 2 == 0
    even_y = place[1] % 2 == 0
    shape = (LEVELS, LANES)
    lane = lane_of(shape)

    def beyond(slot):
        first = x_even[pl.ds(slot * LEVELS, LEVELS), :]
        second = x_odd[pl.ds(slot * LEVELS, LEVELS), :]
        return jnp.where(even_x, second, first), jnp.where(even_x, first, second)

    other = jnp.where(far_both(place[0], place[1]), relayed[...], y_odd[0:16, :])
    low_y = jnp.where(even_y, other, y_even[...])
    high_y = jnp.where(even_y, y_even[...], other)
    columns = jnp.transpose(jnp.concatenate([low_y, high_y, jnp.zeros((96, LANES), F32)], axis=0))
    columns = columns[:LEVELS]
    outer_x = [beyond(slot) for slot in range(5)]

    whole = [[None] * ROWS for _ in range(4)]
    side_u = [None] * ROWS
    for x in range(ROWS):
        u, v = plane(state, 0, x), plane(state, 1, x)
        for f in range(4):
            slot = f * ROWS + x
            side = jnp.where(lane == 0, turn(columns, -slot, 1), 0.0)
            side = jnp.where(lane == LANES - 1, -turn(columns, LANES - 1 - 16 - slot, 1), side)
            side = 0.1 * v * side
            if f == 0:
                side_u[x] = side
            value = inner[pl.ds(slot * LEVELS, LEVELS), :] + side
            if x == 0:
                value = value + 0.1 * u * outer_x[f][0]
            if x == ROWS - 1:
                value = value - 0.1 * u * outer_x[f][1]
            whole[f][x] = value
            star[pl.ds(slot * LEVELS, LEVELS), :] = value

    def east_star(which, neighbour):
        u, v, w = (outer_x[f][which] for f in range(3))
        second = outer_x[4][which]
        along = (neighbour - second) if which == 0 else (second - neighbour)
        return u - 0.1 * (u * along + v * north_difference(u) + w * level_difference(u))

    padded = [east_star(0, plane(state, 0, 0))] + whole[0] + [east_star(1, plane(state, 0, ROWS - 1))]
    divergence = []
    extra = [-0.5 * side_u[ROWS - 1], 0.5 * side_u[0]]
    up, down = level_up[...], level_down[...]
    for x in range(ROWS):
        v, w = whole[1][x], whole[2][x]
        upright = up * turn(w, -1, 0) - down * turn(w, 1, 0)
        divergence.append(0.5 * (padded[x + 2] - padded[x]) + 0.5 * north_difference(v) + upright)
        low, high = LOW + x // 2, HIGH + x // 2
        value = jnp.where(lane == low, 0.5 * turn(v, low, 1), extra[x % 2])
        extra[x % 2] = jnp.where(lane == high, -0.5 * turn(v, high + 1, 1), value)
    pieces = [divergence[0], divergence[2], extra[0], divergence[1], divergence[3], extra[1]]
    modal = dot3(parts(forward[...]), parts(jnp.concatenate(pieces, axis=1)))
    for i in range(6):
        message[pl.ds(i, LEVELS, stride=6), :] = modal[:, i * LANES : (i + 1) * LANES]


def decay(rate, square):
    lam = rate + square
    root = jnp.sqrt(lam * (1.0 + lam))
    inverse = 1.0 + 2.0 * lam + 2.0 * root
    return root, inverse, 1.0 / inverse


def squarings(rho, count):
    powers = [rho]
    for _ in range(count):
        powers.append(powers[-1] * powers[-1])
    return powers


def lane_powers(powers, exponent):
    product = None
    for bit in range(6):
        factor = jnp.where((exponent & (1 << bit)) != 0, powers[bit], 1.0)
        product = factor if product is None else product * factor
    return product


def solve_kernel(place, rates, received, basis_high, basis_low, square, local, moments):
    blocks = received.shape[0] // 6
    half_size = blocks * 2
    size = half_size * 2
    lane = lane_of((blocks, LANES))
    ends = (lane == 0) | (lane == LANES - 1)
    even = place[1] < 4
    inside, outside = [], [None, None]
    for h in range(2):
        first, second, extra = (received[pl.ds(3 * h + j, blocks, stride=6), :] for j in range(3))
        first = first + jnp.where(ends & even, turn(extra, 1, 0), 0.0)
        second = second + jnp.where(ends & ~even, turn(extra, -1, 0), 0.0)
        inside.append(jnp.concatenate([first, second], axis=0))
        for r in range(2):
            value = jnp.zeros_like(extra) if outside[r] is None else outside[r]
            for i in range(4):
                at = 4 * h + i
                value = jnp.where(lane == at, turn(extra, at - (HIGH, LOW)[i % 2] - r, 1), value)
            outside[r] = value
    right = jnp.concatenate(inside + [jnp.concatenate(outside, axis=0)], axis=1)
    spectral = dot3((basis_high[...], basis_low[...]), parts(right))
    source = jnp.concatenate([spectral[:, :LANES], spectral[:, LANES : 2 * LANES]], axis=0)
    ext = spectral[:, 2 * LANES :]
    ext = jnp.concatenate([ext, turn(ext, -4, 1)], axis=0)

    rate = rates[place[0]]
    _, _, rho = decay(rate, square[...])
    powers = squarings(rho, 6)
    lane = lane_of((size, LANES))
    ahead, behind = source, source
    for bit in range(6):
        shift = 2 << bit
        ahead = ahead + powers[bit] * jnp.where(lane >= shift, turn(ahead, shift, 1), 0.0)
        behind = behind + powers[bit] * jnp.where(lane < LANES - shift, turn(behind, -shift, 1), 0.0)
    half = lane >> 1
    rising = lane_powers(powers, half)
    falling = lane_powers(powers, 63 - half)
    odd = (lane & 1) != 0
    first = jnp.broadcast_to(ext[:, 0:1], (size, LANES))
    second = jnp.broadcast_to(ext[:, 1:2], (size, LANES))
    border = rho * jnp.where(odd, rising * second, falling * first)
    local[...] = ahead + behind - source + border
    weight = jnp.where((lane == 1) | (lane == 2), powers[6] * rho, 1.0)
    column = jnp.where(lane < 2, turn(rho * ahead, 2, 1), turn(rho * behind, 2, 1)) + ext * weight
    column = jnp.where(lane < 4, column, 0.0)
    across = jnp.transpose(column)[:8]
    for j in range(4):
        moments[pl.ds(j * 8, 8), :] = across


def back_kernel(place, rates, local, moments, basis_high, basis_low, square, square_row, message):
    size = local.shape[0]
    half_size = size // 2
    blocks = half_size // 2
    rate = rates[place[0]]
    even = place[1] < 4
    mine = place[1] & 3
    root, inverse, rho = decay(rate, square_row[...])
    r64 = squarings(rho, 6)[6]
    r128 = r64 * r64
    r256 = r128 * r128
    row = row_of((8, size))
    carry = jnp.zeros((8, size), F32)
    for j in range(4):
        theirs = moments[pl.ds(j * 8, 8), :]
        for offset, values in ((-1, theirs), (3, turn(theirs, half_size, 1))):
            exponent = jnp.where(row < 2, (mine - j + offset) & 7, (j - mine + offset) & 7)
            weight = jnp.where((exponent & 1) != 0, r64, 1.0)
            weight = weight * jnp.where((exponent & 2) != 0, r128, 1.0)
            weight = weight * jnp.where((exponent & 4) != 0, r256, 1.0)
            carry = carry + weight * values
    carry = carry / (1.0 - r256 * r256)
    own = moments[pl.ds(pl.multiple_of(mine * 8, 8), 8), :]
    scale = -1.0 / root[0:1]
    after = scale * (own[0:1] + carry[0:1] * r64[0:1] + carry[2:3] * inverse[0:1])
    before = scale * (own[3:4] + carry[3:4] * r64[0:1] + carry[1:2] * inverse[0:1])
    stacked = jnp.concatenate([carry[0:4], after, before, jnp.zeros((LANES - 6, size), F32)], axis=0)
    columns = jnp.transpose(stacked)

    root, _, rho = decay(rate, square[...])
    powers = squarings(rho, 5)
    lane = lane_of((size, LANES))
    half = lane >> 1
    odd = (lane & 1) != 0
    spread = lambda i: jnp.broadcast_to(columns[:, i : i + 1], (size, LANES))
    total = local[...] + lane_powers(powers, half) * jnp.where(odd, spread(1), spread(0))
    total = total + lane_powers(powers, 63 - half) * jnp.where(odd, spread(3), spread(2))
    total = -total / root
    ext = jnp.where((lane == 4) | (lane == 5), columns, 0.0)
    ext = ext[:half_size] + turn(ext[half_size:], 2, 1)
    pressure = dot3(
        (basis_high[...], basis_low[...]),
        parts(jnp.concatenate([total[:half_size], total[half_size:], ext], axis=1)),
    )
    lane = lane_of((blocks, LANES))
    ends = (lane == 0) | (lane == LANES - 1)
    outside = [pressure[r * blocks : (r + 1) * blocks, 2 * LANES :] for r in range(2)]
    for h in range(2):
        span = slice(h * LANES, (h + 1) * LANES)
        first, second = pressure[:blocks, span], pressure[blocks:, span]
        extra = jnp.where(ends, jnp.where(even, turn(first, -1, 0), turn(second, 1, 0)), 0.0)
        for r in range(2):
            extra = jnp.where(lane == HIGH + r, turn(outside[r], HIGH + r - 4 - 2 * h, 1), extra)
            extra = jnp.where(lane == LOW + r, turn(outside[r], LOW + r - 5 - 2 * h, 1), extra)
        for j, value in enumerate((first, second, extra)):
            message[pl.ds(3 * h + j, blocks, stride=6), :] = value


def final_kernel(received, sent, star, back, rate, out):
    lane = lane_of((LEVELS, LANES))
    row_at = lambda ref, r: ref[pl.ds(3 * (r % 2) + r // 2, LEVELS, stride=6), :]
    p = [row_at(received, r) for r in range(ROWS)]
    extra = [row_at(received, 4), row_at(received, 5)]
    low = [turn(extra[r % 2], -(LOW + r // 2), 1) for r in range(ROWS)]
    high = [turn(extra[r % 2], LANES - 1 - (HIGH + r // 2), 1) for r in range(ROWS)]
    four_rate = 4.0 * rate[...]

    def next_row(r, opposite):
        here = p[r]
        divergence = row_at(sent, r)
        plus = jnp.where(lane < LANES - 2, turn(here, -2, 1), turn(high[r], -1, 1))
        minus = jnp.where(lane > 1, turn(here, 2, 1), turn(low[r], 1, 1))
        return (
            2.0 * here
            - opposite
            + four_rate * here
            + (2.0 * here - plus - minus)
            + 4.0 * divergence
        )

    ends = (lane == 0) | (lane == LANES - 1)
    before = jnp.where(ends, extra[1], next_row(1, p[3]))
    after = jnp.where(ends, extra[0], next_row(2, p[0]))
    padded = [before] + p + [after]
    slopes = [0.5 * (padded[x + 2] - padded[x]) for x in range(ROWS)]
    slopes += [0.5 * north_difference(p[x], low[x], high[x]) for x in range(ROWS)]
    matrix = back[...]
    slope = dot3(parts(matrix), parts(jnp.concatenate(slopes, axis=1)))
    lift = dot3(parts(0.5 * level_difference(matrix)), parts(jnp.concatenate(p, axis=1)))
    for x in range(ROWS):
        take = lambda values, i: values[:, i * LANES : (i + 1) * LANES]
        for f, change in ((0, take(slope, x)), (1, take(slope, ROWS + x)), (2, take(lift, x)), (3, None)):
            value = star[pl.ds((f * ROWS + x) * LEVELS, LEVELS), :]
            if change is not None:
                value = value - change
            out[pl.ds(f * LEVELS * ROWS + x, LEVELS, stride=ROWS), :] = value


def call(kernel, shapes, smem, args, name):
    vmem = pl.BlockSpec(memory_space=pltpu.VMEM)
    scalar = pl.BlockSpec(memory_space=pltpu.SMEM)
    return pl.pallas_call(
        kernel,
        out_shape=[jax.ShapeDtypeStruct(s, F32) for s in shapes],
        in_specs=[scalar] * smem + [vmem] * (len(args) - smem),
        out_specs=[vmem] * len(shapes),
        compiler_params=pltpu.CompilerParams(vmem_limit_bytes=32 * 1024 * 1024),
        name=name,
    )(*args)


def swap(values, axis, odd):
    count = lax.axis_size(axis)
    pairs = []
    for i in range(odd, count + odd, 2):
        pairs += [(i % count, (i + 1) % count), ((i + 1) % count, i % count)]
    return lax.ppermute(values, axis, pairs)


def swap_odd_y(values):
    count_x, count_y = lax.axis_size("gx"), lax.axis_size("gy")
    pairs = []
    for i in range(count_x):
        for j in range(1, count_y + 1, 2):
            one, two = j % count_y, (j + 1) % count_y
            if not far_both(i, one):
                pairs += [(i * count_y + one, i * count_y + two), (i * count_y + two, i * count_y + one)]
    return lax.ppermute(values, ("gx", "gy"), pairs)


def hand_over(values):
    count_x, count_y = lax.axis_size("gx"), lax.axis_size("gy")
    pairs = [
        ((i ^ 1) * count_y + j, i * count_y + j)
        for i in range(count_x)
        for j in range(count_y)
        if far_both(i, j)
    ]
    return lax.ppermute(values, ("gx", "gy"), pairs)


def exchange(values):
    count_x, count_y = lax.axis_size("gx"), lax.axis_size("gy")
    near = count_y // 2
    groups = [[i * count_y + h * near + y for i in range(count_x) for h in range(2)] for y in range(near)]
    shaped = values.reshape(2 * count_x, 1, values.size // (2 * count_x))
    moved = lax.all_to_all(
        shaped, ("gx", "gy"), 0, 0, tiled=True, axis_index_groups=groups
    )
    return moved.reshape(values.shape)


def on_device(
    model_state, density, layer_in, layer_bias, layer_out, mode_forward, mode_back, mode_rate
):
    blocks = lax.axis_size("gx")
    total_east = blocks * ROWS
    place = jnp.stack([lax.axis_index("gx"), lax.axis_index("gy")]).astype(jnp.int32)
    state = model_state.reshape(4 * LEVELS * ROWS, LANES)
    basis, square = east_tables(total_east // 2, blocks)
    square = np.concatenate([square, square])
    forward_high, forward_low = split_table(basis)
    back_high, back_low = split_table(np.ascontiguousarray(basis.T))
    square_wide = np.ascontiguousarray(np.broadcast_to(square[:, None], (total_east, LANES)))
    square_row = np.ascontiguousarray(np.broadcast_to(square[None, :], (8, total_east)))

    x_even, x_odd, y_even, y_odd = call(
        edges_kernel,
        [(5 * LEVELS + 16, LANES), (5 * LEVELS, LANES)] + [(16, LANES)] * 2,
        1,
        [place, state],
        "edges",
    )
    got_x_even = swap(x_even, "gx", 0)
    y_both = jnp.concatenate([y_odd, got_x_even[5 * LEVELS :]], axis=0)
    y_both, x_odd, y_even = lax.optimization_barrier((y_both, x_odd, y_even))
    got_y_odd = swap_odd_y(y_both)
    got_x_odd = swap(x_odd, "gx", 1)
    got_y_even = swap(y_even, "gy", 0)
    (inner,) = call(
        inner_kernel,
        [(16 * LEVELS, LANES)],
        0,
        [state, layer_in.T, layer_bias[:, None], layer_out.T],
        "inner",
    )
    inner, got_y_odd = lax.optimization_barrier((inner, got_y_odd))
    relayed = hand_over(got_y_odd[16:])
    zero = jnp.zeros((1,), F32)
    level_up = jnp.concatenate([0.5 * density[1:] / density[:-1], zero])
    level_down = jnp.concatenate([zero, 0.5 * density[:-1] / density[1:]])
    star, message = call(
        outer_kernel,
        [(16 * LEVELS, LANES), (blocks * 6, LANES)],
        1,
        [
            place,
            state,
            inner,
            got_x_even,
            got_x_odd,
            got_y_even,
            got_y_odd,
            relayed,
            level_up[:, None],
            level_down[:, None],
            mode_forward,
        ],
        "outer",
    )
    modal = exchange(message)
    local, moments = call(
        solve_kernel,
        [(total_east, LANES), (32, total_east)],
        2,
        [place, mode_rate, modal, forward_high, forward_low, square_wide],
        "solve",
    )
    moments = lax.all_to_all(
        moments.reshape(4, 8, total_east),
        "gy",
        0,
        0,
        tiled=True,
        axis_index_groups=[[0, 1, 2, 3], [4, 5, 6, 7]],
    ).reshape(32, total_east)
    (reply,) = call(
        back_kernel,
        [(blocks * 6, LANES)],
        2,
        [place, mode_rate, local, moments, back_high, back_low, square_wide, square_row],
        "back",
    )
    pressure = exchange(reply)
    (out,) = call(
        final_kernel,
        [(4 * LEVELS * ROWS, LANES)],
        0,
        [pressure, message, star, mode_back, mode_rate[:, None]],
        "final",
    )
    return out.reshape(model_state.shape)


def solution(mesh):
    return jax.shard_map(
        on_device,
        mesh=mesh,
        in_specs=(P(None, None, "gx", "gy"), P(), P(), P(), P(), P(), P(), P()),
        out_specs=P(None, None, "gx", "gy"),
        check_vma=False,
    )
```

```python
import math

import jax
import jax.numpy as jnp
import ml_dtypes
import numpy as np
from jax import lax
from jax.experimental import pallas as pl
from jax.experimental.pallas import tpu as pltpu
from jax.sharding import PartitionSpec as P

F32 = jnp.float32
BF16 = jnp.bfloat16
LEVELS = 64
ROWS = 4
LANES = 128
LOW = 16
HIGH = 32


def split_table(table):
    high = table.astype(np.float32).astype(ml_dtypes.bfloat16)
    low = (table - high.astype(np.float64)).astype(np.float32).astype(ml_dtypes.bfloat16)
    return high, low


def east_tables(total, blocks):
    rows = total // blocks
    x = (np.arange(rows)[:, None] + rows * np.arange(blocks)[None, :]).reshape(-1)
    k = np.arange(total)
    angle = 2.0 * math.pi * ((k[:, None] * x[None, :]) % total) / total
    basis = np.where((k <= total // 2)[:, None], np.cos(angle), np.sin(angle))
    scale = np.where((k == 0) | (k == total // 2), 1.0, math.sqrt(2.0)) / math.sqrt(total)
    basis = basis * scale[:, None]
    square = np.sin(math.pi * k / total) ** 2
    return basis, square.astype(np.float32)


def lane_of(shape):
    return lax.broadcasted_iota(jnp.int32, shape, len(shape) - 1)


def row_of(shape):
    return lax.broadcasted_iota(jnp.int32, shape, 0)


def turn(values, shift, axis):
    size = values.shape[axis]
    return pltpu.roll(values, shift % size, axis) if shift % size else values


def parts(values):
    high = values.astype(BF16)
    return high, (values - high.astype(F32)).astype(BF16)


def dot3(left, right):
    dot = lambda a, b: jnp.dot(a, b, preferred_element_type=F32)
    return dot(left[0], right[0]) + (dot(left[0], right[1]) + dot(left[1], right[0]))


def level_difference(values):
    row = row_of(values.shape)
    last = values.shape[0] - 1
    upper = jnp.where(row < last, turn(values, -1, 0), 0.0)
    lower = jnp.where(row > 0, turn(values, 1, 0), 0.0)
    return upper - lower


def north_difference(values, low=0.0, high=0.0):
    lane = lane_of(values.shape)
    after = jnp.where(lane < LANES - 1, turn(values, -1, 1), high)
    before = jnp.where(lane > 0, turn(values, 1, 1), low)
    return after - before


def plane(ref, field, x):
    return ref[pl.ds((field * ROWS + x) * LEVELS, LEVELS), :]


def far_both(gx, gy):
    return ((gx % 16 == 0) | (gx % 16 == 15)) & ((gy % 4 == 0) | (gy % 4 == 3))


def edges_kernel(place, state, planes, x_even, x_odd, y_even, y_odd):
    even_x = place[0] % 2 == 0
    even_y = place[1] % 2 == 0
    size = LEVELS * ROWS
    lane = lane_of((LEVELS, LANES))
    gathered = jnp.zeros((LEVELS, LANES), F32)
    for field in range(4):
        values = [state[pl.ds(field * size + x, LEVELS, stride=ROWS), :] for x in range(ROWS)]
        for x in range(ROWS):
            slot = field * ROWS + x
            planes[pl.ds(slot * LEVELS, LEVELS), :] = values[x]
            gathered = jnp.where(lane == slot, turn(values[x], slot, 1), gathered)
            gathered = jnp.where(lane == 16 + slot, turn(values[x], 17 + slot, 1), gathered)
        for slot, depth in ((field, 0), (4, 1)) if field == 0 else ((field, 0),):
            span = pl.ds(slot * LEVELS, LEVELS)
            low, high = values[depth], values[ROWS - 1 - depth]
            x_even[span, :] = jnp.where(even_x, high, low)
            x_odd[span, :] = jnp.where(even_x, low, high)
    flat = jnp.transpose(jnp.concatenate([gathered, jnp.zeros_like(gathered)], axis=0))
    low, high = flat[0:16], flat[16:32]
    y_even[...] = jnp.where(even_y, high, low)
    y_odd[...] = jnp.where(even_y, low, high)
    x_even[pl.ds(5 * LEVELS, 16), :] = jnp.where(even_y, low, high)


def column_of(row):
    return jnp.transpose(jnp.broadcast_to(row, (LANES, LANES)))


def inner_kernel(
    place,
    state,
    vectors,
    bias,
    square,
    square_row,
    layer_in,
    layer_out,
    star,
    by_level,
    by_wave,
    by_block,
):
    fields = [[plane(state, f, x) for x in range(ROWS)] for f in range(4)]
    tall = column_of(vectors[...])
    rate, density = tall[:LEVELS], tall[LEVELS:]
    row = row_of((LEVELS, LANES))
    by_level[pl.ds(0, LEVELS), :] = rate
    by_level[pl.ds(LEVELS, LEVELS), :] = jnp.where(
        row < LEVELS - 1, 0.5 * turn(density, -1, 0) / density, 0.0
    )
    by_level[pl.ds(2 * LEVELS, LEVELS), :] = jnp.where(row > 0, 0.5 * turn(density, 1, 0) / density, 0.0)
    own = by_level[pl.ds(place[0], 1), :]

    root, _, rho = decay(own, square[...])
    powers = squarings(rho, 6)
    half = lane_of((LANES, LANES)) >> 1
    rising = lane_powers(powers, half)
    falling = lane_powers(powers, 63 - half)
    for i, value in enumerate(powers + [rising, falling, -1.0 / root]):
        by_wave[pl.ds(i * LANES, LANES), :] = value

    root, inverse, rho = decay(jnp.concatenate([own, own], axis=1), square_row[...])
    r64 = squarings(rho, 6)[6]
    r128 = r64 * r64
    r256 = r128 * r128
    images = 1.0 / (1.0 - r256 * r256)
    mine = place[1] & 3
    row = row_of(rho.shape)
    for j in range(4):
        for i, offset in enumerate((-1, 3)):
            exponent = jnp.where(row < 2, (mine - j + offset) & 7, (j - mine + offset) & 7)
            weight = jnp.where((exponent & 1) != 0, r64, 1.0)
            weight = weight * jnp.where((exponent & 2) != 0, r128, 1.0)
            weight = weight * jnp.where((exponent & 4) != 0, r256, 1.0)
            by_block[pl.ds((2 * j + i) * 8, 8), :] = weight * images
    scale = -1.0 / root
    by_block[pl.ds(64, 8), :] = jnp.where(row == 0, scale, jnp.where(row == 1, scale * r64, scale * inverse))

    for x in range(ROWS):
        u, v, w, th = (fields[f][x] for f in range(4))
        for f in range(4):
            here = fields[f][x]
            change = v * north_difference(here) + w * level_difference(here)
            if x == 0:
                change = change + u * fields[f][1]
            elif x == ROWS - 1:
                change = change - u * fields[f][x - 1]
            else:
                change = change + u * (fields[f][x + 1] - fields[f][x - 1])
            value = here - 0.1 * change
            if f == 2:
                value = value + 0.1 * th
            star[pl.ds((f * ROWS + x) * LEVELS, LEVELS), :] = value

    columns = jnp.concatenate(
        [jnp.concatenate([fields[f][x] for f in range(4)], axis=0).astype(BF16) for x in range(ROWS)],
        axis=1,
    )
    first = (((0,), (0,)), ((), ()))
    shift = jnp.concatenate([column_of(bias[:, :LANES]), column_of(bias[:, LANES:])], axis=0)
    before = lax.dot_general(layer_in[...], columns, first, preferred_element_type=F32)
    before = before + jnp.concatenate([shift] * ROWS, axis=1)
    hidden = (before * (1.0 / (1.0 + jnp.exp(-before)))).astype(BF16)
    forcing = lax.dot_general(layer_out[...], hidden, first, preferred_element_type=F32)
    for x in range(ROWS):
        span = slice(x * LANES, (x + 1) * LANES)
        for f, part in ((2, forcing[LEVELS:, span]), (3, forcing[:LEVELS, span])):
            at = pl.ds((f * ROWS + x) * LEVELS, LEVELS)
            star[at, :] = star[at, :] + 0.2 * part


def outer_kernel(
    place,
    state,
    inner,
    x_even,
    x_odd,
    y_even,
    y_odd,
    relayed,
    by_level,
    forward,
    star,
    message,
):
    even_x = place[0] % 2 == 0
    even_y = place[1] % 2 == 0
    shape = (LEVELS, LANES)
    lane = lane_of(shape)

    def beyond(slot):
        first = x_even[pl.ds(slot * LEVELS, LEVELS), :]
        second = x_odd[pl.ds(slot * LEVELS, LEVELS), :]
        return jnp.where(even_x, second, first), jnp.where(even_x, first, second)

    other = jnp.where(far_both(place[0], place[1]), relayed[...], y_odd[0:16, :])
    low_y = jnp.where(even_y, other, y_even[...])
    high_y = jnp.where(even_y, y_even[...], other)
    columns = jnp.transpose(jnp.concatenate([low_y, high_y, jnp.zeros((96, LANES), F32)], axis=0))
    columns = columns[:LEVELS]
    outer_x = [beyond(slot) for slot in range(5)]

    whole = [[None] * ROWS for _ in range(4)]
    side_u = [None] * ROWS
    for x in range(ROWS):
        u, v = plane(state, 0, x), plane(state, 1, x)
        for f in range(4):
            slot = f * ROWS + x
            side = jnp.where(lane == 0, turn(columns, -slot, 1), 0.0)
            side = jnp.where(lane == LANES - 1, -turn(columns, LANES - 1 - 16 - slot, 1), side)
            side = 0.1 * v * side
            if f == 0:
                side_u[x] = side
            value = inner[pl.ds(slot * LEVELS, LEVELS), :] + side
            if x == 0:
                value = value + 0.1 * u * outer_x[f][0]
            if x == ROWS - 1:
                value = value - 0.1 * u * outer_x[f][1]
            whole[f][x] = value
            star[pl.ds(slot * LEVELS, LEVELS), :] = value

    def east_star(which, neighbour):
        u, v, w = (outer_x[f][which] for f in range(3))
        second = outer_x[4][which]
        along = (neighbour - second) if which == 0 else (second - neighbour)
        return u - 0.1 * (u * along + v * north_difference(u) + w * level_difference(u))

    padded = [east_star(0, plane(state, 0, 0))] + whole[0] + [east_star(1, plane(state, 0, ROWS - 1))]
    divergence = []
    extra = [-0.5 * side_u[ROWS - 1], 0.5 * side_u[0]]
    up, down = by_level[pl.ds(LEVELS, LEVELS), :], by_level[pl.ds(2 * LEVELS, LEVELS), :]
    for x in range(ROWS):
        v, w = whole[1][x], whole[2][x]
        upright = up * turn(w, -1, 0) - down * turn(w, 1, 0)
        divergence.append(0.5 * (padded[x + 2] - padded[x]) + 0.5 * north_difference(v) + upright)
        low, high = LOW + x // 2, HIGH + x // 2
        value = jnp.where(lane == low, 0.5 * turn(v, low, 1), extra[x % 2])
        extra[x % 2] = jnp.where(lane == high, -0.5 * turn(v, high + 1, 1), value)
    pieces = [divergence[0], divergence[2], extra[0], divergence[1], divergence[3], extra[1]]
    modal = dot3(parts(forward[...]), parts(jnp.concatenate(pieces, axis=1)))
    for i in range(6):
        message[pl.ds(i, LEVELS, stride=6), :] = modal[:, i * LANES : (i + 1) * LANES]


def decay(rate, square):
    lam = rate + square
    root = jnp.sqrt(lam * (1.0 + lam))
    inverse = 1.0 + 2.0 * lam + 2.0 * root
    return root, inverse, 1.0 / inverse


def squarings(rho, count):
    powers = [rho]
    for _ in range(count):
        powers.append(powers[-1] * powers[-1])
    return powers


def lane_powers(powers, exponent):
    product = None
    for bit in range(6):
        factor = jnp.where((exponent & (1 << bit)) != 0, powers[bit], 1.0)
        product = factor if product is None else product * factor
    return product


def solve_kernel(place, received, basis_high, basis_low, by_wave, local, moments):
    blocks = received.shape[0] // 6
    half_size = blocks * 2
    size = half_size * 2
    lane = lane_of((blocks, LANES))
    ends = (lane == 0) | (lane == LANES - 1)
    even = place[1] < 4
    inside, outside = [], [None, None]
    for h in range(2):
        first, second, extra = (received[pl.ds(3 * h + j, blocks, stride=6), :] for j in range(3))
        first = first + jnp.where(ends & even, turn(extra, 1, 0), 0.0)
        second = second + jnp.where(ends & ~even, turn(extra, -1, 0), 0.0)
        inside.append(jnp.concatenate([first, second], axis=0))
        for r in range(2):
            value = jnp.zeros_like(extra) if outside[r] is None else outside[r]
            for i in range(4):
                at = 4 * h + i
                value = jnp.where(lane == at, turn(extra, at - (HIGH, LOW)[i % 2] - r, 1), value)
            outside[r] = value
    right = jnp.concatenate(inside + [jnp.concatenate(outside, axis=0)], axis=1)
    spectral = dot3((basis_high[...], basis_low[...]), parts(right))
    source = jnp.concatenate([spectral[:, :LANES], spectral[:, LANES : 2 * LANES]], axis=0)
    ext = spectral[:, 2 * LANES :]
    ext = jnp.concatenate([ext, turn(ext, -4, 1)], axis=0)

    wave = lambda i: jnp.concatenate([by_wave[pl.ds(i * LANES, LANES), :]] * 2, axis=0)
    powers = [wave(i) for i in range(7)]
    rho = powers[0]
    lane = lane_of((size, LANES))
    ahead, behind = source, source
    for bit in range(6):
        shift = 2 << bit
        ahead = ahead + powers[bit] * jnp.where(lane >= shift, turn(ahead, shift, 1), 0.0)
        behind = behind + powers[bit] * jnp.where(lane < LANES - shift, turn(behind, -shift, 1), 0.0)
    odd = (lane & 1) != 0
    first = jnp.broadcast_to(ext[:, 0:1], (size, LANES))
    second = jnp.broadcast_to(ext[:, 1:2], (size, LANES))
    border = rho * jnp.where(odd, wave(7) * second, wave(8) * first)
    local[...] = ahead + behind - source + border
    weight = jnp.where((lane == 1) | (lane == 2), powers[6] * rho, 1.0)
    column = jnp.where(lane < 2, turn(rho * ahead, 2, 1), turn(rho * behind, 2, 1)) + ext * weight
    column = jnp.where(lane < 4, column, 0.0)
    across = jnp.transpose(column)[:8]
    for j in range(4):
        moments[pl.ds(j * 8, 8), :] = across


def back_kernel(place, local, moments, basis_high, basis_low, by_wave, by_block, message):
    size = local.shape[0]
    half_size = size // 2
    blocks = half_size // 2
    even = place[1] < 4
    mine = place[1] & 3
    carry = jnp.zeros((8, size), F32)
    for j in range(4):
        theirs = moments[pl.ds(j * 8, 8), :]
        carry = carry + by_block[pl.ds(16 * j, 8), :] * theirs
        carry = carry + by_block[pl.ds(16 * j + 8, 8), :] * turn(theirs, half_size, 1)
    own = moments[pl.ds(pl.multiple_of(mine * 8, 8), 8), :]
    scale, by_r64, by_inverse = (by_block[pl.ds(64 + i, 1), :] for i in range(3))
    after = scale * own[0:1] + by_r64 * carry[0:1] + by_inverse * carry[2:3]
    before = scale * own[3:4] + by_r64 * carry[3:4] + by_inverse * carry[1:2]
    stacked = jnp.concatenate([carry[0:4], after, before, jnp.zeros((LANES - 6, size), F32)], axis=0)
    columns = jnp.transpose(stacked)

    wave = lambda i: jnp.concatenate([by_wave[pl.ds(i * LANES, LANES), :]] * 2, axis=0)
    lane = lane_of((size, LANES))
    odd = (lane & 1) != 0
    spread = lambda i: jnp.broadcast_to(columns[:, i : i + 1], (size, LANES))
    total = local[...] + wave(7) * jnp.where(odd, spread(1), spread(0))
    total = total + wave(8) * jnp.where(odd, spread(3), spread(2))
    total = total * wave(9)
    ext = jnp.where((lane == 4) | (lane == 5), columns, 0.0)
    ext = ext[:half_size] + turn(ext[half_size:], 2, 1)
    pressure = dot3(
        (basis_high[...], basis_low[...]),
        parts(jnp.concatenate([total[:half_size], total[half_size:], ext], axis=1)),
    )
    lane = lane_of((blocks, LANES))
    ends = (lane == 0) | (lane == LANES - 1)
    outside = [pressure[r * blocks : (r + 1) * blocks, 2 * LANES :] for r in range(2)]
    for h in range(2):
        span = slice(h * LANES, (h + 1) * LANES)
        first, second = pressure[:blocks, span], pressure[blocks:, span]
        extra = jnp.where(ends, jnp.where(even, turn(first, -1, 0), turn(second, 1, 0)), 0.0)
        for r in range(2):
            extra = jnp.where(lane == HIGH + r, turn(outside[r], HIGH + r - 4 - 2 * h, 1), extra)
            extra = jnp.where(lane == LOW + r, turn(outside[r], LOW + r - 5 - 2 * h, 1), extra)
        for j, value in enumerate((first, second, extra)):
            message[pl.ds(3 * h + j, blocks, stride=6), :] = value


def final_kernel(received, sent, star, back, by_level, out):
    lane = lane_of((LEVELS, LANES))
    row_at = lambda ref, r: ref[pl.ds(3 * (r % 2) + r // 2, LEVELS, stride=6), :]
    p = [row_at(received, r) for r in range(ROWS)]
    extra = [row_at(received, 4), row_at(received, 5)]
    low = [turn(extra[r % 2], -(LOW + r // 2), 1) for r in range(ROWS)]
    high = [turn(extra[r % 2], LANES - 1 - (HIGH + r // 2), 1) for r in range(ROWS)]
    four_rate = 4.0 * by_level[pl.ds(0, LEVELS), :]

    def next_row(r, opposite):
        here = p[r]
        divergence = row_at(sent, r)
        plus = jnp.where(lane < LANES - 2, turn(here, -2, 1), turn(high[r], -1, 1))
        minus = jnp.where(lane > 1, turn(here, 2, 1), turn(low[r], 1, 1))
        return (
            2.0 * here
            - opposite
            + four_rate * here
            + (2.0 * here - plus - minus)
            + 4.0 * divergence
        )

    ends = (lane == 0) | (lane == LANES - 1)
    before = jnp.where(ends, extra[1], next_row(1, p[3]))
    after = jnp.where(ends, extra[0], next_row(2, p[0]))
    padded = [before] + p + [after]
    slopes = [0.5 * (padded[x + 2] - padded[x]) for x in range(ROWS)]
    slopes += [0.5 * north_difference(p[x], low[x], high[x]) for x in range(ROWS)]
    matrix = back[...]
    slope = dot3(parts(matrix), parts(jnp.concatenate(slopes, axis=1)))
    lift = dot3(parts(0.5 * level_difference(matrix)), parts(jnp.concatenate(p, axis=1)))
    for x in range(ROWS):
        take = lambda values, i: values[:, i * LANES : (i + 1) * LANES]
        for f, change in ((0, take(slope, x)), (1, take(slope, ROWS + x)), (2, take(lift, x)), (3, None)):
            value = star[pl.ds((f * ROWS + x) * LEVELS, LEVELS), :]
            if change is not None:
                value = value - change
            out[pl.ds(f * LEVELS * ROWS + x, LEVELS, stride=ROWS), :] = value


def call(kernel, shapes, args, name, scalars=1, cost=None):
    vmem = pl.BlockSpec(memory_space=pltpu.VMEM)
    scalar = pl.BlockSpec(memory_space=pltpu.SMEM)
    return pl.pallas_call(
        kernel,
        out_shape=[jax.ShapeDtypeStruct(s, F32) for s in shapes],
        in_specs=[scalar] * scalars + [vmem] * (len(args) - scalars),
        out_specs=[vmem] * len(shapes),
        compiler_params=pltpu.CompilerParams(vmem_limit_bytes=32 * 1024 * 1024),
        name=name,
        cost_estimate=cost,
    )(*args)


def swap(values, axis, odd):
    count = lax.axis_size(axis)
    pairs = []
    for i in range(odd, count + odd, 2):
        pairs += [(i % count, (i + 1) % count), ((i + 1) % count, i % count)]
    return lax.ppermute(values, axis, pairs)


def swap_odd_y(values):
    count_x, count_y = lax.axis_size("gx"), lax.axis_size("gy")
    pairs = []
    for i in range(count_x):
        for j in range(1, count_y + 1, 2):
            one, two = j % count_y, (j + 1) % count_y
            if not far_both(i, one):
                pairs += [(i * count_y + one, i * count_y + two), (i * count_y + two, i * count_y + one)]
    return lax.ppermute(values, ("gx", "gy"), pairs)


def hand_over(values):
    count_x, count_y = lax.axis_size("gx"), lax.axis_size("gy")
    pairs = [
        ((i ^ 1) * count_y + j, i * count_y + j)
        for i in range(count_x)
        for j in range(count_y)
        if far_both(i, j)
    ]
    return lax.ppermute(values, ("gx", "gy"), pairs)


def exchange(values):
    count_x, count_y = lax.axis_size("gx"), lax.axis_size("gy")
    near = count_y // 2
    groups = [[i * count_y + h * near + y for i in range(count_x) for h in range(2)] for y in range(near)]
    shaped = values.reshape(2 * count_x, 1, values.size // (2 * count_x))
    moved = lax.all_to_all(
        shaped, ("gx", "gy"), 0, 0, tiled=True, axis_index_groups=groups
    )
    return moved.reshape(values.shape)


def on_device(
    model_state, density, layer_in, layer_bias, layer_out, mode_forward, mode_back, mode_rate
):
    blocks = lax.axis_size("gx")
    total_east = blocks * ROWS
    place = jnp.stack([lax.axis_index("gx"), lax.axis_index("gy")]).astype(jnp.int32)
    state = model_state.reshape(4 * LEVELS * ROWS, LANES)
    basis, square = east_tables(total_east // 2, blocks)
    forward_high, forward_low = split_table(basis)
    back_high, back_low = split_table(np.ascontiguousarray(basis.T))
    square_wide = np.ascontiguousarray(np.broadcast_to(square[:, None], (total_east // 2, LANES)))
    square_row = np.ascontiguousarray(np.broadcast_to(np.concatenate([square, square]), (8, total_east)))

    planes, x_even, x_odd, y_even, y_odd = call(
        edges_kernel,
        [(16 * LEVELS, LANES)] + [(5 * LEVELS + 16, LANES), (5 * LEVELS, LANES)] + [(16, LANES)] * 2,
        [place, state],
        "edges",
    )
    got_x_even = swap(x_even, "gx", 0)
    y_both = jnp.concatenate([y_odd, got_x_even[5 * LEVELS :]], axis=0)
    y_both, x_odd, y_even = lax.optimization_barrier((y_both, x_odd, y_even))
    got_y_odd = swap_odd_y(y_both)
    got_x_odd = swap(x_odd, "gx", 1)
    got_y_even = swap(y_even, "gy", 0)
    inner, by_level, by_wave, by_block = call(
        inner_kernel,
        [(16 * LEVELS, LANES), (3 * LEVELS, LANES), (10 * LANES, LANES), (72, total_east)],
        [
            place,
            planes,
            jnp.concatenate([mode_rate, density])[None, :],
            layer_bias[None, :],
            square_wide,
            square_row,
            layer_in,
            layer_out,
        ],
        "inner",
        cost=pl.CostEstimate(flops=10**10, transcendentals=0, bytes_accessed=2**24),
    )
    inner, got_y_odd = lax.optimization_barrier((inner, got_y_odd))
    relayed = hand_over(got_y_odd[16:])
    star, message = call(
        outer_kernel,
        [(16 * LEVELS, LANES), (blocks * 6, LANES)],
        [
            place,
            planes,
            inner,
            got_x_even,
            got_x_odd,
            got_y_even,
            got_y_odd,
            relayed,
            by_level,
            mode_forward,
        ],
        "outer",
    )
    modal = exchange(message)
    local, moments = call(
        solve_kernel,
        [(total_east, LANES), (32, total_east)],
        [place, modal, forward_high, forward_low, by_wave],
        "solve",
    )
    moments = lax.all_to_all(
        moments.reshape(4, 8, total_east),
        "gy",
        0,
        0,
        tiled=True,
        axis_index_groups=[[0, 1, 2, 3], [4, 5, 6, 7]],
    ).reshape(32, total_east)
    (reply,) = call(
        back_kernel,
        [(blocks * 6, LANES)],
        [place, local, moments, back_high, back_low, by_wave, by_block],
        "back",
    )
    pressure = exchange(reply)
    (out,) = call(
        final_kernel,
        [(4 * LEVELS * ROWS, LANES)],
        [pressure, message, star, mode_back, by_level],
        "final",
        scalars=0,
    )
    return out.reshape(model_state.shape)


def solution(mesh):
    return jax.shard_map(
        on_device,
        mesh=mesh,
        in_specs=(P(None, None, "gx", "gy"), P(), P(), P(), P(), P(), P(), P()),
        out_specs=P(None, None, "gx", "gy"),
        check_vma=False,
    )
```

```python
import math

import jax
import jax.numpy as jnp
import ml_dtypes
import numpy as np
from jax import lax
from jax.experimental import pallas as pl
from jax.experimental.pallas import tpu as pltpu
from jax.sharding import PartitionSpec as P

F32 = jnp.float32
BF16 = jnp.bfloat16
LEVELS = 64
ROWS = 4
LANES = 128
LOW = 16
HIGH = 32


def split_table(table):
    high = table.astype(np.float32).astype(ml_dtypes.bfloat16)
    low = (table - high.astype(np.float64)).astype(np.float32).astype(ml_dtypes.bfloat16)
    return high, low


def east_tables(total, blocks):
    rows = total // blocks
    x = (np.arange(rows)[:, None] + rows * np.arange(blocks)[None, :]).reshape(-1)
    k = np.arange(total)
    angle = 2.0 * math.pi * ((k[:, None] * x[None, :]) % total) / total
    basis = np.where((k <= total // 2)[:, None], np.cos(angle), np.sin(angle))
    scale = np.where((k == 0) | (k == total // 2), 1.0, math.sqrt(2.0)) / math.sqrt(total)
    basis = basis * scale[:, None]
    square = np.sin(math.pi * k / total) ** 2
    return basis, square.astype(np.float32)


def lane_of(shape):
    return lax.broadcasted_iota(jnp.int32, shape, len(shape) - 1)


def row_of(shape):
    return lax.broadcasted_iota(jnp.int32, shape, 0)


def turn(values, shift, axis):
    size = values.shape[axis]
    return pltpu.roll(values, shift % size, axis) if shift % size else values


def parts(values):
    high = values.astype(BF16)
    return high, (values - high.astype(F32)).astype(BF16)


def dot3(left, right):
    dot = lambda a, b: jnp.dot(a, b, preferred_element_type=F32)
    return dot(left[0], right[0]) + (dot(left[0], right[1]) + dot(left[1], right[0]))


def level_difference(values):
    row = row_of(values.shape)
    last = values.shape[0] - 1
    upper = jnp.where(row < last, turn(values, -1, 0), 0.0)
    lower = jnp.where(row > 0, turn(values, 1, 0), 0.0)
    return upper - lower


def north_difference(values, low=0.0, high=0.0):
    lane = lane_of(values.shape)
    after = jnp.where(lane < LANES - 1, turn(values, -1, 1), high)
    before = jnp.where(lane > 0, turn(values, 1, 1), low)
    return after - before


def plane(ref, field, x):
    return ref[pl.ds((field * ROWS + x) * LEVELS, LEVELS), :]


def far_both(gx, gy):
    return ((gx % 16 == 0) | (gx % 16 == 15)) & ((gy % 4 == 0) | (gy % 4 == 3))


def edges_kernel(place, state, planes, x_even, x_odd, y_even, y_odd, flat):
    even_x = place[0] % 2 == 0
    even_y = place[1] % 2 == 0
    size = LEVELS * ROWS
    lane = lane_of((LEVELS, LANES))
    gathered = jnp.zeros((LEVELS, LANES), F32)
    for field in range(4):
        values = [state[pl.ds(field * size + x, LEVELS, stride=ROWS), :] for x in range(ROWS)]
        for x in range(ROWS):
            slot = field * ROWS + x
            planes[pl.ds(slot * LEVELS, LEVELS), :] = values[x]
            gathered = jnp.where(lane >> 1 == slot, turn(values[x], 2 * slot + 1, 1), gathered)
        for slot, depth in ((field, 0), (4, 1)) if field == 0 else ((field, 0),):
            span = pl.ds(slot * LEVELS, LEVELS)
            low, high = values[depth], values[ROWS - 1 - depth]
            x_even[span, :] = jnp.where(even_x, high, low)
            x_odd[span, :] = jnp.where(even_x, low, high)
    flat[...] = jnp.transpose(jnp.concatenate([gathered, jnp.zeros_like(gathered)], axis=0))
    high, low = flat[pl.ds(0, 16, stride=2), :], flat[pl.ds(1, 16, stride=2), :]
    y_even[...] = jnp.where(even_y, high, low)
    y_odd[...] = jnp.where(even_y, low, high)
    x_even[pl.ds(5 * LEVELS, 16), :] = jnp.zeros((16, LANES), F32)


def column_of(row):
    return jnp.transpose(jnp.broadcast_to(row, (LANES, LANES)))


def inner_kernel(
    state,
    vectors,
    layer_in,
    layer_out,
    star,
    by_level,
):
    fields = [[plane(state, f, x) for x in range(ROWS)] for f in range(4)]
    tall = column_of(vectors[:, :LANES])
    rate, density = tall[:LEVELS], tall[LEVELS:]
    row = row_of((LEVELS, LANES))
    by_level[pl.ds(0, LEVELS), :] = rate
    by_level[pl.ds(LEVELS, LEVELS), :] = jnp.where(
        row < LEVELS - 1, 0.5 * turn(density, -1, 0) / density, 0.0
    )
    by_level[pl.ds(2 * LEVELS, LEVELS), :] = jnp.where(row > 0, 0.5 * turn(density, 1, 0) / density, 0.0)
    for x in range(ROWS):
        u, v, w, th = (fields[f][x] for f in range(4))
        for f in range(4):
            here = fields[f][x]
            change = v * north_difference(here) + w * level_difference(here)
            if x == 0:
                change = change + u * fields[f][1]
            elif x == ROWS - 1:
                change = change - u * fields[f][x - 1]
            else:
                change = change + u * (fields[f][x + 1] - fields[f][x - 1])
            value = here - 0.1 * change
            if f == 2:
                value = value + 0.1 * th
            star[pl.ds((f * ROWS + x) * LEVELS, LEVELS), :] = value

    columns = jnp.concatenate(
        [jnp.concatenate([fields[f][x] for f in range(4)], axis=0).astype(BF16) for x in range(ROWS)],
        axis=1,
    )
    first = (((0,), (0,)), ((), ()))
    shift = [column_of(vectors[:, i * LANES : (i + 1) * LANES]) for i in (1, 2)]
    shift = jnp.concatenate(shift, axis=0)
    before = lax.dot_general(layer_in[...], columns, first, preferred_element_type=F32)
    before = before + jnp.concatenate([shift] * ROWS, axis=1)
    hidden = (before * (1.0 / (1.0 + jnp.exp(-before)))).astype(BF16)
    forcing = lax.dot_general(layer_out[...], hidden, first, preferred_element_type=F32)
    for x in range(ROWS):
        span = slice(x * LANES, (x + 1) * LANES)
        for f, part in ((2, forcing[LEVELS:, span]), (3, forcing[:LEVELS, span])):
            at = pl.ds((f * ROWS + x) * LEVELS, LEVELS)
            star[at, :] = star[at, :] + 0.2 * part


def side_terms(state, edge, low):
    u, v, w = (edge[pl.ds(f * LEVELS, LEVELS), :] for f in range(3))
    second = edge[pl.ds(4 * LEVELS, LEVELS), :]
    own = jnp.where(low, plane(state, 0, 0), plane(state, 0, ROWS - 1))
    sign = jnp.where(low, 0.1, -0.1)
    adds = [sign * own * edge[pl.ds(f * LEVELS, LEVELS), :] for f in range(4)]
    along = u * (own - second)
    beyond = u - (sign * along + 0.1 * (v * north_difference(u) + w * level_difference(u)))
    return adds, beyond


def side_kernel(place, state, x_odd, by_level, square, square_row, terms, by_wave, by_block):
    adds, beyond = side_terms(state, x_odd, place[0] % 2 == 0)
    for i, value in enumerate(adds + [beyond]):
        terms[pl.ds(i * LEVELS, LEVELS), :] = value
    own = by_level[pl.ds(place[0], 1), :]

    root, _, rho = decay(own, square[...])
    powers = squarings(rho, 6)
    half = lane_of((LANES, LANES)) >> 1
    rising = lane_powers(powers, half)
    falling = lane_powers(powers, 63 - half)
    for i, value in enumerate(powers + [rising, falling, -1.0 / root]):
        by_wave[pl.ds(i * LANES, LANES), :] = value

    root, inverse, rho = decay(jnp.concatenate([own, own], axis=1), square_row[...])
    r64 = squarings(rho, 6)[6]
    r128 = r64 * r64
    r256 = r128 * r128
    images = 1.0 / (1.0 - r256 * r256)
    mine = place[1] & 3
    row = row_of(rho.shape)
    for j in range(4):
        for i, offset in enumerate((-1, 3)):
            exponent = jnp.where(row < 2, (mine - j + offset) & 7, (j - mine + offset) & 7)
            weight = jnp.where((exponent & 1) != 0, r64, 1.0)
            weight = weight * jnp.where((exponent & 2) != 0, r128, 1.0)
            weight = weight * jnp.where((exponent & 4) != 0, r256, 1.0)
            by_block[pl.ds((2 * j + i) * 8, 8), :] = weight * images
    scale = -1.0 / root
    by_block[pl.ds(64, 8), :] = jnp.where(row == 0, scale, jnp.where(row == 1, scale * r64, scale * inverse))


def outer_kernel(
    place,
    state,
    inner,
    odd_terms,
    x_even,
    y_even,
    y_odd,
    by_level,
    forward,
    star,
    message,
    flat,
):
    even_x = place[0] % 2 == 0
    even_y = place[1] % 2 == 0
    shape = (LEVELS, LANES)
    lane = lane_of(shape)

    relayed = x_even[pl.ds(5 * LEVELS, 16), :]
    other = jnp.where(far_both(place[0], place[1]), relayed, y_odd[0:16, :])
    flat[...] = jnp.zeros((LANES, LANES), F32)
    flat[pl.ds(0, 16, stride=2), :] = jnp.where(even_y, y_even[...], other)
    flat[pl.ds(1, 16, stride=2), :] = jnp.where(even_y, other, y_even[...])
    columns = jnp.transpose(flat[...])[:LEVELS]
    even_adds, even_beyond = side_terms(state, x_even, ~even_x)
    odd_adds = [odd_terms[pl.ds(f * LEVELS, LEVELS), :] for f in range(4)]
    odd_beyond = odd_terms[pl.ds(4 * LEVELS, LEVELS), :]

    end_sign = jnp.where(lane == 0, 0.1, jnp.where(lane == LANES - 1, -0.1, 0.0))
    whole = [[None] * ROWS for _ in range(4)]
    side_u = [None] * ROWS
    for x in range(ROWS):
        v = plane(state, 1, x)
        for f in range(4):
            slot = f * ROWS + x
            side = end_sign * v * turn(columns, -(2 * slot + 1), 1)
            if f == 0:
                side_u[x] = side
            value = inner[pl.ds(slot * LEVELS, LEVELS), :] + side
            if x == 0:
                value = value + jnp.where(even_x, odd_adds[f], even_adds[f])
            if x == ROWS - 1:
                value = value + jnp.where(even_x, even_adds[f], odd_adds[f])
            whole[f][x] = value
            star[pl.ds(slot * LEVELS, LEVELS), :] = value

    low_beyond = jnp.where(even_x, odd_beyond, even_beyond)
    high_beyond = jnp.where(even_x, even_beyond, odd_beyond)
    padded = [low_beyond] + whole[0] + [high_beyond]
    divergence = []
    extra = [-0.5 * side_u[ROWS - 1], 0.5 * side_u[0]]
    up, down = by_level[pl.ds(LEVELS, LEVELS), :], by_level[pl.ds(2 * LEVELS, LEVELS), :]
    for x in range(ROWS):
        v, w = whole[1][x], whole[2][x]
        upright = up * turn(w, -1, 0) - down * turn(w, 1, 0)
        divergence.append(0.5 * (padded[x + 2] - padded[x]) + 0.5 * north_difference(v) + upright)
        low, high = LOW + x // 2, HIGH + x // 2
        value = jnp.where(lane == low, 0.5 * turn(v, low, 1), extra[x % 2])
        extra[x % 2] = jnp.where(lane == high, -0.5 * turn(v, high + 1, 1), value)
    pieces = [divergence[0], divergence[2], extra[0], divergence[1], divergence[3], extra[1]]
    modal = dot3(parts(forward[...]), parts(jnp.concatenate(pieces, axis=1)))
    for i in range(6):
        message[pl.ds(i, LEVELS, stride=6), :] = modal[:, i * LANES : (i + 1) * LANES]


def decay(rate, square):
    lam = rate + square
    root = jnp.sqrt(lam * (1.0 + lam))
    inverse = 1.0 + 2.0 * lam + 2.0 * root
    return root, inverse, 1.0 / inverse


def squarings(rho, count):
    powers = [rho]
    for _ in range(count):
        powers.append(powers[-1] * powers[-1])
    return powers


def lane_powers(powers, exponent):
    product = None
    for bit in range(6):
        factor = jnp.where((exponent & (1 << bit)) != 0, powers[bit], 1.0)
        product = factor if product is None else product * factor
    return product


def solve_kernel(place, received, basis_high, basis_low, by_wave, local, moments):
    blocks = received.shape[0] // 6
    half_size = blocks * 2
    size = half_size * 2
    lane = lane_of((blocks, LANES))
    ends = (lane == 0) | (lane == LANES - 1)
    even = place[1] < 4
    inside, outside = [], [None, None]
    for h in range(2):
        first, second, extra = (received[pl.ds(3 * h + j, blocks, stride=6), :] for j in range(3))
        first = first + jnp.where(ends & even, turn(extra, 1, 0), 0.0)
        second = second + jnp.where(ends & ~even, turn(extra, -1, 0), 0.0)
        inside.append(jnp.concatenate([first, second], axis=0))
        for r in range(2):
            value = jnp.zeros_like(extra) if outside[r] is None else outside[r]
            for i in range(4):
                at = 4 * h + i
                value = jnp.where(lane == at, turn(extra, at - (HIGH, LOW)[i % 2] - r, 1), value)
            outside[r] = value
    right = jnp.concatenate(inside + [jnp.concatenate(outside, axis=0)], axis=1)
    spectral = dot3((basis_high[...], basis_low[...]), parts(right))
    source = jnp.concatenate([spectral[:, :LANES], spectral[:, LANES : 2 * LANES]], axis=0)
    ext = spectral[:, 2 * LANES :]
    ext = jnp.concatenate([ext, turn(ext, -4, 1)], axis=0)

    wave = lambda i: jnp.concatenate([by_wave[pl.ds(i * LANES, LANES), :]] * 2, axis=0)
    powers = [wave(i) for i in range(7)]
    rho = powers[0]
    lane = lane_of((size, LANES))
    ahead, behind = source, source
    for bit in range(6):
        shift = 2 << bit
        ahead = ahead + powers[bit] * jnp.where(lane >= shift, turn(ahead, shift, 1), 0.0)
        behind = behind + powers[bit] * jnp.where(lane < LANES - shift, turn(behind, -shift, 1), 0.0)
    odd = (lane & 1) != 0
    first = jnp.broadcast_to(ext[:, 0:1], (size, LANES))
    second = jnp.broadcast_to(ext[:, 1:2], (size, LANES))
    border = rho * jnp.where(odd, wave(7) * second, wave(8) * first)
    local[...] = ahead + behind - source + border
    weight = jnp.where((lane == 1) | (lane == 2), powers[6] * rho, 1.0)
    column = jnp.where(lane < 2, turn(rho * ahead, 2, 1), turn(rho * behind, 2, 1)) + ext * weight
    column = jnp.where(lane < 4, column, 0.0)
    across = jnp.transpose(column)[:8]
    for j in range(4):
        moments[pl.ds(j * 8, 8), :] = across


def back_kernel(place, local, moments, basis_high, basis_low, by_wave, by_block, message):
    size = local.shape[0]
    half_size = size // 2
    blocks = half_size // 2
    even = place[1] < 4
    mine = place[1] & 3
    carry = jnp.zeros((8, size), F32)
    for j in range(4):
        theirs = moments[pl.ds(j * 8, 8), :]
        carry = carry + by_block[pl.ds(16 * j, 8), :] * theirs
        carry = carry + by_block[pl.ds(16 * j + 8, 8), :] * turn(theirs, half_size, 1)
    own = moments[pl.ds(pl.multiple_of(mine * 8, 8), 8), :]
    scale, by_r64, by_inverse = (by_block[pl.ds(64 + i, 1), :] for i in range(3))
    after = scale * own[0:1] + by_r64 * carry[0:1] + by_inverse * carry[2:3]
    before = scale * own[3:4] + by_r64 * carry[3:4] + by_inverse * carry[1:2]
    stacked = jnp.concatenate([carry[0:4], after, before, jnp.zeros((LANES - 6, size), F32)], axis=0)
    columns = jnp.transpose(stacked)

    wave = lambda i: jnp.concatenate([by_wave[pl.ds(i * LANES, LANES), :]] * 2, axis=0)
    lane = lane_of((size, LANES))
    odd = (lane & 1) != 0
    spread = lambda i: jnp.broadcast_to(columns[:, i : i + 1], (size, LANES))
    total = local[...] + wave(7) * jnp.where(odd, spread(1), spread(0))
    total = total + wave(8) * jnp.where(odd, spread(3), spread(2))
    total = total * wave(9)
    ext = jnp.where((lane == 4) | (lane == 5), columns, 0.0)
    ext = ext[:half_size] + turn(ext[half_size:], 2, 1)
    pressure = dot3(
        (basis_high[...], basis_low[...]),
        parts(jnp.concatenate([total[:half_size], total[half_size:], ext], axis=1)),
    )
    lane = lane_of((blocks, LANES))
    ends = (lane == 0) | (lane == LANES - 1)
    outside = [pressure[r * blocks : (r + 1) * blocks, 2 * LANES :] for r in range(2)]
    for h in range(2):
        span = slice(h * LANES, (h + 1) * LANES)
        first, second = pressure[:blocks, span], pressure[blocks:, span]
        extra = jnp.where(ends, jnp.where(even, turn(first, -1, 0), turn(second, 1, 0)), 0.0)
        for r in range(2):
            extra = jnp.where(lane == HIGH + r, turn(outside[r], HIGH + r - 4 - 2 * h, 1), extra)
            extra = jnp.where(lane == LOW + r, turn(outside[r], LOW + r - 5 - 2 * h, 1), extra)
        for j, value in enumerate((first, second, extra)):
            message[pl.ds(3 * h + j, blocks, stride=6), :] = value


def final_kernel(received, sent, star, back, by_level, out):
    lane = lane_of((LEVELS, LANES))
    row_at = lambda ref, r: ref[pl.ds(3 * (r % 2) + r // 2, LEVELS, stride=6), :]
    p = [row_at(received, r) for r in range(ROWS)]
    extra = [row_at(received, 4), row_at(received, 5)]
    low = [turn(extra[r % 2], -(LOW + r // 2), 1) for r in range(ROWS)]
    high = [turn(extra[r % 2], LANES - 1 - (HIGH + r // 2), 1) for r in range(ROWS)]
    four_rate = 4.0 * by_level[pl.ds(0, LEVELS), :]

    def next_row(r, opposite):
        here = p[r]
        divergence = row_at(sent, r)
        plus = jnp.where(lane < LANES - 2, turn(here, -2, 1), turn(high[r], -1, 1))
        minus = jnp.where(lane > 1, turn(here, 2, 1), turn(low[r], 1, 1))
        return (
            2.0 * here
            - opposite
            + four_rate * here
            + (2.0 * here - plus - minus)
            + 4.0 * divergence
        )

    ends = (lane == 0) | (lane == LANES - 1)
    before = jnp.where(ends, extra[1], next_row(1, p[3]))
    after = jnp.where(ends, extra[0], next_row(2, p[0]))
    padded = [before] + p + [after]
    slopes = [0.5 * (padded[x + 2] - padded[x]) for x in range(ROWS)]
    slopes += [0.5 * north_difference(p[x], low[x], high[x]) for x in range(ROWS)]
    matrix = back[...]
    slope = dot3(parts(matrix), parts(jnp.concatenate(slopes, axis=1)))
    lift = dot3(parts(0.5 * level_difference(matrix)), parts(jnp.concatenate(p, axis=1)))
    for x in range(ROWS):
        take = lambda values, i: values[:, i * LANES : (i + 1) * LANES]
        for f, change in ((0, take(slope, x)), (1, take(slope, ROWS + x)), (2, take(lift, x)), (3, None)):
            value = star[pl.ds((f * ROWS + x) * LEVELS, LEVELS), :]
            if change is not None:
                value = value - change
            out[pl.ds(f * LEVELS * ROWS + x, LEVELS, stride=ROWS), :] = value


def call(kernel, shapes, args, name, scalars=1, scratch=(), cost=None):
    vmem = pl.BlockSpec(memory_space=pltpu.VMEM)
    scalar = pl.BlockSpec(memory_space=pltpu.SMEM)
    return pl.pallas_call(
        kernel,
        out_shape=[jax.ShapeDtypeStruct(s, F32) for s in shapes],
        in_specs=[scalar] * scalars + [vmem] * (len(args) - scalars),
        out_specs=[vmem] * len(shapes),
        scratch_shapes=[pltpu.VMEM(s, F32) for s in scratch],
        compiler_params=pltpu.CompilerParams(vmem_limit_bytes=32 * 1024 * 1024),
        name=name,
        cost_estimate=cost,
    )(*args)


def swap(values, axis, odd):
    count = lax.axis_size(axis)
    pairs = []
    for i in range(odd, count + odd, 2):
        pairs += [(i % count, (i + 1) % count), ((i + 1) % count, i % count)]
    return lax.ppermute(values, axis, pairs)


def swap_odd_y(values):
    count_x, count_y = lax.axis_size("gx"), lax.axis_size("gy")
    pairs = []
    for i in range(count_x):
        for j in range(1, count_y + 1, 2):
            one, two = j % count_y, (j + 1) % count_y
            if not far_both(i, one):
                pairs += [(i * count_y + one, i * count_y + two), (i * count_y + two, i * count_y + one)]
    return lax.ppermute(values, ("gx", "gy"), pairs)


def exchange(values):
    count_x, count_y = lax.axis_size("gx"), lax.axis_size("gy")
    near = count_y // 2
    groups = [[i * count_y + h * near + y for i in range(count_x) for h in range(2)] for y in range(near)]
    shaped = values.reshape(2 * count_x, 1, values.size // (2 * count_x))
    moved = lax.all_to_all(
        shaped, ("gx", "gy"), 0, 0, tiled=True, axis_index_groups=groups
    )
    return moved.reshape(values.shape)


def on_device(
    model_state, density, layer_in, layer_bias, layer_out, mode_forward, mode_back, mode_rate
):
    blocks = lax.axis_size("gx")
    total_east = blocks * ROWS
    place = jnp.stack([lax.axis_index("gx"), lax.axis_index("gy")]).astype(jnp.int32)
    state = model_state.reshape(4 * LEVELS * ROWS, LANES)
    basis, square = east_tables(total_east // 2, blocks)
    forward_high, forward_low = split_table(basis)
    back_high, back_low = split_table(np.ascontiguousarray(basis.T))
    square_wide = np.ascontiguousarray(np.broadcast_to(square[:, None], (total_east // 2, LANES)))
    square_row = np.ascontiguousarray(np.broadcast_to(np.concatenate([square, square]), (8, total_east)))

    planes, x_even, x_odd, y_even, y_odd = call(
        edges_kernel,
        [(16 * LEVELS, LANES)] + [(5 * LEVELS + 16, LANES), (5 * LEVELS, LANES)] + [(16, LANES)] * 2,
        [place, state],
        "edges",
        scratch=[(LANES, LANES)],
    )
    y_both = jnp.concatenate([y_odd, swap(y_odd, "gx", 0)], axis=0)
    y_both, x_odd, y_even = lax.optimization_barrier((y_both, x_odd, y_even))
    got_y_odd = swap_odd_y(y_both)
    got_x_odd = swap(x_odd, "gx", 1)
    inner, by_level = call(
        inner_kernel,
        [(16 * LEVELS, LANES), (3 * LEVELS, LANES)],
        [
            planes,
            jnp.concatenate([mode_rate, density, layer_bias])[None, :],
            layer_in,
            layer_out,
        ],
        "inner",
        scalars=0,
        cost=pl.CostEstimate(flops=10**10, transcendentals=0, bytes_accessed=2**24),
    )
    inner, y_even = lax.optimization_barrier((inner, y_even))
    got_y_even = swap(y_even, "gy", 0)
    inner, got_y_odd, got_y_even = lax.optimization_barrier((inner, got_y_odd, got_y_even))
    got_x_even = swap(x_even.at[5 * LEVELS :].set(got_y_odd[16:]), "gx", 0)
    odd_terms, by_wave, by_block = call(
        side_kernel,
        [(5 * LEVELS, LANES), (10 * LANES, LANES), (72, total_east)],
        [place, planes, got_x_odd, by_level, square_wide, square_row],
        "side",
        cost=pl.CostEstimate(flops=10**11, transcendentals=0, bytes_accessed=2**27),
    )
    star, message = call(
        outer_kernel,
        [(16 * LEVELS, LANES), (blocks * 6, LANES)],
        [
            place,
            planes,
            inner,
            odd_terms,
            got_x_even,
            got_y_even,
            got_y_odd,
            by_level,
            mode_forward,
        ],
        "outer",
        scratch=[(LANES, LANES)],
    )
    modal = exchange(message)
    local, moments = call(
        solve_kernel,
        [(total_east, LANES), (32, total_east)],
        [place, modal, forward_high, forward_low, by_wave],
        "solve",
    )
    moments = lax.all_to_all(
        moments.reshape(4, 8, total_east),
        "gy",
        0,
        0,
        tiled=True,
        axis_index_groups=[[0, 1, 2, 3], [4, 5, 6, 7]],
    ).reshape(32, total_east)
    (reply,) = call(
        back_kernel,
        [(blocks * 6, LANES)],
        [place, local, moments, back_high, back_low, by_wave, by_block],
        "back",
    )
    pressure = exchange(reply)
    (out,) = call(
        final_kernel,
        [(4 * LEVELS * ROWS, LANES)],
        [pressure, message, star, mode_back, by_level],
        "final",
        scalars=0,
    )
    return out.reshape(model_state.shape)


def solution(mesh):
    return jax.shard_map(
        on_device,
        mesh=mesh,
        in_specs=(P(None, None, "gx", "gy"), P(), P(), P(), P(), P(), P(), P()),
        out_specs=P(None, None, "gx", "gy"),
        check_vma=False,
    )
```

```python
import math

import jax
import jax.numpy as jnp
import ml_dtypes
import numpy as np
from jax import lax
from jax.experimental import pallas as pl
from jax.experimental.pallas import tpu as pltpu
from jax.sharding import PartitionSpec as P

F32 = jnp.float32
BF16 = jnp.bfloat16
LEVELS = 64
ROWS = 4
LANES = 128
LOW = 16
HIGH = 32


def split_table(table):
    high = table.astype(np.float32).astype(ml_dtypes.bfloat16)
    low = (table - high.astype(np.float64)).astype(np.float32).astype(ml_dtypes.bfloat16)
    return high, low


def east_tables(total, blocks):
    rows = total // blocks
    x = (np.arange(rows)[:, None] + rows * np.arange(blocks)[None, :]).reshape(-1)
    k = np.arange(total)
    angle = 2.0 * math.pi * ((k[:, None] * x[None, :]) % total) / total
    basis = np.where((k <= total // 2)[:, None], np.cos(angle), np.sin(angle))
    scale = np.where((k == 0) | (k == total // 2), 1.0, math.sqrt(2.0)) / math.sqrt(total)
    basis = basis * scale[:, None]
    square = np.sin(math.pi * k / total) ** 2
    return basis, square.astype(np.float32)


def lane_of(shape):
    return lax.broadcasted_iota(jnp.int32, shape, len(shape) - 1)


def row_of(shape):
    return lax.broadcasted_iota(jnp.int32, shape, 0)


def turn(values, shift, axis):
    size = values.shape[axis]
    return pltpu.roll(values, shift % size, axis) if shift % size else values


def parts(values):
    high = values.astype(BF16)
    return high, (values - high.astype(F32)).astype(BF16)


def dot3(left, right):
    dot = lambda a, b: jnp.dot(a, b, preferred_element_type=F32)
    return dot(left[0], right[0]) + (dot(left[0], right[1]) + dot(left[1], right[0]))


def level_difference(values):
    row = row_of(values.shape)
    last = values.shape[0] - 1
    upper = jnp.where(row < last, turn(values, -1, 0), 0.0)
    lower = jnp.where(row > 0, turn(values, 1, 0), 0.0)
    return upper - lower


def north_difference(values, low=0.0, high=0.0):
    lane = lane_of(values.shape)
    after = jnp.where(lane < LANES - 1, turn(values, -1, 1), high)
    before = jnp.where(lane > 0, turn(values, 1, 1), low)
    return after - before


def plane(ref, field, x):
    return ref[pl.ds((field * ROWS + x) * LEVELS, LEVELS), :]


def far_both(gx, gy):
    return ((gx % 16 == 0) | (gx % 16 == 15)) & ((gy % 4 == 0) | (gy % 4 == 3))


def edges_kernel(place, state_u, state_v, state_w, state_th, planes, x_even, x_odd, y_even, y_odd, flat):
    even_x = place[0] % 2 == 0
    even_y = place[1] % 2 == 0
    states = (state_u, state_v, state_w, state_th)
    lane = lane_of((LEVELS, LANES))
    gathered = jnp.zeros((LEVELS, LANES), F32)
    for field in range(4):
        values = [states[field][pl.ds(x, LEVELS, stride=ROWS), :] for x in range(ROWS)]
        for x in range(ROWS):
            slot = field * ROWS + x
            planes[pl.ds(slot * LEVELS, LEVELS), :] = values[x]
            gathered = jnp.where(lane >> 1 == slot, turn(values[x], 2 * slot + 1, 1), gathered)
        for slot, depth in ((field, 0), (4, 1)) if field == 0 else ((field, 0),):
            span = pl.ds(slot * LEVELS, LEVELS)
            low, high = values[depth], values[ROWS - 1 - depth]
            x_even[span, :] = jnp.where(even_x, high, low)
            x_odd[span, :] = jnp.where(even_x, low, high)
    flat[...] = jnp.transpose(jnp.concatenate([gathered, jnp.zeros_like(gathered)], axis=0))
    high, low = flat[pl.ds(0, 16, stride=2), :], flat[pl.ds(1, 16, stride=2), :]
    y_even[...] = jnp.where(even_y, high, low)
    y_odd[...] = jnp.where(even_y, low, high)
    x_even[pl.ds(5 * LEVELS, 16), :] = jnp.where(even_y, low, high)


def column_of(row):
    return jnp.transpose(jnp.broadcast_to(row, (LANES, LANES)))


def inner_kernel(
    state,
    vectors,
    layer_in,
    layer_out,
    star,
    by_level,
):
    fields = [[plane(state, f, x) for x in range(ROWS)] for f in range(4)]
    tall = column_of(vectors[:, :LANES])
    rate, density = tall[:LEVELS], tall[LEVELS:]
    row = row_of((LEVELS, LANES))
    by_level[pl.ds(0, LEVELS), :] = rate
    by_level[pl.ds(LEVELS, LEVELS), :] = jnp.where(
        row < LEVELS - 1, 0.5 * turn(density, -1, 0) / density, 0.0
    )
    by_level[pl.ds(2 * LEVELS, LEVELS), :] = jnp.where(row > 0, 0.5 * turn(density, 1, 0) / density, 0.0)
    for x in range(ROWS):
        u, v, w, th = (fields[f][x] for f in range(4))
        for f in range(4):
            here = fields[f][x]
            change = v * north_difference(here) + w * level_difference(here)
            if x == 0:
                change = change + u * fields[f][1]
            elif x == ROWS - 1:
                change = change - u * fields[f][x - 1]
            else:
                change = change + u * (fields[f][x + 1] - fields[f][x - 1])
            value = here - 0.1 * change
            if f == 2:
                value = value + 0.1 * th
            star[pl.ds((f * ROWS + x) * LEVELS, LEVELS), :] = value

    columns = jnp.concatenate(
        [jnp.concatenate([fields[f][x] for f in range(4)], axis=0).astype(BF16) for x in range(ROWS)],
        axis=1,
    )
    first = (((0,), (0,)), ((), ()))
    shift = [column_of(vectors[:, i * LANES : (i + 1) * LANES]) for i in (1, 2)]
    shift = jnp.concatenate(shift, axis=0)
    before = lax.dot_general(layer_in[...], columns, first, preferred_element_type=F32)
    before = before + jnp.concatenate([shift] * ROWS, axis=1)
    hidden = (before * (1.0 / (1.0 + jnp.exp(-before)))).astype(BF16)
    forcing = lax.dot_general(layer_out[...], hidden, first, preferred_element_type=F32)
    for x in range(ROWS):
        span = slice(x * LANES, (x + 1) * LANES)
        for f, part in ((2, forcing[LEVELS:, span]), (3, forcing[:LEVELS, span])):
            at = pl.ds((f * ROWS + x) * LEVELS, LEVELS)
            star[at, :] = star[at, :] + 0.2 * part


def side_terms(state, edge, low):
    u, v, w = (edge[pl.ds(f * LEVELS, LEVELS), :] for f in range(3))
    second = edge[pl.ds(4 * LEVELS, LEVELS), :]
    own = jnp.where(low, plane(state, 0, 0), plane(state, 0, ROWS - 1))
    sign = jnp.where(low, 0.1, -0.1)
    adds = [sign * own * edge[pl.ds(f * LEVELS, LEVELS), :] for f in range(4)]
    along = u * (own - second)
    beyond = u - (sign * along + 0.1 * (v * north_difference(u) + w * level_difference(u)))
    return adds, beyond


def side_kernel(place, state, x_odd, by_level, square_row, terms, by_row, by_wave, by_block):
    adds, beyond = side_terms(state, x_odd, place[0] % 2 == 0)
    for i, value in enumerate(adds + [beyond]):
        terms[pl.ds(i * LEVELS, LEVELS), :] = value
    own = by_level[pl.ds(place[0], 1), :]

    both = jnp.concatenate([own, own], axis=1)
    root, inverse, rho = decay(both, square_row[...])
    powers = squarings(rho, 6)
    for i, value in enumerate(powers + [powers[6] * rho, -1.0 / root]):
        by_row[pl.ds(8 * i, 8), :] = value
    half = row_of((LANES, LANES)) >> 1
    odd = (row_of((LANES, LANES)) & 1) != 0
    narrow = [jnp.broadcast_to(value[0:1, :LANES], (LANES, LANES)) for value in powers[:6]]
    rising = lane_powers(narrow, half)
    falling = lane_powers(narrow, 63 - half)
    by_wave[pl.ds(0, LANES), :] = rising
    by_wave[pl.ds(LANES, LANES), :] = falling
    by_wave[pl.ds(2 * LANES, LANES), :] = narrow[0] * jnp.where(odd, rising, falling)

    r64 = powers[6]
    r128 = r64 * r64
    r256 = r128 * r128
    images = 1.0 / (1.0 - r256 * r256)
    mine = place[1] & 3
    row = row_of(rho.shape)
    for j in range(4):
        for i, offset in enumerate((-1, 3)):
            exponent = jnp.where(row < 2, (mine - j + offset) & 7, (j - mine + offset) & 7)
            weight = jnp.where((exponent & 1) != 0, r64, 1.0)
            weight = weight * jnp.where((exponent & 2) != 0, r128, 1.0)
            weight = weight * jnp.where((exponent & 4) != 0, r256, 1.0)
            by_block[pl.ds((2 * j + i) * 8, 8), :] = weight * images
    scale = -1.0 / root
    by_block[pl.ds(64, 8), :] = jnp.where(row == 0, scale, jnp.where(row == 1, scale * r64, scale * inverse))


def outer_kernel(
    place,
    state,
    inner,
    odd_terms,
    x_even,
    y_even,
    y_odd,
    relayed,
    by_level,
    forward,
    star,
    message,
    flat,
):
    even_x = place[0] % 2 == 0
    even_y = place[1] % 2 == 0
    shape = (LEVELS, LANES)
    lane = lane_of(shape)

    other = jnp.where(far_both(place[0], place[1]), relayed[...], y_odd[0:16, :])
    flat[...] = jnp.zeros((LANES, LANES), F32)
    flat[pl.ds(0, 16, stride=2), :] = jnp.where(even_y, y_even[...], other)
    flat[pl.ds(1, 16, stride=2), :] = jnp.where(even_y, other, y_even[...])
    columns = jnp.transpose(flat[...])[:LEVELS]
    even_adds, even_beyond = side_terms(state, x_even, ~even_x)
    odd_adds = [odd_terms[pl.ds(f * LEVELS, LEVELS), :] for f in range(4)]
    odd_beyond = odd_terms[pl.ds(4 * LEVELS, LEVELS), :]

    end_sign = jnp.where(lane == 0, 0.1, jnp.where(lane == LANES - 1, -0.1, 0.0))
    whole = [[None] * ROWS for _ in range(4)]
    side_u = [None] * ROWS
    for x in range(ROWS):
        v = plane(state, 1, x)
        for f in range(4):
            slot = f * ROWS + x
            side = end_sign * v * turn(columns, -(2 * slot + 1), 1)
            if f == 0:
                side_u[x] = side
            value = inner[pl.ds(slot * LEVELS, LEVELS), :] + side
            if x == 0:
                value = value + jnp.where(even_x, odd_adds[f], even_adds[f])
            if x == ROWS - 1:
                value = value + jnp.where(even_x, even_adds[f], odd_adds[f])
            whole[f][x] = value
            star[pl.ds(slot * LEVELS, LEVELS), :] = value

    low_beyond = jnp.where(even_x, odd_beyond, even_beyond)
    high_beyond = jnp.where(even_x, even_beyond, odd_beyond)
    padded = [low_beyond] + whole[0] + [high_beyond]
    divergence = []
    extra = [-0.5 * side_u[ROWS - 1], 0.5 * side_u[0]]
    up, down = by_level[pl.ds(LEVELS, LEVELS), :], by_level[pl.ds(2 * LEVELS, LEVELS), :]
    for x in range(ROWS):
        v, w = whole[1][x], whole[2][x]
        upright = up * turn(w, -1, 0) - down * turn(w, 1, 0)
        divergence.append(0.5 * (padded[x + 2] - padded[x]) + 0.5 * north_difference(v) + upright)
        low, high = LOW + x // 2, HIGH + x // 2
        value = jnp.where(lane == low, 0.5 * turn(v, low, 1), extra[x % 2])
        extra[x % 2] = jnp.where(lane == high, -0.5 * turn(v, high + 1, 1), value)
    pieces = [divergence[0], divergence[2], extra[0], divergence[1], divergence[3], extra[1]]
    modal = dot3(parts(forward[...]), parts(jnp.concatenate(pieces, axis=1)))
    for i in range(6):
        message[pl.ds(i, LEVELS, stride=6), :] = modal[:, i * LANES : (i + 1) * LANES]


def decay(rate, square):
    lam = rate + square
    root = jnp.sqrt(lam * (1.0 + lam))
    inverse = 1.0 + 2.0 * lam + 2.0 * root
    return root, inverse, 1.0 / inverse


def squarings(rho, count):
    powers = [rho]
    for _ in range(count):
        powers.append(powers[-1] * powers[-1])
    return powers


def lane_powers(powers, exponent):
    product = None
    for bit in range(6):
        factor = jnp.where((exponent & (1 << bit)) != 0, powers[bit], 1.0)
        product = factor if product is None else product * factor
    return product


def shifted(values, shift):
    size = values.shape[0]
    if shift % 8 == 0:
        zeros = jnp.zeros((abs(shift), values.shape[1]), F32)
        if shift > 0:
            return jnp.concatenate([zeros, values[:-shift]], axis=0)
        return jnp.concatenate([values[-shift:], zeros], axis=0)
    row = row_of(values.shape)
    inside = row >= shift if shift > 0 else row < size + shift
    return jnp.where(inside, turn(values, shift, 0), 0.0)


def by_parity(even, odd):
    shape = (8, even.shape[1])
    tile = jnp.where((row_of(shape) & 1) != 0, jnp.broadcast_to(odd, shape), jnp.broadcast_to(even, shape))
    return jnp.concatenate([tile] * (LANES // 8), axis=0)


def halves(values):
    return jnp.concatenate([values, values], axis=1)


def solve_kernel(place, received, basis_high, basis_low, by_row, by_wave, local, moments):
    blocks = received.shape[0] // 6
    lane = lane_of((blocks, LANES))
    ends = (lane == 0) | (lane == LANES - 1)
    even = place[1] < 4
    inside, outside = [], [jnp.zeros((blocks, LANES), F32)] * 2
    for h in range(2):
        first, second, extra = (received[pl.ds(3 * h + j, blocks, stride=6), :] for j in range(3))
        first = first + jnp.where(ends & even, turn(extra, 1, 0), 0.0)
        second = second + jnp.where(ends & ~even, turn(extra, -1, 0), 0.0)
        inside.append(jnp.concatenate([first, second], axis=0))
        for r in range(2):
            for i, start in enumerate((HIGH, LOW)):
                at = 2 * h + i
                outside[r] = jnp.where(lane == at, turn(extra, at - start - r, 1), outside[r])
    right = parts(jnp.concatenate(inside + [jnp.concatenate(outside, axis=0)], axis=1))
    first = (((0,), (0,)), ((), ()))
    dot = lambda a, b: lax.dot_general(a, b[...], first, preferred_element_type=F32)
    spectral = dot(right[0], basis_high) + (dot(right[0], basis_low) + dot(right[1], basis_high))
    source = jnp.concatenate([spectral[:LANES], spectral[LANES : 2 * LANES]], axis=1)
    ext = spectral[2 * LANES : 2 * LANES + 8]
    high = jnp.concatenate([ext[0:1], ext[2:3]], axis=1)
    low = jnp.concatenate([ext[1:2], ext[3:4]], axis=1)

    power = lambda i: by_row[pl.ds(8 * i, 1), :]
    ahead, behind = source, source
    for bit in range(6):
        ahead = ahead + power(bit) * shifted(ahead, 2 << bit)
        behind = behind + power(bit) * shifted(behind, -(2 << bit))
    border = halves(by_wave[pl.ds(2 * LANES, LANES), :]) * by_parity(high, low)
    local[...] = ahead + behind - source + border
    rho, r65 = power(0), power(7)
    across = [
        rho * ahead[LANES - 2 : LANES - 1] + high,
        rho * ahead[LANES - 1 :] + r65 * low,
        rho * behind[0:1] + r65 * high,
        rho * behind[1:2] + low,
        jnp.zeros((4, source.shape[1]), F32),
    ]
    across = jnp.concatenate(across, axis=0)
    for j in range(4):
        moments[pl.ds(j * 8, 8), :] = across


def back_kernel(place, local, moments, basis_high, basis_low, by_row, by_wave, by_block, message):
    width = local.shape[1]
    blocks = basis_high.shape[0] // 2
    even = place[1] < 4
    mine = place[1] & 3
    carry = jnp.zeros((8, width), F32)
    for j in range(4):
        theirs = moments[pl.ds(j * 8, 8), :]
        swapped = jnp.concatenate([theirs[:, LANES:], theirs[:, :LANES]], axis=1)
        carry = carry + by_block[pl.ds(16 * j, 8), :] * theirs + by_block[pl.ds(16 * j + 8, 8), :] * swapped
    own = moments[pl.ds(pl.multiple_of(mine * 8, 8), 8), :]
    scale, by_r64, by_inverse = (by_block[pl.ds(64 + i, 1), :] for i in range(3))
    after = scale * own[0:1] + by_r64 * carry[0:1] + by_inverse * carry[2:3]
    before = scale * own[3:4] + by_r64 * carry[3:4] + by_inverse * carry[1:2]
    total = local[...] + halves(by_wave[pl.ds(0, LANES), :]) * by_parity(carry[0:1], carry[1:2])
    total = total + halves(by_wave[pl.ds(LANES, LANES), :]) * by_parity(carry[2:3], carry[3:4])
    total = total * scale
    pieces = [total[:, :LANES], total[:, LANES:]]
    for h in range(2):
        span = slice(h * LANES, (h + 1) * LANES)
        pieces += [after[:, span], before[:, span]]
    pieces.append(jnp.zeros((LANES - 4, LANES), F32))
    right = parts(jnp.concatenate(pieces, axis=0))
    last = (((1,), (1,)), ((), ()))
    dot = lambda a, b: lax.dot_general(a[...], b, last, preferred_element_type=F32)
    pressure = dot(basis_high, right[0]) + (dot(basis_high, right[1]) + dot(basis_low, right[0]))
    lane = lane_of((blocks, LANES))
    ends = (lane == 0) | (lane == LANES - 1)
    outside = [pressure[r * blocks : (r + 1) * blocks, 2 * LANES :] for r in range(2)]
    for h in range(2):
        span = slice(h * LANES, (h + 1) * LANES)
        first, second = pressure[:blocks, span], pressure[blocks:, span]
        extra = jnp.where(ends, jnp.where(even, turn(first, -1, 0), turn(second, 1, 0)), 0.0)
        for r in range(2):
            extra = jnp.where(lane == HIGH + r, turn(outside[r], HIGH + r - 2 * h, 1), extra)
            extra = jnp.where(lane == LOW + r, turn(outside[r], LOW + r - 1 - 2 * h, 1), extra)
        for j, value in enumerate((first, second, extra)):
            message[pl.ds(3 * h + j, blocks, stride=6), :] = value


def final_kernel(received, sent, star, back, by_level, out, held, sent_out):
    size = LEVELS * ROWS
    span = lambda f: pl.ds(f * size, size)
    copies = [pltpu.make_async_copy(held.at[span(f), :], out.at[span(f), :], sent_out.at[f]) for f in range(4)]

    def put(f, changes):
        for x in range(ROWS):
            value = star[pl.ds((f * ROWS + x) * LEVELS, LEVELS), :]
            if changes is not None:
                value = value - changes[:, x * LANES : (x + 1) * LANES]
            held[pl.ds(f * size + x, LEVELS, stride=ROWS), :] = value
        copies[f].start()

    put(3, None)
    lane = lane_of((LEVELS, LANES))
    row_at = lambda ref, r: ref[pl.ds(3 * (r % 2) + r // 2, LEVELS, stride=6), :]
    p = [row_at(received, r) for r in range(ROWS)]
    extra = [row_at(received, 4), row_at(received, 5)]
    low = [turn(extra[r % 2], -(LOW + r // 2), 1) for r in range(ROWS)]
    high = [turn(extra[r % 2], LANES - 1 - (HIGH + r // 2), 1) for r in range(ROWS)]
    four_rate = 4.0 * by_level[pl.ds(0, LEVELS), :]

    def next_row(r, opposite):
        here = p[r]
        divergence = row_at(sent, r)
        plus = jnp.where(lane < LANES - 2, turn(here, -2, 1), turn(high[r], -1, 1))
        minus = jnp.where(lane > 1, turn(here, 2, 1), turn(low[r], 1, 1))
        return (
            2.0 * here
            - opposite
            + four_rate * here
            + (2.0 * here - plus - minus)
            + 4.0 * divergence
        )

    ends = (lane == 0) | (lane == LANES - 1)
    before = jnp.where(ends, extra[1], next_row(1, p[3]))
    after = jnp.where(ends, extra[0], next_row(2, p[0]))
    padded = [before] + p + [after]
    matrix = back[...]
    joined = lambda values: parts(jnp.concatenate(values, axis=1))
    put(2, dot3(parts(0.5 * level_difference(matrix)), joined(p)))
    matrix = parts(matrix)
    put(1, dot3(matrix, joined([0.5 * north_difference(p[x], low[x], high[x]) for x in range(ROWS)])))
    put(0, dot3(matrix, joined([0.5 * (padded[x + 2] - padded[x]) for x in range(ROWS)])))
    for copy in copies:
        copy.wait()


def call(kernel, shapes, args, name, scalars=1, scratch=(), cost=None, copies=0):
    vmem = pl.BlockSpec(memory_space=pltpu.VMEM)
    scalar = pl.BlockSpec(memory_space=pltpu.SMEM)
    return pl.pallas_call(
        kernel,
        out_shape=[jax.ShapeDtypeStruct(s, F32) for s in shapes],
        in_specs=[scalar] * scalars + [vmem] * (len(args) - scalars),
        out_specs=[pl.BlockSpec(memory_space=pl.ANY) if copies else vmem] * len(shapes),
        scratch_shapes=[pltpu.VMEM(s, F32) for s in scratch]
        + ([pltpu.SemaphoreType.DMA((copies,))] if copies else []),
        compiler_params=pltpu.CompilerParams(vmem_limit_bytes=32 * 1024 * 1024),
        name=name,
        cost_estimate=cost,
    )(*args)


def swap(values, axis, odd):
    count = lax.axis_size(axis)
    pairs = []
    for i in range(odd, count + odd, 2):
        pairs += [(i % count, (i + 1) % count), ((i + 1) % count, i % count)]
    return lax.ppermute(values, axis, pairs)


def swap_odd_y(values):
    count_x, count_y = lax.axis_size("gx"), lax.axis_size("gy")
    pairs = []
    for i in range(count_x):
        for j in range(1, count_y + 1, 2):
            one, two = j % count_y, (j + 1) % count_y
            if not far_both(i, one):
                pairs += [(i * count_y + one, i * count_y + two), (i * count_y + two, i * count_y + one)]
    return lax.ppermute(values, ("gx", "gy"), pairs)


def hand_over(values):
    count_x, count_y = lax.axis_size("gx"), lax.axis_size("gy")
    pairs = [
        ((i ^ 1) * count_y + j, i * count_y + j)
        for i in range(count_x)
        for j in range(count_y)
        if far_both(i, j)
    ]
    return lax.ppermute(values, ("gx", "gy"), pairs)


def exchange(values):
    count_x, count_y = lax.axis_size("gx"), lax.axis_size("gy")
    near = count_y // 2
    groups = [[i * count_y + h * near + y for i in range(count_x) for h in range(2)] for y in range(near)]
    shaped = values.reshape(2 * count_x, 1, values.size // (2 * count_x))
    moved = lax.all_to_all(
        shaped, ("gx", "gy"), 0, 0, tiled=True, axis_index_groups=groups
    )
    return moved.reshape(values.shape)


def on_device(
    model_state, density, layer_in, layer_bias, layer_out, mode_forward, mode_back, mode_rate
):
    blocks = lax.axis_size("gx")
    total_east = blocks * ROWS
    place = jnp.stack([lax.axis_index("gx"), lax.axis_index("gy")]).astype(jnp.int32)
    state = [model_state[f].reshape(LEVELS * ROWS, LANES) for f in range(4)]
    basis, square = east_tables(total_east // 2, blocks)
    basis_high, basis_low = split_table(np.ascontiguousarray(basis.T))
    square_row = np.ascontiguousarray(np.broadcast_to(np.concatenate([square, square]), (8, total_east)))

    planes, x_even, x_odd, y_even, y_odd = call(
        edges_kernel,
        [(16 * LEVELS, LANES)] + [(5 * LEVELS + 16, LANES), (5 * LEVELS, LANES)] + [(16, LANES)] * 2,
        [place, *state],
        "edges",
        scratch=[(LANES, LANES)],
    )
    got_x_even = swap(x_even, "gx", 0)
    y_both = jnp.concatenate([y_odd, got_x_even[5 * LEVELS :]], axis=0)
    y_both, x_odd, y_even = lax.optimization_barrier((y_both, x_odd, y_even))
    got_y_odd = swap_odd_y(y_both)
    got_x_odd = swap(x_odd, "gx", 1)
    got_y_even = swap(y_even, "gy", 0)
    inner, by_level = call(
        inner_kernel,
        [(16 * LEVELS, LANES), (3 * LEVELS, LANES)],
        [
            planes,
            jnp.concatenate([mode_rate, density, layer_bias])[None, :],
            layer_in,
            layer_out,
        ],
        "inner",
        scalars=0,
        cost=pl.CostEstimate(flops=10**10, transcendentals=0, bytes_accessed=2**24),
    )
    inner, got_y_odd = lax.optimization_barrier((inner, got_y_odd))
    relayed = hand_over(got_y_odd[16:])
    odd_terms, by_row, by_wave, by_block = call(
        side_kernel,
        [(5 * LEVELS, LANES), (72, total_east), (3 * LANES, LANES), (72, total_east)],
        [place, planes, got_x_odd, by_level, square_row],
        "side",
        cost=pl.CostEstimate(flops=10**11, transcendentals=0, bytes_accessed=2**27),
    )
    star, message = call(
        outer_kernel,
        [(16 * LEVELS, LANES), (blocks * 6, LANES)],
        [
            place,
            planes,
            inner,
            odd_terms,
            got_x_even,
            got_y_even,
            got_y_odd,
            relayed,
            by_level,
            mode_forward,
        ],
        "outer",
        scratch=[(LANES, LANES)],
    )
    modal = exchange(message)
    local, moments = call(
        solve_kernel,
        [(LANES, total_east), (32, total_east)],
        [place, modal, basis_high, basis_low, by_row, by_wave],
        "solve",
    )
    moments = lax.all_to_all(
        moments.reshape(4, 8, total_east),
        "gy",
        0,
        0,
        tiled=True,
        axis_index_groups=[[0, 1, 2, 3], [4, 5, 6, 7]],
    ).reshape(32, total_east)
    (reply,) = call(
        back_kernel,
        [(blocks * 6, LANES)],
        [place, local, moments, basis_high, basis_low, by_row, by_wave, by_block],
        "back",
    )
    pressure = exchange(reply)
    (out,) = call(
        final_kernel,
        [(4 * LEVELS * ROWS, LANES)],
        [pressure, message, star, mode_back, by_level],
        "final",
        scalars=0,
        scratch=[(4 * LEVELS * ROWS, LANES)],
        copies=4,
    )
    return out.reshape(model_state.shape)


def solution(mesh):
    return jax.shard_map(
        on_device,
        mesh=mesh,
        in_specs=(P(None, None, "gx", "gy"), P(), P(), P(), P(), P(), P(), P()),
        out_specs=P(None, None, "gx", "gy"),
        check_vma=False,
    )
```

```python
import math

import jax
import jax.numpy as jnp
import ml_dtypes
import numpy as np
from jax import lax
from jax.experimental import pallas as pl
from jax.experimental.pallas import tpu as pltpu
from jax.sharding import PartitionSpec as P

F32 = jnp.float32
BF16 = jnp.bfloat16
LEVELS = 64
ROWS = 4
LANES = 128
LOW = 16
HIGH = 32


def split_table(table):
    high = table.astype(np.float32).astype(ml_dtypes.bfloat16)
    low = (table - high.astype(np.float64)).astype(np.float32).astype(ml_dtypes.bfloat16)
    return high, low


def east_tables(total, blocks):
    rows = total // blocks
    x = (np.arange(rows)[:, None] + rows * np.arange(blocks)[None, :]).reshape(-1)
    k = np.arange(total)
    angle = 2.0 * math.pi * ((k[:, None] * x[None, :]) % total) / total
    basis = np.where((k <= total // 2)[:, None], np.cos(angle), np.sin(angle))
    scale = np.where((k == 0) | (k == total // 2), 1.0, math.sqrt(2.0)) / math.sqrt(total)
    basis = basis * scale[:, None]
    square = np.sin(math.pi * k / total) ** 2
    return basis, square.astype(np.float32)


def lane_of(shape):
    return lax.broadcasted_iota(jnp.int32, shape, len(shape) - 1)


def row_of(shape):
    return lax.broadcasted_iota(jnp.int32, shape, 0)


def turn(values, shift, axis):
    size = values.shape[axis]
    return pltpu.roll(values, shift % size, axis) if shift % size else values


def parts(values):
    high = values.astype(BF16)
    return high, (values - high.astype(F32)).astype(BF16)


def dot3(left, right):
    dot = lambda a, b: jnp.dot(a, b, preferred_element_type=F32)
    return dot(left[0], right[0]) + (dot(left[0], right[1]) + dot(left[1], right[0]))


def level_difference(values):
    row = row_of(values.shape)
    last = values.shape[0] - 1
    upper = jnp.where(row < last, turn(values, -1, 0), 0.0)
    lower = jnp.where(row > 0, turn(values, 1, 0), 0.0)
    return upper - lower


def north_difference(values, low=0.0, high=0.0):
    lane = lane_of(values.shape)
    after = jnp.where(lane < LANES - 1, turn(values, -1, 1), high)
    before = jnp.where(lane > 0, turn(values, 1, 1), low)
    return after - before


def plane(ref, field, x):
    return ref[pl.ds((field * ROWS + x) * LEVELS, LEVELS), :]


def far_both(gx, gy):
    return ((gx % 16 == 0) | (gx % 16 == 15)) & ((gy % 4 == 0) | (gy % 4 == 3))


def edges_kernel(place, state_u, state_v, state_w, state_th, planes, x_even, x_odd, y_even, y_odd, flat):
    even_x = place[0] % 2 == 0
    even_y = place[1] % 2 == 0
    states = (state_u, state_v, state_w, state_th)
    lane = lane_of((LEVELS, LANES))
    gathered = jnp.zeros((LEVELS, LANES), F32)
    for field in range(4):
        values = [states[field][pl.ds(x, LEVELS, stride=ROWS), :] for x in range(ROWS)]
        for x in range(ROWS):
            slot = field * ROWS + x
            planes[pl.ds(slot * LEVELS, LEVELS), :] = values[x]
            gathered = jnp.where(lane >> 1 == slot, turn(values[x], 2 * slot + 1, 1), gathered)
        for slot, depth in ((field, 0), (4, 1)) if field == 0 else ((field, 0),):
            span = pl.ds(slot * LEVELS, LEVELS)
            low, high = values[depth], values[ROWS - 1 - depth]
            x_even[span, :] = jnp.where(even_x, high, low)
            x_odd[span, :] = jnp.where(even_x, low, high)
    flat[...] = jnp.transpose(jnp.concatenate([gathered, jnp.zeros_like(gathered)], axis=0))
    high, low = flat[pl.ds(0, 16, stride=2), :], flat[pl.ds(1, 16, stride=2), :]
    y_even[0:16, :] = jnp.where(even_y, high, low)
    y_even[16:32, :] = jnp.zeros((16, LANES), F32)
    y_odd[...] = jnp.where(even_y, low, high)
    x_even[pl.ds(5 * LEVELS, 16), :] = jnp.where(even_y, low, high)


def column_of(row):
    return jnp.transpose(jnp.broadcast_to(row, (LANES, LANES)))


def inner_kernel(
    place,
    state,
    vectors,
    square_row,
    layer_in,
    layer_out,
    star,
    by_level,
    by_row,
    by_wave,
    by_block,
):
    fields = [[plane(state, f, x) for x in range(ROWS)] for f in range(4)]
    tall = column_of(vectors[:, :LANES])
    rate, density = tall[:LEVELS], tall[LEVELS:]
    row = row_of((LEVELS, LANES))
    by_level[pl.ds(0, LEVELS), :] = rate
    by_level[pl.ds(LEVELS, LEVELS), :] = jnp.where(
        row < LEVELS - 1, 0.5 * turn(density, -1, 0) / density, 0.0
    )
    by_level[pl.ds(2 * LEVELS, LEVELS), :] = jnp.where(row > 0, 0.5 * turn(density, 1, 0) / density, 0.0)
    own = by_level[pl.ds(place[0], 1), :]

    both = jnp.concatenate([own, own], axis=1)
    root, inverse, rho = decay(both, square_row[...])
    powers = squarings(rho, 6)
    for i, value in enumerate(powers + [powers[6] * rho, -1.0 / root]):
        by_row[pl.ds(8 * i, 8), :] = value
    half = row_of((LANES, LANES)) >> 1
    odd = (row_of((LANES, LANES)) & 1) != 0
    narrow = [jnp.broadcast_to(value[0:1, :LANES], (LANES, LANES)) for value in powers[:6]]
    rising = lane_powers(narrow, half)
    falling = lane_powers(narrow, 63 - half)
    by_wave[pl.ds(0, LANES), :] = rising
    by_wave[pl.ds(LANES, LANES), :] = falling
    by_wave[pl.ds(2 * LANES, LANES), :] = narrow[0] * jnp.where(odd, rising, falling)

    r64 = powers[6]
    r128 = r64 * r64
    r256 = r128 * r128
    images = 1.0 / (1.0 - r256 * r256)
    mine = place[1] & 3
    row = row_of(rho.shape)
    for j in range(4):
        for i, offset in enumerate((-1, 3)):
            exponent = jnp.where(row < 2, (mine - j + offset) & 7, (j - mine + offset) & 7)
            weight = jnp.where((exponent & 1) != 0, r64, 1.0)
            weight = weight * jnp.where((exponent & 2) != 0, r128, 1.0)
            weight = weight * jnp.where((exponent & 4) != 0, r256, 1.0)
            by_block[pl.ds((2 * j + i) * 8, 8), :] = weight * images
    scale = -1.0 / root
    by_block[pl.ds(64, 8), :] = jnp.where(row == 0, scale, jnp.where(row == 1, scale * r64, scale * inverse))

    for x in range(ROWS):
        u, v, w, th = (fields[f][x] for f in range(4))
        for f in range(4):
            here = fields[f][x]
            change = v * north_difference(here) + w * level_difference(here)
            if x == 0:
                change = change + u * fields[f][1]
            elif x == ROWS - 1:
                change = change - u * fields[f][x - 1]
            else:
                change = change + u * (fields[f][x + 1] - fields[f][x - 1])
            value = here - 0.1 * change
            if f == 2:
                value = value + 0.1 * th
            star[pl.ds((f * ROWS + x) * LEVELS, LEVELS), :] = value

    columns = jnp.concatenate(
        [jnp.concatenate([fields[f][x] for f in range(4)], axis=0).astype(BF16) for x in range(ROWS)],
        axis=1,
    )
    first = (((0,), (0,)), ((), ()))
    shift = [column_of(vectors[:, i * LANES : (i + 1) * LANES]) for i in (1, 2)]
    shift = jnp.concatenate(shift, axis=0)
    before = lax.dot_general(layer_in[...], columns, first, preferred_element_type=F32)
    before = before + jnp.concatenate([shift] * ROWS, axis=1)
    hidden = (before * (1.0 / (1.0 + jnp.exp(-before)))).astype(BF16)
    forcing = lax.dot_general(layer_out[...], hidden, first, preferred_element_type=F32)
    for x in range(ROWS):
        span = slice(x * LANES, (x + 1) * LANES)
        for f, part in ((2, forcing[LEVELS:, span]), (3, forcing[:LEVELS, span])):
            at = pl.ds((f * ROWS + x) * LEVELS, LEVELS)
            star[at, :] = star[at, :] + 0.2 * part


def side_terms(state, edge, low):
    u, v, w = (edge[pl.ds(f * LEVELS, LEVELS), :] for f in range(3))
    second = edge[pl.ds(4 * LEVELS, LEVELS), :]
    own = jnp.where(low, plane(state, 0, 0), plane(state, 0, ROWS - 1))
    sign = jnp.where(low, 0.1, -0.1)
    adds = [sign * own * edge[pl.ds(f * LEVELS, LEVELS), :] for f in range(4)]
    along = u * (own - second)
    beyond = u - (sign * along + 0.1 * (v * north_difference(u) + w * level_difference(u)))
    return adds, beyond


def outer_kernel(
    place,
    state,
    inner,
    x_even,
    x_odd,
    y_even,
    y_odd,
    relayed,
    by_level,
    forward,
    star,
    message,
    flat,
):
    even_x = place[0] % 2 == 0
    even_y = place[1] % 2 == 0
    shape = (LEVELS, LANES)
    lane = lane_of(shape)

    other = jnp.where(far_both(place[0], place[1]), relayed[16:32, :], y_odd[0:16, :])
    flat[...] = jnp.zeros((LANES, LANES), F32)
    flat[pl.ds(0, 16, stride=2), :] = jnp.where(even_y, y_even[0:16, :], other)
    flat[pl.ds(1, 16, stride=2), :] = jnp.where(even_y, other, y_even[0:16, :])
    columns = jnp.transpose(flat[...])[:LEVELS]
    even_adds, even_beyond = side_terms(state, x_even, ~even_x)
    odd_adds, odd_beyond = side_terms(state, x_odd, even_x)
    end_sign = jnp.where(lane == 0, 0.1, jnp.where(lane == LANES - 1, -0.1, 0.0))
    whole = [[None] * ROWS for _ in range(4)]
    side_u = [None] * ROWS
    for x in range(ROWS):
        v = plane(state, 1, x)
        for f in range(4):
            slot = f * ROWS + x
            side = end_sign * v * turn(columns, -(2 * slot + 1), 1)
            if f == 0:
                side_u[x] = side
            value = inner[pl.ds(slot * LEVELS, LEVELS), :] + side
            if x == 0:
                value = value + jnp.where(even_x, odd_adds[f], even_adds[f])
            if x == ROWS - 1:
                value = value + jnp.where(even_x, even_adds[f], odd_adds[f])
            whole[f][x] = value
            star[pl.ds(slot * LEVELS, LEVELS), :] = value

    low_beyond = jnp.where(even_x, odd_beyond, even_beyond)
    high_beyond = jnp.where(even_x, even_beyond, odd_beyond)
    padded = [low_beyond] + whole[0] + [high_beyond]
    divergence = []
    extra = [-0.5 * side_u[ROWS - 1], 0.5 * side_u[0]]
    up, down = by_level[pl.ds(LEVELS, LEVELS), :], by_level[pl.ds(2 * LEVELS, LEVELS), :]
    for x in range(ROWS):
        v, w = whole[1][x], whole[2][x]
        upright = up * turn(w, -1, 0) - down * turn(w, 1, 0)
        divergence.append(0.5 * (padded[x + 2] - padded[x]) + 0.5 * north_difference(v) + upright)
        low, high = LOW + x // 2, HIGH + x // 2
        value = jnp.where(lane == low, 0.5 * turn(v, low, 1), extra[x % 2])
        extra[x % 2] = jnp.where(lane == high, -0.5 * turn(v, high + 1, 1), value)
    pieces = [divergence[0], divergence[2], extra[0], divergence[1], divergence[3], extra[1]]
    modal = dot3(parts(forward[...]), parts(jnp.concatenate(pieces, axis=1)))
    for i in range(6):
        message[pl.ds(i, LEVELS, stride=6), :] = modal[:, i * LANES : (i + 1) * LANES]


def decay(rate, square):
    lam = rate + square
    root = jnp.sqrt(lam * (1.0 + lam))
    inverse = 1.0 + 2.0 * lam + 2.0 * root
    return root, inverse, 1.0 / inverse


def squarings(rho, count):
    powers = [rho]
    for _ in range(count):
        powers.append(powers[-1] * powers[-1])
    return powers


def lane_powers(powers, exponent):
    product = None
    for bit in range(6):
        factor = jnp.where((exponent & (1 << bit)) != 0, powers[bit], 1.0)
        product = factor if product is None else product * factor
    return product


def shifted(values, shift):
    size = values.shape[0]
    if shift % 8 == 0:
        zeros = jnp.zeros((abs(shift), values.shape[1]), F32)
        if shift > 0:
            return jnp.concatenate([zeros, values[:-shift]], axis=0)
        return jnp.concatenate([values[-shift:], zeros], axis=0)
    row = row_of(values.shape)
    inside = row >= shift if shift > 0 else row < size + shift
    return jnp.where(inside, turn(values, shift, 0), 0.0)


def by_parity(even, odd):
    shape = (8, even.shape[1])
    tile = jnp.where((row_of(shape) & 1) != 0, jnp.broadcast_to(odd, shape), jnp.broadcast_to(even, shape))
    return jnp.concatenate([tile] * (LANES // 8), axis=0)


def halves(values):
    return jnp.concatenate([values, values], axis=1)


def solve_kernel(place, received, basis_high, basis_low, by_row, by_wave, local, moments):
    blocks = received.shape[0] // 6
    lane = lane_of((blocks, LANES))
    ends = (lane == 0) | (lane == LANES - 1)
    even = place[1] < 4
    inside, outside = [], [jnp.zeros((blocks, LANES), F32)] * 2
    for h in range(2):
        first, second, extra = (received[pl.ds(3 * h + j, blocks, stride=6), :] for j in range(3))
        first = first + jnp.where(ends & even, turn(extra, 1, 0), 0.0)
        second = second + jnp.where(ends & ~even, turn(extra, -1, 0), 0.0)
        inside.append(jnp.concatenate([first, second], axis=0))
        for r in range(2):
            for i, start in enumerate((HIGH, LOW)):
                at = 2 * h + i
                outside[r] = jnp.where(lane == at, turn(extra, at - start - r, 1), outside[r])
    right = parts(jnp.concatenate(inside + [jnp.concatenate(outside, axis=0)], axis=1))
    first = (((0,), (0,)), ((), ()))
    dot = lambda a, b: lax.dot_general(a, b[...], first, preferred_element_type=F32)
    spectral = dot(right[0], basis_high) + (dot(right[0], basis_low) + dot(right[1], basis_high))
    source = jnp.concatenate([spectral[:LANES], spectral[LANES : 2 * LANES]], axis=1)
    ext = spectral[2 * LANES : 2 * LANES + 8]
    high = jnp.concatenate([ext[0:1], ext[2:3]], axis=1)
    low = jnp.concatenate([ext[1:2], ext[3:4]], axis=1)

    power = lambda i: by_row[pl.ds(8 * i, 1), :]
    ahead, behind = source, source
    for bit in range(6):
        ahead = ahead + power(bit) * shifted(ahead, 2 << bit)
        behind = behind + power(bit) * shifted(behind, -(2 << bit))
    border = halves(by_wave[pl.ds(2 * LANES, LANES), :]) * by_parity(high, low)
    local[...] = ahead + behind - source + border
    rho, r65 = power(0), power(7)
    across = [
        rho * ahead[LANES - 2 : LANES - 1] + high,
        rho * ahead[LANES - 1 :] + r65 * low,
        rho * behind[0:1] + r65 * high,
        rho * behind[1:2] + low,
        jnp.zeros((4, source.shape[1]), F32),
    ]
    across = jnp.concatenate(across, axis=0)
    for j in range(4):
        moments[pl.ds(j * 8, 8), :] = across


def back_kernel(place, local, moments, basis_high, basis_low, by_row, by_wave, by_block, message):
    width = local.shape[1]
    blocks = basis_high.shape[0] // 2
    even = place[1] < 4
    mine = place[1] & 3
    carry = jnp.zeros((8, width), F32)
    for j in range(4):
        theirs = moments[pl.ds(j * 8, 8), :]
        swapped = jnp.concatenate([theirs[:, LANES:], theirs[:, :LANES]], axis=1)
        carry = carry + by_block[pl.ds(16 * j, 8), :] * theirs + by_block[pl.ds(16 * j + 8, 8), :] * swapped
    own = moments[pl.ds(pl.multiple_of(mine * 8, 8), 8), :]
    scale, by_r64, by_inverse = (by_block[pl.ds(64 + i, 1), :] for i in range(3))
    after = scale * own[0:1] + by_r64 * carry[0:1] + by_inverse * carry[2:3]
    before = scale * own[3:4] + by_r64 * carry[3:4] + by_inverse * carry[1:2]
    total = local[...] + halves(by_wave[pl.ds(0, LANES), :]) * by_parity(carry[0:1], carry[1:2])
    total = total + halves(by_wave[pl.ds(LANES, LANES), :]) * by_parity(carry[2:3], carry[3:4])
    total = total * scale
    pieces = [total[:, :LANES], total[:, LANES:]]
    for h in range(2):
        span = slice(h * LANES, (h + 1) * LANES)
        pieces += [after[:, span], before[:, span]]
    pieces.append(jnp.zeros((LANES - 4, LANES), F32))
    right = parts(jnp.concatenate(pieces, axis=0))
    last = (((1,), (1,)), ((), ()))
    dot = lambda a, b: lax.dot_general(a[...], b, last, preferred_element_type=F32)
    pressure = dot(basis_high, right[0]) + (dot(basis_high, right[1]) + dot(basis_low, right[0]))
    lane = lane_of((blocks, LANES))
    ends = (lane == 0) | (lane == LANES - 1)
    outside = [pressure[r * blocks : (r + 1) * blocks, 2 * LANES :] for r in range(2)]
    for h in range(2):
        span = slice(h * LANES, (h + 1) * LANES)
        first, second = pressure[:blocks, span], pressure[blocks:, span]
        extra = jnp.where(ends, jnp.where(even, turn(first, -1, 0), turn(second, 1, 0)), 0.0)
        for r in range(2):
            extra = jnp.where(lane == HIGH + r, turn(outside[r], HIGH + r - 2 * h, 1), extra)
            extra = jnp.where(lane == LOW + r, turn(outside[r], LOW + r - 1 - 2 * h, 1), extra)
        for j, value in enumerate((first, second, extra)):
            message[pl.ds(3 * h + j, blocks, stride=6), :] = value


def final_kernel(received, sent, star, back, by_level, out, held, sent_out):
    size = LEVELS * ROWS
    span = lambda f: pl.ds(f * size, size)
    copies = [pltpu.make_async_copy(held.at[span(f), :], out.at[span(f), :], sent_out.at[f]) for f in range(4)]

    def put(f, changes):
        for x in range(ROWS):
            value = star[pl.ds((f * ROWS + x) * LEVELS, LEVELS), :]
            if changes is not None:
                value = value - changes[:, x * LANES : (x + 1) * LANES]
            held[pl.ds(f * size + x, LEVELS, stride=ROWS), :] = value
        copies[f].start()

    put(3, None)
    lane = lane_of((LEVELS, LANES))
    row_at = lambda ref, r: ref[pl.ds(3 * (r % 2) + r // 2, LEVELS, stride=6), :]
    p = [row_at(received, r) for r in range(ROWS)]
    extra = [row_at(received, 4), row_at(received, 5)]
    low = [turn(extra[r % 2], -(LOW + r // 2), 1) for r in range(ROWS)]
    high = [turn(extra[r % 2], LANES - 1 - (HIGH + r // 2), 1) for r in range(ROWS)]
    four_rate = 4.0 * by_level[pl.ds(0, LEVELS), :]

    def next_row(r, opposite):
        here = p[r]
        divergence = row_at(sent, r)
        plus = jnp.where(lane < LANES - 2, turn(here, -2, 1), turn(high[r], -1, 1))
        minus = jnp.where(lane > 1, turn(here, 2, 1), turn(low[r], 1, 1))
        return (
            2.0 * here
            - opposite
            + four_rate * here
            + (2.0 * here - plus - minus)
            + 4.0 * divergence
        )

    ends = (lane == 0) | (lane == LANES - 1)
    before = jnp.where(ends, extra[1], next_row(1, p[3]))
    after = jnp.where(ends, extra[0], next_row(2, p[0]))
    padded = [before] + p + [after]
    matrix = back[...]
    joined = lambda values: parts(jnp.concatenate(values, axis=1))
    put(2, dot3(parts(0.5 * level_difference(matrix)), joined(p)))
    matrix = parts(matrix)
    put(1, dot3(matrix, joined([0.5 * north_difference(p[x], low[x], high[x]) for x in range(ROWS)])))
    put(0, dot3(matrix, joined([0.5 * (padded[x + 2] - padded[x]) for x in range(ROWS)])))
    for copy in copies:
        copy.wait()


def call(kernel, shapes, args, name, scalars=1, scratch=(), cost=None, copies=0):
    vmem = pl.BlockSpec(memory_space=pltpu.VMEM)
    scalar = pl.BlockSpec(memory_space=pltpu.SMEM)
    return pl.pallas_call(
        kernel,
        out_shape=[jax.ShapeDtypeStruct(s, F32) for s in shapes],
        in_specs=[scalar] * scalars + [vmem] * (len(args) - scalars),
        out_specs=[pl.BlockSpec(memory_space=pl.ANY) if copies else vmem] * len(shapes),
        scratch_shapes=[pltpu.VMEM(s, F32) for s in scratch]
        + ([pltpu.SemaphoreType.DMA((copies,))] if copies else []),
        compiler_params=pltpu.CompilerParams(vmem_limit_bytes=32 * 1024 * 1024),
        name=name,
        cost_estimate=cost,
    )(*args)


def swap(values, axis, odd):
    count = lax.axis_size(axis)
    pairs = []
    for i in range(odd, count + odd, 2):
        pairs += [(i % count, (i + 1) % count), ((i + 1) % count, i % count)]
    return lax.ppermute(values, axis, pairs)


def swap_odd_y(values):
    count_x, count_y = lax.axis_size("gx"), lax.axis_size("gy")
    pairs = []
    for i in range(count_x):
        for j in range(1, count_y + 1, 2):
            one, two = j % count_y, (j + 1) % count_y
            if not far_both(i, one):
                pairs += [(i * count_y + one, i * count_y + two), (i * count_y + two, i * count_y + one)]
    return lax.ppermute(values, ("gx", "gy"), pairs)


def hand_over(values):
    count_x, count_y = lax.axis_size("gx"), lax.axis_size("gy")
    pairs = [
        ((i ^ 1) * count_y + j, i * count_y + j)
        for i in range(count_x)
        for j in range(count_y)
        if far_both(i, j)
    ]
    return lax.ppermute(values, ("gx", "gy"), pairs)


def exchange(values):
    count_x, count_y = lax.axis_size("gx"), lax.axis_size("gy")
    near = count_y // 2
    groups = [[i * count_y + h * near + y for i in range(count_x) for h in range(2)] for y in range(near)]
    shaped = values.reshape(2 * count_x, 1, values.size // (2 * count_x))
    moved = lax.all_to_all(
        shaped, ("gx", "gy"), 0, 0, tiled=True, axis_index_groups=groups
    )
    return moved.reshape(values.shape)


def on_device(
    model_state, density, layer_in, layer_bias, layer_out, mode_forward, mode_back, mode_rate
):
    blocks = lax.axis_size("gx")
    total_east = blocks * ROWS
    place = jnp.stack([lax.axis_index("gx"), lax.axis_index("gy")]).astype(jnp.int32)
    state = [model_state[f].reshape(LEVELS * ROWS, LANES) for f in range(4)]
    basis, square = east_tables(total_east // 2, blocks)
    basis_high, basis_low = split_table(np.ascontiguousarray(basis.T))
    square_row = np.ascontiguousarray(np.broadcast_to(np.concatenate([square, square]), (8, total_east)))

    planes, x_even, x_odd, y_even, y_odd = call(
        edges_kernel,
        [(16 * LEVELS, LANES), (5 * LEVELS + 16, LANES), (5 * LEVELS, LANES), (32, LANES), (16, LANES)],
        [place, *state],
        "edges",
        scratch=[(LANES, LANES)],
    )
    got_x_even = swap(x_even, "gx", 0)
    y_both = jnp.concatenate([y_odd, got_x_even[5 * LEVELS :]], axis=0)
    y_both, x_odd, y_even = lax.optimization_barrier((y_both, x_odd, y_even))
    got_y_odd = swap_odd_y(y_both)
    got_x_odd = swap(x_odd, "gx", 1)
    inner, by_level, by_row, by_wave, by_block = call(
        inner_kernel,
        [(16 * LEVELS, LANES), (3 * LEVELS, LANES), (72, total_east), (3 * LANES, LANES), (72, total_east)],
        [
            place,
            planes,
            jnp.concatenate([mode_rate, density, layer_bias])[None, :],
            square_row,
            layer_in,
            layer_out,
        ],
        "inner",
        cost=pl.CostEstimate(flops=10**10, transcendentals=0, bytes_accessed=2**24),
    )
    inner, y_even = lax.optimization_barrier((inner, y_even))
    got_y_even = swap(y_even, "gy", 0)
    inner, got_y_odd = lax.optimization_barrier((inner, got_y_odd))
    relayed = hand_over(got_y_odd)
    star, message = call(
        outer_kernel,
        [(16 * LEVELS, LANES), (blocks * 6, LANES)],
        [
            place,
            planes,
            inner,
            got_x_even,
            got_x_odd,
            got_y_even,
            got_y_odd,
            relayed,
            by_level,
            mode_forward,
        ],
        "outer",
        scratch=[(LANES, LANES)],
    )
    modal = exchange(message)
    local, moments = call(
        solve_kernel,
        [(LANES, total_east), (32, total_east)],
        [place, modal, basis_high, basis_low, by_row, by_wave],
        "solve",
    )
    moments = lax.all_to_all(
        moments.reshape(4, 8, total_east),
        "gy",
        0,
        0,
        tiled=True,
        axis_index_groups=[[0, 1, 2, 3], [4, 5, 6, 7]],
    ).reshape(32, total_east)
    (reply,) = call(
        back_kernel,
        [(blocks * 6, LANES)],
        [place, local, moments, basis_high, basis_low, by_row, by_wave, by_block],
        "back",
    )
    pressure = exchange(reply)
    (out,) = call(
        final_kernel,
        [(4 * LEVELS * ROWS, LANES)],
        [pressure, message, star, mode_back, by_level],
        "final",
        scalars=0,
        scratch=[(4 * LEVELS * ROWS, LANES)],
        copies=4,
    )
    return out.reshape(model_state.shape)


def solution(mesh):
    return jax.shard_map(
        on_device,
        mesh=mesh,
        in_specs=(P(None, None, "gx", "gy"), P(), P(), P(), P(), P(), P(), P()),
        out_specs=P(None, None, "gx", "gy"),
        check_vma=False,
    )
```

```python
import math

import jax
import jax.numpy as jnp
import ml_dtypes
import numpy as np
from jax import lax
from jax.experimental import pallas as pl
from jax.experimental.pallas import tpu as pltpu
from jax.sharding import PartitionSpec as P

F32 = jnp.float32
BF16 = jnp.bfloat16
LEVELS = 64
ROWS = 4
LANES = 128
LOW = 16
HIGH = 32


def split_table(table):
    high = table.astype(np.float32).astype(ml_dtypes.bfloat16)
    low = (table - high.astype(np.float64)).astype(np.float32).astype(ml_dtypes.bfloat16)
    return high, low


def east_tables(total, blocks):
    rows = total // blocks
    x = (np.arange(rows)[:, None] + rows * np.arange(blocks)[None, :]).reshape(-1)
    k = np.arange(total)
    angle = 2.0 * math.pi * ((k[:, None] * x[None, :]) % total) / total
    basis = np.where((k <= total // 2)[:, None], np.cos(angle), np.sin(angle))
    scale = np.where((k == 0) | (k == total // 2), 1.0, math.sqrt(2.0)) / math.sqrt(total)
    basis = basis * scale[:, None]
    square = np.sin(math.pi * k / total) ** 2
    return basis, square.astype(np.float32)


def position():
    return lax.axis_index("gx"), lax.axis_index("gy")


def lane_of(shape):
    return lax.broadcasted_iota(jnp.int32, shape, len(shape) - 1)


def row_of(shape):
    return lax.broadcasted_iota(jnp.int32, shape, 0)


def turn(values, shift, axis):
    size = values.shape[axis]
    return pltpu.roll(values, shift % size, axis) if shift % size else values


def parts(values):
    high = values.astype(BF16)
    return high, (values - high.astype(F32)).astype(BF16)


def dot3(left, right):
    dot = lambda a, b: jnp.dot(a, b, preferred_element_type=F32)
    return dot(left[0], right[0]) + (dot(left[0], right[1]) + dot(left[1], right[0]))


def level_difference(values):
    row = row_of(values.shape)
    last = values.shape[0] - 1
    upper = jnp.where(row < last, turn(values, -1, 0), 0.0)
    lower = jnp.where(row > 0, turn(values, 1, 0), 0.0)
    return upper - lower


def north_difference(values, low=0.0, high=0.0):
    lane = lane_of(values.shape)
    after = jnp.where(lane < LANES - 1, turn(values, -1, 1), high)
    before = jnp.where(lane > 0, turn(values, 1, 1), low)
    return after - before


def plane(ref, field, x):
    return ref[pl.ds((field * ROWS + x) * LEVELS, LEVELS), :]


def far_both(gx, gy):
    return ((gx % 16 == 0) | (gx % 16 == 15)) & ((gy % 4 == 0) | (gy % 4 == 3))


def edges_kernel(state_u, state_v, state_w, state_th, planes, x_even, x_odd, y_even, y_odd, flat):
    place = position()
    even_x = place[0] % 2 == 0
    even_y = place[1] % 2 == 0
    states = (state_u, state_v, state_w, state_th)
    lane = lane_of((LEVELS, LANES))
    gathered = jnp.zeros((LEVELS, LANES), F32)
    for field in range(4):
        values = [states[field][pl.ds(x, LEVELS, stride=ROWS), :] for x in range(ROWS)]
        for x in range(ROWS):
            slot = field * ROWS + x
            planes[pl.ds(slot * LEVELS, LEVELS), :] = values[x]
            gathered = jnp.where(lane >> 1 == slot, turn(values[x], 2 * slot + 1, 1), gathered)
        for slot, depth in ((field, 0), (4, 1)) if field == 0 else ((field, 0),):
            span = pl.ds(slot * LEVELS, LEVELS)
            low, high = values[depth], values[ROWS - 1 - depth]
            x_even[span, :] = jnp.where(even_x, high, low)
            x_odd[span, :] = jnp.where(even_x, low, high)
    flat[...] = jnp.transpose(jnp.concatenate([gathered, jnp.zeros_like(gathered)], axis=0))
    high, low = flat[pl.ds(0, 16, stride=2), :], flat[pl.ds(1, 16, stride=2), :]
    y_even[0:16, :] = jnp.where(even_y, high, low)
    y_even[16:32, :] = jnp.zeros((16, LANES), F32)
    y_odd[...] = jnp.where(even_y, low, high)
    x_even[pl.ds(5 * LEVELS, 16), :] = jnp.where(even_y, low, high)


def column_of(row):
    return jnp.transpose(jnp.broadcast_to(row, (LANES, LANES)))


def inner_kernel(
    state,
    vectors,
    square_row,
    layer_in,
    layer_out,
    star,
    by_level,
    by_row,
    by_wave,
    by_block,
):
    place = position()
    fields = [[plane(state, f, x) for x in range(ROWS)] for f in range(4)]
    tall = column_of(vectors[:, :LANES])
    rate, density = tall[:LEVELS], tall[LEVELS:]
    row = row_of((LEVELS, LANES))
    by_level[pl.ds(0, LEVELS), :] = rate
    by_level[pl.ds(LEVELS, LEVELS), :] = jnp.where(
        row < LEVELS - 1, 0.5 * turn(density, -1, 0) / density, 0.0
    )
    by_level[pl.ds(2 * LEVELS, LEVELS), :] = jnp.where(row > 0, 0.5 * turn(density, 1, 0) / density, 0.0)
    own = by_level[pl.ds(place[0], 1), :]

    both = jnp.concatenate([own, own], axis=1)
    root, inverse, rho = decay(both, square_row[...])
    powers = squarings(rho, 6)
    for i, value in enumerate(powers + [powers[6] * rho, -1.0 / root]):
        by_row[pl.ds(8 * i, 8), :] = value
    half = row_of((LANES, LANES)) >> 1
    odd = (row_of((LANES, LANES)) & 1) != 0
    narrow = [jnp.broadcast_to(value[0:1, :LANES], (LANES, LANES)) for value in powers[:6]]
    rising = lane_powers(narrow, half)
    falling = lane_powers(narrow, 63 - half)
    by_wave[pl.ds(0, LANES), :] = rising
    by_wave[pl.ds(LANES, LANES), :] = falling
    by_wave[pl.ds(2 * LANES, LANES), :] = narrow[0] * jnp.where(odd, rising, falling)

    r64 = powers[6]
    r128 = r64 * r64
    r256 = r128 * r128
    images = 1.0 / (1.0 - r256 * r256)
    mine = place[1] & 3
    row = row_of(rho.shape)
    for j in range(4):
        for i, offset in enumerate((-1, 3)):
            exponent = jnp.where(row < 2, (mine - j + offset) & 7, (j - mine + offset) & 7)
            weight = jnp.where((exponent & 1) != 0, r64, 1.0)
            weight = weight * jnp.where((exponent & 2) != 0, r128, 1.0)
            weight = weight * jnp.where((exponent & 4) != 0, r256, 1.0)
            by_block[pl.ds((2 * j + i) * 8, 8), :] = weight * images
    scale = -1.0 / root
    by_block[pl.ds(64, 8), :] = jnp.where(row == 0, scale, jnp.where(row == 1, scale * r64, scale * inverse))

    for x in range(ROWS):
        u, v, w, th = (fields[f][x] for f in range(4))
        for f in range(4):
            here = fields[f][x]
            change = v * north_difference(here) + w * level_difference(here)
            if x == 0:
                change = change + u * fields[f][1]
            elif x == ROWS - 1:
                change = change - u * fields[f][x - 1]
            else:
                change = change + u * (fields[f][x + 1] - fields[f][x - 1])
            value = here - 0.1 * change
            if f == 2:
                value = value + 0.1 * th
            star[pl.ds((f * ROWS + x) * LEVELS, LEVELS), :] = value

    columns = jnp.concatenate(
        [jnp.concatenate([fields[f][x] for f in range(4)], axis=0).astype(BF16) for x in range(ROWS)],
        axis=1,
    )
    first = (((0,), (0,)), ((), ()))
    shift = [column_of(vectors[:, i * LANES : (i + 1) * LANES]) for i in (1, 2)]
    shift = jnp.concatenate(shift, axis=0)
    before = lax.dot_general(layer_in[...], columns, first, preferred_element_type=F32)
    before = before + jnp.concatenate([shift] * ROWS, axis=1)
    hidden = (before * (1.0 / (1.0 + jnp.exp(-before)))).astype(BF16)
    forcing = lax.dot_general(layer_out[...], hidden, first, preferred_element_type=F32)
    for x in range(ROWS):
        span = slice(x * LANES, (x + 1) * LANES)
        for f, part in ((2, forcing[LEVELS:, span]), (3, forcing[:LEVELS, span])):
            at = pl.ds((f * ROWS + x) * LEVELS, LEVELS)
            star[at, :] = star[at, :] + 0.2 * part


def side_terms(state, edge, low):
    u, v, w = (edge[pl.ds(f * LEVELS, LEVELS), :] for f in range(3))
    second = edge[pl.ds(4 * LEVELS, LEVELS), :]
    own = jnp.where(low, plane(state, 0, 0), plane(state, 0, ROWS - 1))
    sign = jnp.where(low, 0.1, -0.1)
    adds = [sign * own * edge[pl.ds(f * LEVELS, LEVELS), :] for f in range(4)]
    along = u * (own - second)
    beyond = u - (sign * along + 0.1 * (v * north_difference(u) + w * level_difference(u)))
    return adds, beyond


def outer_kernel(
    state,
    inner,
    x_even,
    x_odd,
    y_even,
    y_odd,
    relayed,
    by_level,
    forward,
    star,
    message,
    flat,
):
    place = position()
    even_x = place[0] % 2 == 0
    even_y = place[1] % 2 == 0
    shape = (LEVELS, LANES)
    lane = lane_of(shape)

    other = jnp.where(far_both(place[0], place[1]), relayed[16:32, :], y_odd[0:16, :])
    flat[...] = jnp.zeros((LANES, LANES), F32)
    flat[pl.ds(0, 16, stride=2), :] = jnp.where(even_y, y_even[0:16, :], other)
    flat[pl.ds(1, 16, stride=2), :] = jnp.where(even_y, other, y_even[0:16, :])
    columns = jnp.transpose(flat[...])[:LEVELS]
    even_adds, even_beyond = side_terms(state, x_even, ~even_x)
    odd_adds, odd_beyond = side_terms(state, x_odd, even_x)
    end_sign = jnp.where(lane == 0, 0.1, jnp.where(lane == LANES - 1, -0.1, 0.0))
    whole = [[None] * ROWS for _ in range(4)]
    side_u = [None] * ROWS
    for x in range(ROWS):
        v = plane(state, 1, x)
        for f in range(4):
            slot = f * ROWS + x
            side = end_sign * v * turn(columns, -(2 * slot + 1), 1)
            if f == 0:
                side_u[x] = side
            value = inner[pl.ds(slot * LEVELS, LEVELS), :] + side
            if x == 0:
                value = value + jnp.where(even_x, odd_adds[f], even_adds[f])
            if x == ROWS - 1:
                value = value + jnp.where(even_x, even_adds[f], odd_adds[f])
            whole[f][x] = value
            star[pl.ds(slot * LEVELS, LEVELS), :] = value

    low_beyond = jnp.where(even_x, odd_beyond, even_beyond)
    high_beyond = jnp.where(even_x, even_beyond, odd_beyond)
    padded = [low_beyond] + whole[0] + [high_beyond]
    divergence = []
    extra = [-0.5 * side_u[ROWS - 1], 0.5 * side_u[0]]
    up, down = by_level[pl.ds(LEVELS, LEVELS), :], by_level[pl.ds(2 * LEVELS, LEVELS), :]
    for x in range(ROWS):
        v, w = whole[1][x], whole[2][x]
        upright = up * turn(w, -1, 0) - down * turn(w, 1, 0)
        divergence.append(0.5 * (padded[x + 2] - padded[x]) + 0.5 * north_difference(v) + upright)
        low, high = LOW + x // 2, HIGH + x // 2
        value = jnp.where(lane == low, 0.5 * turn(v, low, 1), extra[x % 2])
        extra[x % 2] = jnp.where(lane == high, -0.5 * turn(v, high + 1, 1), value)
    pieces = [divergence[0], divergence[2], extra[0], divergence[1], divergence[3], extra[1]]
    modal = dot3(parts(forward[...]), parts(jnp.concatenate(pieces, axis=1)))
    for i in range(6):
        message[pl.ds(i, LEVELS, stride=6), :] = modal[:, i * LANES : (i + 1) * LANES]


def decay(rate, square):
    lam = rate + square
    root = jnp.sqrt(lam * (1.0 + lam))
    inverse = 1.0 + 2.0 * lam + 2.0 * root
    return root, inverse, 1.0 / inverse


def squarings(rho, count):
    powers = [rho]
    for _ in range(count):
        powers.append(powers[-1] * powers[-1])
    return powers


def lane_powers(powers, exponent):
    product = None
    for bit in range(6):
        factor = jnp.where((exponent & (1 << bit)) != 0, powers[bit], 1.0)
        product = factor if product is None else product * factor
    return product


def shifted(values, shift):
    size = values.shape[0]
    if shift % 8 == 0:
        zeros = jnp.zeros((abs(shift), values.shape[1]), F32)
        if shift > 0:
            return jnp.concatenate([zeros, values[:-shift]], axis=0)
        return jnp.concatenate([values[-shift:], zeros], axis=0)
    row = row_of(values.shape)
    inside = row >= shift if shift > 0 else row < size + shift
    return jnp.where(inside, turn(values, shift, 0), 0.0)


def by_parity(even, odd):
    shape = (8, even.shape[1])
    tile = jnp.where((row_of(shape) & 1) != 0, jnp.broadcast_to(odd, shape), jnp.broadcast_to(even, shape))
    return jnp.concatenate([tile] * (LANES // 8), axis=0)


def halves(values):
    return jnp.concatenate([values, values], axis=1)


def solve_kernel(received, basis_high, basis_low, by_row, by_wave, local, moments):
    place = position()
    blocks = received.shape[0] // 6
    lane = lane_of((blocks, LANES))
    ends = (lane == 0) | (lane == LANES - 1)
    even = place[1] < 4
    inside, outside = [], [jnp.zeros((blocks, LANES), F32)] * 2
    for h in range(2):
        first, second, extra = (received[pl.ds(3 * h + j, blocks, stride=6), :] for j in range(3))
        first = first + jnp.where(ends & even, turn(extra, 1, 0), 0.0)
        second = second + jnp.where(ends & ~even, turn(extra, -1, 0), 0.0)
        inside.append(jnp.concatenate([first, second], axis=0))
        for r in range(2):
            for i, start in enumerate((HIGH, LOW)):
                at = 2 * h + i
                outside[r] = jnp.where(lane == at, turn(extra, at - start - r, 1), outside[r])
    right = parts(jnp.concatenate(inside + [jnp.concatenate(outside, axis=0)], axis=1))
    first = (((0,), (0,)), ((), ()))
    dot = lambda a, b: lax.dot_general(a, b[...], first, preferred_element_type=F32)
    spectral = dot(right[0], basis_high) + (dot(right[0], basis_low) + dot(right[1], basis_high))
    source = jnp.concatenate([spectral[:LANES], spectral[LANES : 2 * LANES]], axis=1)
    ext = spectral[2 * LANES : 2 * LANES + 8]
    high = jnp.concatenate([ext[0:1], ext[2:3]], axis=1)
    low = jnp.concatenate([ext[1:2], ext[3:4]], axis=1)

    power = lambda i: by_row[pl.ds(8 * i, 1), :]
    ahead, behind = source, source
    for bit in range(6):
        ahead = ahead + power(bit) * shifted(ahead, 2 << bit)
        behind = behind + power(bit) * shifted(behind, -(2 << bit))
    border = halves(by_wave[pl.ds(2 * LANES, LANES), :]) * by_parity(high, low)
    local[...] = ahead + behind - source + border
    rho, r65 = power(0), power(7)
    across = [
        rho * ahead[LANES - 2 : LANES - 1] + high,
        rho * ahead[LANES - 1 :] + r65 * low,
        rho * behind[0:1] + r65 * high,
        rho * behind[1:2] + low,
        jnp.zeros((4, source.shape[1]), F32),
    ]
    across = jnp.concatenate(across, axis=0)
    for j in range(4):
        moments[pl.ds(j * 8, 8), :] = across


def back_kernel(local, moments, basis_high, basis_low, by_row, by_wave, by_block, message):
    place = position()
    width = local.shape[1]
    blocks = basis_high.shape[0] // 2
    even = place[1] < 4
    mine = place[1] & 3
    carry = jnp.zeros((8, width), F32)
    for j in range(4):
        theirs = moments[pl.ds(j * 8, 8), :]
        swapped = jnp.concatenate([theirs[:, LANES:], theirs[:, :LANES]], axis=1)
        carry = carry + by_block[pl.ds(16 * j, 8), :] * theirs + by_block[pl.ds(16 * j + 8, 8), :] * swapped
    own = moments[pl.ds(pl.multiple_of(mine * 8, 8), 8), :]
    scale, by_r64, by_inverse = (by_block[pl.ds(64 + i, 1), :] for i in range(3))
    after = scale * own[0:1] + by_r64 * carry[0:1] + by_inverse * carry[2:3]
    before = scale * own[3:4] + by_r64 * carry[3:4] + by_inverse * carry[1:2]
    total = local[...] + halves(by_wave[pl.ds(0, LANES), :]) * by_parity(carry[0:1], carry[1:2])
    total = total + halves(by_wave[pl.ds(LANES, LANES), :]) * by_parity(carry[2:3], carry[3:4])
    total = total * scale
    pieces = [total[:, :LANES], total[:, LANES:]]
    for h in range(2):
        span = slice(h * LANES, (h + 1) * LANES)
        pieces += [after[:, span], before[:, span]]
    pieces.append(jnp.zeros((LANES - 4, LANES), F32))
    right = parts(jnp.concatenate(pieces, axis=0))
    last = (((1,), (1,)), ((), ()))
    dot = lambda a, b: lax.dot_general(a[...], b, last, preferred_element_type=F32)
    pressure = dot(basis_high, right[0]) + (dot(basis_high, right[1]) + dot(basis_low, right[0]))
    lane = lane_of((blocks, LANES))
    ends = (lane == 0) | (lane == LANES - 1)
    outside = [pressure[r * blocks : (r + 1) * blocks, 2 * LANES :] for r in range(2)]
    for h in range(2):
        span = slice(h * LANES, (h + 1) * LANES)
        first, second = pressure[:blocks, span], pressure[blocks:, span]
        extra = jnp.where(ends, jnp.where(even, turn(first, -1, 0), turn(second, 1, 0)), 0.0)
        for r in range(2):
            extra = jnp.where(lane == HIGH + r, turn(outside[r], HIGH + r - 2 * h, 1), extra)
            extra = jnp.where(lane == LOW + r, turn(outside[r], LOW + r - 1 - 2 * h, 1), extra)
        for j, value in enumerate((first, second, extra)):
            message[pl.ds(3 * h + j, blocks, stride=6), :] = value


def final_kernel(received, sent, star, back, by_level, out, held, sent_out):
    size = LEVELS * ROWS
    span = lambda f: pl.ds(f * size, size)
    copies = [pltpu.make_async_copy(held.at[span(f), :], out.at[span(f), :], sent_out.at[f]) for f in range(4)]

    def put(f, changes):
        for x in range(ROWS):
            value = star[pl.ds((f * ROWS + x) * LEVELS, LEVELS), :]
            if changes is not None:
                value = value - changes[:, x * LANES : (x + 1) * LANES]
            held[pl.ds(f * size + x, LEVELS, stride=ROWS), :] = value
        copies[f].start()

    put(3, None)
    lane = lane_of((LEVELS, LANES))
    row_at = lambda ref, r: ref[pl.ds(3 * (r % 2) + r // 2, LEVELS, stride=6), :]
    p = [row_at(received, r) for r in range(ROWS)]
    extra = [row_at(received, 4), row_at(received, 5)]
    low = [turn(extra[r % 2], -(LOW + r // 2), 1) for r in range(ROWS)]
    high = [turn(extra[r % 2], LANES - 1 - (HIGH + r // 2), 1) for r in range(ROWS)]
    four_rate = 4.0 * by_level[pl.ds(0, LEVELS), :]

    def next_row(r, opposite):
        here = p[r]
        divergence = row_at(sent, r)
        plus = jnp.where(lane < LANES - 2, turn(here, -2, 1), turn(high[r], -1, 1))
        minus = jnp.where(lane > 1, turn(here, 2, 1), turn(low[r], 1, 1))
        return (
            2.0 * here
            - opposite
            + four_rate * here
            + (2.0 * here - plus - minus)
            + 4.0 * divergence
        )

    ends = (lane == 0) | (lane == LANES - 1)
    before = jnp.where(ends, extra[1], next_row(1, p[3]))
    after = jnp.where(ends, extra[0], next_row(2, p[0]))
    padded = [before] + p + [after]
    matrix = back[...]
    joined = lambda values: parts(jnp.concatenate(values, axis=1))
    put(2, dot3(parts(0.5 * level_difference(matrix)), joined(p)))
    matrix = parts(matrix)
    put(1, dot3(matrix, joined([0.5 * north_difference(p[x], low[x], high[x]) for x in range(ROWS)])))
    put(0, dot3(matrix, joined([0.5 * (padded[x + 2] - padded[x]) for x in range(ROWS)])))
    for copy in copies:
        copy.wait()


def call(kernel, shapes, args, name, scratch=(), cost=None, copies=0):
    vmem = pl.BlockSpec(memory_space=pltpu.VMEM)
    return pl.pallas_call(
        kernel,
        out_shape=[jax.ShapeDtypeStruct(s, F32) for s in shapes],
        in_specs=[vmem] * len(args),
        out_specs=[pl.BlockSpec(memory_space=pl.ANY) if copies else vmem] * len(shapes),
        scratch_shapes=[pltpu.VMEM(s, F32) for s in scratch]
        + ([pltpu.SemaphoreType.DMA((copies,))] if copies else []),
        compiler_params=pltpu.CompilerParams(vmem_limit_bytes=32 * 1024 * 1024),
        name=name,
        cost_estimate=cost,
    )(*args)


def swap(values, axis, odd):
    count = lax.axis_size(axis)
    pairs = []
    for i in range(odd, count + odd, 2):
        pairs += [(i % count, (i + 1) % count), ((i + 1) % count, i % count)]
    return lax.ppermute(values, axis, pairs)


def swap_odd_y(values):
    count_x, count_y = lax.axis_size("gx"), lax.axis_size("gy")
    pairs = []
    for i in range(count_x):
        for j in range(1, count_y + 1, 2):
            one, two = j % count_y, (j + 1) % count_y
            if not far_both(i, one):
                pairs += [(i * count_y + one, i * count_y + two), (i * count_y + two, i * count_y + one)]
    return lax.ppermute(values, ("gx", "gy"), pairs)


def hand_over(values):
    count_x, count_y = lax.axis_size("gx"), lax.axis_size("gy")
    pairs = [
        ((i ^ 1) * count_y + j, i * count_y + j)
        for i in range(count_x)
        for j in range(count_y)
        if far_both(i, j)
    ]
    return lax.ppermute(values, ("gx", "gy"), pairs)


def exchange(values):
    count_x, count_y = lax.axis_size("gx"), lax.axis_size("gy")
    near = count_y // 2
    groups = [[i * count_y + h * near + y for i in range(count_x) for h in range(2)] for y in range(near)]
    shaped = values.reshape(2 * count_x, 1, values.size // (2 * count_x))
    moved = lax.all_to_all(
        shaped, ("gx", "gy"), 0, 0, tiled=True, axis_index_groups=groups
    )
    return moved.reshape(values.shape)


def on_device(
    model_state, density, layer_in, layer_bias, layer_out, mode_forward, mode_back, mode_rate
):
    blocks = lax.axis_size("gx")
    total_east = blocks * ROWS
    state = [model_state[f].reshape(LEVELS * ROWS, LANES) for f in range(4)]
    basis, square = east_tables(total_east // 2, blocks)
    basis_high, basis_low = split_table(np.ascontiguousarray(basis.T))
    square_row = np.ascontiguousarray(np.broadcast_to(np.concatenate([square, square]), (8, total_east)))

    planes, x_even, x_odd, y_even, y_odd = call(
        edges_kernel,
        [(16 * LEVELS, LANES), (5 * LEVELS + 16, LANES), (5 * LEVELS, LANES), (32, LANES), (16, LANES)],
        [*state],
        "edges",
        scratch=[(LANES, LANES)],
    )
    got_x_even = swap(x_even, "gx", 0)
    y_both = jnp.concatenate([y_odd, got_x_even[5 * LEVELS :]], axis=0)
    y_both, x_odd, y_even = lax.optimization_barrier((y_both, x_odd, y_even))
    got_y_odd = swap_odd_y(y_both)
    got_x_odd = swap(x_odd, "gx", 1)
    inner, by_level, by_row, by_wave, by_block = call(
        inner_kernel,
        [(16 * LEVELS, LANES), (3 * LEVELS, LANES), (72, total_east), (3 * LANES, LANES), (72, total_east)],
        [
            planes,
            jnp.concatenate([mode_rate, density, layer_bias])[None, :],
            square_row,
            layer_in,
            layer_out,
        ],
        "inner",
        cost=pl.CostEstimate(flops=10**10, transcendentals=0, bytes_accessed=2**24),
    )
    inner, y_even = lax.optimization_barrier((inner, y_even))
    got_y_even = swap(y_even, "gy", 0)
    inner, got_y_odd = lax.optimization_barrier((inner, got_y_odd))
    relayed = hand_over(got_y_odd)
    star, message = call(
        outer_kernel,
        [(16 * LEVELS, LANES), (blocks * 6, LANES)],
        [
            planes,
            inner,
            got_x_even,
            got_x_odd,
            got_y_even,
            got_y_odd,
            relayed,
            by_level,
            mode_forward,
        ],
        "outer",
        scratch=[(LANES, LANES)],
    )
    modal = exchange(message)
    local, moments = call(
        solve_kernel,
        [(LANES, total_east), (32, total_east)],
        [modal, basis_high, basis_low, by_row, by_wave],
        "solve",
    )
    moments = lax.all_to_all(
        moments.reshape(4, 8, total_east),
        "gy",
        0,
        0,
        tiled=True,
        axis_index_groups=[[0, 1, 2, 3], [4, 5, 6, 7]],
    ).reshape(32, total_east)
    (reply,) = call(
        back_kernel,
        [(blocks * 6, LANES)],
        [local, moments, basis_high, basis_low, by_row, by_wave, by_block],
        "back",
    )
    pressure = exchange(reply)
    (out,) = call(
        final_kernel,
        [(4 * LEVELS * ROWS, LANES)],
        [pressure, message, star, mode_back, by_level],
        "final",
        scratch=[(4 * LEVELS * ROWS, LANES)],
        copies=4,
    )
    return out.reshape(model_state.shape)


def solution(mesh):
    return jax.shard_map(
        on_device,
        mesh=mesh,
        in_specs=(P(None, None, "gx", "gy"), P(), P(), P(), P(), P(), P(), P()),
        out_specs=P(None, None, "gx", "gy"),
        check_vma=False,
    )
```

```python
import math

import jax
import jax.numpy as jnp
import ml_dtypes
import numpy as np
from jax import lax
from jax.experimental import pallas as pl
from jax.experimental.pallas import tpu as pltpu
from jax.sharding import PartitionSpec as P

F32 = jnp.float32
BF16 = jnp.bfloat16
LEVELS = 64
ROWS = 4
LANES = 128
LOW = 16
HIGH = 32
OTHER = 48


def split_table(table):
    high = table.astype(np.float32).astype(ml_dtypes.bfloat16)
    low = (table - high.astype(np.float64)).astype(np.float32).astype(ml_dtypes.bfloat16)
    return high, low


def east_tables(total, blocks):
    rows = total // blocks
    x = (np.arange(rows)[:, None] + rows * np.arange(blocks)[None, :]).reshape(-1)
    k = np.arange(total)
    angle = 2.0 * math.pi * ((k[:, None] * x[None, :]) % total) / total
    basis = np.where((k <= total // 2)[:, None], np.cos(angle), np.sin(angle))
    scale = np.where((k == 0) | (k == total // 2), 1.0, math.sqrt(2.0)) / math.sqrt(total)
    basis = basis * scale[:, None]
    square = np.sin(math.pi * k / total) ** 2
    return basis, square.astype(np.float32)


def position():
    return lax.axis_index("gx"), lax.axis_index("gy")


def lane_of(shape):
    return lax.broadcasted_iota(jnp.int32, shape, len(shape) - 1)


def row_of(shape):
    return lax.broadcasted_iota(jnp.int32, shape, 0)


def turn(values, shift, axis):
    size = values.shape[axis]
    return pltpu.roll(values, shift % size, axis) if shift % size else values


def parts(values):
    high = values.astype(BF16)
    return high, (values - high.astype(F32)).astype(BF16)


def dot3(left, right):
    dot = lambda a, b: jnp.dot(a, b, preferred_element_type=F32)
    return dot(left[0], right[0]) + (dot(left[0], right[1]) + dot(left[1], right[0]))


def level_difference(values):
    row = row_of(values.shape)
    last = values.shape[0] - 1
    upper = jnp.where(row < last, turn(values, -1, 0), 0.0)
    lower = jnp.where(row > 0, turn(values, 1, 0), 0.0)
    return upper - lower


def north_difference(values, low=0.0, high=0.0):
    lane = lane_of(values.shape)
    after = jnp.where(lane < LANES - 1, turn(values, -1, 1), high)
    before = jnp.where(lane > 0, turn(values, 1, 1), low)
    return after - before


def plane(ref, field, x):
    return ref[pl.ds((field * ROWS + x) * LEVELS, LEVELS), :]


def far_both(gx, gy):
    return ((gx % 16 == 0) | (gx % 16 == 15)) & ((gy % 4 == 0) | (gy % 4 == 3))


def edges_kernel(state_u, state_v, state_w, state_th, planes, x_even, x_odd, y_even, y_odd, flat):
    place = position()
    even_x = place[0] % 2 == 0
    even_y = place[1] % 2 == 0
    states = (state_u, state_v, state_w, state_th)
    lane = lane_of((LEVELS, LANES))
    gathered = jnp.zeros((LEVELS, LANES), F32)
    for field in range(4):
        values = [states[field][pl.ds(x, LEVELS, stride=ROWS), :] for x in range(ROWS)]
        for x in range(ROWS):
            slot = field * ROWS + x
            planes[pl.ds(slot * LEVELS, LEVELS), :] = values[x]
            gathered = jnp.where(lane >> 1 == slot, turn(values[x], 2 * slot + 1, 1), gathered)
        for slot, depth in ((field, 0), (4, 1)) if field == 0 else ((field, 0),):
            span = pl.ds(slot * LEVELS, LEVELS)
            low, high = values[depth], values[ROWS - 1 - depth]
            x_even[span, :] = jnp.where(even_x, high, low)
            x_odd[span, :] = jnp.where(even_x, low, high)
    flat[...] = jnp.transpose(jnp.concatenate([gathered, jnp.zeros_like(gathered)], axis=0))
    high, low = flat[pl.ds(0, 16, stride=2), :], flat[pl.ds(1, 16, stride=2), :]
    y_even[0:16, :] = jnp.where(even_y, high, low)
    y_odd[...] = jnp.where(even_y, low, high)
    x_even[pl.ds(5 * LEVELS, 16), :] = jnp.where(even_y, low, high)


def column_of(row):
    return jnp.transpose(jnp.broadcast_to(row, (LANES, LANES)))


def inner_kernel(
    state,
    vectors,
    square_row,
    layer_in,
    layer_out,
    star,
    by_level,
    by_row,
    by_wave,
    by_block,
):
    place = position()
    fields = [[plane(state, f, x) for x in range(ROWS)] for f in range(4)]
    tall = column_of(vectors[:, :LANES])
    rate, density = tall[:LEVELS], tall[LEVELS:]
    row = row_of((LEVELS, LANES))
    by_level[pl.ds(0, LEVELS), :] = rate
    by_level[pl.ds(LEVELS, LEVELS), :] = jnp.where(
        row < LEVELS - 1, 0.5 * turn(density, -1, 0) / density, 0.0
    )
    by_level[pl.ds(2 * LEVELS, LEVELS), :] = jnp.where(row > 0, 0.5 * turn(density, 1, 0) / density, 0.0)
    own = by_level[pl.ds(place[0], 1), :]

    both = jnp.concatenate([own, own], axis=1)
    root, inverse, rho = decay(both, square_row[...])
    powers = squarings(rho, 6)
    for i, value in enumerate(powers + [powers[6] * rho, -1.0 / root]):
        by_row[pl.ds(8 * i, 8), :] = value
    half = row_of((LANES, LANES)) >> 1
    odd = (row_of((LANES, LANES)) & 1) != 0
    narrow = [jnp.broadcast_to(value[0:1, :LANES], (LANES, LANES)) for value in powers[:6]]
    rising = lane_powers(narrow, half)
    falling = lane_powers(narrow, 63 - half)
    by_wave[pl.ds(0, LANES), :] = rising
    by_wave[pl.ds(LANES, LANES), :] = falling
    by_wave[pl.ds(2 * LANES, LANES), :] = narrow[0] * jnp.where(odd, rising, falling)

    r64 = powers[6]
    r128 = r64 * r64
    r256 = r128 * r128
    images = 1.0 / (1.0 - r256 * r256)
    mine = place[1] & 3
    row = row_of(rho.shape)
    for j in range(4):
        for i, offset in enumerate((-1, 3)):
            exponent = jnp.where(row < 2, (mine - j + offset) & 7, (j - mine + offset) & 7)
            weight = jnp.where((exponent & 1) != 0, r64, 1.0)
            weight = weight * jnp.where((exponent & 2) != 0, r128, 1.0)
            weight = weight * jnp.where((exponent & 4) != 0, r256, 1.0)
            by_block[pl.ds((2 * j + i) * 8, 8), :] = weight * images
    scale = -1.0 / root
    by_block[pl.ds(64, 8), :] = jnp.where(row == 0, scale, jnp.where(row == 1, scale * r64, scale * inverse))

    for x in range(ROWS):
        u, v, w, th = (fields[f][x] for f in range(4))
        for f in range(4):
            here = fields[f][x]
            change = v * north_difference(here) + w * level_difference(here)
            if x == 0:
                change = change + u * fields[f][1]
            elif x == ROWS - 1:
                change = change - u * fields[f][x - 1]
            else:
                change = change + u * (fields[f][x + 1] - fields[f][x - 1])
            value = here - 0.1 * change
            if f == 2:
                value = value + 0.1 * th
            star[pl.ds((f * ROWS + x) * LEVELS, LEVELS), :] = value

    columns = jnp.concatenate(
        [jnp.concatenate([fields[f][x] for f in range(4)], axis=0).astype(BF16) for x in range(ROWS)],
        axis=1,
    )
    first = (((0,), (0,)), ((), ()))
    shift = [column_of(vectors[:, i * LANES : (i + 1) * LANES]) for i in (1, 2)]
    shift = jnp.concatenate(shift, axis=0)
    before = lax.dot_general(layer_in[...], columns, first, preferred_element_type=F32)
    before = before + jnp.concatenate([shift] * ROWS, axis=1)
    hidden = (before * (1.0 / (1.0 + jnp.exp(-before)))).astype(BF16)
    forcing = lax.dot_general(layer_out[...], hidden, first, preferred_element_type=F32)
    for x in range(ROWS):
        span = slice(x * LANES, (x + 1) * LANES)
        for f, part in ((2, forcing[LEVELS:, span]), (3, forcing[:LEVELS, span])):
            at = pl.ds((f * ROWS + x) * LEVELS, LEVELS)
            star[at, :] = star[at, :] + 0.2 * part


def side_terms(state, edge, low):
    u, v, w, _, second = edge
    own = jnp.where(low, plane(state, 0, 0), plane(state, 0, ROWS - 1))
    sign = jnp.where(low, 0.1, -0.1)
    adds = [sign * own * value for value in edge[:4]]
    along = u * (own - second)
    beyond = u - (sign * along + 0.1 * (v * north_difference(u) + w * level_difference(u)))
    return adds, beyond


def outer_kernel(
    state,
    inner,
    x_even,
    x_far,
    x_near,
    y_even,
    y_odd,
    by_level,
    forward,
    star,
    message,
    flat,
):
    place = position()
    even_x = place[0] % 2 == 0
    even_y = place[1] % 2 == 0
    shape = (LEVELS, LANES)
    lane = lane_of(shape)

    other = jnp.where(far_both(place[0], place[1]), 0.0, y_odd[0:16, :])
    flat[...] = jnp.zeros((LANES, LANES), F32)
    flat[pl.ds(0, 16, stride=2), :] = jnp.where(even_y, y_even[0:16, :], other)
    flat[pl.ds(1, 16, stride=2), :] = jnp.where(even_y, other, y_even[0:16, :])
    low_side = place[1] % 4 == 0
    scale = jnp.where(low_side, 0.1, -0.1) * jnp.where(far_both(place[0] ^ 1, place[1]), 1.0, 0.0)
    theirs = x_even[pl.ds(5 * LEVELS + 4, 4), :]
    flat[pl.ds(32, 16), :] = scale * jnp.concatenate([theirs] * 4, axis=0) * y_odd[16:32, :]
    columns = jnp.transpose(flat[...])[:LEVELS]
    spans = [pl.ds(i * LEVELS, LEVELS) for i in range(5)]
    even_adds, even_beyond = side_terms(state, [x_even[at, :] for at in spans], ~even_x)
    far_x = (place[0] % 16 == 0) | (place[0] % 16 == 15)
    odd_edge = [jnp.where(far_x, x_far[at, :], x_near[at, :]) for at in spans]
    odd_adds, odd_beyond = side_terms(state, odd_edge, even_x)
    end_sign = jnp.where(lane == 0, 0.1, jnp.where(lane == LANES - 1, -0.1, 0.0))
    whole = [[None] * ROWS for _ in range(4)]
    side_u = [None] * ROWS
    for x in range(ROWS):
        v = plane(state, 1, x)
        for f in range(4):
            slot = f * ROWS + x
            side = end_sign * v * turn(columns, -(2 * slot + 1), 1)
            if f == 0:
                side_u[x] = side
            value = inner[pl.ds(slot * LEVELS, LEVELS), :] + side
            if x == 0:
                value = value + jnp.where(even_x, odd_adds[f], even_adds[f])
            if x == ROWS - 1:
                value = value + jnp.where(even_x, even_adds[f], odd_adds[f])
            whole[f][x] = value
            star[pl.ds(slot * LEVELS, LEVELS), :] = value

    low_beyond = jnp.where(even_x, odd_beyond, even_beyond)
    high_beyond = jnp.where(even_x, even_beyond, odd_beyond)
    padded = [low_beyond] + whole[0] + [high_beyond]
    divergence = []
    up, down = by_level[pl.ds(LEVELS, LEVELS), :], by_level[pl.ds(2 * LEVELS, LEVELS), :]
    step = jnp.where(lane < 35, turn(columns, -1, 1), 0.0) - jnp.where(lane > 32, turn(columns, 1, 1), 0.0)
    lifted = turn(columns, -8, 1)
    step = 0.5 * step + up * turn(lifted, -1, 0) - down * turn(lifted, 1, 0)
    left_out = jnp.where((lane >= 32) & (lane < 36), step, 0.0)
    beside = jnp.where(low_side, 0.5, -0.5) * columns
    left_out = jnp.where((lane >= 36) & (lane < 40), beside, left_out)
    left_out = jnp.where(lane == 40, -0.5 * turn(columns, 5, 1), left_out)
    left_out = jnp.where(lane == 41, 0.5 * turn(columns, 9, 1), left_out)
    left_out = turn(left_out, OTHER - 32, 1)
    extra = [left_out - 0.5 * side_u[ROWS - 1], left_out + 0.5 * side_u[0]]
    for x in range(ROWS):
        v, w = whole[1][x], whole[2][x]
        upright = up * turn(w, -1, 0) - down * turn(w, 1, 0)
        divergence.append(0.5 * (padded[x + 2] - padded[x]) + 0.5 * north_difference(v) + upright)
        low, high = LOW + x // 2, HIGH + x // 2
        value = jnp.where(lane == low, 0.5 * turn(v, low, 1), extra[x % 2])
        extra[x % 2] = jnp.where(lane == high, -0.5 * turn(v, high + 1, 1), value)
    pieces = [divergence[0], divergence[2], extra[0], divergence[1], divergence[3], extra[1]]
    modal = dot3(parts(forward[...]), parts(jnp.concatenate(pieces, axis=1)))
    for i in range(6):
        message[pl.ds(i, LEVELS, stride=6), :] = modal[:, i * LANES : (i + 1) * LANES]


def decay(rate, square):
    lam = rate + square
    root = jnp.sqrt(lam * (1.0 + lam))
    inverse = 1.0 + 2.0 * lam + 2.0 * root
    return root, inverse, 1.0 / inverse


def squarings(rho, count):
    powers = [rho]
    for _ in range(count):
        powers.append(powers[-1] * powers[-1])
    return powers


def lane_powers(powers, exponent):
    product = None
    for bit in range(6):
        factor = jnp.where((exponent & (1 << bit)) != 0, powers[bit], 1.0)
        product = factor if product is None else product * factor
    return product


def shifted(values, shift):
    size = values.shape[0]
    if shift % 8 == 0:
        zeros = jnp.zeros((abs(shift), values.shape[1]), F32)
        if shift > 0:
            return jnp.concatenate([zeros, values[:-shift]], axis=0)
        return jnp.concatenate([values[-shift:], zeros], axis=0)
    row = row_of(values.shape)
    inside = row >= shift if shift > 0 else row < size + shift
    return jnp.where(inside, turn(values, shift, 0), 0.0)


def by_parity(even, odd):
    shape = (8, even.shape[1])
    tile = jnp.where((row_of(shape) & 1) != 0, jnp.broadcast_to(odd, shape), jnp.broadcast_to(even, shape))
    return jnp.concatenate([tile] * (LANES // 8), axis=0)


def halves(values):
    return jnp.concatenate([values, values], axis=1)


def solve_kernel(received, basis_high, basis_low, by_row, by_wave, local, moments):
    place = position()
    blocks = received.shape[0] // 6
    lane = lane_of((blocks, LANES))
    ends = (lane == 0) | (lane == LANES - 1)
    even = place[1] < 4
    parity = jnp.where(even, 0, 1)
    low_side = place[1] % 4 == 0
    edge = jnp.where(low_side, 0, LANES - 1)
    within = jnp.where(low_side, 1, LANES - 2)
    row = row_of((blocks, LANES))
    inside, outside = [], [jnp.zeros((blocks, LANES), F32)] * 2
    for h in range(2):
        first, second, extra = (received[pl.ds(3 * h + j, blocks, stride=6), :] for j in range(3))
        first = first + jnp.where(ends & even, turn(extra, 1, 0), 0.0)
        second = second + jnp.where(ends & ~even, turn(extra, -1, 0), 0.0)
        other = jnp.where(row % 16 == 0, turn(extra, -1, 0), jnp.where(row % 16 == 15, turn(extra, 1, 0), 0.0))
        value = lambda i: jnp.sum(jnp.where(lane == OTHER + i + parity, other, 0.0), axis=1, keepdims=True)
        beside = [value(4), value(6)]
        corner = jnp.broadcast_to(value(8), (blocks, LANES))
        first = first + jnp.where(lane == edge, value(0), jnp.where(lane == within, -beside[0], 0.0))
        second = second + jnp.where(lane == edge, value(2), jnp.where(lane == within, -beside[1], 0.0))
        first = first + jnp.where((lane == edge) & even, turn(corner, 1, 0), 0.0)
        second = second + jnp.where((lane == edge) & ~even, turn(corner, -1, 0), 0.0)
        inside.append(jnp.concatenate([first, second], axis=0))
        for r in range(2):
            for i, start in enumerate((HIGH, LOW)):
                at = 2 * h + i
                outside[r] = jnp.where(lane == at, turn(extra, at - start - r, 1), outside[r])
            at = 2 * h + jnp.where(low_side, 1, 0)
            outside[r] = outside[r] + jnp.where(lane == at, beside[r], 0.0)
    right = parts(jnp.concatenate(inside + [jnp.concatenate(outside, axis=0)], axis=1))
    first = (((0,), (0,)), ((), ()))
    dot = lambda a, b: lax.dot_general(a, b[...], first, preferred_element_type=F32)
    spectral = dot(right[0], basis_high) + (dot(right[0], basis_low) + dot(right[1], basis_high))
    source = jnp.concatenate([spectral[:LANES], spectral[LANES : 2 * LANES]], axis=1)
    ext = spectral[2 * LANES : 2 * LANES + 8]
    high = jnp.concatenate([ext[0:1], ext[2:3]], axis=1)
    low = jnp.concatenate([ext[1:2], ext[3:4]], axis=1)

    power = lambda i: by_row[pl.ds(8 * i, 1), :]
    ahead, behind = source, source
    for bit in range(6):
        ahead = ahead + power(bit) * shifted(ahead, 2 << bit)
        behind = behind + power(bit) * shifted(behind, -(2 << bit))
    border = halves(by_wave[pl.ds(2 * LANES, LANES), :]) * by_parity(high, low)
    local[...] = ahead + behind - source + border
    rho, r65 = power(0), power(7)
    across = [
        rho * ahead[LANES - 2 : LANES - 1] + high,
        rho * ahead[LANES - 1 :] + r65 * low,
        rho * behind[0:1] + r65 * high,
        rho * behind[1:2] + low,
        jnp.zeros((4, source.shape[1]), F32),
    ]
    across = jnp.concatenate(across, axis=0)
    for j in range(4):
        moments[pl.ds(j * 8, 8), :] = across


def back_kernel(local, moments, basis_high, basis_low, by_row, by_wave, by_block, message):
    place = position()
    width = local.shape[1]
    blocks = basis_high.shape[0] // 2
    even = place[1] < 4
    mine = place[1] & 3
    carry = jnp.zeros((8, width), F32)
    for j in range(4):
        theirs = moments[pl.ds(j * 8, 8), :]
        swapped = jnp.concatenate([theirs[:, LANES:], theirs[:, :LANES]], axis=1)
        carry = carry + by_block[pl.ds(16 * j, 8), :] * theirs + by_block[pl.ds(16 * j + 8, 8), :] * swapped
    own = moments[pl.ds(pl.multiple_of(mine * 8, 8), 8), :]
    scale, by_r64, by_inverse = (by_block[pl.ds(64 + i, 1), :] for i in range(3))
    after = scale * own[0:1] + by_r64 * carry[0:1] + by_inverse * carry[2:3]
    before = scale * own[3:4] + by_r64 * carry[3:4] + by_inverse * carry[1:2]
    total = local[...] + halves(by_wave[pl.ds(0, LANES), :]) * by_parity(carry[0:1], carry[1:2])
    total = total + halves(by_wave[pl.ds(LANES, LANES), :]) * by_parity(carry[2:3], carry[3:4])
    total = total * scale
    pieces = [total[:, :LANES], total[:, LANES:]]
    for h in range(2):
        span = slice(h * LANES, (h + 1) * LANES)
        pieces += [after[:, span], before[:, span]]
    pieces.append(jnp.zeros((LANES - 4, LANES), F32))
    right = parts(jnp.concatenate(pieces, axis=0))
    last = (((1,), (1,)), ((), ()))
    dot = lambda a, b: lax.dot_general(a[...], b, last, preferred_element_type=F32)
    pressure = dot(basis_high, right[0]) + (dot(basis_high, right[1]) + dot(basis_low, right[0]))
    lane = lane_of((blocks, LANES))
    ends = (lane == 0) | (lane == LANES - 1)
    outside = [pressure[r * blocks : (r + 1) * blocks, 2 * LANES :] for r in range(2)]
    for h in range(2):
        span = slice(h * LANES, (h + 1) * LANES)
        first, second = pressure[:blocks, span], pressure[blocks:, span]
        extra = jnp.where(ends, jnp.where(even, turn(first, -1, 0), turn(second, 1, 0)), 0.0)
        for r in range(2):
            extra = jnp.where(lane == HIGH + r, turn(outside[r], HIGH + r - 2 * h, 1), extra)
            extra = jnp.where(lane == LOW + r, turn(outside[r], LOW + r - 1 - 2 * h, 1), extra)
        for j, value in enumerate((first, second, extra)):
            message[pl.ds(3 * h + j, blocks, stride=6), :] = value


def mend_kernel(star, message, state, relayed, forward, whole, middle, flat):
    place = position()
    both = far_both(place[0], place[1])
    whole[...] = star[...]
    for i, r in enumerate((1, 2)):
        middle[pl.ds(i * LEVELS, LEVELS), :] = message[pl.ds(3 * (r % 2) + r // 2, LEVELS, stride=6), :]

    @pl.when(both)
    def _():
        lane = lane_of((LEVELS, LANES))
        even_y = place[1] % 2 == 0
        far = relayed[16:32, :]
        flat[...] = jnp.zeros((LANES, LANES), F32)
        flat[pl.ds(0, 16, stride=2), :] = jnp.where(even_y, 0.0, far)
        flat[pl.ds(1, 16, stride=2), :] = jnp.where(even_y, far, 0.0)
        columns = jnp.transpose(flat[...])[:LEVELS]
        end_sign = jnp.where(lane == 0, 0.1, jnp.where(lane == LANES - 1, -0.1, 0.0))
        steps = []
        for x in range(ROWS):
            v = plane(state, 1, x)
            for f in range(4):
                slot = f * ROWS + x
                side = end_sign * v * turn(columns, -(2 * slot + 1), 1)
                at = pl.ds(slot * LEVELS, LEVELS)
                whole[at, :] = whole[at, :] + side
                if f == 1 and x in (1, 2):
                    steps.append(0.5 * north_difference(side))
        modal = dot3(parts(forward[...]), parts(jnp.concatenate(steps, axis=1)))
        for i in range(2):
            at = pl.ds(i * LEVELS, LEVELS)
            middle[at, :] = middle[at, :] + modal[:, i * LANES : (i + 1) * LANES]


def final_kernel(received, middle, star, back, by_level, out, held, sent_out):
    size = LEVELS * ROWS
    span = lambda f: pl.ds(f * size, size)
    copies = [pltpu.make_async_copy(held.at[span(f), :], out.at[span(f), :], sent_out.at[f]) for f in range(4)]

    def put(f, changes):
        for x in range(ROWS):
            value = star[pl.ds((f * ROWS + x) * LEVELS, LEVELS), :]
            if changes is not None:
                value = value - changes[:, x * LANES : (x + 1) * LANES]
            held[pl.ds(f * size + x, LEVELS, stride=ROWS), :] = value
        copies[f].start()

    put(3, None)
    lane = lane_of((LEVELS, LANES))
    row_at = lambda ref, r: ref[pl.ds(3 * (r % 2) + r // 2, LEVELS, stride=6), :]
    p = [row_at(received, r) for r in range(ROWS)]
    extra = [row_at(received, 4), row_at(received, 5)]
    low = [turn(extra[r % 2], -(LOW + r // 2), 1) for r in range(ROWS)]
    high = [turn(extra[r % 2], LANES - 1 - (HIGH + r // 2), 1) for r in range(ROWS)]
    four_rate = 4.0 * by_level[pl.ds(0, LEVELS), :]

    def next_row(r, opposite):
        here = p[r]
        divergence = middle[pl.ds((r - 1) * LEVELS, LEVELS), :]
        plus = jnp.where(lane < LANES - 2, turn(here, -2, 1), turn(high[r], -1, 1))
        minus = jnp.where(lane > 1, turn(here, 2, 1), turn(low[r], 1, 1))
        return (
            2.0 * here
            - opposite
            + four_rate * here
            + (2.0 * here - plus - minus)
            + 4.0 * divergence
        )

    ends = (lane == 0) | (lane == LANES - 1)
    before = jnp.where(ends, extra[1], next_row(1, p[3]))
    after = jnp.where(ends, extra[0], next_row(2, p[0]))
    padded = [before] + p + [after]
    matrix = back[...]
    joined = lambda values: parts(jnp.concatenate(values, axis=1))
    put(2, dot3(parts(0.5 * level_difference(matrix)), joined(p)))
    matrix = parts(matrix)
    put(1, dot3(matrix, joined([0.5 * north_difference(p[x], low[x], high[x]) for x in range(ROWS)])))
    put(0, dot3(matrix, joined([0.5 * (padded[x + 2] - padded[x]) for x in range(ROWS)])))
    for copy in copies:
        copy.wait()


def call(kernel, shapes, args, name, scratch=(), cost=None, copies=0):
    vmem = pl.BlockSpec(memory_space=pltpu.VMEM)
    return pl.pallas_call(
        kernel,
        out_shape=[jax.ShapeDtypeStruct(s, F32) for s in shapes],
        in_specs=[vmem] * len(args),
        out_specs=[pl.BlockSpec(memory_space=pl.ANY) if copies else vmem] * len(shapes),
        scratch_shapes=[pltpu.VMEM(s, F32) for s in scratch]
        + ([pltpu.SemaphoreType.DMA((copies,))] if copies else []),
        compiler_params=pltpu.CompilerParams(vmem_limit_bytes=32 * 1024 * 1024),
        name=name,
        cost_estimate=cost,
    )(*args)


def swap(values, axis, odd):
    count = lax.axis_size(axis)
    pairs = []
    for i in range(odd, count + odd, 2):
        pairs += [(i % count, (i + 1) % count), ((i + 1) % count, i % count)]
    return lax.ppermute(values, axis, pairs)


def swap_odd_x(values, far):
    count = lax.axis_size("gx")
    pairs = []
    for i in range(1, count + 1, 2):
        one, two = i % count, (i + 1) % count
        if (one % 16 == 15) == far:
            pairs += [(one, two), (two, one)]
    return lax.ppermute(values, "gx", pairs)


def swap_odd_y(values):
    count_x, count_y = lax.axis_size("gx"), lax.axis_size("gy")
    pairs = []
    for i in range(count_x):
        for j in range(1, count_y + 1, 2):
            one, two = j % count_y, (j + 1) % count_y
            if not far_both(i, one):
                pairs += [(i * count_y + one, i * count_y + two), (i * count_y + two, i * count_y + one)]
    return lax.ppermute(values, ("gx", "gy"), pairs)


def hand_over(values):
    count_x, count_y = lax.axis_size("gx"), lax.axis_size("gy")
    pairs = [
        ((i ^ 1) * count_y + j, i * count_y + j)
        for i in range(count_x)
        for j in range(count_y)
        if far_both(i, j)
    ]
    return lax.ppermute(values, ("gx", "gy"), pairs)


def exchange(values):
    count_x, count_y = lax.axis_size("gx"), lax.axis_size("gy")
    near = count_y // 2
    groups = [[i * count_y + h * near + y for i in range(count_x) for h in range(2)] for y in range(near)]
    shaped = values.reshape(2 * count_x, 1, values.size // (2 * count_x))
    moved = lax.all_to_all(
        shaped, ("gx", "gy"), 0, 0, tiled=True, axis_index_groups=groups
    )
    return moved.reshape(values.shape)


def on_device(
    model_state, density, layer_in, layer_bias, layer_out, mode_forward, mode_back, mode_rate
):
    blocks = lax.axis_size("gx")
    total_east = blocks * ROWS
    state = [model_state[f].reshape(LEVELS * ROWS, LANES) for f in range(4)]
    basis, square = east_tables(total_east // 2, blocks)
    basis_high, basis_low = split_table(np.ascontiguousarray(basis.T))
    square_row = np.ascontiguousarray(np.broadcast_to(np.concatenate([square, square]), (8, total_east)))

    planes, x_even, x_odd, y_even, y_odd = call(
        edges_kernel,
        [(16 * LEVELS, LANES), (5 * LEVELS + 16, LANES), (5 * LEVELS, LANES), (16, LANES), (16, LANES)],
        [*state],
        "edges",
        scratch=[(LANES, LANES)],
    )
    got_x_even = swap(x_even, "gx", 0)
    got_x_far = swap_odd_x(x_odd, True)
    y_both = jnp.concatenate([y_odd, got_x_even[5 * LEVELS :]], axis=0)
    y_both, x_odd, y_even = lax.optimization_barrier((y_both, x_odd, y_even))
    got_y_odd = swap_odd_y(y_both)
    got_x_near = swap_odd_x(x_odd, False)
    inner, by_level, by_row, by_wave, by_block = call(
        inner_kernel,
        [(16 * LEVELS, LANES), (3 * LEVELS, LANES), (72, total_east), (3 * LANES, LANES), (72, total_east)],
        [
            planes,
            jnp.concatenate([mode_rate, density, layer_bias])[None, :],
            square_row,
            layer_in,
            layer_out,
        ],
        "inner",
        cost=pl.CostEstimate(flops=10**10, transcendentals=0, bytes_accessed=2**24),
    )
    inner, y_even = lax.optimization_barrier((inner, y_even))
    got_y_even = swap(y_even, "gy", 0)
    star, message = call(
        outer_kernel,
        [(16 * LEVELS, LANES), (blocks * 6, LANES)],
        [
            planes,
            inner,
            got_x_even,
            got_x_far,
            got_x_near,
            got_y_even,
            got_y_odd,
            by_level,
            mode_forward,
        ],
        "outer",
        scratch=[(LANES, LANES)],
    )
    modal = exchange(message)
    local, moments = call(
        solve_kernel,
        [(LANES, total_east), (32, total_east)],
        [modal, basis_high, basis_low, by_row, by_wave],
        "solve",
    )
    moments, got_y_odd = lax.optimization_barrier((moments, got_y_odd))
    relayed = hand_over(got_y_odd)
    whole, middle = call(
        mend_kernel,
        [(16 * LEVELS, LANES), (2 * LEVELS, LANES)],
        [star, message, planes, relayed, mode_forward],
        "mend",
        scratch=[(LANES, LANES)],
    )
    moments = lax.all_to_all(
        moments.reshape(4, 8, total_east),
        "gy",
        0,
        0,
        tiled=True,
        axis_index_groups=[[0, 1, 2, 3], [4, 5, 6, 7]],
    ).reshape(32, total_east)
    moments, whole, middle = lax.optimization_barrier((moments, whole, middle))
    (reply,) = call(
        back_kernel,
        [(blocks * 6, LANES)],
        [local, moments, basis_high, basis_low, by_row, by_wave, by_block],
        "back",
    )
    pressure = exchange(reply)
    (out,) = call(
        final_kernel,
        [(4 * LEVELS * ROWS, LANES)],
        [pressure, middle, whole, mode_back, by_level],
        "final",
        scratch=[(4 * LEVELS * ROWS, LANES)],
        copies=4,
    )
    return out.reshape(model_state.shape)


def solution(mesh):
    return jax.shard_map(
        on_device,
        mesh=mesh,
        in_specs=(P(None, None, "gx", "gy"), P(), P(), P(), P(), P(), P(), P()),
        out_specs=P(None, None, "gx", "gy"),
        check_vma=False,
    )
```

```python
import math

import jax
import jax.numpy as jnp
import ml_dtypes
import numpy as np
from jax import lax
from jax.experimental import pallas as pl
from jax.experimental.pallas import tpu as pltpu
from jax.sharding import PartitionSpec as P

F32 = jnp.float32
BF16 = jnp.bfloat16
LEVELS = 64
ROWS = 4
LANES = 128
LOW = 16
HIGH = 32
OTHER = 48


def split_table(table):
    high = table.astype(np.float32).astype(ml_dtypes.bfloat16)
    low = (table - high.astype(np.float64)).astype(np.float32).astype(ml_dtypes.bfloat16)
    return high, low


def east_tables(total, blocks):
    rows = total // blocks
    x = (np.arange(rows)[:, None] + rows * np.arange(blocks)[None, :]).reshape(-1)
    k = np.arange(total)
    angle = 2.0 * math.pi * ((k[:, None] * x[None, :]) % total) / total
    basis = np.where((k <= total // 2)[:, None], np.cos(angle), np.sin(angle))
    scale = np.where((k == 0) | (k == total // 2), 1.0, math.sqrt(2.0)) / math.sqrt(total)
    basis = basis * scale[:, None]
    square = np.sin(math.pi * k / total) ** 2
    return basis, square.astype(np.float32)


def position():
    return lax.axis_index("gx"), lax.axis_index("gy")


def lane_of(shape):
    return lax.broadcasted_iota(jnp.int32, shape, len(shape) - 1)


def row_of(shape):
    return lax.broadcasted_iota(jnp.int32, shape, 0)


def turn(values, shift, axis):
    size = values.shape[axis]
    return pltpu.roll(values, shift % size, axis) if shift % size else values


def parts(values):
    high = values.astype(BF16)
    return high, (values - high.astype(F32)).astype(BF16)


def dot3(left, right):
    dot = lambda a, b: jnp.dot(a, b, preferred_element_type=F32)
    return dot(left[0], right[0]) + (dot(left[0], right[1]) + dot(left[1], right[0]))


def level_difference(values):
    row = row_of(values.shape)
    last = values.shape[0] - 1
    upper = jnp.where(row < last, turn(values, -1, 0), 0.0)
    lower = jnp.where(row > 0, turn(values, 1, 0), 0.0)
    return upper - lower


def north_difference(values, low=0.0, high=0.0):
    lane = lane_of(values.shape)
    after = jnp.where(lane < LANES - 1, turn(values, -1, 1), high)
    before = jnp.where(lane > 0, turn(values, 1, 1), low)
    return after - before


def plane(ref, field, x):
    return ref[pl.ds((field * ROWS + x) * LEVELS, LEVELS), :]


def far_both(gx, gy):
    return ((gx % 16 == 0) | (gx % 16 == 15)) & ((gy % 4 == 0) | (gy % 4 == 3))


def edges_kernel(state_u, state_v, state_w, state_th, planes, x_even, x_odd, y_even, y_odd, flat):
    place = position()
    even_x = place[0] % 2 == 0
    even_y = place[1] % 2 == 0
    states = (state_u, state_v, state_w, state_th)
    lane = lane_of((LEVELS, LANES))
    gathered = jnp.zeros((LEVELS, LANES), F32)
    for field in range(4):
        values = [states[field][pl.ds(x, LEVELS, stride=ROWS), :] for x in range(ROWS)]
        for x in range(ROWS):
            slot = field * ROWS + x
            planes[pl.ds(slot * LEVELS, LEVELS), :] = values[x]
            gathered = jnp.where(lane >> 1 == slot, turn(values[x], 2 * slot + 1, 1), gathered)
        for slot, depth in ((field, 0), (4, 1)) if field == 0 else ((field, 0),):
            span = pl.ds(slot * LEVELS, LEVELS)
            low, high = values[depth], values[ROWS - 1 - depth]
            x_even[span, :] = jnp.where(even_x, high, low)
            x_odd[span, :] = jnp.where(even_x, low, high)
    flat[...] = jnp.transpose(jnp.concatenate([gathered, jnp.zeros_like(gathered)], axis=0))
    high, low = flat[pl.ds(0, 16, stride=2), :], flat[pl.ds(1, 16, stride=2), :]
    y_even[0:16, :] = jnp.where(even_y, high, low)
    y_odd[...] = jnp.where(even_y, low, high)
    x_even[pl.ds(5 * LEVELS, 16), :] = jnp.where(even_y, low, high)


def column_of(row):
    return jnp.transpose(jnp.broadcast_to(row, (LANES, LANES)))


def tables_kernel(vectors, square_row, by_level, by_row, by_wave, by_block):
    place = position()
    tall = column_of(vectors[:, :LANES])
    rate, density = tall[:LEVELS], tall[LEVELS:]
    row = row_of((LEVELS, LANES))
    by_level[pl.ds(0, LEVELS), :] = rate
    by_level[pl.ds(LEVELS, LEVELS), :] = jnp.where(
        row < LEVELS - 1, 0.5 * turn(density, -1, 0) / density, 0.0
    )
    by_level[pl.ds(2 * LEVELS, LEVELS), :] = jnp.where(row > 0, 0.5 * turn(density, 1, 0) / density, 0.0)
    own = by_level[pl.ds(place[0], 1), :]

    both = jnp.concatenate([own, own], axis=1)
    root, inverse, rho = decay(both, square_row[...])
    powers = squarings(rho, 6)
    for i, value in enumerate(powers + [powers[6] * rho, -1.0 / root]):
        by_row[pl.ds(8 * i, 8), :] = value
    half = row_of((LANES, LANES)) >> 1
    odd = (row_of((LANES, LANES)) & 1) != 0
    narrow = [jnp.broadcast_to(value[0:1, :LANES], (LANES, LANES)) for value in powers[:6]]
    rising = lane_powers(narrow, half)
    falling = lane_powers(narrow, 63 - half)
    by_wave[pl.ds(0, LANES), :] = rising
    by_wave[pl.ds(LANES, LANES), :] = falling
    by_wave[pl.ds(2 * LANES, LANES), :] = narrow[0] * jnp.where(odd, rising, falling)

    r64 = powers[6]
    r128 = r64 * r64
    r256 = r128 * r128
    images = 1.0 / (1.0 - r256 * r256)
    mine = place[1] & 3
    row = row_of(rho.shape)
    for j in range(4):
        for i, offset in enumerate((-1, 3)):
            exponent = jnp.where(row < 2, (mine - j + offset) & 7, (j - mine + offset) & 7)
            weight = jnp.where((exponent & 1) != 0, r64, 1.0)
            weight = weight * jnp.where((exponent & 2) != 0, r128, 1.0)
            weight = weight * jnp.where((exponent & 4) != 0, r256, 1.0)
            by_block[pl.ds((2 * j + i) * 8, 8), :] = weight * images
    scale = -1.0 / root
    by_block[pl.ds(64, 8), :] = jnp.where(row == 0, scale, jnp.where(row == 1, scale * r64, scale * inverse))


def inner_kernel(state, vectors, layer_in, layer_out, star):
    fields = [[plane(state, f, x) for x in range(ROWS)] for f in range(4)]
    for x in range(ROWS):
        u, v, w, th = (fields[f][x] for f in range(4))
        for f in range(4):
            here = fields[f][x]
            change = v * north_difference(here) + w * level_difference(here)
            if x == 0:
                change = change + u * fields[f][1]
            elif x == ROWS - 1:
                change = change - u * fields[f][x - 1]
            else:
                change = change + u * (fields[f][x + 1] - fields[f][x - 1])
            value = here - 0.1 * change
            if f == 2:
                value = value + 0.1 * th
            star[pl.ds((f * ROWS + x) * LEVELS, LEVELS), :] = value

    columns = jnp.concatenate(
        [jnp.concatenate([fields[f][x] for f in range(4)], axis=0).astype(BF16) for x in range(ROWS)],
        axis=1,
    )
    first = (((0,), (0,)), ((), ()))
    shift = [column_of(vectors[:, i * LANES : (i + 1) * LANES]) for i in (1, 2)]
    shift = jnp.concatenate(shift, axis=0)
    before = lax.dot_general(layer_in[...], columns, first, preferred_element_type=F32)
    before = before + jnp.concatenate([shift] * ROWS, axis=1)
    hidden = (before * (1.0 / (1.0 + jnp.exp(-before)))).astype(BF16)
    forcing = lax.dot_general(layer_out[...], hidden, first, preferred_element_type=F32)
    for x in range(ROWS):
        span = slice(x * LANES, (x + 1) * LANES)
        for f, part in ((2, forcing[LEVELS:, span]), (3, forcing[:LEVELS, span])):
            at = pl.ds((f * ROWS + x) * LEVELS, LEVELS)
            star[at, :] = star[at, :] + 0.2 * part


def side_terms(state, edge, low):
    u, v, w, _, second = edge
    own = jnp.where(low, plane(state, 0, 0), plane(state, 0, ROWS - 1))
    sign = jnp.where(low, 0.1, -0.1)
    adds = [sign * own * value for value in edge[:4]]
    along = u * (own - second)
    beyond = u - (sign * along + 0.1 * (v * north_difference(u) + w * level_difference(u)))
    return adds, beyond


def outer_kernel(
    state,
    inner,
    x_even,
    x_far,
    x_near,
    y_even,
    y_odd,
    y_both,
    by_level,
    forward,
    star,
    message,
    flat,
):
    place = position()
    even_x = place[0] % 2 == 0
    even_y = place[1] % 2 == 0
    shape = (LEVELS, LANES)
    lane = lane_of(shape)

    helping = far_both(place[0] ^ 1, place[1])
    other = jnp.where(helping, y_both[0:16, :], y_odd[...])
    other = jnp.where(far_both(place[0], place[1]), 0.0, other)
    flat[...] = jnp.zeros((LANES, LANES), F32)
    flat[pl.ds(0, 16, stride=2), :] = jnp.where(even_y, y_even[0:16, :], other)
    flat[pl.ds(1, 16, stride=2), :] = jnp.where(even_y, other, y_even[0:16, :])
    low_side = place[1] % 4 == 0
    scale = jnp.where(low_side, 0.1, -0.1) * jnp.where(helping, 1.0, 0.0)
    theirs = x_even[pl.ds(5 * LEVELS + 4, 4), :]
    flat[pl.ds(32, 16), :] = scale * jnp.concatenate([theirs] * 4, axis=0) * y_both[16:32, :]
    columns = jnp.transpose(flat[...])[:LEVELS]
    spans = [pl.ds(i * LEVELS, LEVELS) for i in range(5)]
    even_adds, even_beyond = side_terms(state, [x_even[at, :] for at in spans], ~even_x)
    far_x = (place[0] % 16 == 0) | (place[0] % 16 == 15)
    odd_edge = [jnp.where(far_x, x_far[at, :], x_near[at, :]) for at in spans]
    odd_adds, odd_beyond = side_terms(state, odd_edge, even_x)
    end_sign = jnp.where(lane == 0, 0.1, jnp.where(lane == LANES - 1, -0.1, 0.0))
    whole = [[None] * ROWS for _ in range(4)]
    side_u = [None] * ROWS
    for x in range(ROWS):
        v = plane(state, 1, x)
        for f in range(4):
            slot = f * ROWS + x
            side = end_sign * v * turn(columns, -(2 * slot + 1), 1)
            if f == 0:
                side_u[x] = side
            value = inner[pl.ds(slot * LEVELS, LEVELS), :] + side
            if x == 0:
                value = value + jnp.where(even_x, odd_adds[f], even_adds[f])
            if x == ROWS - 1:
                value = value + jnp.where(even_x, even_adds[f], odd_adds[f])
            whole[f][x] = value
            star[pl.ds(slot * LEVELS, LEVELS), :] = value

    low_beyond = jnp.where(even_x, odd_beyond, even_beyond)
    high_beyond = jnp.where(even_x, even_beyond, odd_beyond)
    padded = [low_beyond] + whole[0] + [high_beyond]
    divergence = []
    up, down = by_level[pl.ds(LEVELS, LEVELS), :], by_level[pl.ds(2 * LEVELS, LEVELS), :]
    step = jnp.where(lane < 35, turn(columns, -1, 1), 0.0) - jnp.where(lane > 32, turn(columns, 1, 1), 0.0)
    lifted = turn(columns, -8, 1)
    step = 0.5 * step + up * turn(lifted, -1, 0) - down * turn(lifted, 1, 0)
    left_out = jnp.where((lane >= 32) & (lane < 36), step, 0.0)
    beside = jnp.where(low_side, 0.5, -0.5) * columns
    left_out = jnp.where((lane >= 36) & (lane < 40), beside, left_out)
    left_out = jnp.where(lane == 40, -0.5 * turn(columns, 5, 1), left_out)
    left_out = jnp.where(lane == 41, 0.5 * turn(columns, 9, 1), left_out)
    left_out = turn(left_out, OTHER - 32, 1)
    extra = [left_out - 0.5 * side_u[ROWS - 1], left_out + 0.5 * side_u[0]]
    for x in range(ROWS):
        v, w = whole[1][x], whole[2][x]
        upright = up * turn(w, -1, 0) - down * turn(w, 1, 0)
        divergence.append(0.5 * (padded[x + 2] - padded[x]) + 0.5 * north_difference(v) + upright)
        low, high = LOW + x // 2, HIGH + x // 2
        value = jnp.where(lane == low, 0.5 * turn(v, low, 1), extra[x % 2])
        extra[x % 2] = jnp.where(lane == high, -0.5 * turn(v, high + 1, 1), value)
    pieces = [divergence[0], divergence[2], extra[0], divergence[1], divergence[3], extra[1]]
    modal = dot3(parts(forward[...]), parts(jnp.concatenate(pieces, axis=1)))
    for i in range(6):
        message[pl.ds(i, LEVELS, stride=6), :] = modal[:, i * LANES : (i + 1) * LANES]


def decay(rate, square):
    lam = rate + square
    root = jnp.sqrt(lam * (1.0 + lam))
    inverse = 1.0 + 2.0 * lam + 2.0 * root
    return root, inverse, 1.0 / inverse


def squarings(rho, count):
    powers = [rho]
    for _ in range(count):
        powers.append(powers[-1] * powers[-1])
    return powers


def lane_powers(powers, exponent):
    product = None
    for bit in range(6):
        factor = jnp.where((exponent & (1 << bit)) != 0, powers[bit], 1.0)
        product = factor if product is None else product * factor
    return product


def shifted(values, shift):
    size = values.shape[0]
    if shift % 8 == 0:
        zeros = jnp.zeros((abs(shift), values.shape[1]), F32)
        if shift > 0:
            return jnp.concatenate([zeros, values[:-shift]], axis=0)
        return jnp.concatenate([values[-shift:], zeros], axis=0)
    row = row_of(values.shape)
    inside = row >= shift if shift > 0 else row < size + shift
    return jnp.where(inside, turn(values, shift, 0), 0.0)


def by_parity(even, odd):
    shape = (8, even.shape[1])
    tile = jnp.where((row_of(shape) & 1) != 0, jnp.broadcast_to(odd, shape), jnp.broadcast_to(even, shape))
    return jnp.concatenate([tile] * (LANES // 8), axis=0)


def halves(values):
    return jnp.concatenate([values, values], axis=1)


def solve_kernel(received, basis_high, basis_low, by_row, by_wave, local, moments):
    place = position()
    blocks = received.shape[0] // 6
    lane = lane_of((blocks, LANES))
    ends = (lane == 0) | (lane == LANES - 1)
    even = place[1] < 4
    parity = jnp.where(even, 0, 1)
    low_side = place[1] % 4 == 0
    edge = jnp.where(low_side, 0, LANES - 1)
    within = jnp.where(low_side, 1, LANES - 2)
    row = row_of((blocks, LANES))
    inside, outside = [], [jnp.zeros((blocks, LANES), F32)] * 2
    for h in range(2):
        first, second, extra = (received[pl.ds(3 * h + j, blocks, stride=6), :] for j in range(3))
        first = first + jnp.where(ends & even, turn(extra, 1, 0), 0.0)
        second = second + jnp.where(ends & ~even, turn(extra, -1, 0), 0.0)
        other = jnp.where(row % 16 == 0, turn(extra, -1, 0), jnp.where(row % 16 == 15, turn(extra, 1, 0), 0.0))
        value = lambda i: jnp.sum(jnp.where(lane == OTHER + i + parity, other, 0.0), axis=1, keepdims=True)
        beside = [value(4), value(6)]
        corner = jnp.broadcast_to(value(8), (blocks, LANES))
        first = first + jnp.where(lane == edge, value(0), jnp.where(lane == within, -beside[0], 0.0))
        second = second + jnp.where(lane == edge, value(2), jnp.where(lane == within, -beside[1], 0.0))
        first = first + jnp.where((lane == edge) & even, turn(corner, 1, 0), 0.0)
        second = second + jnp.where((lane == edge) & ~even, turn(corner, -1, 0), 0.0)
        inside.append(jnp.concatenate([first, second], axis=0))
        for r in range(2):
            for i, start in enumerate((HIGH, LOW)):
                at = 2 * h + i
                outside[r] = jnp.where(lane == at, turn(extra, at - start - r, 1), outside[r])
            at = 2 * h + jnp.where(low_side, 1, 0)
            outside[r] = outside[r] + jnp.where(lane == at, beside[r], 0.0)
    right = parts(jnp.concatenate(inside + [jnp.concatenate(outside, axis=0)], axis=1))
    first = (((0,), (0,)), ((), ()))
    dot = lambda a, b: lax.dot_general(a, b[...], first, preferred_element_type=F32)
    spectral = dot(right[0], basis_high) + (dot(right[0], basis_low) + dot(right[1], basis_high))
    source = jnp.concatenate([spectral[:LANES], spectral[LANES : 2 * LANES]], axis=1)
    ext = spectral[2 * LANES : 2 * LANES + 8]
    high = jnp.concatenate([ext[0:1], ext[2:3]], axis=1)
    low = jnp.concatenate([ext[1:2], ext[3:4]], axis=1)

    power = lambda i: by_row[pl.ds(8 * i, 1), :]
    ahead, behind = source, source
    for bit in range(6):
        ahead = ahead + power(bit) * shifted(ahead, 2 << bit)
        behind = behind + power(bit) * shifted(behind, -(2 << bit))
    border = halves(by_wave[pl.ds(2 * LANES, LANES), :]) * by_parity(high, low)
    local[...] = ahead + behind - source + border
    rho, r65 = power(0), power(7)
    across = [
        rho * ahead[LANES - 2 : LANES - 1] + high,
        rho * ahead[LANES - 1 :] + r65 * low,
        rho * behind[0:1] + r65 * high,
        rho * behind[1:2] + low,
        jnp.zeros((4, source.shape[1]), F32),
    ]
    across = jnp.concatenate(across, axis=0)
    for j in range(4):
        moments[pl.ds(j * 8, 8), :] = across


def back_kernel(local, moments, basis_high, basis_low, by_row, by_wave, by_block, message):
    place = position()
    width = local.shape[1]
    blocks = basis_high.shape[0] // 2
    even = place[1] < 4
    mine = place[1] & 3
    carry = jnp.zeros((8, width), F32)
    for j in range(4):
        theirs = moments[pl.ds(j * 8, 8), :]
        swapped = jnp.concatenate([theirs[:, LANES:], theirs[:, :LANES]], axis=1)
        carry = carry + by_block[pl.ds(16 * j, 8), :] * theirs + by_block[pl.ds(16 * j + 8, 8), :] * swapped
    own = moments[pl.ds(pl.multiple_of(mine * 8, 8), 8), :]
    scale, by_r64, by_inverse = (by_block[pl.ds(64 + i, 1), :] for i in range(3))
    after = scale * own[0:1] + by_r64 * carry[0:1] + by_inverse * carry[2:3]
    before = scale * own[3:4] + by_r64 * carry[3:4] + by_inverse * carry[1:2]
    total = local[...] + halves(by_wave[pl.ds(0, LANES), :]) * by_parity(carry[0:1], carry[1:2])
    total = total + halves(by_wave[pl.ds(LANES, LANES), :]) * by_parity(carry[2:3], carry[3:4])
    total = total * scale
    pieces = [total[:, :LANES], total[:, LANES:]]
    for h in range(2):
        span = slice(h * LANES, (h + 1) * LANES)
        pieces += [after[:, span], before[:, span]]
    pieces.append(jnp.zeros((LANES - 4, LANES), F32))
    right = parts(jnp.concatenate(pieces, axis=0))
    last = (((1,), (1,)), ((), ()))
    dot = lambda a, b: lax.dot_general(a[...], b, last, preferred_element_type=F32)
    pressure = dot(basis_high, right[0]) + (dot(basis_high, right[1]) + dot(basis_low, right[0]))
    lane = lane_of((blocks, LANES))
    ends = (lane == 0) | (lane == LANES - 1)
    outside = [pressure[r * blocks : (r + 1) * blocks, 2 * LANES :] for r in range(2)]
    for h in range(2):
        span = slice(h * LANES, (h + 1) * LANES)
        first, second = pressure[:blocks, span], pressure[blocks:, span]
        extra = jnp.where(ends, jnp.where(even, turn(first, -1, 0), turn(second, 1, 0)), 0.0)
        for r in range(2):
            extra = jnp.where(lane == HIGH + r, turn(outside[r], HIGH + r - 2 * h, 1), extra)
            extra = jnp.where(lane == LOW + r, turn(outside[r], LOW + r - 1 - 2 * h, 1), extra)
        for j, value in enumerate((first, second, extra)):
            message[pl.ds(3 * h + j, blocks, stride=6), :] = value


def mend_kernel(star, message, state, relayed, forward, whole, middle, flat):
    place = position()
    both = far_both(place[0], place[1])
    whole[...] = star[...]
    for i, r in enumerate((1, 2)):
        middle[pl.ds(i * LEVELS, LEVELS), :] = message[pl.ds(3 * (r % 2) + r // 2, LEVELS, stride=6), :]

    @pl.when(both)
    def _():
        lane = lane_of((LEVELS, LANES))
        even_y = place[1] % 2 == 0
        far = relayed[16:32, :]
        flat[...] = jnp.zeros((LANES, LANES), F32)
        flat[pl.ds(0, 16, stride=2), :] = jnp.where(even_y, 0.0, far)
        flat[pl.ds(1, 16, stride=2), :] = jnp.where(even_y, far, 0.0)
        columns = jnp.transpose(flat[...])[:LEVELS]
        end_sign = jnp.where(lane == 0, 0.1, jnp.where(lane == LANES - 1, -0.1, 0.0))
        steps = []
        for x in range(ROWS):
            v = plane(state, 1, x)
            for f in range(4):
                slot = f * ROWS + x
                side = end_sign * v * turn(columns, -(2 * slot + 1), 1)
                at = pl.ds(slot * LEVELS, LEVELS)
                whole[at, :] = whole[at, :] + side
                if f == 1 and x in (1, 2):
                    steps.append(0.5 * north_difference(side))
        modal = dot3(parts(forward[...]), parts(jnp.concatenate(steps, axis=1)))
        for i in range(2):
            at = pl.ds(i * LEVELS, LEVELS)
            middle[at, :] = middle[at, :] + modal[:, i * LANES : (i + 1) * LANES]


def final_kernel(received, middle, star, back, by_level, out, held, sent_out):
    size = LEVELS * ROWS
    span = lambda f: pl.ds(f * size, size)
    copies = [pltpu.make_async_copy(held.at[span(f), :], out.at[span(f), :], sent_out.at[f]) for f in range(4)]

    def put(f, changes):
        for x in range(ROWS):
            value = star[pl.ds((f * ROWS + x) * LEVELS, LEVELS), :]
            if changes is not None:
                value = value - changes[:, x * LANES : (x + 1) * LANES]
            held[pl.ds(f * size + x, LEVELS, stride=ROWS), :] = value
        copies[f].start()

    put(3, None)
    lane = lane_of((LEVELS, LANES))
    row_at = lambda ref, r: ref[pl.ds(3 * (r % 2) + r // 2, LEVELS, stride=6), :]
    p = [row_at(received, r) for r in range(ROWS)]
    extra = [row_at(received, 4), row_at(received, 5)]
    low = [turn(extra[r % 2], -(LOW + r // 2), 1) for r in range(ROWS)]
    high = [turn(extra[r % 2], LANES - 1 - (HIGH + r // 2), 1) for r in range(ROWS)]
    four_rate = 4.0 * by_level[pl.ds(0, LEVELS), :]

    def next_row(r, opposite):
        here = p[r]
        divergence = middle[pl.ds((r - 1) * LEVELS, LEVELS), :]
        plus = jnp.where(lane < LANES - 2, turn(here, -2, 1), turn(high[r], -1, 1))
        minus = jnp.where(lane > 1, turn(here, 2, 1), turn(low[r], 1, 1))
        return (
            2.0 * here
            - opposite
            + four_rate * here
            + (2.0 * here - plus - minus)
            + 4.0 * divergence
        )

    ends = (lane == 0) | (lane == LANES - 1)
    before = jnp.where(ends, extra[1], next_row(1, p[3]))
    after = jnp.where(ends, extra[0], next_row(2, p[0]))
    padded = [before] + p + [after]
    matrix = back[...]
    joined = lambda values: parts(jnp.concatenate(values, axis=1))
    put(2, dot3(parts(0.5 * level_difference(matrix)), joined(p)))
    matrix = parts(matrix)
    put(1, dot3(matrix, joined([0.5 * north_difference(p[x], low[x], high[x]) for x in range(ROWS)])))
    put(0, dot3(matrix, joined([0.5 * (padded[x + 2] - padded[x]) for x in range(ROWS)])))
    for copy in copies:
        copy.wait()


def call(kernel, shapes, args, name, scratch=(), cost=None, copies=0):
    vmem = pl.BlockSpec(memory_space=pltpu.VMEM)
    return pl.pallas_call(
        kernel,
        out_shape=[jax.ShapeDtypeStruct(s, F32) for s in shapes],
        in_specs=[vmem] * len(args),
        out_specs=[pl.BlockSpec(memory_space=pl.ANY) if copies else vmem] * len(shapes),
        scratch_shapes=[pltpu.VMEM(s, F32) for s in scratch]
        + ([pltpu.SemaphoreType.DMA((copies,))] if copies else []),
        compiler_params=pltpu.CompilerParams(vmem_limit_bytes=32 * 1024 * 1024),
        name=name,
        cost_estimate=cost,
    )(*args)


def swap(values, axis, odd):
    count = lax.axis_size(axis)
    pairs = []
    for i in range(odd, count + odd, 2):
        pairs += [(i % count, (i + 1) % count), ((i + 1) % count, i % count)]
    return lax.ppermute(values, axis, pairs)


def swap_odd_x(values, far):
    count = lax.axis_size("gx")
    pairs = []
    for i in range(1, count + 1, 2):
        one, two = i % count, (i + 1) % count
        if (one % 16 == 15) == far:
            pairs += [(one, two), (two, one)]
    return lax.ppermute(values, "gx", pairs)


def swap_odd_y(values, helping):
    count_x, count_y = lax.axis_size("gx"), lax.axis_size("gy")
    pairs = []
    for i in range(count_x):
        for j in range(1, count_y + 1, 2):
            one, two = j % count_y, (j + 1) % count_y
            if not far_both(i, one) and far_both(i ^ 1, one) == helping:
                pairs += [(i * count_y + one, i * count_y + two), (i * count_y + two, i * count_y + one)]
    return lax.ppermute(values, ("gx", "gy"), pairs)


def hand_over(values):
    count_x, count_y = lax.axis_size("gx"), lax.axis_size("gy")
    pairs = [
        ((i ^ 1) * count_y + j, i * count_y + j)
        for i in range(count_x)
        for j in range(count_y)
        if far_both(i, j)
    ]
    return lax.ppermute(values, ("gx", "gy"), pairs)


def exchange(values):
    count_x, count_y = lax.axis_size("gx"), lax.axis_size("gy")
    near = count_y // 2
    groups = [[i * count_y + h * near + y for i in range(count_x) for h in range(2)] for y in range(near)]
    shaped = values.reshape(2 * count_x, 1, values.size // (2 * count_x))
    moved = lax.all_to_all(
        shaped, ("gx", "gy"), 0, 0, tiled=True, axis_index_groups=groups
    )
    return moved.reshape(values.shape)


def on_device(
    model_state, density, layer_in, layer_bias, layer_out, mode_forward, mode_back, mode_rate
):
    blocks = lax.axis_size("gx")
    total_east = blocks * ROWS
    state = [model_state[f].reshape(LEVELS * ROWS, LANES) for f in range(4)]
    basis, square = east_tables(total_east // 2, blocks)
    basis_high, basis_low = split_table(np.ascontiguousarray(basis.T))
    square_row = np.ascontiguousarray(np.broadcast_to(np.concatenate([square, square]), (8, total_east)))

    planes, x_even, x_odd, y_even, y_odd = call(
        edges_kernel,
        [(16 * LEVELS, LANES), (5 * LEVELS + 16, LANES), (5 * LEVELS, LANES), (16, LANES), (16, LANES)],
        [*state],
        "edges",
        scratch=[(LANES, LANES)],
    )
    got_x_even = swap(x_even, "gx", 0)
    got_x_far = swap_odd_x(x_odd, True)
    got_y_odd = swap_odd_y(y_odd, False)
    y_both = jnp.concatenate([y_odd, got_x_even[5 * LEVELS :]], axis=0)
    y_both, x_odd, y_even = lax.optimization_barrier((y_both, x_odd, y_even))
    got_y_both = swap_odd_y(y_both, True)
    got_x_near = swap_odd_x(x_odd, False)
    vectors = jnp.concatenate([mode_rate, density, layer_bias])[None, :]
    long = pl.CostEstimate(flops=10**10, transcendentals=0, bytes_accessed=2**24)
    by_level, by_row, by_wave, by_block = call(
        tables_kernel,
        [(3 * LEVELS, LANES), (72, total_east), (3 * LANES, LANES), (72, total_east)],
        [vectors, square_row],
        "tables",
        cost=long,
    )
    by_level, y_even = lax.optimization_barrier((by_level, y_even))
    got_y_even = swap(y_even, "gy", 0)
    (inner,) = call(
        inner_kernel,
        [(16 * LEVELS, LANES)],
        [planes, vectors, layer_in, layer_out],
        "inner",
        cost=None,
    )
    star, message = call(
        outer_kernel,
        [(16 * LEVELS, LANES), (blocks * 6, LANES)],
        [
            planes,
            inner,
            got_x_even,
            got_x_far,
            got_x_near,
            got_y_even,
            got_y_odd,
            got_y_both,
            by_level,
            mode_forward,
        ],
        "outer",
        scratch=[(LANES, LANES)],
    )
    message, got_y_both = lax.optimization_barrier((message, got_y_both))
    relayed = hand_over(got_y_both)
    modal = exchange(message)
    whole, middle = call(
        mend_kernel,
        [(16 * LEVELS, LANES), (2 * LEVELS, LANES)],
        [star, message, planes, relayed, mode_forward],
        "mend",
        scratch=[(LANES, LANES)],
    )
    modal, whole, middle = lax.optimization_barrier((modal, whole, middle))
    local, moments = call(
        solve_kernel,
        [(LANES, total_east), (32, total_east)],
        [modal, basis_high, basis_low, by_row, by_wave],
        "solve",
    )
    moments = lax.all_to_all(
        moments.reshape(4, 8, total_east),
        "gy",
        0,
        0,
        tiled=True,
        axis_index_groups=[[0, 1, 2, 3], [4, 5, 6, 7]],
    ).reshape(32, total_east)
    (reply,) = call(
        back_kernel,
        [(blocks * 6, LANES)],
        [local, moments, basis_high, basis_low, by_row, by_wave, by_block],
        "back",
    )
    pressure = exchange(reply)
    (out,) = call(
        final_kernel,
        [(4 * LEVELS * ROWS, LANES)],
        [pressure, middle, whole, mode_back, by_level],
        "final",
        scratch=[(4 * LEVELS * ROWS, LANES)],
        copies=4,
    )
    return out.reshape(model_state.shape)


def solution(mesh):
    return jax.shard_map(
        on_device,
        mesh=mesh,
        in_specs=(P(None, None, "gx", "gy"), P(), P(), P(), P(), P(), P(), P()),
        out_specs=P(None, None, "gx", "gy"),
        check_vma=False,
    )
```

```python
import math

import jax
import jax.numpy as jnp
import ml_dtypes
import numpy as np
from jax import lax
from jax.experimental import pallas as pl
from jax.experimental.pallas import tpu as pltpu
from jax.sharding import PartitionSpec as P

F32 = jnp.float32
BF16 = jnp.bfloat16
LEVELS = 64
ROWS = 4
LANES = 128
LOW = 16
HIGH = 32
OTHER = 48


def split_table(table):
    high = table.astype(np.float32).astype(ml_dtypes.bfloat16)
    low = (table - high.astype(np.float64)).astype(np.float32).astype(ml_dtypes.bfloat16)
    return high, low


def east_tables(total, blocks):
    rows = total // blocks
    x = (np.arange(rows)[:, None] + rows * np.arange(blocks)[None, :]).reshape(-1)
    k = np.arange(total)
    angle = 2.0 * math.pi * ((k[:, None] * x[None, :]) % total) / total
    basis = np.where((k <= total // 2)[:, None], np.cos(angle), np.sin(angle))
    scale = np.where((k == 0) | (k == total // 2), 1.0, math.sqrt(2.0)) / math.sqrt(total)
    basis = basis * scale[:, None]
    square = np.sin(math.pi * k / total) ** 2
    return basis, square.astype(np.float32)


def position():
    return lax.axis_index("gx"), lax.axis_index("gy")


def lane_of(shape):
    return lax.broadcasted_iota(jnp.int32, shape, len(shape) - 1)


def row_of(shape):
    return lax.broadcasted_iota(jnp.int32, shape, 0)


def turn(values, shift, axis):
    size = values.shape[axis]
    return pltpu.roll(values, shift % size, axis) if shift % size else values


def parts(values):
    high = values.astype(BF16)
    return high, (values - high.astype(F32)).astype(BF16)


def dot3(left, right):
    dot = lambda a, b: jnp.dot(a, b, preferred_element_type=F32)
    return dot(left[0], right[0]) + (dot(left[0], right[1]) + dot(left[1], right[0]))


def level_difference(values):
    row = row_of(values.shape)
    last = values.shape[0] - 1
    upper = jnp.where(row < last, turn(values, -1, 0), 0.0)
    lower = jnp.where(row > 0, turn(values, 1, 0), 0.0)
    return upper - lower


def north_difference(values, low=0.0, high=0.0):
    lane = lane_of(values.shape)
    after = jnp.where(lane < LANES - 1, turn(values, -1, 1), high)
    before = jnp.where(lane > 0, turn(values, 1, 1), low)
    return after - before


def plane(ref, field, x):
    return ref[pl.ds((field * ROWS + x) * LEVELS, LEVELS), :]


def far_both(gx, gy):
    return ((gx % 16 == 0) | (gx % 16 == 15)) & ((gy % 4 == 0) | (gy % 4 == 3))


def edges_kernel(state, planes, x_even, x_odd, y_even, y_odd, flat):
    place = position()
    even_x = place[0] % 2 == 0
    even_y = place[1] % 2 == 0
    size = LEVELS * ROWS
    lane = lane_of((LEVELS, LANES))
    gathered = jnp.zeros((LEVELS, LANES), F32)
    for field in range(4):
        values = [state[pl.ds(field * size + x, LEVELS, stride=ROWS), :] for x in range(ROWS)]
        for x in range(ROWS):
            slot = field * ROWS + x
            planes[pl.ds(slot * LEVELS, LEVELS), :] = values[x]
            gathered = jnp.where(lane >> 1 == slot, turn(values[x], 2 * slot + 1, 1), gathered)
        for slot, depth in ((field, 0), (4, 1)) if field == 0 else ((field, 0),):
            span = pl.ds(slot * LEVELS, LEVELS)
            low, high = values[depth], values[ROWS - 1 - depth]
            x_even[span, :] = jnp.where(even_x, high, low)
            x_odd[span, :] = jnp.where(even_x, low, high)
    flat[...] = jnp.transpose(jnp.concatenate([gathered, jnp.zeros_like(gathered)], axis=0))
    high, low = flat[pl.ds(0, 16, stride=2), :], flat[pl.ds(1, 16, stride=2), :]
    y_even[0:16, :] = jnp.where(even_y, high, low)
    y_odd[...] = jnp.where(even_y, low, high)
    x_even[pl.ds(5 * LEVELS, 16), :] = jnp.where(even_y, low, high)


def column_of(row):
    return jnp.transpose(jnp.broadcast_to(row, (LANES, LANES)))


def tables_kernel(vectors, square_row, by_level, by_row, by_wave, by_block):
    place = position()
    tall = column_of(vectors[:, :LANES])
    rate, density = tall[:LEVELS], tall[LEVELS:]
    row = row_of((LEVELS, LANES))
    by_level[pl.ds(0, LEVELS), :] = rate
    by_level[pl.ds(LEVELS, LEVELS), :] = jnp.where(
        row < LEVELS - 1, 0.5 * turn(density, -1, 0) / density, 0.0
    )
    by_level[pl.ds(2 * LEVELS, LEVELS), :] = jnp.where(row > 0, 0.5 * turn(density, 1, 0) / density, 0.0)
    own = by_level[pl.ds(place[0], 1), :]

    both = jnp.concatenate([own, own], axis=1)
    root, inverse, rho = decay(both, square_row[...])
    powers = squarings(rho, 6)
    for i, value in enumerate(powers + [powers[6] * rho, -1.0 / root]):
        by_row[pl.ds(8 * i, 8), :] = value
    half = row_of((LANES, LANES)) >> 1
    odd = (row_of((LANES, LANES)) & 1) != 0
    narrow = [jnp.broadcast_to(value[0:1, :LANES], (LANES, LANES)) for value in powers[:6]]
    rising = lane_powers(narrow, half)
    falling = lane_powers(narrow, 63 - half)
    by_wave[pl.ds(0, LANES), :] = rising
    by_wave[pl.ds(LANES, LANES), :] = falling
    by_wave[pl.ds(2 * LANES, LANES), :] = narrow[0] * jnp.where(odd, rising, falling)

    r64 = powers[6]
    r128 = r64 * r64
    r256 = r128 * r128
    images = 1.0 / (1.0 - r256 * r256)
    mine = place[1] & 3
    row = row_of(rho.shape)
    for j in range(4):
        for i, offset in enumerate((-1, 3)):
            exponent = jnp.where(row < 2, (mine - j + offset) & 7, (j - mine + offset) & 7)
            weight = jnp.where((exponent & 1) != 0, r64, 1.0)
            weight = weight * jnp.where((exponent & 2) != 0, r128, 1.0)
            weight = weight * jnp.where((exponent & 4) != 0, r256, 1.0)
            by_block[pl.ds((2 * j + i) * 8, 8), :] = weight * images
    scale = -1.0 / root
    by_block[pl.ds(64, 8), :] = jnp.where(row == 0, scale, jnp.where(row == 1, scale * r64, scale * inverse))


def inner_kernel(state, vectors, layer_in, layer_out, star):
    fields = [[plane(state, f, x) for x in range(ROWS)] for f in range(4)]
    for x in range(ROWS):
        u, v, w, th = (fields[f][x] for f in range(4))
        for f in range(4):
            here = fields[f][x]
            change = v * north_difference(here) + w * level_difference(here)
            if x == 0:
                change = change + u * fields[f][1]
            elif x == ROWS - 1:
                change = change - u * fields[f][x - 1]
            else:
                change = change + u * (fields[f][x + 1] - fields[f][x - 1])
            value = here - 0.1 * change
            if f == 2:
                value = value + 0.1 * th
            star[pl.ds((f * ROWS + x) * LEVELS, LEVELS), :] = value

    columns = jnp.concatenate(
        [jnp.concatenate([fields[f][x] for f in range(4)], axis=0).astype(BF16) for x in range(ROWS)],
        axis=1,
    )
    first = (((0,), (0,)), ((), ()))
    shift = [column_of(vectors[:, i * LANES : (i + 1) * LANES]) for i in (1, 2)]
    shift = jnp.concatenate(shift, axis=0)
    before = lax.dot_general(layer_in[...], columns, first, preferred_element_type=F32)
    before = before + jnp.concatenate([shift] * ROWS, axis=1)
    hidden = (before * (1.0 / (1.0 + jnp.exp(-before)))).astype(BF16)
    forcing = lax.dot_general(layer_out[...], hidden, first, preferred_element_type=F32)
    for x in range(ROWS):
        span = slice(x * LANES, (x + 1) * LANES)
        for f, part in ((2, forcing[LEVELS:, span]), (3, forcing[:LEVELS, span])):
            at = pl.ds((f * ROWS + x) * LEVELS, LEVELS)
            star[at, :] = star[at, :] + 0.2 * part


def side_terms(state, edge, low):
    u, v, w, _, second = edge
    own = jnp.where(low, plane(state, 0, 0), plane(state, 0, ROWS - 1))
    sign = jnp.where(low, 0.1, -0.1)
    adds = [sign * own * value for value in edge[:4]]
    along = u * (own - second)
    beyond = u - (sign * along + 0.1 * (v * north_difference(u) + w * level_difference(u)))
    return adds, beyond


def outer_kernel(
    state,
    inner,
    x_even,
    x_far,
    x_near,
    y_even,
    y_odd,
    y_both,
    by_level,
    forward,
    star,
    message,
    flat,
):
    place = position()
    even_x = place[0] % 2 == 0
    even_y = place[1] % 2 == 0
    shape = (LEVELS, LANES)
    lane = lane_of(shape)

    helping = far_both(place[0] ^ 1, place[1])
    other = jnp.where(helping, y_both[0:16, :], y_odd[...])
    other = jnp.where(far_both(place[0], place[1]), 0.0, other)
    flat[...] = jnp.zeros((LANES, LANES), F32)
    flat[pl.ds(0, 16, stride=2), :] = jnp.where(even_y, y_even[0:16, :], other)
    flat[pl.ds(1, 16, stride=2), :] = jnp.where(even_y, other, y_even[0:16, :])
    low_side = place[1] % 4 == 0
    scale = jnp.where(low_side, 0.1, -0.1) * jnp.where(helping, 1.0, 0.0)
    theirs = x_even[pl.ds(5 * LEVELS + 4, 4), :]
    flat[pl.ds(32, 16), :] = scale * jnp.concatenate([theirs] * 4, axis=0) * y_both[16:32, :]
    columns = jnp.transpose(flat[...])[:LEVELS]
    spans = [pl.ds(i * LEVELS, LEVELS) for i in range(5)]
    even_adds, even_beyond = side_terms(state, [x_even[at, :] for at in spans], ~even_x)
    far_x = (place[0] % 16 == 0) | (place[0] % 16 == 15)
    odd_edge = [jnp.where(far_x, x_far[at, :], x_near[at, :]) for at in spans]
    odd_adds, odd_beyond = side_terms(state, odd_edge, even_x)
    end_sign = jnp.where(lane == 0, 0.1, jnp.where(lane == LANES - 1, -0.1, 0.0))
    whole = [[None] * ROWS for _ in range(4)]
    side_u = [None] * ROWS
    for x in range(ROWS):
        v = plane(state, 1, x)
        for f in range(4):
            slot = f * ROWS + x
            side = end_sign * v * turn(columns, -(2 * slot + 1), 1)
            if f == 0:
                side_u[x] = side
            value = inner[pl.ds(slot * LEVELS, LEVELS), :] + side
            if x == 0:
                value = value + jnp.where(even_x, odd_adds[f], even_adds[f])
            if x == ROWS - 1:
                value = value + jnp.where(even_x, even_adds[f], odd_adds[f])
            whole[f][x] = value
            star[pl.ds(slot * LEVELS, LEVELS), :] = value

    low_beyond = jnp.where(even_x, odd_beyond, even_beyond)
    high_beyond = jnp.where(even_x, even_beyond, odd_beyond)
    padded = [low_beyond] + whole[0] + [high_beyond]
    divergence = []
    up, down = by_level[pl.ds(LEVELS, LEVELS), :], by_level[pl.ds(2 * LEVELS, LEVELS), :]
    step = jnp.where(lane < 35, turn(columns, -1, 1), 0.0) - jnp.where(lane > 32, turn(columns, 1, 1), 0.0)
    lifted = turn(columns, -8, 1)
    step = 0.5 * step + up * turn(lifted, -1, 0) - down * turn(lifted, 1, 0)
    left_out = jnp.where((lane >= 32) & (lane < 36), step, 0.0)
    beside = jnp.where(low_side, 0.5, -0.5) * columns
    left_out = jnp.where((lane >= 36) & (lane < 40), beside, left_out)
    left_out = jnp.where(lane == 40, -0.5 * turn(columns, 5, 1), left_out)
    left_out = jnp.where(lane == 41, 0.5 * turn(columns, 9, 1), left_out)
    left_out = turn(left_out, OTHER - 32, 1)
    extra = [left_out - 0.5 * side_u[ROWS - 1], left_out + 0.5 * side_u[0]]
    for x in range(ROWS):
        v, w = whole[1][x], whole[2][x]
        upright = up * turn(w, -1, 0) - down * turn(w, 1, 0)
        divergence.append(0.5 * (padded[x + 2] - padded[x]) + 0.5 * north_difference(v) + upright)
        low, high = LOW + x // 2, HIGH + x // 2
        value = jnp.where(lane == low, 0.5 * turn(v, low, 1), extra[x % 2])
        extra[x % 2] = jnp.where(lane == high, -0.5 * turn(v, high + 1, 1), value)
    pieces = [divergence[0], divergence[2], extra[0], divergence[1], divergence[3], extra[1]]
    modal = dot3(parts(forward[...]), parts(jnp.concatenate(pieces, axis=1)))
    for i in range(6):
        message[pl.ds(i, LEVELS, stride=6), :] = modal[:, i * LANES : (i + 1) * LANES]


def decay(rate, square):
    lam = rate + square
    root = jnp.sqrt(lam * (1.0 + lam))
    inverse = 1.0 + 2.0 * lam + 2.0 * root
    return root, inverse, 1.0 / inverse


def squarings(rho, count):
    powers = [rho]
    for _ in range(count):
        powers.append(powers[-1] * powers[-1])
    return powers


def lane_powers(powers, exponent):
    product = None
    for bit in range(6):
        factor = jnp.where((exponent & (1 << bit)) != 0, powers[bit], 1.0)
        product = factor if product is None else product * factor
    return product


def shifted(values, shift):
    size = values.shape[0]
    if shift % 8 == 0:
        zeros = jnp.zeros((abs(shift), values.shape[1]), F32)
        if shift > 0:
            return jnp.concatenate([zeros, values[:-shift]], axis=0)
        return jnp.concatenate([values[-shift:], zeros], axis=0)
    row = row_of(values.shape)
    inside = row >= shift if shift > 0 else row < size + shift
    return jnp.where(inside, turn(values, shift, 0), 0.0)


def by_parity(even, odd):
    shape = (8, even.shape[1])
    tile = jnp.where((row_of(shape) & 1) != 0, jnp.broadcast_to(odd, shape), jnp.broadcast_to(even, shape))
    return jnp.concatenate([tile] * (LANES // 8), axis=0)


def halves(values):
    return jnp.concatenate([values, values], axis=1)


def solve_kernel(received, basis_high, basis_low, by_row, by_wave, local, moments):
    place = position()
    blocks = received.shape[0] // 6
    lane = lane_of((blocks, LANES))
    ends = (lane == 0) | (lane == LANES - 1)
    even = place[1] < 4
    parity = jnp.where(even, 0, 1)
    low_side = place[1] % 4 == 0
    edge = jnp.where(low_side, 0, LANES - 1)
    within = jnp.where(low_side, 1, LANES - 2)
    row = row_of((blocks, LANES))
    inside, outside = [], [jnp.zeros((blocks, LANES), F32)] * 2
    for h in range(2):
        first, second, extra = (received[pl.ds(3 * h + j, blocks, stride=6), :] for j in range(3))
        first = first + jnp.where(ends & even, turn(extra, 1, 0), 0.0)
        second = second + jnp.where(ends & ~even, turn(extra, -1, 0), 0.0)
        other = jnp.where(row % 16 == 0, turn(extra, -1, 0), jnp.where(row % 16 == 15, turn(extra, 1, 0), 0.0))
        value = lambda i: jnp.sum(jnp.where(lane == OTHER + i + parity, other, 0.0), axis=1, keepdims=True)
        beside = [value(4), value(6)]
        corner = jnp.broadcast_to(value(8), (blocks, LANES))
        first = first + jnp.where(lane == edge, value(0), jnp.where(lane == within, -beside[0], 0.0))
        second = second + jnp.where(lane == edge, value(2), jnp.where(lane == within, -beside[1], 0.0))
        first = first + jnp.where((lane == edge) & even, turn(corner, 1, 0), 0.0)
        second = second + jnp.where((lane == edge) & ~even, turn(corner, -1, 0), 0.0)
        inside.append(jnp.concatenate([first, second], axis=0))
        for r in range(2):
            for i, start in enumerate((HIGH, LOW)):
                at = 2 * h + i
                outside[r] = jnp.where(lane == at, turn(extra, at - start - r, 1), outside[r])
            at = 2 * h + jnp.where(low_side, 1, 0)
            outside[r] = outside[r] + jnp.where(lane == at, beside[r], 0.0)
    right = parts(jnp.concatenate(inside + [jnp.concatenate(outside, axis=0)], axis=1))
    first = (((0,), (0,)), ((), ()))
    dot = lambda a, b: lax.dot_general(a, b[...], first, preferred_element_type=F32)
    spectral = dot(right[0], basis_high) + (dot(right[0], basis_low) + dot(right[1], basis_high))
    source = jnp.concatenate([spectral[:LANES], spectral[LANES : 2 * LANES]], axis=1)
    ext = spectral[2 * LANES : 2 * LANES + 8]
    high = jnp.concatenate([ext[0:1], ext[2:3]], axis=1)
    low = jnp.concatenate([ext[1:2], ext[3:4]], axis=1)

    power = lambda i: by_row[pl.ds(8 * i, 1), :]
    ahead, behind = source, source
    for bit in range(6):
        ahead = ahead + power(bit) * shifted(ahead, 2 << bit)
        behind = behind + power(bit) * shifted(behind, -(2 << bit))
    border = halves(by_wave[pl.ds(2 * LANES, LANES), :]) * by_parity(high, low)
    local[...] = ahead + behind - source + border
    rho, r65 = power(0), power(7)
    across = [
        rho * ahead[LANES - 2 : LANES - 1] + high,
        rho * ahead[LANES - 1 :] + r65 * low,
        rho * behind[0:1] + r65 * high,
        rho * behind[1:2] + low,
        jnp.zeros((4, source.shape[1]), F32),
    ]
    across = jnp.concatenate(across, axis=0)
    for j in range(4):
        moments[pl.ds(j * 8, 8), :] = across


def back_kernel(local, moments, basis_high, basis_low, by_row, by_wave, by_block, message):
    place = position()
    width = local.shape[1]
    blocks = basis_high.shape[0] // 2
    even = place[1] < 4
    mine = place[1] & 3
    carry = jnp.zeros((8, width), F32)
    for j in range(4):
        theirs = moments[pl.ds(j * 8, 8), :]
        swapped = jnp.concatenate([theirs[:, LANES:], theirs[:, :LANES]], axis=1)
        carry = carry + by_block[pl.ds(16 * j, 8), :] * theirs + by_block[pl.ds(16 * j + 8, 8), :] * swapped
    own = moments[pl.ds(pl.multiple_of(mine * 8, 8), 8), :]
    scale, by_r64, by_inverse = (by_block[pl.ds(64 + i, 1), :] for i in range(3))
    after = scale * own[0:1] + by_r64 * carry[0:1] + by_inverse * carry[2:3]
    before = scale * own[3:4] + by_r64 * carry[3:4] + by_inverse * carry[1:2]
    total = local[...] + halves(by_wave[pl.ds(0, LANES), :]) * by_parity(carry[0:1], carry[1:2])
    total = total + halves(by_wave[pl.ds(LANES, LANES), :]) * by_parity(carry[2:3], carry[3:4])
    total = total * scale
    pieces = [total[:, :LANES], total[:, LANES:]]
    for h in range(2):
        span = slice(h * LANES, (h + 1) * LANES)
        pieces += [after[:, span], before[:, span]]
    pieces.append(jnp.zeros((LANES - 4, LANES), F32))
    right = parts(jnp.concatenate(pieces, axis=0))
    last = (((1,), (1,)), ((), ()))
    dot = lambda a, b: lax.dot_general(a[...], b, last, preferred_element_type=F32)
    pressure = dot(basis_high, right[0]) + (dot(basis_high, right[1]) + dot(basis_low, right[0]))
    lane = lane_of((blocks, LANES))
    ends = (lane == 0) | (lane == LANES - 1)
    outside = [pressure[r * blocks : (r + 1) * blocks, 2 * LANES :] for r in range(2)]
    for h in range(2):
        span = slice(h * LANES, (h + 1) * LANES)
        first, second = pressure[:blocks, span], pressure[blocks:, span]
        extra = jnp.where(ends, jnp.where(even, turn(first, -1, 0), turn(second, 1, 0)), 0.0)
        for r in range(2):
            extra = jnp.where(lane == HIGH + r, turn(outside[r], HIGH + r - 2 * h, 1), extra)
            extra = jnp.where(lane == LOW + r, turn(outside[r], LOW + r - 1 - 2 * h, 1), extra)
        for j, value in enumerate((first, second, extra)):
            message[pl.ds(3 * h + j, blocks, stride=6), :] = value


def mend_kernel(star, message, state, relayed, forward, whole, middle, flat):
    place = position()
    both = far_both(place[0], place[1])
    whole[...] = star[...]
    for i, r in enumerate((1, 2)):
        middle[pl.ds(i * LEVELS, LEVELS), :] = message[pl.ds(3 * (r % 2) + r // 2, LEVELS, stride=6), :]

    @pl.when(both)
    def _():
        lane = lane_of((LEVELS, LANES))
        even_y = place[1] % 2 == 0
        far = relayed[16:32, :]
        flat[...] = jnp.zeros((LANES, LANES), F32)
        flat[pl.ds(0, 16, stride=2), :] = jnp.where(even_y, 0.0, far)
        flat[pl.ds(1, 16, stride=2), :] = jnp.where(even_y, far, 0.0)
        columns = jnp.transpose(flat[...])[:LEVELS]
        end_sign = jnp.where(lane == 0, 0.1, jnp.where(lane == LANES - 1, -0.1, 0.0))
        steps = []
        for x in range(ROWS):
            v = plane(state, 1, x)
            for f in range(4):
                slot = f * ROWS + x
                side = end_sign * v * turn(columns, -(2 * slot + 1), 1)
                at = pl.ds(slot * LEVELS, LEVELS)
                whole[at, :] = whole[at, :] + side
                if f == 1 and x in (1, 2):
                    steps.append(0.5 * north_difference(side))
        modal = dot3(parts(forward[...]), parts(jnp.concatenate(steps, axis=1)))
        for i in range(2):
            at = pl.ds(i * LEVELS, LEVELS)
            middle[at, :] = middle[at, :] + modal[:, i * LANES : (i + 1) * LANES]


def final_kernel(received, middle, star, back, by_level, out, held, sent_out):
    size = LEVELS * ROWS
    span = lambda i: pl.ds(i * size // 2, size // 2)
    copies = [pltpu.make_async_copy(held.at[span(i), :], out.at[span(i), :], sent_out.at[i]) for i in range(8)]
    some = LEVELS // 2

    def put(f, matrix, right):
        for half in range(2):
            if right is not None:
                changes = dot3(parts(matrix[half * some : (half + 1) * some]), right)
            for x in range(ROWS):
                value = star[pl.ds((f * ROWS + x) * LEVELS + half * some, some), :]
                if right is not None:
                    value = value - changes[:, x * LANES : (x + 1) * LANES]
                held[pl.ds(f * size + half * some * ROWS + x, some, stride=ROWS), :] = value
            copies[2 * f + half].start()

    put(3, None, None)
    lane = lane_of((LEVELS, LANES))
    row_at = lambda ref, r: ref[pl.ds(3 * (r % 2) + r // 2, LEVELS, stride=6), :]
    p = [row_at(received, r) for r in range(ROWS)]
    extra = [row_at(received, 4), row_at(received, 5)]
    low = [turn(extra[r % 2], -(LOW + r // 2), 1) for r in range(ROWS)]
    high = [turn(extra[r % 2], LANES - 1 - (HIGH + r // 2), 1) for r in range(ROWS)]
    four_rate = 4.0 * by_level[pl.ds(0, LEVELS), :]

    def next_row(r, opposite):
        here = p[r]
        divergence = middle[pl.ds((r - 1) * LEVELS, LEVELS), :]
        plus = jnp.where(lane < LANES - 2, turn(here, -2, 1), turn(high[r], -1, 1))
        minus = jnp.where(lane > 1, turn(here, 2, 1), turn(low[r], 1, 1))
        return (
            2.0 * here
            - opposite
            + four_rate * here
            + (2.0 * here - plus - minus)
            + 4.0 * divergence
        )

    ends = (lane == 0) | (lane == LANES - 1)
    before = jnp.where(ends, extra[1], next_row(1, p[3]))
    after = jnp.where(ends, extra[0], next_row(2, p[0]))
    padded = [before] + p + [after]
    matrix = back[...]
    joined = lambda values: parts(jnp.concatenate(values, axis=1))
    put(2, 0.5 * level_difference(matrix), joined(p))
    put(1, matrix, joined([0.5 * north_difference(p[x], low[x], high[x]) for x in range(ROWS)]))
    put(0, matrix, joined([0.5 * (padded[x + 2] - padded[x]) for x in range(ROWS)]))
    for copy in copies:
        copy.wait()


def call(kernel, shapes, args, name, scratch=(), cost=None, copies=0):
    vmem = pl.BlockSpec(memory_space=pltpu.VMEM)
    return pl.pallas_call(
        kernel,
        out_shape=[jax.ShapeDtypeStruct(s, F32) for s in shapes],
        in_specs=[vmem] * len(args),
        out_specs=[pl.BlockSpec(memory_space=pl.ANY) if copies else vmem] * len(shapes),
        scratch_shapes=[pltpu.VMEM(s, F32) for s in scratch]
        + ([pltpu.SemaphoreType.DMA((copies,))] if copies else []),
        compiler_params=pltpu.CompilerParams(vmem_limit_bytes=32 * 1024 * 1024),
        name=name,
        cost_estimate=cost,
    )(*args)


def swap(values, axis, odd):
    count = lax.axis_size(axis)
    pairs = []
    for i in range(odd, count + odd, 2):
        pairs += [(i % count, (i + 1) % count), ((i + 1) % count, i % count)]
    return lax.ppermute(values, axis, pairs)


def swap_odd_x(values, far):
    count = lax.axis_size("gx")
    pairs = []
    for i in range(1, count + 1, 2):
        one, two = i % count, (i + 1) % count
        if (one % 16 == 15) == far:
            pairs += [(one, two), (two, one)]
    return lax.ppermute(values, "gx", pairs)


def swap_odd_y(values, helping):
    count_x, count_y = lax.axis_size("gx"), lax.axis_size("gy")
    pairs = []
    for i in range(count_x):
        for j in range(1, count_y + 1, 2):
            one, two = j % count_y, (j + 1) % count_y
            if not far_both(i, one) and far_both(i ^ 1, one) == helping:
                pairs += [(i * count_y + one, i * count_y + two), (i * count_y + two, i * count_y + one)]
    return lax.ppermute(values, ("gx", "gy"), pairs)


def hand_over(values):
    count_x, count_y = lax.axis_size("gx"), lax.axis_size("gy")
    pairs = [
        ((i ^ 1) * count_y + j, i * count_y + j)
        for i in range(count_x)
        for j in range(count_y)
        if far_both(i, j)
    ]
    return lax.ppermute(values, ("gx", "gy"), pairs)


def exchange(values):
    count_x, count_y = lax.axis_size("gx"), lax.axis_size("gy")
    near = count_y // 2
    groups = [[i * count_y + h * near + y for i in range(count_x) for h in range(2)] for y in range(near)]
    shaped = values.reshape(2 * count_x, 1, values.size // (2 * count_x))
    moved = lax.all_to_all(
        shaped, ("gx", "gy"), 0, 0, tiled=True, axis_index_groups=groups
    )
    return moved.reshape(values.shape)


def on_device(
    model_state, density, layer_in, layer_bias, layer_out, mode_forward, mode_back, mode_rate
):
    blocks = lax.axis_size("gx")
    total_east = blocks * ROWS
    state = model_state.reshape(4 * LEVELS * ROWS, LANES)
    basis, square = east_tables(total_east // 2, blocks)
    basis_high, basis_low = split_table(np.ascontiguousarray(basis.T))
    square_row = np.ascontiguousarray(np.broadcast_to(np.concatenate([square, square]), (8, total_east)))

    planes, x_even, x_odd, y_even, y_odd = call(
        edges_kernel,
        [(16 * LEVELS, LANES), (5 * LEVELS + 16, LANES), (5 * LEVELS, LANES), (16, LANES), (16, LANES)],
        [state],
        "edges",
        scratch=[(LANES, LANES)],
    )
    got_x_even = swap(x_even, "gx", 0)
    got_x_far = swap_odd_x(x_odd, True)
    got_y_odd = swap_odd_y(y_odd, False)
    y_both = jnp.concatenate([y_odd, got_x_even[5 * LEVELS :]], axis=0)
    y_both, x_odd, y_even = lax.optimization_barrier((y_both, x_odd, y_even))
    got_y_both = swap_odd_y(y_both, True)
    got_x_near = swap_odd_x(x_odd, False)
    vectors = jnp.concatenate([mode_rate, density, layer_bias])[None, :]
    long = pl.CostEstimate(flops=10**10, transcendentals=0, bytes_accessed=2**24)
    by_level, by_row, by_wave, by_block = call(
        tables_kernel,
        [(3 * LEVELS, LANES), (72, total_east), (3 * LANES, LANES), (72, total_east)],
        [vectors, square_row],
        "tables",
        cost=long,
    )
    by_level, y_even = lax.optimization_barrier((by_level, y_even))
    got_y_even = swap(y_even, "gy", 0)
    (inner,) = call(
        inner_kernel,
        [(16 * LEVELS, LANES)],
        [planes, vectors, layer_in, layer_out],
        "inner",
        cost=None,
    )
    star, message = call(
        outer_kernel,
        [(16 * LEVELS, LANES), (blocks * 6, LANES)],
        [
            planes,
            inner,
            got_x_even,
            got_x_far,
            got_x_near,
            got_y_even,
            got_y_odd,
            got_y_both,
            by_level,
            mode_forward,
        ],
        "outer",
        scratch=[(LANES, LANES)],
    )
    message, got_y_both = lax.optimization_barrier((message, got_y_both))
    relayed = hand_over(got_y_both)
    modal = exchange(message)
    whole, middle = call(
        mend_kernel,
        [(16 * LEVELS, LANES), (2 * LEVELS, LANES)],
        [star, message, planes, relayed, mode_forward],
        "mend",
        scratch=[(LANES, LANES)],
    )
    modal, whole, middle = lax.optimization_barrier((modal, whole, middle))
    local, moments = call(
        solve_kernel,
        [(LANES, total_east), (32, total_east)],
        [modal, basis_high, basis_low, by_row, by_wave],
        "solve",
    )
    moments = lax.all_to_all(
        moments.reshape(4, 8, total_east),
        "gy",
        0,
        0,
        tiled=True,
        axis_index_groups=[[0, 1, 2, 3], [4, 5, 6, 7]],
    ).reshape(32, total_east)
    (reply,) = call(
        back_kernel,
        [(blocks * 6, LANES)],
        [local, moments, basis_high, basis_low, by_row, by_wave, by_block],
        "back",
    )
    pressure = exchange(reply)
    (out,) = call(
        final_kernel,
        [(4 * LEVELS * ROWS, LANES)],
        [pressure, middle, whole, mode_back, by_level],
        "final",
        scratch=[(4 * LEVELS * ROWS, LANES)],
        copies=8,
    )
    return out.reshape(model_state.shape)


def solution(mesh):
    return jax.shard_map(
        on_device,
        mesh=mesh,
        in_specs=(P(None, None, "gx", "gy"), P(), P(), P(), P(), P(), P(), P()),
        out_specs=P(None, None, "gx", "gy"),
        check_vma=False,
    )
```

```python
import math

import jax
import jax.numpy as jnp
import ml_dtypes
import numpy as np
from jax import lax
from jax.experimental import pallas as pl
from jax.experimental.pallas import tpu as pltpu
from jax.sharding import PartitionSpec as P

F32 = jnp.float32
BF16 = jnp.bfloat16
LEVELS = 64
ROWS = 4
LANES = 128
LOW = 16
HIGH = 32
OTHER = 48


def split_table(table):
    high = table.astype(np.float32).astype(ml_dtypes.bfloat16)
    low = (table - high.astype(np.float64)).astype(np.float32).astype(ml_dtypes.bfloat16)
    return high, low


def east_tables(total, blocks):
    rows = total // blocks
    x = (np.arange(rows)[:, None] + rows * np.arange(blocks)[None, :]).reshape(-1)
    k = np.arange(total)
    angle = 2.0 * math.pi * ((k[:, None] * x[None, :]) % total) / total
    basis = np.where((k <= total // 2)[:, None], np.cos(angle), np.sin(angle))
    scale = np.where((k == 0) | (k == total // 2), 1.0, math.sqrt(2.0)) / math.sqrt(total)
    basis = basis * scale[:, None]
    square = np.sin(math.pi * k / total) ** 2
    return basis, square.astype(np.float32)


def position():
    return lax.axis_index("gx"), lax.axis_index("gy")


def lane_of(shape):
    return lax.broadcasted_iota(jnp.int32, shape, len(shape) - 1)


def row_of(shape):
    return lax.broadcasted_iota(jnp.int32, shape, 0)


def turn(values, shift, axis):
    size = values.shape[axis]
    return pltpu.roll(values, shift % size, axis) if shift % size else values


def parts(values):
    high = values.astype(BF16)
    return high, (values - high.astype(F32)).astype(BF16)


def dot3(left, right):
    dot = lambda a, b: jnp.dot(a, b, preferred_element_type=F32)
    return dot(left[0], right[0]) + (dot(left[0], right[1]) + dot(left[1], right[0]))


def level_difference(values):
    row = row_of(values.shape)
    last = values.shape[0] - 1
    upper = jnp.where(row < last, turn(values, -1, 0), 0.0)
    lower = jnp.where(row > 0, turn(values, 1, 0), 0.0)
    return upper - lower


def north_difference(values, low=0.0, high=0.0):
    lane = lane_of(values.shape)
    after = jnp.where(lane < LANES - 1, turn(values, -1, 1), high)
    before = jnp.where(lane > 0, turn(values, 1, 1), low)
    return after - before


def plane(ref, field, x):
    return ref[pl.ds((field * ROWS + x) * LEVELS, LEVELS), :]


def far_both(gx, gy):
    return ((gx % 16 == 0) | (gx % 16 == 15)) & ((gy % 4 == 0) | (gy % 4 == 3))


def edges_kernel(state, planes, x_even, x_odd, y_even, y_odd, flat):
    place = position()
    even_x = place[0] % 2 == 0
    even_y = place[1] % 2 == 0
    size = LEVELS * ROWS
    lane = lane_of((LEVELS, LANES))
    gathered = jnp.zeros((LEVELS, LANES), F32)
    for field in range(4):
        values = [state[pl.ds(field * size + x, LEVELS, stride=ROWS), :] for x in range(ROWS)]
        for x in range(ROWS):
            slot = field * ROWS + x
            planes[pl.ds(slot * LEVELS, LEVELS), :] = values[x]
            gathered = jnp.where(lane >> 1 == slot, turn(values[x], 2 * slot + 1, 1), gathered)
        for slot, depth in ((field, 0), (4, 1)) if field == 0 else ((field, 0),):
            span = pl.ds(slot * LEVELS, LEVELS)
            low, high = values[depth], values[ROWS - 1 - depth]
            x_even[span, :] = jnp.where(even_x, high, low)
            x_odd[span, :] = jnp.where(even_x, low, high)
    flat[...] = jnp.transpose(jnp.concatenate([gathered, jnp.zeros_like(gathered)], axis=0))
    high, low = flat[pl.ds(0, 16, stride=2), :], flat[pl.ds(1, 16, stride=2), :]
    y_even[0:16, :] = jnp.where(even_y, high, low)
    y_odd[...] = jnp.where(even_y, low, high)
    x_even[pl.ds(5 * LEVELS, 16), :] = jnp.where(even_y, low, high)


def column_of(row):
    return jnp.transpose(jnp.broadcast_to(row, (LANES, LANES)))


def tables_kernel(vectors, square_row, by_level, by_row, by_wave, by_block):
    place = position()
    tall = column_of(vectors[:, :LANES])
    rate, density = tall[:LEVELS], tall[LEVELS:]
    row = row_of((LEVELS, LANES))
    by_level[pl.ds(0, LEVELS), :] = rate
    by_level[pl.ds(LEVELS, LEVELS), :] = jnp.where(
        row < LEVELS - 1, 0.5 * turn(density, -1, 0) / density, 0.0
    )
    by_level[pl.ds(2 * LEVELS, LEVELS), :] = jnp.where(row > 0, 0.5 * turn(density, 1, 0) / density, 0.0)
    own = by_level[pl.ds(place[0], 1), :]

    both = jnp.concatenate([own, own], axis=1)
    root, inverse, rho = decay(both, square_row[...])
    powers = squarings(rho, 6)
    for i, value in enumerate(powers + [powers[6] * rho, -1.0 / root]):
        by_row[pl.ds(8 * i, 8), :] = value
    half = row_of((LANES, LANES)) >> 1
    odd = (row_of((LANES, LANES)) & 1) != 0
    narrow = [jnp.broadcast_to(value[0:1, :LANES], (LANES, LANES)) for value in powers[:6]]
    rising = lane_powers(narrow, half)
    falling = lane_powers(narrow, 63 - half)
    by_wave[pl.ds(0, LANES), :] = rising
    by_wave[pl.ds(LANES, LANES), :] = falling
    by_wave[pl.ds(2 * LANES, LANES), :] = narrow[0] * jnp.where(odd, rising, falling)

    r64 = powers[6]
    r128 = r64 * r64
    r256 = r128 * r128
    images = 1.0 / (1.0 - r256 * r256)
    mine = place[1] & 3
    row = row_of(rho.shape)
    for j in range(4):
        for i, offset in enumerate((-1, 3)):
            exponent = jnp.where(row < 2, (mine - j + offset) & 7, (j - mine + offset) & 7)
            weight = jnp.where((exponent & 1) != 0, r64, 1.0)
            weight = weight * jnp.where((exponent & 2) != 0, r128, 1.0)
            weight = weight * jnp.where((exponent & 4) != 0, r256, 1.0)
            by_block[pl.ds((2 * j + i) * 8, 8), :] = weight * images
    scale = -1.0 / root
    by_block[pl.ds(64, 8), :] = jnp.where(row == 0, scale, jnp.where(row == 1, scale * r64, scale * inverse))


def inner_kernel(state, vectors, layer_in, layer_out, star):
    fields = [[plane(state, f, x) for x in range(ROWS)] for f in range(4)]
    for x in range(ROWS):
        u, v, w, th = (fields[f][x] for f in range(4))
        for f in range(4):
            here = fields[f][x]
            change = v * north_difference(here) + w * level_difference(here)
            if x == 0:
                change = change + u * fields[f][1]
            elif x == ROWS - 1:
                change = change - u * fields[f][x - 1]
            else:
                change = change + u * (fields[f][x + 1] - fields[f][x - 1])
            value = here - 0.1 * change
            if f == 2:
                value = value + 0.1 * th
            star[pl.ds((f * ROWS + x) * LEVELS, LEVELS), :] = value

    columns = jnp.concatenate(
        [jnp.concatenate([fields[f][x] for f in range(4)], axis=0).astype(BF16) for x in range(ROWS)],
        axis=1,
    )
    first = (((0,), (0,)), ((), ()))
    shift = [column_of(vectors[:, i * LANES : (i + 1) * LANES]) for i in (1, 2)]
    shift = jnp.concatenate(shift, axis=0)
    before = lax.dot_general(layer_in[...], columns, first, preferred_element_type=F32)
    before = before + jnp.concatenate([shift] * ROWS, axis=1)
    hidden = (before * (1.0 / (1.0 + jnp.exp(-before)))).astype(BF16)
    forcing = lax.dot_general(layer_out[...], hidden, first, preferred_element_type=F32)
    for x in range(ROWS):
        span = slice(x * LANES, (x + 1) * LANES)
        for f, part in ((2, forcing[LEVELS:, span]), (3, forcing[:LEVELS, span])):
            at = pl.ds((f * ROWS + x) * LEVELS, LEVELS)
            star[at, :] = star[at, :] + 0.2 * part


def side_terms(state, edge, low):
    u, v, w, _, second = edge
    own = jnp.where(low, plane(state, 0, 0), plane(state, 0, ROWS - 1))
    sign = jnp.where(low, 0.1, -0.1)
    adds = [sign * own * value for value in edge[:4]]
    along = u * (own - second)
    beyond = u - (sign * along + 0.1 * (v * north_difference(u) + w * level_difference(u)))
    return adds, beyond


def outer_kernel(
    state,
    inner,
    x_even,
    x_far,
    x_near,
    y_even,
    y_odd,
    y_both,
    by_level,
    forward,
    star,
    message,
    flat,
):
    place = position()
    even_x = place[0] % 2 == 0
    even_y = place[1] % 2 == 0
    shape = (LEVELS, LANES)
    lane = lane_of(shape)

    helping = far_both(place[0] ^ 1, place[1])
    other = jnp.where(helping, y_both[0:16, :], y_odd[...])
    other = jnp.where(far_both(place[0], place[1]), 0.0, other)
    flat[...] = jnp.zeros((LANES, LANES), F32)
    flat[pl.ds(0, 16, stride=2), :] = jnp.where(even_y, y_even[0:16, :], other)
    flat[pl.ds(1, 16, stride=2), :] = jnp.where(even_y, other, y_even[0:16, :])
    low_side = place[1] % 4 == 0
    scale = jnp.where(low_side, 0.1, -0.1) * jnp.where(helping, 1.0, 0.0)
    theirs = x_even[pl.ds(5 * LEVELS + 4, 4), :]
    flat[pl.ds(32, 16), :] = scale * jnp.concatenate([theirs] * 4, axis=0) * y_both[16:32, :]
    columns = jnp.transpose(flat[...])[:LEVELS]
    spans = [pl.ds(i * LEVELS, LEVELS) for i in range(5)]
    even_adds, even_beyond = side_terms(state, [x_even[at, :] for at in spans], ~even_x)
    far_x = (place[0] % 16 == 0) | (place[0] % 16 == 15)
    odd_edge = [jnp.where(far_x, x_far[at, :], x_near[at, :]) for at in spans]
    odd_adds, odd_beyond = side_terms(state, odd_edge, even_x)
    end_sign = jnp.where(lane == 0, 0.1, jnp.where(lane == LANES - 1, -0.1, 0.0))
    whole = [[None] * ROWS for _ in range(4)]
    side_u = [None] * ROWS
    for x in range(ROWS):
        v = plane(state, 1, x)
        for f in range(4):
            slot = f * ROWS + x
            side = end_sign * v * turn(columns, -(2 * slot + 1), 1)
            if f == 0:
                side_u[x] = side
            value = inner[pl.ds(slot * LEVELS, LEVELS), :] + side
            if x == 0:
                value = value + jnp.where(even_x, odd_adds[f], even_adds[f])
            if x == ROWS - 1:
                value = value + jnp.where(even_x, even_adds[f], odd_adds[f])
            whole[f][x] = value
            star[pl.ds(slot * LEVELS, LEVELS), :] = value

    low_beyond = jnp.where(even_x, odd_beyond, even_beyond)
    high_beyond = jnp.where(even_x, even_beyond, odd_beyond)
    padded = [low_beyond] + whole[0] + [high_beyond]
    divergence = []
    up, down = by_level[pl.ds(LEVELS, LEVELS), :], by_level[pl.ds(2 * LEVELS, LEVELS), :]
    step = jnp.where(lane < 35, turn(columns, -1, 1), 0.0) - jnp.where(lane > 32, turn(columns, 1, 1), 0.0)
    lifted = turn(columns, -8, 1)
    step = 0.5 * step + up * turn(lifted, -1, 0) - down * turn(lifted, 1, 0)
    left_out = jnp.where((lane >= 32) & (lane < 36), step, 0.0)
    beside = jnp.where(low_side, 0.5, -0.5) * columns
    left_out = jnp.where((lane >= 36) & (lane < 40), beside, left_out)
    left_out = jnp.where(lane == 40, -0.5 * turn(columns, 5, 1), left_out)
    left_out = jnp.where(lane == 41, 0.5 * turn(columns, 9, 1), left_out)
    left_out = turn(left_out, OTHER - 32, 1)
    extra = [left_out - 0.5 * side_u[ROWS - 1], left_out + 0.5 * side_u[0]]
    for x in range(ROWS):
        v, w = whole[1][x], whole[2][x]
        upright = up * turn(w, -1, 0) - down * turn(w, 1, 0)
        divergence.append(0.5 * (padded[x + 2] - padded[x]) + 0.5 * north_difference(v) + upright)
        low, high = LOW + x // 2, HIGH + x // 2
        value = jnp.where(lane == low, 0.5 * turn(v, low, 1), extra[x % 2])
        extra[x % 2] = jnp.where(lane == high, -0.5 * turn(v, high + 1, 1), value)
    pieces = [divergence[0], divergence[2], extra[0], divergence[1], divergence[3], extra[1]]
    modal = dot3(parts(forward[...]), parts(jnp.concatenate(pieces, axis=1)))
    for i in range(6):
        message[pl.ds(i, LEVELS, stride=6), :] = modal[:, i * LANES : (i + 1) * LANES]


def decay(rate, square):
    lam = rate + square
    root = jnp.sqrt(lam * (1.0 + lam))
    inverse = 1.0 + 2.0 * lam + 2.0 * root
    return root, inverse, 1.0 / inverse


def squarings(rho, count):
    powers = [rho]
    for _ in range(count):
        powers.append(powers[-1] * powers[-1])
    return powers


def lane_powers(powers, exponent):
    product = None
    for bit in range(6):
        factor = jnp.where((exponent & (1 << bit)) != 0, powers[bit], 1.0)
        product = factor if product is None else product * factor
    return product


def shifted(values, shift):
    size = values.shape[0]
    if shift % 8 == 0:
        zeros = jnp.zeros((abs(shift), values.shape[1]), F32)
        if shift > 0:
            return jnp.concatenate([zeros, values[:-shift]], axis=0)
        return jnp.concatenate([values[-shift:], zeros], axis=0)
    row = row_of(values.shape)
    inside = row >= shift if shift > 0 else row < size + shift
    return jnp.where(inside, turn(values, shift, 0), 0.0)


def by_parity(even, odd):
    shape = (8, even.shape[1])
    tile = jnp.where((row_of(shape) & 1) != 0, jnp.broadcast_to(odd, shape), jnp.broadcast_to(even, shape))
    return jnp.concatenate([tile] * (LANES // 8), axis=0)


def halves(values):
    return jnp.concatenate([values, values], axis=1)


def solve_kernel(received, basis_high, basis_low, by_row, by_wave, local, moments):
    place = position()
    blocks = received.shape[0] // 6
    lane = lane_of((blocks, LANES))
    ends = (lane == 0) | (lane == LANES - 1)
    even = place[1] < 4
    parity = jnp.where(even, 0, 1)
    low_side = place[1] % 4 == 0
    edge = jnp.where(low_side, 0, LANES - 1)
    within = jnp.where(low_side, 1, LANES - 2)
    row = row_of((blocks, LANES))
    inside, outside = [], [jnp.zeros((blocks, LANES), F32)] * 2
    for h in range(2):
        first, second, extra = (received[pl.ds(3 * h + j, blocks, stride=6), :] for j in range(3))
        first = first + jnp.where(ends & even, turn(extra, 1, 0), 0.0)
        second = second + jnp.where(ends & ~even, turn(extra, -1, 0), 0.0)
        other = jnp.where(row % 16 == 0, turn(extra, -1, 0), jnp.where(row % 16 == 15, turn(extra, 1, 0), 0.0))
        value = lambda i: jnp.sum(jnp.where(lane == OTHER + i + parity, other, 0.0), axis=1, keepdims=True)
        beside = [value(4), value(6)]
        corner = jnp.broadcast_to(value(8), (blocks, LANES))
        first = first + jnp.where(lane == edge, value(0), jnp.where(lane == within, -beside[0], 0.0))
        second = second + jnp.where(lane == edge, value(2), jnp.where(lane == within, -beside[1], 0.0))
        first = first + jnp.where((lane == edge) & even, turn(corner, 1, 0), 0.0)
        second = second + jnp.where((lane == edge) & ~even, turn(corner, -1, 0), 0.0)
        inside.append(jnp.concatenate([first, second], axis=0))
        for r in range(2):
            for i, start in enumerate((HIGH, LOW)):
                at = 2 * h + i
                outside[r] = jnp.where(lane == at, turn(extra, at - start - r, 1), outside[r])
            at = 2 * h + jnp.where(low_side, 1, 0)
            outside[r] = outside[r] + jnp.where(lane == at, beside[r], 0.0)
    right = parts(jnp.concatenate(inside + [jnp.concatenate(outside, axis=0)], axis=1))
    first = (((0,), (0,)), ((), ()))
    dot = lambda a, b: lax.dot_general(a, b[...], first, preferred_element_type=F32)
    spectral = dot(right[0], basis_high) + (dot(right[0], basis_low) + dot(right[1], basis_high))
    source = jnp.concatenate([spectral[:LANES], spectral[LANES : 2 * LANES]], axis=1)
    ext = spectral[2 * LANES : 2 * LANES + 8]
    high = jnp.concatenate([ext[0:1], ext[2:3]], axis=1)
    low = jnp.concatenate([ext[1:2], ext[3:4]], axis=1)

    power = lambda i: by_row[pl.ds(8 * i, 1), :]
    ahead, behind = source, source
    for bit in range(6):
        ahead = ahead + power(bit) * shifted(ahead, 2 << bit)
        behind = behind + power(bit) * shifted(behind, -(2 << bit))
    border = halves(by_wave[pl.ds(2 * LANES, LANES), :]) * by_parity(high, low)
    local[...] = ahead + behind - source + border
    rho, r65 = power(0), power(7)
    across = [
        rho * ahead[LANES - 2 : LANES - 1] + high,
        rho * ahead[LANES - 1 :] + r65 * low,
        rho * behind[0:1] + r65 * high,
        rho * behind[1:2] + low,
    ]
    across = jnp.concatenate(across, axis=0)
    for j in range(4):
        moments[pl.ds(j * 4, 4), :] = across


def back_kernel(local, moments, basis_high, basis_low, by_row, by_wave, by_block, message):
    place = position()
    width = local.shape[1]
    blocks = basis_high.shape[0] // 2
    even = place[1] < 4
    mine = place[1] & 3
    carry = jnp.zeros((4, width), F32)
    own = jnp.zeros((4, width), F32)
    for j in range(4):
        theirs = moments[pl.ds(j * 4, 4), :]
        own = jnp.where(mine == j, theirs, own)
        swapped = jnp.concatenate([theirs[:, LANES:], theirs[:, :LANES]], axis=1)
        carry = carry + by_block[pl.ds(16 * j, 4), :] * theirs + by_block[pl.ds(16 * j + 8, 4), :] * swapped
    scale, by_r64, by_inverse = (by_block[pl.ds(64 + i, 1), :] for i in range(3))
    after = scale * own[0:1] + by_r64 * carry[0:1] + by_inverse * carry[2:3]
    before = scale * own[3:4] + by_r64 * carry[3:4] + by_inverse * carry[1:2]
    total = local[...] + halves(by_wave[pl.ds(0, LANES), :]) * by_parity(carry[0:1], carry[1:2])
    total = total + halves(by_wave[pl.ds(LANES, LANES), :]) * by_parity(carry[2:3], carry[3:4])
    total = total * scale
    pieces = [total[:, :LANES], total[:, LANES:]]
    for h in range(2):
        span = slice(h * LANES, (h + 1) * LANES)
        pieces += [after[:, span], before[:, span]]
    pieces.append(jnp.zeros((LANES - 4, LANES), F32))
    right = parts(jnp.concatenate(pieces, axis=0))
    last = (((1,), (1,)), ((), ()))
    dot = lambda a, b: lax.dot_general(a[...], b, last, preferred_element_type=F32)
    pressure = dot(basis_high, right[0]) + (dot(basis_high, right[1]) + dot(basis_low, right[0]))
    lane = lane_of((blocks, LANES))
    ends = (lane == 0) | (lane == LANES - 1)
    outside = [pressure[r * blocks : (r + 1) * blocks, 2 * LANES :] for r in range(2)]
    for h in range(2):
        span = slice(h * LANES, (h + 1) * LANES)
        first, second = pressure[:blocks, span], pressure[blocks:, span]
        extra = jnp.where(ends, jnp.where(even, turn(first, -1, 0), turn(second, 1, 0)), 0.0)
        for r in range(2):
            extra = jnp.where(lane == HIGH + r, turn(outside[r], HIGH + r - 2 * h, 1), extra)
            extra = jnp.where(lane == LOW + r, turn(outside[r], LOW + r - 1 - 2 * h, 1), extra)
        for j, value in enumerate((first, second, extra)):
            message[pl.ds(3 * h + j, blocks, stride=6), :] = value


def mend_kernel(star, message, state, relayed, forward, whole, middle, flat):
    place = position()
    both = far_both(place[0], place[1])
    whole[...] = star[...]
    for i, r in enumerate((1, 2)):
        middle[pl.ds(i * LEVELS, LEVELS), :] = message[pl.ds(3 * (r % 2) + r // 2, LEVELS, stride=6), :]

    @pl.when(both)
    def _():
        lane = lane_of((LEVELS, LANES))
        even_y = place[1] % 2 == 0
        far = relayed[16:32, :]
        flat[...] = jnp.zeros((LANES, LANES), F32)
        flat[pl.ds(0, 16, stride=2), :] = jnp.where(even_y, 0.0, far)
        flat[pl.ds(1, 16, stride=2), :] = jnp.where(even_y, far, 0.0)
        columns = jnp.transpose(flat[...])[:LEVELS]
        end_sign = jnp.where(lane == 0, 0.1, jnp.where(lane == LANES - 1, -0.1, 0.0))
        steps = []
        for x in range(ROWS):
            v = plane(state, 1, x)
            for f in range(4):
                slot = f * ROWS + x
                side = end_sign * v * turn(columns, -(2 * slot + 1), 1)
                at = pl.ds(slot * LEVELS, LEVELS)
                whole[at, :] = whole[at, :] + side
                if f == 1 and x in (1, 2):
                    steps.append(0.5 * north_difference(side))
        modal = dot3(parts(forward[...]), parts(jnp.concatenate(steps, axis=1)))
        for i in range(2):
            at = pl.ds(i * LEVELS, LEVELS)
            middle[at, :] = middle[at, :] + modal[:, i * LANES : (i + 1) * LANES]


def final_kernel(received, middle, star, back, by_level, out, held, sent_out):
    size = LEVELS * ROWS
    span = lambda i: pl.ds(i * size // 2, size // 2)
    copies = [pltpu.make_async_copy(held.at[span(i), :], out.at[span(i), :], sent_out.at[i]) for i in range(8)]
    some = LEVELS // 2

    def put(f, matrix, right):
        for half in range(2):
            if right is not None:
                changes = dot3(parts(matrix[half * some : (half + 1) * some]), right)
            for x in range(ROWS):
                value = star[pl.ds((f * ROWS + x) * LEVELS + half * some, some), :]
                if right is not None:
                    value = value - changes[:, x * LANES : (x + 1) * LANES]
                held[pl.ds(f * size + half * some * ROWS + x, some, stride=ROWS), :] = value
            copies[2 * f + half].start()

    put(3, None, None)
    lane = lane_of((LEVELS, LANES))
    row_at = lambda ref, r: ref[pl.ds(3 * (r % 2) + r // 2, LEVELS, stride=6), :]
    p = [row_at(received, r) for r in range(ROWS)]
    extra = [row_at(received, 4), row_at(received, 5)]
    low = [turn(extra[r % 2], -(LOW + r // 2), 1) for r in range(ROWS)]
    high = [turn(extra[r % 2], LANES - 1 - (HIGH + r // 2), 1) for r in range(ROWS)]
    four_rate = 4.0 * by_level[pl.ds(0, LEVELS), :]

    def next_row(r, opposite):
        here = p[r]
        divergence = middle[pl.ds((r - 1) * LEVELS, LEVELS), :]
        plus = jnp.where(lane < LANES - 2, turn(here, -2, 1), turn(high[r], -1, 1))
        minus = jnp.where(lane > 1, turn(here, 2, 1), turn(low[r], 1, 1))
        return (
            2.0 * here
            - opposite
            + four_rate * here
            + (2.0 * here - plus - minus)
            + 4.0 * divergence
        )

    ends = (lane == 0) | (lane == LANES - 1)
    before = jnp.where(ends, extra[1], next_row(1, p[3]))
    after = jnp.where(ends, extra[0], next_row(2, p[0]))
    padded = [before] + p + [after]
    matrix = back[...]
    joined = lambda values: parts(jnp.concatenate(values, axis=1))
    put(2, 0.5 * level_difference(matrix), joined(p))
    put(1, matrix, joined([0.5 * north_difference(p[x], low[x], high[x]) for x in range(ROWS)]))
    put(0, matrix, joined([0.5 * (padded[x + 2] - padded[x]) for x in range(ROWS)]))
    for copy in copies:
        copy.wait()


def call(kernel, shapes, args, name, scratch=(), cost=None, copies=0):
    vmem = pl.BlockSpec(memory_space=pltpu.VMEM)
    return pl.pallas_call(
        kernel,
        out_shape=[jax.ShapeDtypeStruct(s, F32) for s in shapes],
        in_specs=[vmem] * len(args),
        out_specs=[pl.BlockSpec(memory_space=pl.ANY) if copies else vmem] * len(shapes),
        scratch_shapes=[pltpu.VMEM(s, F32) for s in scratch]
        + ([pltpu.SemaphoreType.DMA((copies,))] if copies else []),
        compiler_params=pltpu.CompilerParams(vmem_limit_bytes=32 * 1024 * 1024),
        name=name,
        cost_estimate=cost,
    )(*args)


def swap(values, axis, odd):
    count = lax.axis_size(axis)
    pairs = []
    for i in range(odd, count + odd, 2):
        pairs += [(i % count, (i + 1) % count), ((i + 1) % count, i % count)]
    return lax.ppermute(values, axis, pairs)


def swap_odd_x(values, far):
    count = lax.axis_size("gx")
    pairs = []
    for i in range(1, count + 1, 2):
        one, two = i % count, (i + 1) % count
        if (one % 16 == 15) == far:
            pairs += [(one, two), (two, one)]
    return lax.ppermute(values, "gx", pairs)


def swap_odd_y(values, helping):
    count_x, count_y = lax.axis_size("gx"), lax.axis_size("gy")
    pairs = []
    for i in range(count_x):
        for j in range(1, count_y + 1, 2):
            one, two = j % count_y, (j + 1) % count_y
            if not far_both(i, one) and far_both(i ^ 1, one) == helping:
                pairs += [(i * count_y + one, i * count_y + two), (i * count_y + two, i * count_y + one)]
    return lax.ppermute(values, ("gx", "gy"), pairs)


def hand_over(values):
    count_x, count_y = lax.axis_size("gx"), lax.axis_size("gy")
    pairs = [
        ((i ^ 1) * count_y + j, i * count_y + j)
        for i in range(count_x)
        for j in range(count_y)
        if far_both(i, j)
    ]
    return lax.ppermute(values, ("gx", "gy"), pairs)


def exchange(values):
    count_x, count_y = lax.axis_size("gx"), lax.axis_size("gy")
    near = count_y // 2
    groups = [[i * count_y + h * near + y for i in range(count_x) for h in range(2)] for y in range(near)]
    shaped = values.reshape(2 * count_x, 1, values.size // (2 * count_x))
    moved = lax.all_to_all(
        shaped, ("gx", "gy"), 0, 0, tiled=True, axis_index_groups=groups
    )
    return moved.reshape(values.shape)


def on_device(
    model_state, density, layer_in, layer_bias, layer_out, mode_forward, mode_back, mode_rate
):
    blocks = lax.axis_size("gx")
    total_east = blocks * ROWS
    state = model_state.reshape(4 * LEVELS * ROWS, LANES)
    basis, square = east_tables(total_east // 2, blocks)
    basis_high, basis_low = split_table(np.ascontiguousarray(basis.T))
    square_row = np.ascontiguousarray(np.broadcast_to(np.concatenate([square, square]), (8, total_east)))

    planes, x_even, x_odd, y_even, y_odd = call(
        edges_kernel,
        [(16 * LEVELS, LANES), (5 * LEVELS + 16, LANES), (5 * LEVELS, LANES), (16, LANES), (16, LANES)],
        [state],
        "edges",
        scratch=[(LANES, LANES)],
    )
    got_x_even = swap(x_even, "gx", 0)
    got_x_far = swap_odd_x(x_odd, True)
    got_y_odd = swap_odd_y(y_odd, False)
    y_both = jnp.concatenate([y_odd, got_x_even[5 * LEVELS :]], axis=0)
    y_both, x_odd, y_even = lax.optimization_barrier((y_both, x_odd, y_even))
    got_y_both = swap_odd_y(y_both, True)
    got_x_near = swap_odd_x(x_odd, False)
    vectors = jnp.concatenate([mode_rate, density, layer_bias])[None, :]
    long = pl.CostEstimate(flops=10**10, transcendentals=0, bytes_accessed=2**24)
    by_level, by_row, by_wave, by_block = call(
        tables_kernel,
        [(3 * LEVELS, LANES), (72, total_east), (3 * LANES, LANES), (72, total_east)],
        [vectors, square_row],
        "tables",
        cost=long,
    )
    by_level, y_even = lax.optimization_barrier((by_level, y_even))
    got_y_even = swap(y_even, "gy", 0)
    (inner,) = call(
        inner_kernel,
        [(16 * LEVELS, LANES)],
        [planes, vectors, layer_in, layer_out],
        "inner",
        cost=None,
    )
    star, message = call(
        outer_kernel,
        [(16 * LEVELS, LANES), (blocks * 6, LANES)],
        [
            planes,
            inner,
            got_x_even,
            got_x_far,
            got_x_near,
            got_y_even,
            got_y_odd,
            got_y_both,
            by_level,
            mode_forward,
        ],
        "outer",
        scratch=[(LANES, LANES)],
    )
    message, got_y_both = lax.optimization_barrier((message, got_y_both))
    relayed = hand_over(got_y_both)
    modal = exchange(message)
    whole, middle = call(
        mend_kernel,
        [(16 * LEVELS, LANES), (2 * LEVELS, LANES)],
        [star, message, planes, relayed, mode_forward],
        "mend",
        scratch=[(LANES, LANES)],
    )
    modal, whole, middle = lax.optimization_barrier((modal, whole, middle))
    local, moments = call(
        solve_kernel,
        [(LANES, total_east), (16, total_east)],
        [modal, basis_high, basis_low, by_row, by_wave],
        "solve",
    )
    moments = lax.all_to_all(
        moments.reshape(4, 4, total_east),
        "gy",
        0,
        0,
        tiled=True,
        axis_index_groups=[[0, 1, 2, 3], [4, 5, 6, 7]],
    ).reshape(16, total_east)
    (reply,) = call(
        back_kernel,
        [(blocks * 6, LANES)],
        [local, moments, basis_high, basis_low, by_row, by_wave, by_block],
        "back",
    )
    pressure = exchange(reply)
    (out,) = call(
        final_kernel,
        [(4 * LEVELS * ROWS, LANES)],
        [pressure, middle, whole, mode_back, by_level],
        "final",
        scratch=[(4 * LEVELS * ROWS, LANES)],
        copies=8,
    )
    return out.reshape(model_state.shape)


def solution(mesh):
    return jax.shard_map(
        on_device,
        mesh=mesh,
        in_specs=(P(None, None, "gx", "gy"), P(), P(), P(), P(), P(), P(), P()),
        out_specs=P(None, None, "gx", "gy"),
        check_vma=False,
    )
```

```python
import math

import jax
import jax.numpy as jnp
import ml_dtypes
import numpy as np
from jax import lax
from jax.experimental import pallas as pl
from jax.experimental.pallas import tpu as pltpu
from jax.sharding import PartitionSpec as P

F32 = jnp.float32
BF16 = jnp.bfloat16
LEVELS = 64
ROWS = 4
LANES = 128
LOW = 16
HIGH = 32
OTHER = 48


def split_table(table):
    high = table.astype(np.float32).astype(ml_dtypes.bfloat16)
    low = (table - high.astype(np.float64)).astype(np.float32).astype(ml_dtypes.bfloat16)
    return high, low


def east_tables(total, blocks):
    rows = total // blocks
    x = (np.arange(rows)[:, None] + rows * np.arange(blocks)[None, :]).reshape(-1)
    k = np.arange(total)
    angle = 2.0 * math.pi * ((k[:, None] * x[None, :]) % total) / total
    basis = np.where((k <= total // 2)[:, None], np.cos(angle), np.sin(angle))
    scale = np.where((k == 0) | (k == total // 2), 1.0, math.sqrt(2.0)) / math.sqrt(total)
    basis = basis * scale[:, None]
    square = np.sin(math.pi * k / total) ** 2
    return basis, square.astype(np.float32)


def position():
    return lax.axis_index("gx"), lax.axis_index("gy")


def lane_of(shape):
    return lax.broadcasted_iota(jnp.int32, shape, len(shape) - 1)


def row_of(shape):
    return lax.broadcasted_iota(jnp.int32, shape, 0)


def turn(values, shift, axis):
    size = values.shape[axis]
    return pltpu.roll(values, shift % size, axis) if shift % size else values


def parts(values):
    high = values.astype(BF16)
    return high, (values - high.astype(F32)).astype(BF16)


def dot3(left, right):
    dot = lambda a, b: jnp.dot(a, b, preferred_element_type=F32)
    return dot(left[0], right[0]) + (dot(left[0], right[1]) + dot(left[1], right[0]))


def level_difference(values):
    row = row_of(values.shape)
    last = values.shape[0] - 1
    upper = jnp.where(row < last, turn(values, -1, 0), 0.0)
    lower = jnp.where(row > 0, turn(values, 1, 0), 0.0)
    return upper - lower


def north_difference(values, low=0.0, high=0.0):
    lane = lane_of(values.shape)
    after = jnp.where(lane < LANES - 1, turn(values, -1, 1), high)
    before = jnp.where(lane > 0, turn(values, 1, 1), low)
    return after - before


def plane(ref, field, x):
    return ref[pl.ds((field * ROWS + x) * LEVELS, LEVELS), :]


def far_both(gx, gy):
    return ((gx % 16 == 0) | (gx % 16 == 15)) & ((gy % 4 == 0) | (gy % 4 == 3))


def edges_kernel(state, planes, x_even, x_odd, y_even, y_odd, flat):
    place = position()
    even_x = place[0] % 2 == 0
    even_y = place[1] % 2 == 0
    size = LEVELS * ROWS
    lane = lane_of((LEVELS, LANES))
    gathered = jnp.zeros((LEVELS, LANES), F32)
    for field in range(4):
        values = [state[pl.ds(field * size + x, LEVELS, stride=ROWS), :] for x in range(ROWS)]
        for x in range(ROWS):
            slot = field * ROWS + x
            planes[pl.ds(slot * LEVELS, LEVELS), :] = values[x]
            gathered = jnp.where(lane >> 1 == slot, turn(values[x], 2 * slot + 1, 1), gathered)
        for slot, depth in ((field, 0), (4, 1)) if field == 0 else ((field, 0),):
            span = pl.ds(slot * LEVELS, LEVELS)
            low, high = values[depth], values[ROWS - 1 - depth]
            x_even[span, :] = jnp.where(even_x, high, low)
            x_odd[span, :] = jnp.where(even_x, low, high)
    flat[...] = jnp.transpose(jnp.concatenate([gathered, jnp.zeros_like(gathered)], axis=0))
    high, low = flat[pl.ds(0, 16, stride=2), :], flat[pl.ds(1, 16, stride=2), :]
    y_even[0:16, :] = jnp.where(even_y, high, low)
    y_odd[...] = jnp.where(even_y, low, high)
    x_even[pl.ds(5 * LEVELS, 16), :] = jnp.where(even_y, low, high)


def column_of(row):
    return jnp.transpose(jnp.broadcast_to(row, (LANES, LANES)))


def inner_kernel(
    state,
    vectors,
    square_row,
    layer_in,
    layer_out,
    star,
    by_level,
    by_row,
    by_wave,
    by_block,
):
    place = position()
    fields = [[plane(state, f, x) for x in range(ROWS)] for f in range(4)]
    tall = column_of(vectors[:, :LANES])
    rate, density = tall[:LEVELS], tall[LEVELS:]
    row = row_of((LEVELS, LANES))
    by_level[pl.ds(0, LEVELS), :] = rate
    by_level[pl.ds(LEVELS, LEVELS), :] = jnp.where(
        row < LEVELS - 1, 0.5 * turn(density, -1, 0) / density, 0.0
    )
    by_level[pl.ds(2 * LEVELS, LEVELS), :] = jnp.where(row > 0, 0.5 * turn(density, 1, 0) / density, 0.0)
    own = by_level[pl.ds(place[0], 1), :]

    both = jnp.concatenate([own, own], axis=1)
    root, inverse, rho = decay(both, square_row[...])
    powers = squarings(rho, 6)
    for i, value in enumerate(powers + [powers[6] * rho, -1.0 / root]):
        by_row[pl.ds(8 * i, 8), :] = value
    half = row_of((LANES, LANES)) >> 1
    odd = (row_of((LANES, LANES)) & 1) != 0
    narrow = [jnp.broadcast_to(value[0:1, :LANES], (LANES, LANES)) for value in powers[:6]]
    rising = lane_powers(narrow, half)
    falling = lane_powers(narrow, 63 - half)
    by_wave[pl.ds(0, LANES), :] = rising
    by_wave[pl.ds(LANES, LANES), :] = falling
    by_wave[pl.ds(2 * LANES, LANES), :] = narrow[0] * jnp.where(odd, rising, falling)

    r64 = powers[6]
    r128 = r64 * r64
    r256 = r128 * r128
    images = 1.0 / (1.0 - r256 * r256)
    mine = place[1] & 3
    row = row_of(rho.shape)
    for j in range(4):
        for i, offset in enumerate((-1, 3)):
            exponent = jnp.where(row < 2, (mine - j + offset) & 7, (j - mine + offset) & 7)
            weight = jnp.where((exponent & 1) != 0, r64, 1.0)
            weight = weight * jnp.where((exponent & 2) != 0, r128, 1.0)
            weight = weight * jnp.where((exponent & 4) != 0, r256, 1.0)
            by_block[pl.ds((2 * j + i) * 8, 8), :] = weight * images
    scale = -1.0 / root
    by_block[pl.ds(64, 8), :] = jnp.where(row == 0, scale, jnp.where(row == 1, scale * r64, scale * inverse))

    for x in range(ROWS):
        u, v, w, th = (fields[f][x] for f in range(4))
        for f in range(4):
            here = fields[f][x]
            change = v * north_difference(here) + w * level_difference(here)
            if x == 0:
                change = change + u * fields[f][1]
            elif x == ROWS - 1:
                change = change - u * fields[f][x - 1]
            else:
                change = change + u * (fields[f][x + 1] - fields[f][x - 1])
            value = here - 0.1 * change
            if f == 2:
                value = value + 0.1 * th
            star[pl.ds((f * ROWS + x) * LEVELS, LEVELS), :] = value

    columns = jnp.concatenate(
        [jnp.concatenate([fields[f][x] for f in range(4)], axis=0).astype(BF16) for x in range(ROWS)],
        axis=1,
    )
    first = (((0,), (0,)), ((), ()))
    shift = [column_of(vectors[:, i * LANES : (i + 1) * LANES]) for i in (1, 2)]
    shift = jnp.concatenate(shift, axis=0)
    before = lax.dot_general(layer_in[...], columns, first, preferred_element_type=F32)
    before = before + jnp.concatenate([shift] * ROWS, axis=1)
    hidden = (before * (1.0 / (1.0 + jnp.exp(-before)))).astype(BF16)
    forcing = lax.dot_general(layer_out[...], hidden, first, preferred_element_type=F32)
    for x in range(ROWS):
        span = slice(x * LANES, (x + 1) * LANES)
        for f, part in ((2, forcing[LEVELS:, span]), (3, forcing[:LEVELS, span])):
            at = pl.ds((f * ROWS + x) * LEVELS, LEVELS)
            star[at, :] = star[at, :] + 0.2 * part


def side_terms(state, edge, low):
    u, v, w, _, second = edge
    own = jnp.where(low, plane(state, 0, 0), plane(state, 0, ROWS - 1))
    sign = jnp.where(low, 0.1, -0.1)
    adds = [sign * own * value for value in edge[:4]]
    along = u * (own - second)
    beyond = u - (sign * along + 0.1 * (v * north_difference(u) + w * level_difference(u)))
    return adds, beyond


def outer_kernel(
    state,
    inner,
    x_even,
    x_far,
    x_near,
    y_even,
    y_odd,
    y_both,
    by_level,
    forward,
    star,
    message,
    flat,
):
    place = position()
    even_x = place[0] % 2 == 0
    even_y = place[1] % 2 == 0
    shape = (LEVELS, LANES)
    lane = lane_of(shape)

    helping = far_both(place[0] ^ 1, place[1])
    other = jnp.where(helping, y_both[0:16, :], y_odd[...])
    other = jnp.where(far_both(place[0], place[1]), 0.0, other)
    flat[...] = jnp.zeros((LANES, LANES), F32)
    flat[pl.ds(0, 16, stride=2), :] = jnp.where(even_y, y_even[0:16, :], other)
    flat[pl.ds(1, 16, stride=2), :] = jnp.where(even_y, other, y_even[0:16, :])
    low_side = place[1] % 4 == 0
    scale = jnp.where(low_side, 0.1, -0.1) * jnp.where(helping, 1.0, 0.0)
    theirs = x_even[pl.ds(5 * LEVELS + 4, 4), :]
    flat[pl.ds(32, 16), :] = scale * jnp.concatenate([theirs] * 4, axis=0) * y_both[16:32, :]
    columns = jnp.transpose(flat[...])[:LEVELS]
    spans = [pl.ds(i * LEVELS, LEVELS) for i in range(5)]
    even_adds, even_beyond = side_terms(state, [x_even[at, :] for at in spans], ~even_x)
    far_x = (place[0] % 16 == 0) | (place[0] % 16 == 15)
    odd_edge = [jnp.where(far_x, x_far[at, :], x_near[at, :]) for at in spans]
    odd_adds, odd_beyond = side_terms(state, odd_edge, even_x)
    end_sign = jnp.where(lane == 0, 0.1, jnp.where(lane == LANES - 1, -0.1, 0.0))
    whole = [[None] * ROWS for _ in range(4)]
    side_u = [None] * ROWS
    for x in range(ROWS):
        v = plane(state, 1, x)
        for f in range(4):
            slot = f * ROWS + x
            side = end_sign * v * turn(columns, -(2 * slot + 1), 1)
            if f == 0:
                side_u[x] = side
            value = inner[pl.ds(slot * LEVELS, LEVELS), :] + side
            if x == 0:
                value = value + jnp.where(even_x, odd_adds[f], even_adds[f])
            if x == ROWS - 1:
                value = value + jnp.where(even_x, even_adds[f], odd_adds[f])
            whole[f][x] = value
            star[pl.ds(slot * LEVELS, LEVELS), :] = value

    low_beyond = jnp.where(even_x, odd_beyond, even_beyond)
    high_beyond = jnp.where(even_x, even_beyond, odd_beyond)
    padded = [low_beyond] + whole[0] + [high_beyond]
    divergence = []
    up, down = by_level[pl.ds(LEVELS, LEVELS), :], by_level[pl.ds(2 * LEVELS, LEVELS), :]
    step = jnp.where(lane < 35, turn(columns, -1, 1), 0.0) - jnp.where(lane > 32, turn(columns, 1, 1), 0.0)
    lifted = turn(columns, -8, 1)
    step = 0.5 * step + up * turn(lifted, -1, 0) - down * turn(lifted, 1, 0)
    left_out = jnp.where((lane >= 32) & (lane < 36), step, 0.0)
    beside = jnp.where(low_side, 0.5, -0.5) * columns
    left_out = jnp.where((lane >= 36) & (lane < 40), beside, left_out)
    left_out = jnp.where(lane == 40, -0.5 * turn(columns, 5, 1), left_out)
    left_out = jnp.where(lane == 41, 0.5 * turn(columns, 9, 1), left_out)
    left_out = turn(left_out, OTHER - 32, 1)
    extra = [left_out - 0.5 * side_u[ROWS - 1], left_out + 0.5 * side_u[0]]
    for x in range(ROWS):
        v, w = whole[1][x], whole[2][x]
        upright = up * turn(w, -1, 0) - down * turn(w, 1, 0)
        divergence.append(0.5 * (padded[x + 2] - padded[x]) + 0.5 * north_difference(v) + upright)
        low, high = LOW + x // 2, HIGH + x // 2
        value = jnp.where(lane == low, 0.5 * turn(v, low, 1), extra[x % 2])
        extra[x % 2] = jnp.where(lane == high, -0.5 * turn(v, high + 1, 1), value)
    pieces = [divergence[0], divergence[2], extra[0], divergence[1], divergence[3], extra[1]]
    modal = dot3(parts(forward[...]), parts(jnp.concatenate(pieces, axis=1)))
    for i in range(6):
        message[pl.ds(i, LEVELS, stride=6), :] = modal[:, i * LANES : (i + 1) * LANES]


def decay(rate, square):
    lam = rate + square
    root = jnp.sqrt(lam * (1.0 + lam))
    inverse = 1.0 + 2.0 * lam + 2.0 * root
    return root, inverse, 1.0 / inverse


def squarings(rho, count):
    powers = [rho]
    for _ in range(count):
        powers.append(powers[-1] * powers[-1])
    return powers


def lane_powers(powers, exponent):
    product = None
    for bit in range(6):
        factor = jnp.where((exponent & (1 << bit)) != 0, powers[bit], 1.0)
        product = factor if product is None else product * factor
    return product


def shifted(values, shift):
    size = values.shape[0]
    if shift % 8 == 0:
        zeros = jnp.zeros((abs(shift), values.shape[1]), F32)
        if shift > 0:
            return jnp.concatenate([zeros, values[:-shift]], axis=0)
        return jnp.concatenate([values[-shift:], zeros], axis=0)
    row = row_of(values.shape)
    inside = row >= shift if shift > 0 else row < size + shift
    return jnp.where(inside, turn(values, shift, 0), 0.0)


def by_parity(even, odd):
    shape = (8, even.shape[1])
    tile = jnp.where((row_of(shape) & 1) != 0, jnp.broadcast_to(odd, shape), jnp.broadcast_to(even, shape))
    return jnp.concatenate([tile] * (LANES // 8), axis=0)


def halves(values):
    return jnp.concatenate([values, values], axis=1)


def solve_kernel(received, basis_high, basis_low, by_row, by_wave, local, moments):
    place = position()
    blocks = received.shape[0] // 6
    lane = lane_of((blocks, LANES))
    ends = (lane == 0) | (lane == LANES - 1)
    even = place[1] < 4
    parity = jnp.where(even, 0, 1)
    low_side = place[1] % 4 == 0
    edge = jnp.where(low_side, 0, LANES - 1)
    within = jnp.where(low_side, 1, LANES - 2)
    row = row_of((blocks, LANES))
    inside, outside = [], [jnp.zeros((blocks, LANES), F32)] * 2
    for h in range(2):
        first, second, extra = (received[pl.ds(3 * h + j, blocks, stride=6), :] for j in range(3))
        first = first + jnp.where(ends & even, turn(extra, 1, 0), 0.0)
        second = second + jnp.where(ends & ~even, turn(extra, -1, 0), 0.0)
        other = jnp.where(row % 16 == 0, turn(extra, -1, 0), jnp.where(row % 16 == 15, turn(extra, 1, 0), 0.0))
        value = lambda i: jnp.sum(jnp.where(lane == OTHER + i + parity, other, 0.0), axis=1, keepdims=True)
        beside = [value(4), value(6)]
        corner = jnp.broadcast_to(value(8), (blocks, LANES))
        first = first + jnp.where(lane == edge, value(0), jnp.where(lane == within, -beside[0], 0.0))
        second = second + jnp.where(lane == edge, value(2), jnp.where(lane == within, -beside[1], 0.0))
        first = first + jnp.where((lane == edge) & even, turn(corner, 1, 0), 0.0)
        second = second + jnp.where((lane == edge) & ~even, turn(corner, -1, 0), 0.0)
        inside.append(jnp.concatenate([first, second], axis=0))
        for r in range(2):
            for i, start in enumerate((HIGH, LOW)):
                at = 2 * h + i
                outside[r] = jnp.where(lane == at, turn(extra, at - start - r, 1), outside[r])
            at = 2 * h + jnp.where(low_side, 1, 0)
            outside[r] = outside[r] + jnp.where(lane == at, beside[r], 0.0)
    right = parts(jnp.concatenate(inside + [jnp.concatenate(outside, axis=0)], axis=1))
    first = (((0,), (0,)), ((), ()))
    dot = lambda a, b: lax.dot_general(a, b[...], first, preferred_element_type=F32)
    spectral = dot(right[0], basis_high) + (dot(right[0], basis_low) + dot(right[1], basis_high))
    source = jnp.concatenate([spectral[:LANES], spectral[LANES : 2 * LANES]], axis=1)
    ext = spectral[2 * LANES : 2 * LANES + 8]
    high = jnp.concatenate([ext[0:1], ext[2:3]], axis=1)
    low = jnp.concatenate([ext[1:2], ext[3:4]], axis=1)

    power = lambda i: by_row[pl.ds(8 * i, 1), :]
    ahead, behind = source, source
    for bit in range(6):
        ahead = ahead + power(bit) * shifted(ahead, 2 << bit)
        behind = behind + power(bit) * shifted(behind, -(2 << bit))
    border = halves(by_wave[pl.ds(2 * LANES, LANES), :]) * by_parity(high, low)
    local[...] = ahead + behind - source + border
    rho, r65 = power(0), power(7)
    across = [
        rho * ahead[LANES - 2 : LANES - 1] + high,
        rho * ahead[LANES - 1 :] + r65 * low,
        rho * behind[0:1] + r65 * high,
        rho * behind[1:2] + low,
    ]
    across = jnp.concatenate(across, axis=0)
    for j in range(4):
        moments[pl.ds(j * 4, 4), :] = across


def back_kernel(local, moments, basis_high, basis_low, by_row, by_wave, by_block, message):
    place = position()
    width = local.shape[1]
    blocks = basis_high.shape[0] // 2
    even = place[1] < 4
    mine = place[1] & 3
    carry = jnp.zeros((4, width), F32)
    own = jnp.zeros((4, width), F32)
    for j in range(4):
        theirs = moments[pl.ds(j * 4, 4), :]
        own = jnp.where(mine == j, theirs, own)
        swapped = jnp.concatenate([theirs[:, LANES:], theirs[:, :LANES]], axis=1)
        carry = carry + by_block[pl.ds(16 * j, 4), :] * theirs + by_block[pl.ds(16 * j + 8, 4), :] * swapped
    scale, by_r64, by_inverse = (by_block[pl.ds(64 + i, 1), :] for i in range(3))
    after = scale * own[0:1] + by_r64 * carry[0:1] + by_inverse * carry[2:3]
    before = scale * own[3:4] + by_r64 * carry[3:4] + by_inverse * carry[1:2]
    total = local[...] + halves(by_wave[pl.ds(0, LANES), :]) * by_parity(carry[0:1], carry[1:2])
    total = total + halves(by_wave[pl.ds(LANES, LANES), :]) * by_parity(carry[2:3], carry[3:4])
    total = total * scale
    pieces = [total[:, :LANES], total[:, LANES:]]
    for h in range(2):
        span = slice(h * LANES, (h + 1) * LANES)
        pieces += [after[:, span], before[:, span]]
    pieces.append(jnp.zeros((LANES - 4, LANES), F32))
    right = parts(jnp.concatenate(pieces, axis=0))
    last = (((1,), (1,)), ((), ()))
    dot = lambda a, b: lax.dot_general(a[...], b, last, preferred_element_type=F32)
    pressure = dot(basis_high, right[0]) + (dot(basis_high, right[1]) + dot(basis_low, right[0]))
    lane = lane_of((blocks, LANES))
    ends = (lane == 0) | (lane == LANES - 1)
    outside = [pressure[r * blocks : (r + 1) * blocks, 2 * LANES :] for r in range(2)]
    for h in range(2):
        span = slice(h * LANES, (h + 1) * LANES)
        first, second = pressure[:blocks, span], pressure[blocks:, span]
        extra = jnp.where(ends, jnp.where(even, turn(first, -1, 0), turn(second, 1, 0)), 0.0)
        for r in range(2):
            extra = jnp.where(lane == HIGH + r, turn(outside[r], HIGH + r - 2 * h, 1), extra)
            extra = jnp.where(lane == LOW + r, turn(outside[r], LOW + r - 1 - 2 * h, 1), extra)
        for j, value in enumerate((first, second, extra)):
            message[pl.ds(3 * h + j, blocks, stride=6), :] = value


def mend_kernel(star, message, state, relayed, forward, whole, middle, flat):
    place = position()
    both = far_both(place[0], place[1])
    whole[...] = star[...]
    for i, r in enumerate((1, 2)):
        middle[pl.ds(i * LEVELS, LEVELS), :] = message[pl.ds(3 * (r % 2) + r // 2, LEVELS, stride=6), :]

    @pl.when(both)
    def _():
        lane = lane_of((LEVELS, LANES))
        even_y = place[1] % 2 == 0
        far = relayed[16:32, :]
        flat[...] = jnp.zeros((LANES, LANES), F32)
        flat[pl.ds(0, 16, stride=2), :] = jnp.where(even_y, 0.0, far)
        flat[pl.ds(1, 16, stride=2), :] = jnp.where(even_y, far, 0.0)
        columns = jnp.transpose(flat[...])[:LEVELS]
        end_sign = jnp.where(lane == 0, 0.1, jnp.where(lane == LANES - 1, -0.1, 0.0))
        steps = []
        for x in range(ROWS):
            v = plane(state, 1, x)
            for f in range(4):
                slot = f * ROWS + x
                side = end_sign * v * turn(columns, -(2 * slot + 1), 1)
                at = pl.ds(slot * LEVELS, LEVELS)
                whole[at, :] = whole[at, :] + side
                if f == 1 and x in (1, 2):
                    steps.append(0.5 * north_difference(side))
        modal = dot3(parts(forward[...]), parts(jnp.concatenate(steps, axis=1)))
        for i in range(2):
            at = pl.ds(i * LEVELS, LEVELS)
            middle[at, :] = middle[at, :] + modal[:, i * LANES : (i + 1) * LANES]


def final_kernel(received, middle, star, back, by_level, out, held, sent_out):
    size = LEVELS * ROWS
    span = lambda i: pl.ds(i * size // 2, size // 2)
    copies = [pltpu.make_async_copy(held.at[span(i), :], out.at[span(i), :], sent_out.at[i]) for i in range(8)]
    some = LEVELS // 2

    def put(f, matrix, right):
        for half in range(2):
            if right is not None:
                changes = dot3(parts(matrix[half * some : (half + 1) * some]), right)
            for x in range(ROWS):
                value = star[pl.ds((f * ROWS + x) * LEVELS + half * some, some), :]
                if right is not None:
                    value = value - changes[:, x * LANES : (x + 1) * LANES]
                held[pl.ds(f * size + half * some * ROWS + x, some, stride=ROWS), :] = value
            copies[2 * f + half].start()

    put(3, None, None)
    lane = lane_of((LEVELS, LANES))
    row_at = lambda ref, r: ref[pl.ds(3 * (r % 2) + r // 2, LEVELS, stride=6), :]
    p = [row_at(received, r) for r in range(ROWS)]
    extra = [row_at(received, 4), row_at(received, 5)]
    low = [turn(extra[r % 2], -(LOW + r // 2), 1) for r in range(ROWS)]
    high = [turn(extra[r % 2], LANES - 1 - (HIGH + r // 2), 1) for r in range(ROWS)]
    four_rate = 4.0 * by_level[pl.ds(0, LEVELS), :]

    def next_row(r, opposite):
        here = p[r]
        divergence = middle[pl.ds((r - 1) * LEVELS, LEVELS), :]
        plus = jnp.where(lane < LANES - 2, turn(here, -2, 1), turn(high[r], -1, 1))
        minus = jnp.where(lane > 1, turn(here, 2, 1), turn(low[r], 1, 1))
        return (
            2.0 * here
            - opposite
            + four_rate * here
            + (2.0 * here - plus - minus)
            + 4.0 * divergence
        )

    ends = (lane == 0) | (lane == LANES - 1)
    before = jnp.where(ends, extra[1], next_row(1, p[3]))
    after = jnp.where(ends, extra[0], next_row(2, p[0]))
    padded = [before] + p + [after]
    matrix = back[...]
    joined = lambda values: parts(jnp.concatenate(values, axis=1))
    put(2, 0.5 * level_difference(matrix), joined(p))
    put(1, matrix, joined([0.5 * north_difference(p[x], low[x], high[x]) for x in range(ROWS)]))
    put(0, matrix, joined([0.5 * (padded[x + 2] - padded[x]) for x in range(ROWS)]))
    for copy in copies:
        copy.wait()


def call(kernel, shapes, args, name, scratch=(), cost=None, copies=0):
    vmem = pl.BlockSpec(memory_space=pltpu.VMEM)
    return pl.pallas_call(
        kernel,
        out_shape=[jax.ShapeDtypeStruct(s, F32) for s in shapes],
        in_specs=[vmem] * len(args),
        out_specs=[pl.BlockSpec(memory_space=pl.ANY) if copies else vmem] * len(shapes),
        scratch_shapes=[pltpu.VMEM(s, F32) for s in scratch]
        + ([pltpu.SemaphoreType.DMA((copies,))] if copies else []),
        compiler_params=pltpu.CompilerParams(vmem_limit_bytes=32 * 1024 * 1024),
        name=name,
        cost_estimate=cost,
    )(*args)


def swap(values, axis, odd):
    count = lax.axis_size(axis)
    pairs = []
    for i in range(odd, count + odd, 2):
        pairs += [(i % count, (i + 1) % count), ((i + 1) % count, i % count)]
    return lax.ppermute(values, axis, pairs)


def swap_odd_x(values, far):
    count = lax.axis_size("gx")
    pairs = []
    for i in range(1, count + 1, 2):
        one, two = i % count, (i + 1) % count
        if (one % 16 == 15) == far:
            pairs += [(one, two), (two, one)]
    return lax.ppermute(values, "gx", pairs)


def swap_odd_y(values, helping):
    count_x, count_y = lax.axis_size("gx"), lax.axis_size("gy")
    pairs = []
    for i in range(count_x):
        for j in range(1, count_y + 1, 2):
            one, two = j % count_y, (j + 1) % count_y
            if not far_both(i, one) and far_both(i ^ 1, one) == helping:
                pairs += [(i * count_y + one, i * count_y + two), (i * count_y + two, i * count_y + one)]
    return lax.ppermute(values, ("gx", "gy"), pairs)


def hand_over(values):
    count_x, count_y = lax.axis_size("gx"), lax.axis_size("gy")
    pairs = [
        ((i ^ 1) * count_y + j, i * count_y + j)
        for i in range(count_x)
        for j in range(count_y)
        if far_both(i, j)
    ]
    return lax.ppermute(values, ("gx", "gy"), pairs)


def exchange(values):
    count_x, count_y = lax.axis_size("gx"), lax.axis_size("gy")
    near = count_y // 2
    groups = [[i * count_y + h * near + y for i in range(count_x) for h in range(2)] for y in range(near)]
    shaped = values.reshape(2 * count_x, 1, values.size // (2 * count_x))
    moved = lax.all_to_all(
        shaped, ("gx", "gy"), 0, 0, tiled=True, axis_index_groups=groups
    )
    return moved.reshape(values.shape)


def on_device(
    model_state, density, layer_in, layer_bias, layer_out, mode_forward, mode_back, mode_rate
):
    blocks = lax.axis_size("gx")
    total_east = blocks * ROWS
    state = model_state.reshape(4 * LEVELS * ROWS, LANES)
    basis, square = east_tables(total_east // 2, blocks)
    basis_high, basis_low = split_table(np.ascontiguousarray(basis.T))
    square_row = np.ascontiguousarray(np.broadcast_to(np.concatenate([square, square]), (8, total_east)))

    planes, x_even, x_odd, y_even, y_odd = call(
        edges_kernel,
        [(16 * LEVELS, LANES), (5 * LEVELS + 16, LANES), (5 * LEVELS, LANES), (16, LANES), (16, LANES)],
        [state],
        "edges",
        scratch=[(LANES, LANES)],
    )
    got_x_even = swap(x_even, "gx", 0)
    got_x_far = swap_odd_x(x_odd, True)
    got_y_odd = swap_odd_y(y_odd, False)
    y_both = jnp.concatenate([y_odd, got_x_even[5 * LEVELS :]], axis=0)
    y_both, x_odd, y_even = lax.optimization_barrier((y_both, x_odd, y_even))
    got_y_both = swap_odd_y(y_both, True)
    got_x_near = swap_odd_x(x_odd, False)
    inner, by_level, by_row, by_wave, by_block = call(
        inner_kernel,
        [(16 * LEVELS, LANES), (3 * LEVELS, LANES), (72, total_east), (3 * LANES, LANES), (72, total_east)],
        [
            planes,
            jnp.concatenate([mode_rate, density, layer_bias])[None, :],
            square_row,
            layer_in,
            layer_out,
        ],
        "inner",
        cost=pl.CostEstimate(flops=10**10, transcendentals=0, bytes_accessed=2**24),
    )
    inner, y_even = lax.optimization_barrier((inner, y_even))
    got_y_even = swap(y_even, "gy", 0)
    star, message = call(
        outer_kernel,
        [(16 * LEVELS, LANES), (blocks * 6, LANES)],
        [
            planes,
            inner,
            got_x_even,
            got_x_far,
            got_x_near,
            got_y_even,
            got_y_odd,
            got_y_both,
            by_level,
            mode_forward,
        ],
        "outer",
        scratch=[(LANES, LANES)],
    )
    message, got_y_both = lax.optimization_barrier((message, got_y_both))
    relayed = hand_over(got_y_both)
    modal = exchange(message)
    whole, middle = call(
        mend_kernel,
        [(16 * LEVELS, LANES), (2 * LEVELS, LANES)],
        [star, message, planes, relayed, mode_forward],
        "mend",
        scratch=[(LANES, LANES)],
    )
    modal, whole, middle = lax.optimization_barrier((modal, whole, middle))
    local, moments = call(
        solve_kernel,
        [(LANES, total_east), (16, total_east)],
        [modal, basis_high, basis_low, by_row, by_wave],
        "solve",
    )
    moments = lax.all_to_all(
        moments.reshape(4, 4, total_east),
        "gy",
        0,
        0,
        tiled=True,
        axis_index_groups=[[0, 1, 2, 3], [4, 5, 6, 7]],
    ).reshape(16, total_east)
    (reply,) = call(
        back_kernel,
        [(blocks * 6, LANES)],
        [local, moments, basis_high, basis_low, by_row, by_wave, by_block],
        "back",
    )
    pressure = exchange(reply)
    (out,) = call(
        final_kernel,
        [(4 * LEVELS * ROWS, LANES)],
        [pressure, middle, whole, mode_back, by_level],
        "final",
        scratch=[(4 * LEVELS * ROWS, LANES)],
        copies=8,
    )
    return out.reshape(model_state.shape)


def solution(mesh):
    return jax.shard_map(
        on_device,
        mesh=mesh,
        in_specs=(P(None, None, "gx", "gy"), P(), P(), P(), P(), P(), P(), P()),
        out_specs=P(None, None, "gx", "gy"),
        check_vma=False,
    )
```

```python
import math

import jax
import jax.numpy as jnp
import ml_dtypes
import numpy as np
from jax import lax
from jax.experimental import pallas as pl
from jax.experimental.pallas import tpu as pltpu
from jax.sharding import PartitionSpec as P

F32 = jnp.float32
BF16 = jnp.bfloat16
LEVELS = 64
ROWS = 4
LANES = 128
LOW = 16
HIGH = 32
OTHER = 48


def split_table(table):
    high = table.astype(np.float32).astype(ml_dtypes.bfloat16)
    low = (table - high.astype(np.float64)).astype(np.float32).astype(ml_dtypes.bfloat16)
    return high, low


def east_tables(total, blocks):
    rows = total // blocks
    x = (np.arange(rows)[:, None] + rows * np.arange(blocks)[None, :]).reshape(-1)
    k = np.arange(total)
    angle = 2.0 * math.pi * ((k[:, None] * x[None, :]) % total) / total
    basis = np.where((k <= total // 2)[:, None], np.cos(angle), np.sin(angle))
    scale = np.where((k == 0) | (k == total // 2), 1.0, math.sqrt(2.0)) / math.sqrt(total)
    basis = basis * scale[:, None]
    square = np.sin(math.pi * k / total) ** 2
    return basis, square.astype(np.float32)


def position():
    return lax.axis_index("gx"), lax.axis_index("gy")


def lane_of(shape):
    return lax.broadcasted_iota(jnp.int32, shape, len(shape) - 1)


def row_of(shape):
    return lax.broadcasted_iota(jnp.int32, shape, 0)


def turn(values, shift, axis):
    size = values.shape[axis]
    return pltpu.roll(values, shift % size, axis) if shift % size else values


def parts(values):
    high = values.astype(BF16)
    return high, (values - high.astype(F32)).astype(BF16)


def dot3(left, right):
    dot = lambda a, b: jnp.dot(a, b, preferred_element_type=F32)
    return dot(left[0], right[0]) + (dot(left[0], right[1]) + dot(left[1], right[0]))


def level_difference(values):
    row = row_of(values.shape)
    last = values.shape[0] - 1
    upper = jnp.where(row < last, turn(values, -1, 0), 0.0)
    lower = jnp.where(row > 0, turn(values, 1, 0), 0.0)
    return upper - lower


def north_difference(values, low=0.0, high=0.0):
    lane = lane_of(values.shape)
    after = jnp.where(lane < LANES - 1, turn(values, -1, 1), high)
    before = jnp.where(lane > 0, turn(values, 1, 1), low)
    return after - before


def plane(ref, field, x):
    return ref[pl.ds((field * ROWS + x) * LEVELS, LEVELS), :]


def far_both(gx, gy):
    return ((gx % 16 == 0) | (gx % 16 == 15)) & ((gy % 4 == 0) | (gy % 4 == 3))


def edges_kernel(state, planes, x_even, x_odd, y_even, y_odd, flat):
    place = position()
    even_x = place[0] % 2 == 0
    even_y = place[1] % 2 == 0
    size = LEVELS * ROWS
    lane = lane_of((LEVELS, LANES))
    gathered = jnp.zeros((LEVELS, LANES), F32)
    for field in range(4):
        values = [state[pl.ds(field * size + x, LEVELS, stride=ROWS), :] for x in range(ROWS)]
        for x in range(ROWS):
            slot = field * ROWS + x
            planes[pl.ds(slot * LEVELS, LEVELS), :] = values[x]
            gathered = jnp.where(lane >> 1 == slot, turn(values[x], 2 * slot + 1, 1), gathered)
        for slot, depth in ((field, 0), (4, 1)) if field == 0 else ((field, 0),):
            span = pl.ds(slot * LEVELS, LEVELS)
            low, high = values[depth], values[ROWS - 1 - depth]
            x_even[span, :] = jnp.where(even_x, high, low)
            x_odd[span, :] = jnp.where(even_x, low, high)
    flat[...] = jnp.transpose(jnp.concatenate([gathered, jnp.zeros_like(gathered)], axis=0))
    high, low = flat[pl.ds(0, 16, stride=2), :], flat[pl.ds(1, 16, stride=2), :]
    y_even[0:16, :] = jnp.where(even_y, high, low)
    y_odd[...] = jnp.where(even_y, low, high)
    x_even[pl.ds(5 * LEVELS, 16), :] = jnp.where(even_y, low, high)


def column_of(row):
    return jnp.transpose(jnp.broadcast_to(row, (LANES, LANES)))


def inner_kernel(
    state,
    vectors,
    square_row,
    layer_in,
    layer_out,
    star,
    by_level,
    by_row,
    by_wave,
    by_block,
):
    place = position()
    fields = [[plane(state, f, x) for x in range(ROWS)] for f in range(4)]
    tall = column_of(vectors[:, :LANES])
    rate, density = tall[:LEVELS], tall[LEVELS:]
    row = row_of((LEVELS, LANES))
    by_level[pl.ds(0, LEVELS), :] = rate
    by_level[pl.ds(LEVELS, LEVELS), :] = jnp.where(
        row < LEVELS - 1, 0.5 * turn(density, -1, 0) / density, 0.0
    )
    by_level[pl.ds(2 * LEVELS, LEVELS), :] = jnp.where(row > 0, 0.5 * turn(density, 1, 0) / density, 0.0)
    own = by_level[pl.ds(place[0], 1), :]

    both = jnp.concatenate([own, own], axis=1)
    root, inverse, rho = decay(both, square_row[...])
    powers = squarings(rho, 6)
    for i, value in enumerate(powers + [powers[6] * rho, -1.0 / root]):
        by_row[pl.ds(8 * i, 8), :] = value
    half = row_of((LANES, LANES)) >> 1
    odd = (row_of((LANES, LANES)) & 1) != 0
    narrow = [jnp.broadcast_to(value[0:1, :LANES], (LANES, LANES)) for value in powers[:6]]
    rising = lane_powers(narrow, half)
    falling = lane_powers(narrow, 63 - half)
    by_wave[pl.ds(0, LANES), :] = rising
    by_wave[pl.ds(LANES, LANES), :] = falling
    by_wave[pl.ds(2 * LANES, LANES), :] = narrow[0] * jnp.where(odd, rising, falling)

    r64 = powers[6]
    r128 = r64 * r64
    r256 = r128 * r128
    images = 1.0 / (1.0 - r256 * r256)
    mine = place[1] & 3
    row = row_of(rho.shape)
    for j in range(4):
        for i, offset in enumerate((-1, 3)):
            exponent = jnp.where(row < 2, (mine - j + offset) & 7, (j - mine + offset) & 7)
            weight = jnp.where((exponent & 1) != 0, r64, 1.0)
            weight = weight * jnp.where((exponent & 2) != 0, r128, 1.0)
            weight = weight * jnp.where((exponent & 4) != 0, r256, 1.0)
            by_block[pl.ds((2 * j + i) * 8, 8), :] = weight * images
    scale = -1.0 / root
    by_block[pl.ds(64, 8), :] = jnp.where(row == 0, scale, jnp.where(row == 1, scale * r64, scale * inverse))

    for x in range(ROWS):
        u, v, w, th = (fields[f][x] for f in range(4))
        for f in range(4):
            here = fields[f][x]
            change = v * north_difference(here) + w * level_difference(here)
            if x == 0:
                change = change + u * fields[f][1]
            elif x == ROWS - 1:
                change = change - u * fields[f][x - 1]
            else:
                change = change + u * (fields[f][x + 1] - fields[f][x - 1])
            value = here - 0.1 * change
            if f == 2:
                value = value + 0.1 * th
            star[pl.ds((f * ROWS + x) * LEVELS, LEVELS), :] = value

    columns = jnp.concatenate(
        [jnp.concatenate([fields[f][x] for f in range(4)], axis=0).astype(BF16) for x in range(ROWS)],
        axis=1,
    )
    first = (((0,), (0,)), ((), ()))
    shift = [column_of(vectors[:, i * LANES : (i + 1) * LANES]) for i in (1, 2)]
    shift = jnp.concatenate(shift, axis=0)
    before = lax.dot_general(layer_in[...], columns, first, preferred_element_type=F32)
    before = before + jnp.concatenate([shift] * ROWS, axis=1)
    hidden = (before * (1.0 / (1.0 + jnp.exp(-before)))).astype(BF16)
    forcing = lax.dot_general(layer_out[...], hidden, first, preferred_element_type=F32)
    for x in range(ROWS):
        span = slice(x * LANES, (x + 1) * LANES)
        for f, part in ((2, forcing[LEVELS:, span]), (3, forcing[:LEVELS, span])):
            at = pl.ds((f * ROWS + x) * LEVELS, LEVELS)
            star[at, :] = star[at, :] + 0.2 * part


def side_terms(state, edge, low):
    u, v, w, _, second = edge
    own = jnp.where(low, plane(state, 0, 0), plane(state, 0, ROWS - 1))
    sign = jnp.where(low, 0.1, -0.1)
    adds = [sign * own * value for value in edge[:4]]
    along = u * (own - second)
    beyond = u - (sign * along + 0.1 * (v * north_difference(u) + w * level_difference(u)))
    return adds, beyond


def outer_kernel(
    state,
    inner,
    x_even,
    x_far,
    x_near,
    y_even,
    y_odd,
    y_both,
    by_level,
    forward,
    star,
    message,
    flat,
):
    place = position()
    even_x = place[0] % 2 == 0
    even_y = place[1] % 2 == 0
    shape = (LEVELS, LANES)
    lane = lane_of(shape)

    helping = far_both(place[0] ^ 1, place[1])
    other = jnp.where(helping, y_both[0:16, :], y_odd[...])
    other = jnp.where(far_both(place[0], place[1]), 0.0, other)
    flat[...] = jnp.zeros((LANES, LANES), F32)
    flat[pl.ds(0, 16, stride=2), :] = jnp.where(even_y, y_even[0:16, :], other)
    flat[pl.ds(1, 16, stride=2), :] = jnp.where(even_y, other, y_even[0:16, :])
    low_side = place[1] % 4 == 0
    scale = jnp.where(low_side, 0.1, -0.1) * jnp.where(helping, 1.0, 0.0)
    theirs = x_even[pl.ds(5 * LEVELS + 4, 4), :]
    flat[pl.ds(32, 16), :] = scale * jnp.concatenate([theirs] * 4, axis=0) * y_both[16:32, :]
    columns = jnp.transpose(flat[...])[:LEVELS]
    spans = [pl.ds(i * LEVELS, LEVELS) for i in range(5)]
    even_adds, even_beyond = side_terms(state, [x_even[at, :] for at in spans], ~even_x)
    far_x = (place[0] % 16 == 0) | (place[0] % 16 == 15)
    odd_edge = [jnp.where(far_x, x_far[at, :], x_near[at, :]) for at in spans]
    odd_adds, odd_beyond = side_terms(state, odd_edge, even_x)
    end_sign = jnp.where(lane == 0, 0.1, jnp.where(lane == LANES - 1, -0.1, 0.0))
    whole = [[None] * ROWS for _ in range(4)]
    side_u = [None] * ROWS
    for x in range(ROWS):
        v = plane(state, 1, x)
        for f in range(4):
            slot = f * ROWS + x
            side = end_sign * v * turn(columns, -(2 * slot + 1), 1)
            if f == 0:
                side_u[x] = side
            value = inner[pl.ds(slot * LEVELS, LEVELS), :] + side
            if x == 0:
                value = value + jnp.where(even_x, odd_adds[f], even_adds[f])
            if x == ROWS - 1:
                value = value + jnp.where(even_x, even_adds[f], odd_adds[f])
            whole[f][x] = value
            star[pl.ds(slot * LEVELS, LEVELS), :] = value

    low_beyond = jnp.where(even_x, odd_beyond, even_beyond)
    high_beyond = jnp.where(even_x, even_beyond, odd_beyond)
    padded = [low_beyond] + whole[0] + [high_beyond]
    divergence = []
    up, down = by_level[pl.ds(LEVELS, LEVELS), :], by_level[pl.ds(2 * LEVELS, LEVELS), :]
    step = jnp.where(lane < 35, turn(columns, -1, 1), 0.0) - jnp.where(lane > 32, turn(columns, 1, 1), 0.0)
    lifted = turn(columns, -8, 1)
    step = 0.5 * step + up * turn(lifted, -1, 0) - down * turn(lifted, 1, 0)
    left_out = jnp.where((lane >= 32) & (lane < 36), step, 0.0)
    beside = jnp.where(low_side, 0.5, -0.5) * columns
    left_out = jnp.where((lane >= 36) & (lane < 40), beside, left_out)
    left_out = jnp.where(lane == 40, -0.5 * turn(columns, 5, 1), left_out)
    left_out = jnp.where(lane == 41, 0.5 * turn(columns, 9, 1), left_out)
    left_out = turn(left_out, OTHER - 32, 1)
    extra = [left_out - 0.5 * side_u[ROWS - 1], left_out + 0.5 * side_u[0]]
    for x in range(ROWS):
        v, w = whole[1][x], whole[2][x]
        upright = up * turn(w, -1, 0) - down * turn(w, 1, 0)
        divergence.append(0.5 * (padded[x + 2] - padded[x]) + 0.5 * north_difference(v) + upright)
        low, high = LOW + x // 2, HIGH + x // 2
        value = jnp.where(lane == low, 0.5 * turn(v, low, 1), extra[x % 2])
        extra[x % 2] = jnp.where(lane == high, -0.5 * turn(v, high + 1, 1), value)
    pieces = [divergence[0], divergence[2], extra[0], divergence[1], divergence[3], extra[1]]
    modal = dot3(parts(forward[...]), parts(jnp.concatenate(pieces, axis=1)))
    for i in range(6):
        message[pl.ds(i, LEVELS, stride=6), :] = modal[:, i * LANES : (i + 1) * LANES]


def decay(rate, square):
    lam = rate + square
    root = jnp.sqrt(lam * (1.0 + lam))
    inverse = 1.0 + 2.0 * lam + 2.0 * root
    return root, inverse, 1.0 / inverse


def squarings(rho, count):
    powers = [rho]
    for _ in range(count):
        powers.append(powers[-1] * powers[-1])
    return powers


def lane_powers(powers, exponent):
    product = None
    for bit in range(6):
        factor = jnp.where((exponent & (1 << bit)) != 0, powers[bit], 1.0)
        product = factor if product is None else product * factor
    return product


def shifted(values, shift):
    size = values.shape[0]
    if shift % 8 == 0:
        zeros = jnp.zeros((abs(shift), values.shape[1]), F32)
        if shift > 0:
            return jnp.concatenate([zeros, values[:-shift]], axis=0)
        return jnp.concatenate([values[-shift:], zeros], axis=0)
    row = row_of(values.shape)
    inside = row >= shift if shift > 0 else row < size + shift
    return jnp.where(inside, turn(values, shift, 0), 0.0)


def by_parity(even, odd):
    shape = (8, even.shape[1])
    tile = jnp.where((row_of(shape) & 1) != 0, jnp.broadcast_to(odd, shape), jnp.broadcast_to(even, shape))
    return jnp.concatenate([tile] * (LANES // 8), axis=0)


def halves(values):
    return jnp.concatenate([values, values], axis=1)


def solve_kernel(received, basis_high, basis_low, by_row, by_wave, local, moments):
    place = position()
    blocks = received.shape[0] // 6
    lane = lane_of((blocks, LANES))
    ends = (lane == 0) | (lane == LANES - 1)
    even = place[1] < 4
    parity = jnp.where(even, 0, 1)
    low_side = place[1] % 4 == 0
    edge = jnp.where(low_side, 0, LANES - 1)
    within = jnp.where(low_side, 1, LANES - 2)
    row = row_of((blocks, LANES))
    inside, outside = [], [jnp.zeros((blocks, LANES), F32)] * 2
    for h in range(2):
        first, second, extra = (received[pl.ds(3 * h + j, blocks, stride=6), :] for j in range(3))
        first = first + jnp.where(ends & even, turn(extra, 1, 0), 0.0)
        second = second + jnp.where(ends & ~even, turn(extra, -1, 0), 0.0)
        other = jnp.where(row % 16 == 0, turn(extra, -1, 0), jnp.where(row % 16 == 15, turn(extra, 1, 0), 0.0))
        value = lambda i: jnp.sum(jnp.where(lane == OTHER + i + parity, other, 0.0), axis=1, keepdims=True)
        beside = [value(4), value(6)]
        corner = jnp.broadcast_to(value(8), (blocks, LANES))
        first = first + jnp.where(lane == edge, value(0), jnp.where(lane == within, -beside[0], 0.0))
        second = second + jnp.where(lane == edge, value(2), jnp.where(lane == within, -beside[1], 0.0))
        first = first + jnp.where((lane == edge) & even, turn(corner, 1, 0), 0.0)
        second = second + jnp.where((lane == edge) & ~even, turn(corner, -1, 0), 0.0)
        inside.append(jnp.concatenate([first, second], axis=0))
        for r in range(2):
            for i, start in enumerate((HIGH, LOW)):
                at = 2 * h + i
                outside[r] = jnp.where(lane == at, turn(extra, at - start - r, 1), outside[r])
            at = 2 * h + jnp.where(low_side, 1, 0)
            outside[r] = outside[r] + jnp.where(lane == at, beside[r], 0.0)
    right = parts(jnp.concatenate(inside + [jnp.concatenate(outside, axis=0)], axis=1))
    first = (((0,), (0,)), ((), ()))
    dot = lambda a, b: lax.dot_general(a, b[...], first, preferred_element_type=F32)
    spectral = dot(right[0], basis_high) + (dot(right[0], basis_low) + dot(right[1], basis_high))
    source = jnp.concatenate([spectral[:LANES], spectral[LANES : 2 * LANES]], axis=1)
    ext = spectral[2 * LANES : 2 * LANES + 8]
    high = jnp.concatenate([ext[0:1], ext[2:3]], axis=1)
    low = jnp.concatenate([ext[1:2], ext[3:4]], axis=1)

    power = lambda i: by_row[pl.ds(8 * i, 1), :]
    ahead, behind = source, source
    for bit in range(6):
        ahead = ahead + power(bit) * shifted(ahead, 2 << bit)
        behind = behind + power(bit) * shifted(behind, -(2 << bit))
    border = halves(by_wave[pl.ds(2 * LANES, LANES), :]) * by_parity(high, low)
    local[...] = ahead + behind - source + border
    rho, r65 = power(0), power(7)
    across = [
        rho * ahead[LANES - 2 : LANES - 1] + high,
        rho * ahead[LANES - 1 :] + r65 * low,
        rho * behind[0:1] + r65 * high,
        rho * behind[1:2] + low,
    ]
    across = jnp.concatenate(across, axis=0)
    for j in range(4):
        moments[pl.ds(j * 4, 4), :] = across


def back_kernel(local, moments, basis_high, basis_low, by_row, by_wave, by_block, message):
    place = position()
    width = local.shape[1]
    blocks = basis_high.shape[0] // 2
    even = place[1] < 4
    mine = place[1] & 3
    carry = jnp.zeros((4, width), F32)
    own = jnp.zeros((4, width), F32)
    for j in range(4):
        theirs = moments[pl.ds(j * 4, 4), :]
        own = jnp.where(mine == j, theirs, own)
        swapped = jnp.concatenate([theirs[:, LANES:], theirs[:, :LANES]], axis=1)
        carry = carry + by_block[pl.ds(16 * j, 4), :] * theirs + by_block[pl.ds(16 * j + 8, 4), :] * swapped
    scale, by_r64, by_inverse = (by_block[pl.ds(64 + i, 1), :] for i in range(3))
    after = scale * own[0:1] + by_r64 * carry[0:1] + by_inverse * carry[2:3]
    before = scale * own[3:4] + by_r64 * carry[3:4] + by_inverse * carry[1:2]
    total = local[...] + halves(by_wave[pl.ds(0, LANES), :]) * by_parity(carry[0:1], carry[1:2])
    total = total + halves(by_wave[pl.ds(LANES, LANES), :]) * by_parity(carry[2:3], carry[3:4])
    total = total * scale
    pieces = [total[:, :LANES], total[:, LANES:]]
    for h in range(2):
        span = slice(h * LANES, (h + 1) * LANES)
        pieces += [after[:, span], before[:, span]]
    pieces.append(jnp.zeros((LANES - 4, LANES), F32))
    right = parts(jnp.concatenate(pieces, axis=0))
    last = (((1,), (1,)), ((), ()))
    dot = lambda a, b: lax.dot_general(a[...], b, last, preferred_element_type=F32)
    pressure = dot(basis_high, right[0]) + (dot(basis_high, right[1]) + dot(basis_low, right[0]))
    lane = lane_of((blocks, LANES))
    ends = (lane == 0) | (lane == LANES - 1)
    outside = [pressure[r * blocks : (r + 1) * blocks, 2 * LANES :] for r in range(2)]
    for h in range(2):
        span = slice(h * LANES, (h + 1) * LANES)
        first, second = pressure[:blocks, span], pressure[blocks:, span]
        extra = jnp.where(ends, jnp.where(even, turn(first, -1, 0), turn(second, 1, 0)), 0.0)
        for r in range(2):
            extra = jnp.where(lane == HIGH + r, turn(outside[r], HIGH + r - 2 * h, 1), extra)
            extra = jnp.where(lane == LOW + r, turn(outside[r], LOW + r - 1 - 2 * h, 1), extra)
        for j, value in enumerate((first, second, extra)):
            message[pl.ds(3 * h + j, blocks, stride=6), :] = value


def mend_kernel(star, message, state, relayed, forward, whole, middle, flat):
    place = position()
    both = far_both(place[0], place[1])
    whole[...] = star[...]
    for i, r in enumerate((1, 2)):
        middle[pl.ds(i * LEVELS, LEVELS), :] = message[pl.ds(3 * (r % 2) + r // 2, LEVELS, stride=6), :]

    @pl.when(both)
    def _():
        lane = lane_of((LEVELS, LANES))
        even_y = place[1] % 2 == 0
        far = relayed[16:32, :]
        flat[...] = jnp.zeros((LANES, LANES), F32)
        flat[pl.ds(0, 16, stride=2), :] = jnp.where(even_y, 0.0, far)
        flat[pl.ds(1, 16, stride=2), :] = jnp.where(even_y, far, 0.0)
        columns = jnp.transpose(flat[...])[:LEVELS]
        end_sign = jnp.where(lane == 0, 0.1, jnp.where(lane == LANES - 1, -0.1, 0.0))
        steps = []
        for x in range(ROWS):
            v = plane(state, 1, x)
            for f in range(4):
                slot = f * ROWS + x
                side = end_sign * v * turn(columns, -(2 * slot + 1), 1)
                at = pl.ds(slot * LEVELS, LEVELS)
                whole[at, :] = whole[at, :] + side
                if f == 1 and x in (1, 2):
                    steps.append(0.5 * north_difference(side))
        modal = dot3(parts(forward[...]), parts(jnp.concatenate(steps, axis=1)))
        for i in range(2):
            at = pl.ds(i * LEVELS, LEVELS)
            middle[at, :] = middle[at, :] + modal[:, i * LANES : (i + 1) * LANES]


def final_kernel(received, middle, star, back, by_level, out, held, sent_out):
    size = LEVELS * ROWS
    span = lambda i: pl.ds(i * size // 2, size // 2)
    copies = [pltpu.make_async_copy(held.at[span(i), :], out.at[span(i), :], sent_out.at[i]) for i in range(8)]
    some = LEVELS // 2

    def put(f, matrix, right):
        for half in range(2):
            if right is not None:
                changes = dot3(parts(matrix[half * some : (half + 1) * some]), right)
            for x in range(ROWS):
                value = star[pl.ds((f * ROWS + x) * LEVELS + half * some, some), :]
                if right is not None:
                    value = value - changes[:, x * LANES : (x + 1) * LANES]
                held[pl.ds(f * size + half * some * ROWS + x, some, stride=ROWS), :] = value
            copies[2 * f + half].start()

    put(3, None, None)
    lane = lane_of((LEVELS, LANES))
    row_at = lambda ref, r: ref[pl.ds(3 * (r % 2) + r // 2, LEVELS, stride=6), :]
    p = [row_at(received, r) for r in range(ROWS)]
    extra = [row_at(received, 4), row_at(received, 5)]
    low = [turn(extra[r % 2], -(LOW + r // 2), 1) for r in range(ROWS)]
    high = [turn(extra[r % 2], LANES - 1 - (HIGH + r // 2), 1) for r in range(ROWS)]
    four_rate = 4.0 * by_level[pl.ds(0, LEVELS), :]

    def next_row(r, opposite):
        here = p[r]
        divergence = middle[pl.ds((r - 1) * LEVELS, LEVELS), :]
        plus = jnp.where(lane < LANES - 2, turn(here, -2, 1), turn(high[r], -1, 1))
        minus = jnp.where(lane > 1, turn(here, 2, 1), turn(low[r], 1, 1))
        return (
            2.0 * here
            - opposite
            + four_rate * here
            + (2.0 * here - plus - minus)
            + 4.0 * divergence
        )

    ends = (lane == 0) | (lane == LANES - 1)
    before = jnp.where(ends, extra[1], next_row(1, p[3]))
    after = jnp.where(ends, extra[0], next_row(2, p[0]))
    padded = [before] + p + [after]
    matrix = back[...]
    joined = lambda values: parts(jnp.concatenate(values, axis=1))
    put(2, 0.5 * level_difference(matrix), joined(p))
    put(1, matrix, joined([0.5 * north_difference(p[x], low[x], high[x]) for x in range(ROWS)]))
    put(0, matrix, joined([0.5 * (padded[x + 2] - padded[x]) for x in range(ROWS)]))
    for copy in copies:
        copy.wait()


def call(kernel, shapes, args, name, scratch=(), cost=None, copies=0):
    vmem = pl.BlockSpec(memory_space=pltpu.VMEM)
    return pl.pallas_call(
        kernel,
        out_shape=[jax.ShapeDtypeStruct(s, F32) for s in shapes],
        in_specs=[vmem] * len(args),
        out_specs=[pl.BlockSpec(memory_space=pl.ANY) if copies else vmem] * len(shapes),
        scratch_shapes=[pltpu.VMEM(s, F32) for s in scratch]
        + ([pltpu.SemaphoreType.DMA((copies,))] if copies else []),
        compiler_params=pltpu.CompilerParams(vmem_limit_bytes=32 * 1024 * 1024),
        name=name,
        cost_estimate=cost,
    )(*args)


def swap(values, axis, odd):
    count = lax.axis_size(axis)
    pairs = []
    for i in range(odd, count + odd, 2):
        pairs += [(i % count, (i + 1) % count), ((i + 1) % count, i % count)]
    return lax.ppermute(values, axis, pairs)


def swap_odd_x(values, far):
    count = lax.axis_size("gx")
    pairs = []
    for i in range(1, count + 1, 2):
        one, two = i % count, (i + 1) % count
        if (one % 16 == 15) == far:
            pairs += [(one, two), (two, one)]
    return lax.ppermute(values, "gx", pairs)


def swap_odd_y(values, helping):
    count_x, count_y = lax.axis_size("gx"), lax.axis_size("gy")
    pairs = []
    for i in range(count_x):
        for j in range(1, count_y + 1, 2):
            one, two = j % count_y, (j + 1) % count_y
            if not far_both(i, one) and far_both(i ^ 1, one) == helping:
                pairs += [(i * count_y + one, i * count_y + two), (i * count_y + two, i * count_y + one)]
    return lax.ppermute(values, ("gx", "gy"), pairs)


def hand_over(values):
    count_x, count_y = lax.axis_size("gx"), lax.axis_size("gy")
    pairs = [
        ((i ^ 1) * count_y + j, i * count_y + j)
        for i in range(count_x)
        for j in range(count_y)
        if far_both(i, j)
    ]
    return lax.ppermute(values, ("gx", "gy"), pairs)


def exchange(values):
    count_x, count_y = lax.axis_size("gx"), lax.axis_size("gy")
    near = count_y // 2
    groups = [[i * count_y + h * near + y for i in range(count_x) for h in range(2)] for y in range(near)]
    shaped = values.reshape(2 * count_x, 1, values.size // (2 * count_x))
    moved = lax.all_to_all(
        shaped, ("gx", "gy"), 0, 0, tiled=True, axis_index_groups=groups
    )
    return moved.reshape(values.shape)


def on_device(
    model_state, density, layer_in, layer_bias, layer_out, mode_forward, mode_back, mode_rate
):
    blocks = lax.axis_size("gx")
    total_east = blocks * ROWS
    state = model_state.reshape(4 * LEVELS * ROWS, LANES)
    basis, square = east_tables(total_east // 2, blocks)
    basis_high, basis_low = split_table(np.ascontiguousarray(basis.T))
    square_row = np.ascontiguousarray(np.broadcast_to(np.concatenate([square, square]), (8, total_east)))

    planes, x_even, x_odd, y_even, y_odd = call(
        edges_kernel,
        [(16 * LEVELS, LANES), (5 * LEVELS + 16, LANES), (5 * LEVELS, LANES), (16, LANES), (16, LANES)],
        [state],
        "edges",
        scratch=[(LANES, LANES)],
    )
    got_x_even = swap(x_even, "gx", 0)
    got_x_far = swap_odd_x(x_odd, True)
    got_y_odd = swap_odd_y(y_odd, False)
    y_both = jnp.concatenate([y_odd, got_x_even[5 * LEVELS :]], axis=0)
    y_both, x_odd, y_even = lax.optimization_barrier((y_both, x_odd, y_even))
    got_y_both = swap_odd_y(y_both, True)
    got_x_near = swap_odd_x(x_odd, False)
    inner, by_level, by_row, by_wave, by_block = call(
        inner_kernel,
        [(16 * LEVELS, LANES), (3 * LEVELS, LANES), (72, total_east), (3 * LANES, LANES), (72, total_east)],
        [
            planes,
            jnp.concatenate([mode_rate, density, layer_bias])[None, :],
            square_row,
            layer_in,
            layer_out,
        ],
        "inner",
        cost=pl.CostEstimate(flops=10**10, transcendentals=0, bytes_accessed=2**24),
    )
    inner, y_even = lax.optimization_barrier((inner, y_even))
    got_y_even = swap(y_even, "gy", 0)
    star, message = call(
        outer_kernel,
        [(16 * LEVELS, LANES), (blocks * 6, LANES)],
        [
            planes,
            inner,
            got_x_even,
            got_x_far,
            got_x_near,
            got_y_even,
            got_y_odd,
            got_y_both,
            by_level,
            mode_forward,
        ],
        "outer",
        scratch=[(LANES, LANES)],
    )
    modal = exchange(message)
    local, moments = call(
        solve_kernel,
        [(LANES, total_east), (16, total_east)],
        [modal, basis_high, basis_low, by_row, by_wave],
        "solve",
    )
    moments = lax.all_to_all(
        moments.reshape(4, 4, total_east),
        "gy",
        0,
        0,
        tiled=True,
        axis_index_groups=[[0, 1, 2, 3], [4, 5, 6, 7]],
    ).reshape(16, total_east)
    (reply,) = call(
        back_kernel,
        [(blocks * 6, LANES)],
        [local, moments, basis_high, basis_low, by_row, by_wave, by_block],
        "back",
    )
    reply, got_y_both = lax.optimization_barrier((reply, got_y_both))
    relayed = hand_over(got_y_both)
    pressure = exchange(reply)
    whole, middle = call(
        mend_kernel,
        [(16 * LEVELS, LANES), (2 * LEVELS, LANES)],
        [star, message, planes, relayed, mode_forward],
        "mend",
        scratch=[(LANES, LANES)],
    )
    (out,) = call(
        final_kernel,
        [(4 * LEVELS * ROWS, LANES)],
        [pressure, middle, whole, mode_back, by_level],
        "final",
        scratch=[(4 * LEVELS * ROWS, LANES)],
        copies=8,
    )
    return out.reshape(model_state.shape)


def solution(mesh):
    return jax.shard_map(
        on_device,
        mesh=mesh,
        in_specs=(P(None, None, "gx", "gy"), P(), P(), P(), P(), P(), P(), P()),
        out_specs=P(None, None, "gx", "gy"),
        check_vma=False,
    )
```

```python
import math

import jax
import jax.numpy as jnp
import ml_dtypes
import numpy as np
from jax import lax
from jax.experimental import pallas as pl
from jax.experimental.pallas import tpu as pltpu
from jax.sharding import PartitionSpec as P

F32 = jnp.float32
BF16 = jnp.bfloat16
LEVELS = 64
ROWS = 4
LANES = 128
LOW = 16
HIGH = 32
OTHER = 48


def split_table(table):
    high = table.astype(np.float32).astype(ml_dtypes.bfloat16)
    low = (table - high.astype(np.float64)).astype(np.float32).astype(ml_dtypes.bfloat16)
    return high, low


def east_tables(total, blocks):
    rows = total // blocks
    x = (np.arange(rows)[:, None] + rows * np.arange(blocks)[None, :]).reshape(-1)
    k = np.arange(total)
    angle = 2.0 * math.pi * ((k[:, None] * x[None, :]) % total) / total
    basis = np.where((k <= total // 2)[:, None], np.cos(angle), np.sin(angle))
    scale = np.where((k == 0) | (k == total // 2), 1.0, math.sqrt(2.0)) / math.sqrt(total)
    basis = basis * scale[:, None]
    square = np.sin(math.pi * k / total) ** 2
    return basis, square.astype(np.float32)


def position():
    return lax.axis_index("gx"), lax.axis_index("gy")


def lane_of(shape):
    return lax.broadcasted_iota(jnp.int32, shape, len(shape) - 1)


def row_of(shape):
    return lax.broadcasted_iota(jnp.int32, shape, 0)


def turn(values, shift, axis):
    size = values.shape[axis]
    return pltpu.roll(values, shift % size, axis) if shift % size else values


def parts(values):
    high = values.astype(BF16)
    return high, (values - high.astype(F32)).astype(BF16)


def dot3(left, right):
    dot = lambda a, b: jnp.dot(a, b, preferred_element_type=F32)
    return dot(left[0], right[0]) + (dot(left[0], right[1]) + dot(left[1], right[0]))


def level_difference(values):
    row = row_of(values.shape)
    last = values.shape[0] - 1
    upper = jnp.where(row < last, turn(values, -1, 0), 0.0)
    lower = jnp.where(row > 0, turn(values, 1, 0), 0.0)
    return upper - lower


def north_difference(values, low=0.0, high=0.0):
    lane = lane_of(values.shape)
    after = jnp.where(lane < LANES - 1, turn(values, -1, 1), high)
    before = jnp.where(lane > 0, turn(values, 1, 1), low)
    return after - before


def plane(ref, field, x):
    return ref[pl.ds((field * ROWS + x) * LEVELS, LEVELS), :]


def far_both(gx, gy):
    return ((gx % 16 == 0) | (gx % 16 == 15)) & ((gy % 4 == 0) | (gy % 4 == 3))


def edges_kernel(state, planes, x_even, x_odd, y_even, y_odd, y_pair, flat):
    place = position()
    even_x = place[0] % 2 == 0
    even_y = place[1] % 2 == 0
    size = LEVELS * ROWS
    lane = lane_of((LEVELS, LANES))
    gathered = jnp.zeros((LEVELS, LANES), F32)
    for field in range(4):
        values = [state[pl.ds(field * size + x, LEVELS, stride=ROWS), :] for x in range(ROWS)]
        for x in range(ROWS):
            slot = field * ROWS + x
            planes[pl.ds(slot * LEVELS, LEVELS), :] = values[x]
            gathered = jnp.where(lane >> 1 == slot, turn(values[x], 2 * slot + 1, 1), gathered)
        for slot, depth in ((field, 0), (4, 1)) if field == 0 else ((field, 0),):
            span = pl.ds(slot * LEVELS, LEVELS)
            low, high = values[depth], values[ROWS - 1 - depth]
            x_even[span, :] = jnp.where(even_x, high, low)
            x_odd[span, :] = jnp.where(even_x, low, high)
    flat[...] = jnp.transpose(jnp.concatenate([gathered, jnp.zeros_like(gathered)], axis=0))
    high, low = flat[pl.ds(0, 16, stride=2), :], flat[pl.ds(1, 16, stride=2), :]
    y_even[0:16, :] = jnp.where(even_y, high, low)
    y_odd[...] = jnp.where(even_y, low, high)
    x_even[pl.ds(5 * LEVELS, 16), :] = jnp.where(even_y, low, high)
    y_pair[0:16, :] = jnp.where(even_y, low, high)
    y_pair[16:32, :] = jnp.zeros((16, LANES), F32)


def column_of(row):
    return jnp.transpose(jnp.broadcast_to(row, (LANES, LANES)))


def inner_kernel(
    state,
    vectors,
    square_row,
    layer_in,
    layer_out,
    star,
    by_level,
    by_row,
    by_wave,
    by_block,
):
    place = position()
    fields = [[plane(state, f, x) for x in range(ROWS)] for f in range(4)]
    tall = column_of(vectors[:, :LANES])
    rate, density = tall[:LEVELS], tall[LEVELS:]
    row = row_of((LEVELS, LANES))
    by_level[pl.ds(0, LEVELS), :] = rate
    by_level[pl.ds(LEVELS, LEVELS), :] = jnp.where(
        row < LEVELS - 1, 0.5 * turn(density, -1, 0) / density, 0.0
    )
    by_level[pl.ds(2 * LEVELS, LEVELS), :] = jnp.where(row > 0, 0.5 * turn(density, 1, 0) / density, 0.0)
    own = by_level[pl.ds(place[0], 1), :]

    both = jnp.concatenate([own, own], axis=1)
    root, inverse, rho = decay(both, square_row[...])
    powers = squarings(rho, 6)
    for i, value in enumerate(powers + [powers[6] * rho, -1.0 / root]):
        by_row[pl.ds(8 * i, 8), :] = value
    half = row_of((LANES, LANES)) >> 1
    odd = (row_of((LANES, LANES)) & 1) != 0
    narrow = [jnp.broadcast_to(value[0:1, :LANES], (LANES, LANES)) for value in powers[:6]]
    rising = lane_powers(narrow, half)
    falling = lane_powers(narrow, 63 - half)
    by_wave[pl.ds(0, LANES), :] = rising
    by_wave[pl.ds(LANES, LANES), :] = falling
    by_wave[pl.ds(2 * LANES, LANES), :] = narrow[0] * jnp.where(odd, rising, falling)

    r64 = powers[6]
    r128 = r64 * r64
    r256 = r128 * r128
    images = 1.0 / (1.0 - r256 * r256)
    mine = place[1] & 3
    row = row_of(rho.shape)
    for j in range(4):
        for i, offset in enumerate((-1, 3)):
            exponent = jnp.where(row < 2, (mine - j + offset) & 7, (j - mine + offset) & 7)
            weight = jnp.where((exponent & 1) != 0, r64, 1.0)
            weight = weight * jnp.where((exponent & 2) != 0, r128, 1.0)
            weight = weight * jnp.where((exponent & 4) != 0, r256, 1.0)
            by_block[pl.ds((2 * j + i) * 8, 8), :] = weight * images
    scale = -1.0 / root
    by_block[pl.ds(64, 8), :] = jnp.where(row == 0, scale, jnp.where(row == 1, scale * r64, scale * inverse))

    for x in range(ROWS):
        u, v, w, th = (fields[f][x] for f in range(4))
        for f in range(4):
            here = fields[f][x]
            change = v * north_difference(here) + w * level_difference(here)
            if x == 0:
                change = change + u * fields[f][1]
            elif x == ROWS - 1:
                change = change - u * fields[f][x - 1]
            else:
                change = change + u * (fields[f][x + 1] - fields[f][x - 1])
            value = here - 0.1 * change
            if f == 2:
                value = value + 0.1 * th
            star[pl.ds((f * ROWS + x) * LEVELS, LEVELS), :] = value

    columns = jnp.concatenate(
        [jnp.concatenate([fields[f][x] for f in range(4)], axis=0).astype(BF16) for x in range(ROWS)],
        axis=1,
    )
    first = (((0,), (0,)), ((), ()))
    shift = [column_of(vectors[:, i * LANES : (i + 1) * LANES]) for i in (1, 2)]
    shift = jnp.concatenate(shift, axis=0)
    before = lax.dot_general(layer_in[...], columns, first, preferred_element_type=F32)
    before = before + jnp.concatenate([shift] * ROWS, axis=1)
    hidden = (before * (1.0 / (1.0 + jnp.exp(-before)))).astype(BF16)
    forcing = lax.dot_general(layer_out[...], hidden, first, preferred_element_type=F32)
    for x in range(ROWS):
        span = slice(x * LANES, (x + 1) * LANES)
        for f, part in ((2, forcing[LEVELS:, span]), (3, forcing[:LEVELS, span])):
            at = pl.ds((f * ROWS + x) * LEVELS, LEVELS)
            star[at, :] = star[at, :] + 0.2 * part


def side_terms(state, edge, low):
    u, v, w, _, second = edge
    own = jnp.where(low, plane(state, 0, 0), plane(state, 0, ROWS - 1))
    sign = jnp.where(low, 0.1, -0.1)
    adds = [sign * own * value for value in edge[:4]]
    along = u * (own - second)
    beyond = u - (sign * along + 0.1 * (v * north_difference(u) + w * level_difference(u)))
    return adds, beyond


def outer_kernel(
    state,
    inner,
    x_even,
    x_far,
    x_near,
    y_even,
    y_odd,
    y_both,
    by_level,
    forward,
    star,
    message,
    flat,
):
    place = position()
    even_x = place[0] % 2 == 0
    even_y = place[1] % 2 == 0
    shape = (LEVELS, LANES)
    lane = lane_of(shape)

    helping = far_both(place[0] ^ 1, place[1])
    other = jnp.where(helping, y_both[0:16, :], y_odd[...])
    other = jnp.where(far_both(place[0], place[1]), 0.0, other)
    flat[...] = jnp.zeros((LANES, LANES), F32)
    flat[pl.ds(0, 16, stride=2), :] = jnp.where(even_y, y_even[0:16, :], other)
    flat[pl.ds(1, 16, stride=2), :] = jnp.where(even_y, other, y_even[0:16, :])
    low_side = place[1] % 4 == 0
    scale = jnp.where(low_side, 0.1, -0.1) * jnp.where(helping, 1.0, 0.0)
    theirs = x_even[pl.ds(5 * LEVELS + 4, 4), :]
    flat[pl.ds(32, 16), :] = scale * jnp.concatenate([theirs] * 4, axis=0) * y_both[16:32, :]
    columns = jnp.transpose(flat[...])[:LEVELS]
    spans = [pl.ds(i * LEVELS, LEVELS) for i in range(5)]
    even_adds, even_beyond = side_terms(state, [x_even[at, :] for at in spans], ~even_x)
    far_x = (place[0] % 16 == 0) | (place[0] % 16 == 15)
    odd_edge = [jnp.where(far_x, x_far[at, :], x_near[at, :]) for at in spans]
    odd_adds, odd_beyond = side_terms(state, odd_edge, even_x)
    end_sign = jnp.where(lane == 0, 0.1, jnp.where(lane == LANES - 1, -0.1, 0.0))
    whole = [[None] * ROWS for _ in range(4)]
    side_u = [None] * ROWS
    for x in range(ROWS):
        v = plane(state, 1, x)
        for f in range(4):
            slot = f * ROWS + x
            side = end_sign * v * turn(columns, -(2 * slot + 1), 1)
            if f == 0:
                side_u[x] = side
            value = inner[pl.ds(slot * LEVELS, LEVELS), :] + side
            if x == 0:
                value = value + jnp.where(even_x, odd_adds[f], even_adds[f])
            if x == ROWS - 1:
                value = value + jnp.where(even_x, even_adds[f], odd_adds[f])
            whole[f][x] = value
            star[pl.ds(slot * LEVELS, LEVELS), :] = value

    low_beyond = jnp.where(even_x, odd_beyond, even_beyond)
    high_beyond = jnp.where(even_x, even_beyond, odd_beyond)
    padded = [low_beyond] + whole[0] + [high_beyond]
    divergence = []
    up, down = by_level[pl.ds(LEVELS, LEVELS), :], by_level[pl.ds(2 * LEVELS, LEVELS), :]
    step = jnp.where(lane < 35, turn(columns, -1, 1), 0.0) - jnp.where(lane > 32, turn(columns, 1, 1), 0.0)
    lifted = turn(columns, -8, 1)
    step = 0.5 * step + up * turn(lifted, -1, 0) - down * turn(lifted, 1, 0)
    left_out = jnp.where((lane >= 32) & (lane < 36), step, 0.0)
    beside = jnp.where(low_side, 0.5, -0.5) * columns
    left_out = jnp.where((lane >= 36) & (lane < 40), beside, left_out)
    left_out = jnp.where(lane == 40, -0.5 * turn(columns, 5, 1), left_out)
    left_out = jnp.where(lane == 41, 0.5 * turn(columns, 9, 1), left_out)
    left_out = turn(left_out, OTHER - 32, 1)
    extra = [left_out - 0.5 * side_u[ROWS - 1], left_out + 0.5 * side_u[0]]
    for x in range(ROWS):
        v, w = whole[1][x], whole[2][x]
        upright = up * turn(w, -1, 0) - down * turn(w, 1, 0)
        divergence.append(0.5 * (padded[x + 2] - padded[x]) + 0.5 * north_difference(v) + upright)
        low, high = LOW + x // 2, HIGH + x // 2
        value = jnp.where(lane == low, 0.5 * turn(v, low, 1), extra[x % 2])
        extra[x % 2] = jnp.where(lane == high, -0.5 * turn(v, high + 1, 1), value)
    pieces = [divergence[0], divergence[2], extra[0], divergence[1], divergence[3], extra[1]]
    modal = dot3(parts(forward[...]), parts(jnp.concatenate(pieces, axis=1)))
    for i in range(6):
        message[pl.ds(i, LEVELS, stride=6), :] = modal[:, i * LANES : (i + 1) * LANES]


def decay(rate, square):
    lam = rate + square
    root = jnp.sqrt(lam * (1.0 + lam))
    inverse = 1.0 + 2.0 * lam + 2.0 * root
    return root, inverse, 1.0 / inverse


def squarings(rho, count):
    powers = [rho]
    for _ in range(count):
        powers.append(powers[-1] * powers[-1])
    return powers


def lane_powers(powers, exponent):
    product = None
    for bit in range(6):
        factor = jnp.where((exponent & (1 << bit)) != 0, powers[bit], 1.0)
        product = factor if product is None else product * factor
    return product


def shifted(values, shift):
    size = values.shape[0]
    if shift % 8 == 0:
        zeros = jnp.zeros((abs(shift), values.shape[1]), F32)
        if shift > 0:
            return jnp.concatenate([zeros, values[:-shift]], axis=0)
        return jnp.concatenate([values[-shift:], zeros], axis=0)
    row = row_of(values.shape)
    inside = row >= shift if shift > 0 else row < size + shift
    return jnp.where(inside, turn(values, shift, 0), 0.0)


def by_parity(even, odd):
    shape = (8, even.shape[1])
    tile = jnp.where((row_of(shape) & 1) != 0, jnp.broadcast_to(odd, shape), jnp.broadcast_to(even, shape))
    return jnp.concatenate([tile] * (LANES // 8), axis=0)


def halves(values):
    return jnp.concatenate([values, values], axis=1)


def solve_kernel(received, basis_high, basis_low, by_row, by_wave, local, moments):
    place = position()
    blocks = received.shape[0] // 6
    lane = lane_of((blocks, LANES))
    ends = (lane == 0) | (lane == LANES - 1)
    even = place[1] < 4
    parity = jnp.where(even, 0, 1)
    low_side = place[1] % 4 == 0
    edge = jnp.where(low_side, 0, LANES - 1)
    within = jnp.where(low_side, 1, LANES - 2)
    row = row_of((blocks, LANES))
    inside, outside = [], [jnp.zeros((blocks, LANES), F32)] * 2
    for h in range(2):
        first, second, extra = (received[pl.ds(3 * h + j, blocks, stride=6), :] for j in range(3))
        first = first + jnp.where(ends & even, turn(extra, 1, 0), 0.0)
        second = second + jnp.where(ends & ~even, turn(extra, -1, 0), 0.0)
        other = jnp.where(row % 16 == 0, turn(extra, -1, 0), jnp.where(row % 16 == 15, turn(extra, 1, 0), 0.0))
        value = lambda i: jnp.sum(jnp.where(lane == OTHER + i + parity, other, 0.0), axis=1, keepdims=True)
        beside = [value(4), value(6)]
        corner = jnp.broadcast_to(value(8), (blocks, LANES))
        first = first + jnp.where(lane == edge, value(0), jnp.where(lane == within, -beside[0], 0.0))
        second = second + jnp.where(lane == edge, value(2), jnp.where(lane == within, -beside[1], 0.0))
        first = first + jnp.where((lane == edge) & even, turn(corner, 1, 0), 0.0)
        second = second + jnp.where((lane == edge) & ~even, turn(corner, -1, 0), 0.0)
        inside.append(jnp.concatenate([first, second], axis=0))
        for r in range(2):
            for i, start in enumerate((HIGH, LOW)):
                at = 2 * h + i
                outside[r] = jnp.where(lane == at, turn(extra, at - start - r, 1), outside[r])
            at = 2 * h + jnp.where(low_side, 1, 0)
            outside[r] = outside[r] + jnp.where(lane == at, beside[r], 0.0)
    right = parts(jnp.concatenate(inside + [jnp.concatenate(outside, axis=0)], axis=1))
    first = (((0,), (0,)), ((), ()))
    dot = lambda a, b: lax.dot_general(a, b[...], first, preferred_element_type=F32)
    spectral = dot(right[0], basis_high) + (dot(right[0], basis_low) + dot(right[1], basis_high))
    source = jnp.concatenate([spectral[:LANES], spectral[LANES : 2 * LANES]], axis=1)
    ext = spectral[2 * LANES : 2 * LANES + 8]
    high = jnp.concatenate([ext[0:1], ext[2:3]], axis=1)
    low = jnp.concatenate([ext[1:2], ext[3:4]], axis=1)

    power = lambda i: by_row[pl.ds(8 * i, 1), :]
    ahead, behind = source, source
    for bit in range(6):
        ahead = ahead + power(bit) * shifted(ahead, 2 << bit)
        behind = behind + power(bit) * shifted(behind, -(2 << bit))
    border = halves(by_wave[pl.ds(2 * LANES, LANES), :]) * by_parity(high, low)
    local[...] = ahead + behind - source + border
    rho, r65 = power(0), power(7)
    across = [
        rho * ahead[LANES - 2 : LANES - 1] + high,
        rho * ahead[LANES - 1 :] + r65 * low,
        rho * behind[0:1] + r65 * high,
        rho * behind[1:2] + low,
    ]
    across = jnp.concatenate(across, axis=0)
    for j in range(4):
        moments[pl.ds(j * 4, 4), :] = across


def back_kernel(local, moments, basis_high, basis_low, by_row, by_wave, by_block, message):
    place = position()
    width = local.shape[1]
    blocks = basis_high.shape[0] // 2
    even = place[1] < 4
    mine = place[1] & 3
    carry = jnp.zeros((4, width), F32)
    own = jnp.zeros((4, width), F32)
    for j in range(4):
        theirs = moments[pl.ds(j * 4, 4), :]
        own = jnp.where(mine == j, theirs, own)
        swapped = jnp.concatenate([theirs[:, LANES:], theirs[:, :LANES]], axis=1)
        carry = carry + by_block[pl.ds(16 * j, 4), :] * theirs + by_block[pl.ds(16 * j + 8, 4), :] * swapped
    scale, by_r64, by_inverse = (by_block[pl.ds(64 + i, 1), :] for i in range(3))
    after = scale * own[0:1] + by_r64 * carry[0:1] + by_inverse * carry[2:3]
    before = scale * own[3:4] + by_r64 * carry[3:4] + by_inverse * carry[1:2]
    total = local[...] + halves(by_wave[pl.ds(0, LANES), :]) * by_parity(carry[0:1], carry[1:2])
    total = total + halves(by_wave[pl.ds(LANES, LANES), :]) * by_parity(carry[2:3], carry[3:4])
    total = total * scale
    pieces = [total[:, :LANES], total[:, LANES:]]
    for h in range(2):
        span = slice(h * LANES, (h + 1) * LANES)
        pieces += [after[:, span], before[:, span]]
    pieces.append(jnp.zeros((LANES - 4, LANES), F32))
    right = parts(jnp.concatenate(pieces, axis=0))
    last = (((1,), (1,)), ((), ()))
    dot = lambda a, b: lax.dot_general(a[...], b, last, preferred_element_type=F32)
    pressure = dot(basis_high, right[0]) + (dot(basis_high, right[1]) + dot(basis_low, right[0]))
    lane = lane_of((blocks, LANES))
    ends = (lane == 0) | (lane == LANES - 1)
    outside = [pressure[r * blocks : (r + 1) * blocks, 2 * LANES :] for r in range(2)]
    for h in range(2):
        span = slice(h * LANES, (h + 1) * LANES)
        first, second = pressure[:blocks, span], pressure[blocks:, span]
        extra = jnp.where(ends, jnp.where(even, turn(first, -1, 0), turn(second, 1, 0)), 0.0)
        for r in range(2):
            extra = jnp.where(lane == HIGH + r, turn(outside[r], HIGH + r - 2 * h, 1), extra)
            extra = jnp.where(lane == LOW + r, turn(outside[r], LOW + r - 1 - 2 * h, 1), extra)
        for j, value in enumerate((first, second, extra)):
            message[pl.ds(3 * h + j, blocks, stride=6), :] = value


def mend_kernel(star, message, state, relayed, forward, whole, middle, flat):
    place = position()
    both = far_both(place[0], place[1])
    whole[...] = star[...]
    for i, r in enumerate((1, 2)):
        middle[pl.ds(i * LEVELS, LEVELS), :] = message[pl.ds(3 * (r % 2) + r // 2, LEVELS, stride=6), :]

    @pl.when(both)
    def _():
        lane = lane_of((LEVELS, LANES))
        even_y = place[1] % 2 == 0
        far = relayed[16:32, :]
        flat[...] = jnp.zeros((LANES, LANES), F32)
        flat[pl.ds(0, 16, stride=2), :] = jnp.where(even_y, 0.0, far)
        flat[pl.ds(1, 16, stride=2), :] = jnp.where(even_y, far, 0.0)
        columns = jnp.transpose(flat[...])[:LEVELS]
        end_sign = jnp.where(lane == 0, 0.1, jnp.where(lane == LANES - 1, -0.1, 0.0))
        steps = []
        for x in range(ROWS):
            v = plane(state, 1, x)
            for f in range(4):
                slot = f * ROWS + x
                side = end_sign * v * turn(columns, -(2 * slot + 1), 1)
                at = pl.ds(slot * LEVELS, LEVELS)
                whole[at, :] = whole[at, :] + side
                if f == 1 and x in (1, 2):
                    steps.append(0.5 * north_difference(side))
        modal = dot3(parts(forward[...]), parts(jnp.concatenate(steps, axis=1)))
        for i in range(2):
            at = pl.ds(i * LEVELS, LEVELS)
            middle[at, :] = middle[at, :] + modal[:, i * LANES : (i + 1) * LANES]


def final_kernel(received, middle, star, back, by_level, out, held, sent_out):
    size = LEVELS * ROWS
    span = lambda i: pl.ds(i * size // 2, size // 2)
    copies = [pltpu.make_async_copy(held.at[span(i), :], out.at[span(i), :], sent_out.at[i]) for i in range(8)]
    some = LEVELS // 2

    def put(f, matrix, right):
        for half in range(2):
            if right is not None:
                changes = dot3(parts(matrix[half * some : (half + 1) * some]), right)
            for x in range(ROWS):
                value = star[pl.ds((f * ROWS + x) * LEVELS + half * some, some), :]
                if right is not None:
                    value = value - changes[:, x * LANES : (x + 1) * LANES]
                held[pl.ds(f * size + half * some * ROWS + x, some, stride=ROWS), :] = value
            copies[2 * f + half].start()

    put(3, None, None)
    lane = lane_of((LEVELS, LANES))
    row_at = lambda ref, r: ref[pl.ds(3 * (r % 2) + r // 2, LEVELS, stride=6), :]
    p = [row_at(received, r) for r in range(ROWS)]
    extra = [row_at(received, 4), row_at(received, 5)]
    low = [turn(extra[r % 2], -(LOW + r // 2), 1) for r in range(ROWS)]
    high = [turn(extra[r % 2], LANES - 1 - (HIGH + r // 2), 1) for r in range(ROWS)]
    four_rate = 4.0 * by_level[pl.ds(0, LEVELS), :]

    def next_row(r, opposite):
        here = p[r]
        divergence = middle[pl.ds((r - 1) * LEVELS, LEVELS), :]
        plus = jnp.where(lane < LANES - 2, turn(here, -2, 1), turn(high[r], -1, 1))
        minus = jnp.where(lane > 1, turn(here, 2, 1), turn(low[r], 1, 1))
        return (
            2.0 * here
            - opposite
            + four_rate * here
            + (2.0 * here - plus - minus)
            + 4.0 * divergence
        )

    ends = (lane == 0) | (lane == LANES - 1)
    before = jnp.where(ends, extra[1], next_row(1, p[3]))
    after = jnp.where(ends, extra[0], next_row(2, p[0]))
    padded = [before] + p + [after]
    matrix = back[...]
    joined = lambda values: parts(jnp.concatenate(values, axis=1))
    put(2, 0.5 * level_difference(matrix), joined(p))
    put(1, matrix, joined([0.5 * north_difference(p[x], low[x], high[x]) for x in range(ROWS)]))
    put(0, matrix, joined([0.5 * (padded[x + 2] - padded[x]) for x in range(ROWS)]))
    for copy in copies:
        copy.wait()


def call(kernel, shapes, args, name, scratch=(), cost=None, copies=0):
    vmem = pl.BlockSpec(memory_space=pltpu.VMEM)
    return pl.pallas_call(
        kernel,
        out_shape=[jax.ShapeDtypeStruct(s, F32) for s in shapes],
        in_specs=[vmem] * len(args),
        out_specs=[pl.BlockSpec(memory_space=pl.ANY) if copies else vmem] * len(shapes),
        scratch_shapes=[pltpu.VMEM(s, F32) for s in scratch]
        + ([pltpu.SemaphoreType.DMA((copies,))] if copies else []),
        compiler_params=pltpu.CompilerParams(vmem_limit_bytes=32 * 1024 * 1024),
        name=name,
        cost_estimate=cost,
    )(*args)


def swap(values, axis, odd):
    count = lax.axis_size(axis)
    pairs = []
    for i in range(odd, count + odd, 2):
        pairs += [(i % count, (i + 1) % count), ((i + 1) % count, i % count)]
    return lax.ppermute(values, axis, pairs)


def swap_odd_x(values, far):
    count = lax.axis_size("gx")
    pairs = []
    for i in range(1, count + 1, 2):
        one, two = i % count, (i + 1) % count
        if (one % 16 == 15) == far:
            pairs += [(one, two), (two, one)]
    return lax.ppermute(values, "gx", pairs)


def swap_odd_y(values, helping):
    count_x, count_y = lax.axis_size("gx"), lax.axis_size("gy")
    pairs = []
    for i in range(count_x):
        for j in range(1, count_y + 1, 2):
            one, two = j % count_y, (j + 1) % count_y
            if not far_both(i, one) and far_both(i ^ 1, one) == helping:
                pairs += [(i * count_y + one, i * count_y + two), (i * count_y + two, i * count_y + one)]
    return lax.ppermute(values, ("gx", "gy"), pairs)


def hand_over(values):
    count_x, count_y = lax.axis_size("gx"), lax.axis_size("gy")
    pairs = [
        ((i ^ 1) * count_y + j, i * count_y + j)
        for i in range(count_x)
        for j in range(count_y)
        if far_both(i, j)
    ]
    return lax.ppermute(values, ("gx", "gy"), pairs)


def exchange(values):
    count_x, count_y = lax.axis_size("gx"), lax.axis_size("gy")
    near = count_y // 2
    groups = [[i * count_y + h * near + y for i in range(count_x) for h in range(2)] for y in range(near)]
    shaped = values.reshape(2 * count_x, 1, values.size // (2 * count_x))
    moved = lax.all_to_all(
        shaped, ("gx", "gy"), 0, 0, tiled=True, axis_index_groups=groups
    )
    return moved.reshape(values.shape)


def on_device(
    model_state, density, layer_in, layer_bias, layer_out, mode_forward, mode_back, mode_rate
):
    blocks = lax.axis_size("gx")
    total_east = blocks * ROWS
    state = model_state.reshape(4 * LEVELS * ROWS, LANES)
    basis, square = east_tables(total_east // 2, blocks)
    basis_high, basis_low = split_table(np.ascontiguousarray(basis.T))
    square_row = np.ascontiguousarray(np.broadcast_to(np.concatenate([square, square]), (8, total_east)))

    planes, x_even, x_odd, y_even, y_odd, y_pair = call(
        edges_kernel,
        [(16 * LEVELS, LANES), (5 * LEVELS + 16, LANES), (5 * LEVELS, LANES), (16, LANES), (16, LANES), (32, LANES)],
        [state],
        "edges",
        scratch=[(LANES, LANES)],
    )
    got_x_even = swap(x_even, "gx", 0)
    got_x_far = swap_odd_x(x_odd, True)
    got_y_odd = swap_odd_y(y_odd, False)
    y_both = y_pair.at[16:].set(got_x_even[5 * LEVELS :])
    y_both, x_odd, y_even = lax.optimization_barrier((y_both, x_odd, y_even))
    got_y_both = swap_odd_y(y_both, True)
    got_x_near = swap_odd_x(x_odd, False)
    inner, by_level, by_row, by_wave, by_block = call(
        inner_kernel,
        [(16 * LEVELS, LANES), (3 * LEVELS, LANES), (72, total_east), (3 * LANES, LANES), (72, total_east)],
        [
            planes,
            jnp.concatenate([mode_rate, density, layer_bias])[None, :],
            square_row,
            layer_in,
            layer_out,
        ],
        "inner",
        cost=pl.CostEstimate(flops=10**10, transcendentals=0, bytes_accessed=2**24),
    )
    inner, y_even = lax.optimization_barrier((inner, y_even))
    got_y_even = swap(y_even, "gy", 0)
    star, message = call(
        outer_kernel,
        [(16 * LEVELS, LANES), (blocks * 6, LANES)],
        [
            planes,
            inner,
            got_x_even,
            got_x_far,
            got_x_near,
            got_y_even,
            got_y_odd,
            got_y_both,
            by_level,
            mode_forward,
        ],
        "outer",
        scratch=[(LANES, LANES)],
    )
    modal = exchange(message)
    local, moments = call(
        solve_kernel,
        [(LANES, total_east), (16, total_east)],
        [modal, basis_high, basis_low, by_row, by_wave],
        "solve",
    )
    moments = lax.all_to_all(
        moments.reshape(4, 4, total_east),
        "gy",
        0,
        0,
        tiled=True,
        axis_index_groups=[[0, 1, 2, 3], [4, 5, 6, 7]],
    ).reshape(16, total_east)
    (reply,) = call(
        back_kernel,
        [(blocks * 6, LANES)],
        [local, moments, basis_high, basis_low, by_row, by_wave, by_block],
        "back",
    )
    reply, got_y_both = lax.optimization_barrier((reply, got_y_both))
    relayed = hand_over(got_y_both)
    pressure = exchange(reply)
    whole, middle = call(
        mend_kernel,
        [(16 * LEVELS, LANES), (2 * LEVELS, LANES)],
        [star, message, planes, relayed, mode_forward],
        "mend",
        scratch=[(LANES, LANES)],
    )
    (out,) = call(
        final_kernel,
        [(4 * LEVELS * ROWS, LANES)],
        [pressure, middle, whole, mode_back, by_level],
        "final",
        scratch=[(4 * LEVELS * ROWS, LANES)],
        copies=8,
    )
    return out.reshape(model_state.shape)


def solution(mesh):
    return jax.shard_map(
        on_device,
        mesh=mesh,
        in_specs=(P(None, None, "gx", "gy"), P(), P(), P(), P(), P(), P(), P()),
        out_specs=P(None, None, "gx", "gy"),
        check_vma=False,
    )
```

```python
import math

import jax
import jax.numpy as jnp
import ml_dtypes
import numpy as np
from jax import lax
from jax.experimental import pallas as pl
from jax.experimental.pallas import tpu as pltpu
from jax.sharding import PartitionSpec as P

F32 = jnp.float32
BF16 = jnp.bfloat16
LEVELS = 64
ROWS = 4
LANES = 128
LOW = 16
HIGH = 32
OTHER = 48


def split_table(table):
    high = table.astype(np.float32).astype(ml_dtypes.bfloat16)
    low = (table - high.astype(np.float64)).astype(np.float32).astype(ml_dtypes.bfloat16)
    return high, low


def east_tables(total, blocks):
    rows = total // blocks
    x = (np.arange(rows)[:, None] + rows * np.arange(blocks)[None, :]).reshape(-1)
    k = np.arange(total)
    angle = 2.0 * math.pi * ((k[:, None] * x[None, :]) % total) / total
    basis = np.where((k <= total // 2)[:, None], np.cos(angle), np.sin(angle))
    scale = np.where((k == 0) | (k == total // 2), 1.0, math.sqrt(2.0)) / math.sqrt(total)
    basis = basis * scale[:, None]
    square = np.sin(math.pi * k / total) ** 2
    return basis, square.astype(np.float32)


def position():
    return lax.axis_index("gx"), lax.axis_index("gy")


def lane_of(shape):
    return lax.broadcasted_iota(jnp.int32, shape, len(shape) - 1)


def row_of(shape):
    return lax.broadcasted_iota(jnp.int32, shape, 0)


def turn(values, shift, axis):
    size = values.shape[axis]
    return pltpu.roll(values, shift % size, axis) if shift % size else values


def parts(values):
    high = values.astype(BF16)
    return high, (values - high.astype(F32)).astype(BF16)


def dot3(left, right):
    long_left = jnp.concatenate([left[1], left[0], left[0]], axis=1)
    long_right = jnp.concatenate([right[0], right[1], right[0]], axis=0)
    return jnp.dot(long_left, long_right, preferred_element_type=F32)


def level_difference(values):
    row = row_of(values.shape)
    last = values.shape[0] - 1
    upper = jnp.where(row < last, turn(values, -1, 0), 0.0)
    lower = jnp.where(row > 0, turn(values, 1, 0), 0.0)
    return upper - lower


def north_difference(values, low=0.0, high=0.0):
    lane = lane_of(values.shape)
    after = jnp.where(lane < LANES - 1, turn(values, -1, 1), high)
    before = jnp.where(lane > 0, turn(values, 1, 1), low)
    return after - before


def plane(ref, field, x):
    return ref[pl.ds((field * ROWS + x) * LEVELS, LEVELS), :]


def far_both(gx, gy):
    return ((gx % 16 == 0) | (gx % 16 == 15)) & ((gy % 4 == 0) | (gy % 4 == 3))


def edges_kernel(state, planes, x_even, x_odd, y_even, y_odd, flat):
    place = position()
    even_x = place[0] % 2 == 0
    even_y = place[1] % 2 == 0
    size = LEVELS * ROWS
    lane = lane_of((LEVELS, LANES))
    gathered = jnp.zeros((LEVELS, LANES), F32)
    for field in range(4):
        values = [state[pl.ds(field * size + x, LEVELS, stride=ROWS), :] for x in range(ROWS)]
        for x in range(ROWS):
            slot = field * ROWS + x
            planes[pl.ds(slot * LEVELS, LEVELS), :] = values[x]
            gathered = jnp.where(lane >> 1 == slot, turn(values[x], 2 * slot + 1, 1), gathered)
        for slot, depth in ((field, 0), (4, 1)) if field == 0 else ((field, 0),):
            span = pl.ds(slot * LEVELS, LEVELS)
            low, high = values[depth], values[ROWS - 1 - depth]
            x_even[span, :] = jnp.where(even_x, high, low)
            x_odd[span, :] = jnp.where(even_x, low, high)
    flat[...] = jnp.transpose(jnp.concatenate([gathered, jnp.zeros_like(gathered)], axis=0))
    high, low = flat[pl.ds(0, 16, stride=2), :], flat[pl.ds(1, 16, stride=2), :]
    y_even[0:16, :] = jnp.where(even_y, high, low)
    y_odd[...] = jnp.where(even_y, low, high)
    x_even[pl.ds(5 * LEVELS, 16), :] = jnp.where(even_y, low, high)


def column_of(row):
    return jnp.transpose(jnp.broadcast_to(row, (LANES, LANES)))


def inner_kernel(
    state,
    vectors,
    square_row,
    layer_in,
    layer_out,
    star,
    by_level,
    by_row,
    by_wave,
    by_block,
):
    place = position()
    fields = [[plane(state, f, x) for x in range(ROWS)] for f in range(4)]
    tall = column_of(vectors[:, :LANES])
    rate, density = tall[:LEVELS], tall[LEVELS:]
    row = row_of((LEVELS, LANES))
    by_level[pl.ds(0, LEVELS), :] = rate
    by_level[pl.ds(LEVELS, LEVELS), :] = jnp.where(
        row < LEVELS - 1, 0.5 * turn(density, -1, 0) / density, 0.0
    )
    by_level[pl.ds(2 * LEVELS, LEVELS), :] = jnp.where(row > 0, 0.5 * turn(density, 1, 0) / density, 0.0)
    own = by_level[pl.ds(place[0], 1), :]

    both = jnp.concatenate([own, own], axis=1)
    root, inverse, rho = decay(both, square_row[...])
    powers = squarings(rho, 6)
    for i, value in enumerate(powers + [powers[6] * rho, -1.0 / root]):
        by_row[pl.ds(8 * i, 8), :] = value
    half = row_of((LANES, LANES)) >> 1
    odd = (row_of((LANES, LANES)) & 1) != 0
    narrow = [jnp.broadcast_to(value[0:1, :LANES], (LANES, LANES)) for value in powers[:6]]
    rising = lane_powers(narrow, half)
    falling = lane_powers(narrow, 63 - half)
    by_wave[pl.ds(0, LANES), :] = rising
    by_wave[pl.ds(LANES, LANES), :] = falling
    by_wave[pl.ds(2 * LANES, LANES), :] = narrow[0] * jnp.where(odd, rising, falling)

    r64 = powers[6]
    r128 = r64 * r64
    r256 = r128 * r128
    images = 1.0 / (1.0 - r256 * r256)
    mine = place[1] & 3
    row = row_of(rho.shape)
    for j in range(4):
        for i, offset in enumerate((-1, 3)):
            exponent = jnp.where(row < 2, (mine - j + offset) & 7, (j - mine + offset) & 7)
            weight = jnp.where((exponent & 1) != 0, r64, 1.0)
            weight = weight * jnp.where((exponent & 2) != 0, r128, 1.0)
            weight = weight * jnp.where((exponent & 4) != 0, r256, 1.0)
            by_block[pl.ds((2 * j + i) * 8, 8), :] = weight * images
    scale = -1.0 / root
    by_block[pl.ds(64, 8), :] = jnp.where(row == 0, scale, jnp.where(row == 1, scale * r64, scale * inverse))

    for x in range(ROWS):
        u, v, w, th = (fields[f][x] for f in range(4))
        for f in range(4):
            here = fields[f][x]
            change = v * north_difference(here) + w * level_difference(here)
            if x == 0:
                change = change + u * fields[f][1]
            elif x == ROWS - 1:
                change = change - u * fields[f][x - 1]
            else:
                change = change + u * (fields[f][x + 1] - fields[f][x - 1])
            value = here - 0.1 * change
            if f == 2:
                value = value + 0.1 * th
            star[pl.ds((f * ROWS + x) * LEVELS, LEVELS), :] = value

    columns = jnp.concatenate(
        [jnp.concatenate([fields[f][x] for f in range(4)], axis=0).astype(BF16) for x in range(ROWS)],
        axis=1,
    )
    first = (((0,), (0,)), ((), ()))
    shift = [column_of(vectors[:, i * LANES : (i + 1) * LANES]) for i in (1, 2)]
    shift = jnp.concatenate(shift, axis=0)
    before = lax.dot_general(layer_in[...], columns, first, preferred_element_type=F32)
    before = before + jnp.concatenate([shift] * ROWS, axis=1)
    hidden = (before * (1.0 / (1.0 + jnp.exp(-before)))).astype(BF16)
    forcing = lax.dot_general(layer_out[...], hidden, first, preferred_element_type=F32)
    for x in range(ROWS):
        span = slice(x * LANES, (x + 1) * LANES)
        for f, part in ((2, forcing[LEVELS:, span]), (3, forcing[:LEVELS, span])):
            at = pl.ds((f * ROWS + x) * LEVELS, LEVELS)
            star[at, :] = star[at, :] + 0.2 * part


def side_terms(state, edge, low):
    u, v, w, _, second = edge
    own = jnp.where(low, plane(state, 0, 0), plane(state, 0, ROWS - 1))
    sign = jnp.where(low, 0.1, -0.1)
    adds = [sign * own * value for value in edge[:4]]
    along = u * (own - second)
    beyond = u - (sign * along + 0.1 * (v * north_difference(u) + w * level_difference(u)))
    return adds, beyond


def outer_kernel(
    state,
    inner,
    x_even,
    x_far,
    x_near,
    y_even,
    y_odd,
    y_both,
    by_level,
    forward,
    star,
    message,
    flat,
):
    place = position()
    even_x = place[0] % 2 == 0
    even_y = place[1] % 2 == 0
    shape = (LEVELS, LANES)
    lane = lane_of(shape)

    helping = far_both(place[0] ^ 1, place[1])
    other = jnp.where(helping, y_both[0:16, :], y_odd[...])
    other = jnp.where(far_both(place[0], place[1]), 0.0, other)
    flat[...] = jnp.zeros((LANES, LANES), F32)
    flat[pl.ds(0, 16, stride=2), :] = jnp.where(even_y, y_even[0:16, :], other)
    flat[pl.ds(1, 16, stride=2), :] = jnp.where(even_y, other, y_even[0:16, :])
    low_side = place[1] % 4 == 0
    scale = jnp.where(low_side, 0.1, -0.1) * jnp.where(helping, 1.0, 0.0)
    theirs = x_even[pl.ds(5 * LEVELS + 4, 4), :]
    flat[pl.ds(32, 16), :] = scale * jnp.concatenate([theirs] * 4, axis=0) * y_both[16:32, :]
    columns = jnp.transpose(flat[...])[:LEVELS]
    spans = [pl.ds(i * LEVELS, LEVELS) for i in range(5)]
    even_adds, even_beyond = side_terms(state, [x_even[at, :] for at in spans], ~even_x)
    far_x = (place[0] % 16 == 0) | (place[0] % 16 == 15)
    odd_edge = [jnp.where(far_x, x_far[at, :], x_near[at, :]) for at in spans]
    odd_adds, odd_beyond = side_terms(state, odd_edge, even_x)
    end_sign = jnp.where(lane == 0, 0.1, jnp.where(lane == LANES - 1, -0.1, 0.0))
    whole = [[None] * ROWS for _ in range(4)]
    side_u = [None] * ROWS
    for x in range(ROWS):
        v = plane(state, 1, x)
        for f in range(4):
            slot = f * ROWS + x
            side = end_sign * v * turn(columns, -(2 * slot + 1), 1)
            if f == 0:
                side_u[x] = side
            value = inner[pl.ds(slot * LEVELS, LEVELS), :] + side
            if x == 0:
                value = value + jnp.where(even_x, odd_adds[f], even_adds[f])
            if x == ROWS - 1:
                value = value + jnp.where(even_x, even_adds[f], odd_adds[f])
            whole[f][x] = value
            star[pl.ds(slot * LEVELS, LEVELS), :] = value

    low_beyond = jnp.where(even_x, odd_beyond, even_beyond)
    high_beyond = jnp.where(even_x, even_beyond, odd_beyond)
    padded = [low_beyond] + whole[0] + [high_beyond]
    divergence = []
    up, down = by_level[pl.ds(LEVELS, LEVELS), :], by_level[pl.ds(2 * LEVELS, LEVELS), :]
    step = jnp.where(lane < 35, turn(columns, -1, 1), 0.0) - jnp.where(lane > 32, turn(columns, 1, 1), 0.0)
    lifted = turn(columns, -8, 1)
    step = 0.5 * step + up * turn(lifted, -1, 0) - down * turn(lifted, 1, 0)
    left_out = jnp.where((lane >= 32) & (lane < 36), step, 0.0)
    beside = jnp.where(low_side, 0.5, -0.5) * columns
    left_out = jnp.where((lane >= 36) & (lane < 40), beside, left_out)
    left_out = jnp.where(lane == 40, -0.5 * turn(columns, 5, 1), left_out)
    left_out = jnp.where(lane == 41, 0.5 * turn(columns, 9, 1), left_out)
    left_out = turn(left_out, OTHER - 32, 1)
    extra = [left_out - 0.5 * side_u[ROWS - 1], left_out + 0.5 * side_u[0]]
    for x in range(ROWS):
        v, w = whole[1][x], whole[2][x]
        upright = up * turn(w, -1, 0) - down * turn(w, 1, 0)
        divergence.append(0.5 * (padded[x + 2] - padded[x]) + 0.5 * north_difference(v) + upright)
        low, high = LOW + x // 2, HIGH + x // 2
        value = jnp.where(lane == low, 0.5 * turn(v, low, 1), extra[x % 2])
        extra[x % 2] = jnp.where(lane == high, -0.5 * turn(v, high + 1, 1), value)
    pieces = [divergence[0], divergence[2], extra[0], divergence[1], divergence[3], extra[1]]
    modal = dot3(parts(forward[...]), parts(jnp.concatenate(pieces, axis=1)))
    for i in range(6):
        message[pl.ds(i, LEVELS, stride=6), :] = modal[:, i * LANES : (i + 1) * LANES]


def decay(rate, square):
    lam = rate + square
    root = jnp.sqrt(lam * (1.0 + lam))
    inverse = 1.0 + 2.0 * lam + 2.0 * root
    return root, inverse, 1.0 / inverse


def squarings(rho, count):
    powers = [rho]
    for _ in range(count):
        powers.append(powers[-1] * powers[-1])
    return powers


def lane_powers(powers, exponent):
    product = None
    for bit in range(6):
        factor = jnp.where((exponent & (1 << bit)) != 0, powers[bit], 1.0)
        product = factor if product is None else product * factor
    return product


def shifted(values, shift):
    size = values.shape[0]
    if shift % 8 == 0:
        zeros = jnp.zeros((abs(shift), values.shape[1]), F32)
        if shift > 0:
            return jnp.concatenate([zeros, values[:-shift]], axis=0)
        return jnp.concatenate([values[-shift:], zeros], axis=0)
    row = row_of(values.shape)
    inside = row >= shift if shift > 0 else row < size + shift
    return jnp.where(inside, turn(values, shift, 0), 0.0)


def by_parity(even, odd):
    shape = (8, even.shape[1])
    tile = jnp.where((row_of(shape) & 1) != 0, jnp.broadcast_to(odd, shape), jnp.broadcast_to(even, shape))
    return jnp.concatenate([tile] * (LANES // 8), axis=0)


def halves(values):
    return jnp.concatenate([values, values], axis=1)


def solve_kernel(received, basis_high, basis_low, by_row, by_wave, local, moments):
    place = position()
    blocks = received.shape[0] // 6
    lane = lane_of((blocks, LANES))
    ends = (lane == 0) | (lane == LANES - 1)
    even = place[1] < 4
    parity = jnp.where(even, 0, 1)
    low_side = place[1] % 4 == 0
    edge = jnp.where(low_side, 0, LANES - 1)
    within = jnp.where(low_side, 1, LANES - 2)
    row = row_of((blocks, LANES))
    inside, outside = [], [jnp.zeros((blocks, LANES), F32)] * 2
    for h in range(2):
        first, second, extra = (received[pl.ds(3 * h + j, blocks, stride=6), :] for j in range(3))
        first = first + jnp.where(ends & even, turn(extra, 1, 0), 0.0)
        second = second + jnp.where(ends & ~even, turn(extra, -1, 0), 0.0)
        other = jnp.where(row % 16 == 0, turn(extra, -1, 0), jnp.where(row % 16 == 15, turn(extra, 1, 0), 0.0))
        value = lambda i: jnp.sum(jnp.where(lane == OTHER + i + parity, other, 0.0), axis=1, keepdims=True)
        beside = [value(4), value(6)]
        corner = jnp.broadcast_to(value(8), (blocks, LANES))
        first = first + jnp.where(lane == edge, value(0), jnp.where(lane == within, -beside[0], 0.0))
        second = second + jnp.where(lane == edge, value(2), jnp.where(lane == within, -beside[1], 0.0))
        first = first + jnp.where((lane == edge) & even, turn(corner, 1, 0), 0.0)
        second = second + jnp.where((lane == edge) & ~even, turn(corner, -1, 0), 0.0)
        inside.append(jnp.concatenate([first, second], axis=0))
        for r in range(2):
            for i, start in enumerate((HIGH, LOW)):
                at = 2 * h + i
                outside[r] = jnp.where(lane == at, turn(extra, at - start - r, 1), outside[r])
            at = 2 * h + jnp.where(low_side, 1, 0)
            outside[r] = outside[r] + jnp.where(lane == at, beside[r], 0.0)
    right = parts(jnp.concatenate(inside + [jnp.concatenate(outside, axis=0)], axis=1))
    first = (((0,), (0,)), ((), ()))
    dot = lambda a, b: lax.dot_general(a, b[...], first, preferred_element_type=F32)
    spectral = dot(right[0], basis_high) + (dot(right[0], basis_low) + dot(right[1], basis_high))
    source = jnp.concatenate([spectral[:LANES], spectral[LANES : 2 * LANES]], axis=1)
    ext = spectral[2 * LANES : 2 * LANES + 8]
    high = jnp.concatenate([ext[0:1], ext[2:3]], axis=1)
    low = jnp.concatenate([ext[1:2], ext[3:4]], axis=1)

    power = lambda i: by_row[pl.ds(8 * i, 1), :]
    ahead, behind = source, source
    for bit in range(6):
        ahead = ahead + power(bit) * shifted(ahead, 2 << bit)
        behind = behind + power(bit) * shifted(behind, -(2 << bit))
    border = halves(by_wave[pl.ds(2 * LANES, LANES), :]) * by_parity(high, low)
    local[...] = ahead + behind - source + border
    rho, r65 = power(0), power(7)
    across = [
        rho * ahead[LANES - 2 : LANES - 1] + high,
        rho * ahead[LANES - 1 :] + r65 * low,
        rho * behind[0:1] + r65 * high,
        rho * behind[1:2] + low,
    ]
    across = jnp.concatenate(across, axis=0)
    for j in range(4):
        moments[pl.ds(j * 4, 4), :] = across


def back_kernel(local, moments, basis_high, basis_low, by_row, by_wave, by_block, message):
    place = position()
    width = local.shape[1]
    blocks = basis_high.shape[0] // 2
    even = place[1] < 4
    mine = place[1] & 3
    carry = jnp.zeros((4, width), F32)
    own = jnp.zeros((4, width), F32)
    for j in range(4):
        theirs = moments[pl.ds(j * 4, 4), :]
        own = jnp.where(mine == j, theirs, own)
        swapped = jnp.concatenate([theirs[:, LANES:], theirs[:, :LANES]], axis=1)
        carry = carry + by_block[pl.ds(16 * j, 4), :] * theirs + by_block[pl.ds(16 * j + 8, 4), :] * swapped
    scale, by_r64, by_inverse = (by_block[pl.ds(64 + i, 1), :] for i in range(3))
    after = scale * own[0:1] + by_r64 * carry[0:1] + by_inverse * carry[2:3]
    before = scale * own[3:4] + by_r64 * carry[3:4] + by_inverse * carry[1:2]
    total = local[...] + halves(by_wave[pl.ds(0, LANES), :]) * by_parity(carry[0:1], carry[1:2])
    total = total + halves(by_wave[pl.ds(LANES, LANES), :]) * by_parity(carry[2:3], carry[3:4])
    total = total * scale
    pieces = [total[:, :LANES], total[:, LANES:]]
    for h in range(2):
        span = slice(h * LANES, (h + 1) * LANES)
        pieces += [after[:, span], before[:, span]]
    pieces.append(jnp.zeros((LANES - 4, LANES), F32))
    right = parts(jnp.concatenate(pieces, axis=0))
    last = (((1,), (1,)), ((), ()))
    dot = lambda a, b: lax.dot_general(a[...], b, last, preferred_element_type=F32)
    pressure = dot(basis_high, right[0]) + (dot(basis_high, right[1]) + dot(basis_low, right[0]))
    lane = lane_of((blocks, LANES))
    ends = (lane == 0) | (lane == LANES - 1)
    outside = [pressure[r * blocks : (r + 1) * blocks, 2 * LANES :] for r in range(2)]
    for h in range(2):
        span = slice(h * LANES, (h + 1) * LANES)
        first, second = pressure[:blocks, span], pressure[blocks:, span]
        extra = jnp.where(ends, jnp.where(even, turn(first, -1, 0), turn(second, 1, 0)), 0.0)
        for r in range(2):
            extra = jnp.where(lane == HIGH + r, turn(outside[r], HIGH + r - 2 * h, 1), extra)
            extra = jnp.where(lane == LOW + r, turn(outside[r], LOW + r - 1 - 2 * h, 1), extra)
        for j, value in enumerate((first, second, extra)):
            message[pl.ds(3 * h + j, blocks, stride=6), :] = value


def mend_kernel(star, message, state, relayed, forward, whole, middle, flat):
    place = position()
    both = far_both(place[0], place[1])
    whole[...] = star[...]
    for i, r in enumerate((1, 2)):
        middle[pl.ds(i * LEVELS, LEVELS), :] = message[pl.ds(3 * (r % 2) + r // 2, LEVELS, stride=6), :]

    @pl.when(both)
    def _():
        lane = lane_of((LEVELS, LANES))
        even_y = place[1] % 2 == 0
        far = relayed[16:32, :]
        flat[...] = jnp.zeros((LANES, LANES), F32)
        flat[pl.ds(0, 16, stride=2), :] = jnp.where(even_y, 0.0, far)
        flat[pl.ds(1, 16, stride=2), :] = jnp.where(even_y, far, 0.0)
        columns = jnp.transpose(flat[...])[:LEVELS]
        end_sign = jnp.where(lane == 0, 0.1, jnp.where(lane == LANES - 1, -0.1, 0.0))
        steps = []
        for x in range(ROWS):
            v = plane(state, 1, x)
            for f in range(4):
                slot = f * ROWS + x
                side = end_sign * v * turn(columns, -(2 * slot + 1), 1)
                at = pl.ds(slot * LEVELS, LEVELS)
                whole[at, :] = whole[at, :] + side
                if f == 1 and x in (1, 2):
                    steps.append(0.5 * north_difference(side))
        modal = dot3(parts(forward[...]), parts(jnp.concatenate(steps, axis=1)))
        for i in range(2):
            at = pl.ds(i * LEVELS, LEVELS)
            middle[at, :] = middle[at, :] + modal[:, i * LANES : (i + 1) * LANES]


def final_kernel(received, middle, star, back, by_level, out, held, sent_out):
    size = LEVELS * ROWS
    span = lambda i: pl.ds(i * size // 2, size // 2)
    copies = [pltpu.make_async_copy(held.at[span(i), :], out.at[span(i), :], sent_out.at[i]) for i in range(8)]
    some = LEVELS // 2

    def put(f, matrix, right):
        for half in range(2):
            if right is not None:
                changes = dot3(parts(matrix[half * some : (half + 1) * some]), right)
            for x in range(ROWS):
                value = star[pl.ds((f * ROWS + x) * LEVELS + half * some, some), :]
                if right is not None:
                    value = value - changes[:, x * LANES : (x + 1) * LANES]
                held[pl.ds(f * size + half * some * ROWS + x, some, stride=ROWS), :] = value
            copies[2 * f + half].start()

    put(3, None, None)
    lane = lane_of((LEVELS, LANES))
    row_at = lambda ref, r: ref[pl.ds(3 * (r % 2) + r // 2, LEVELS, stride=6), :]
    p = [row_at(received, r) for r in range(ROWS)]
    extra = [row_at(received, 4), row_at(received, 5)]
    low = [turn(extra[r % 2], -(LOW + r // 2), 1) for r in range(ROWS)]
    high = [turn(extra[r % 2], LANES - 1 - (HIGH + r // 2), 1) for r in range(ROWS)]
    four_rate = 4.0 * by_level[pl.ds(0, LEVELS), :]

    def next_row(r, opposite):
        here = p[r]
        divergence = middle[pl.ds((r - 1) * LEVELS, LEVELS), :]
        plus = jnp.where(lane < LANES - 2, turn(here, -2, 1), turn(high[r], -1, 1))
        minus = jnp.where(lane > 1, turn(here, 2, 1), turn(low[r], 1, 1))
        return (
            2.0 * here
            - opposite
            + four_rate * here
            + (2.0 * here - plus - minus)
            + 4.0 * divergence
        )

    ends = (lane == 0) | (lane == LANES - 1)
    before = jnp.where(ends, extra[1], next_row(1, p[3]))
    after = jnp.where(ends, extra[0], next_row(2, p[0]))
    padded = [before] + p + [after]
    matrix = back[...]
    joined = lambda values: parts(jnp.concatenate(values, axis=1))
    put(2, 0.5 * level_difference(matrix), joined(p))
    put(1, matrix, joined([0.5 * north_difference(p[x], low[x], high[x]) for x in range(ROWS)]))
    put(0, matrix, joined([0.5 * (padded[x + 2] - padded[x]) for x in range(ROWS)]))
    for copy in copies:
        copy.wait()


def call(kernel, shapes, args, name, scratch=(), cost=None, copies=0):
    vmem = pl.BlockSpec(memory_space=pltpu.VMEM)
    return pl.pallas_call(
        kernel,
        out_shape=[jax.ShapeDtypeStruct(s, F32) for s in shapes],
        in_specs=[vmem] * len(args),
        out_specs=[pl.BlockSpec(memory_space=pl.ANY) if copies else vmem] * len(shapes),
        scratch_shapes=[pltpu.VMEM(s, F32) for s in scratch]
        + ([pltpu.SemaphoreType.DMA((copies,))] if copies else []),
        compiler_params=pltpu.CompilerParams(vmem_limit_bytes=32 * 1024 * 1024),
        name=name,
        cost_estimate=cost,
    )(*args)


def swap(values, axis, odd):
    count = lax.axis_size(axis)
    pairs = []
    for i in range(odd, count + odd, 2):
        pairs += [(i % count, (i + 1) % count), ((i + 1) % count, i % count)]
    return lax.ppermute(values, axis, pairs)


def swap_odd_x(values, far):
    count = lax.axis_size("gx")
    pairs = []
    for i in range(1, count + 1, 2):
        one, two = i % count, (i + 1) % count
        if (one % 16 == 15) == far:
            pairs += [(one, two), (two, one)]
    return lax.ppermute(values, "gx", pairs)


def swap_odd_y(values, helping):
    count_x, count_y = lax.axis_size("gx"), lax.axis_size("gy")
    pairs = []
    for i in range(count_x):
        for j in range(1, count_y + 1, 2):
            one, two = j % count_y, (j + 1) % count_y
            if not far_both(i, one) and far_both(i ^ 1, one) == helping:
                pairs += [(i * count_y + one, i * count_y + two), (i * count_y + two, i * count_y + one)]
    return lax.ppermute(values, ("gx", "gy"), pairs)


def hand_over(values):
    count_x, count_y = lax.axis_size("gx"), lax.axis_size("gy")
    pairs = [
        ((i ^ 1) * count_y + j, i * count_y + j)
        for i in range(count_x)
        for j in range(count_y)
        if far_both(i, j)
    ]
    return lax.ppermute(values, ("gx", "gy"), pairs)


def exchange(values):
    count_x, count_y = lax.axis_size("gx"), lax.axis_size("gy")
    near = count_y // 2
    groups = [[i * count_y + h * near + y for i in range(count_x) for h in range(2)] for y in range(near)]
    shaped = values.reshape(2 * count_x, 1, values.size // (2 * count_x))
    moved = lax.all_to_all(
        shaped, ("gx", "gy"), 0, 0, tiled=True, axis_index_groups=groups
    )
    return moved.reshape(values.shape)


def on_device(
    model_state, density, layer_in, layer_bias, layer_out, mode_forward, mode_back, mode_rate
):
    blocks = lax.axis_size("gx")
    total_east = blocks * ROWS
    state = model_state.reshape(4 * LEVELS * ROWS, LANES)
    basis, square = east_tables(total_east // 2, blocks)
    basis_high, basis_low = split_table(np.ascontiguousarray(basis.T))
    square_row = np.ascontiguousarray(np.broadcast_to(np.concatenate([square, square]), (8, total_east)))

    planes, x_even, x_odd, y_even, y_odd = call(
        edges_kernel,
        [(16 * LEVELS, LANES), (5 * LEVELS + 16, LANES), (5 * LEVELS, LANES), (16, LANES), (16, LANES)],
        [state],
        "edges",
        scratch=[(LANES, LANES)],
    )
    got_x_even = swap(x_even, "gx", 0)
    got_x_far = swap_odd_x(x_odd, True)
    got_y_odd = swap_odd_y(y_odd, False)
    y_both = jnp.concatenate([y_odd, got_x_even[5 * LEVELS :]], axis=0)
    y_both, x_odd, y_even = lax.optimization_barrier((y_both, x_odd, y_even))
    got_y_both = swap_odd_y(y_both, True)
    got_x_near = swap_odd_x(x_odd, False)
    inner, by_level, by_row, by_wave, by_block = call(
        inner_kernel,
        [(16 * LEVELS, LANES), (3 * LEVELS, LANES), (72, total_east), (3 * LANES, LANES), (72, total_east)],
        [
            planes,
            jnp.concatenate([mode_rate, density, layer_bias])[None, :],
            square_row,
            layer_in,
            layer_out,
        ],
        "inner",
        cost=pl.CostEstimate(flops=10**10, transcendentals=0, bytes_accessed=2**24),
    )
    inner, y_even = lax.optimization_barrier((inner, y_even))
    got_y_even = swap(y_even, "gy", 0)
    star, message = call(
        outer_kernel,
        [(16 * LEVELS, LANES), (blocks * 6, LANES)],
        [
            planes,
            inner,
            got_x_even,
            got_x_far,
            got_x_near,
            got_y_even,
            got_y_odd,
            got_y_both,
            by_level,
            mode_forward,
        ],
        "outer",
        scratch=[(LANES, LANES)],
    )
    modal = exchange(message)
    local, moments = call(
        solve_kernel,
        [(LANES, total_east), (16, total_east)],
        [modal, basis_high, basis_low, by_row, by_wave],
        "solve",
    )
    moments = lax.all_to_all(
        moments.reshape(4, 4, total_east),
        "gy",
        0,
        0,
        tiled=True,
        axis_index_groups=[[0, 1, 2, 3], [4, 5, 6, 7]],
    ).reshape(16, total_east)
    (reply,) = call(
        back_kernel,
        [(blocks * 6, LANES)],
        [local, moments, basis_high, basis_low, by_row, by_wave, by_block],
        "back",
    )
    reply, got_y_both = lax.optimization_barrier((reply, got_y_both))
    relayed = hand_over(got_y_both)
    pressure = exchange(reply)
    whole, middle = call(
        mend_kernel,
        [(16 * LEVELS, LANES), (2 * LEVELS, LANES)],
        [star, message, planes, relayed, mode_forward],
        "mend",
        scratch=[(LANES, LANES)],
    )
    (out,) = call(
        final_kernel,
        [(4 * LEVELS * ROWS, LANES)],
        [pressure, middle, whole, mode_back, by_level],
        "final",
        scratch=[(4 * LEVELS * ROWS, LANES)],
        copies=8,
    )
    return out.reshape(model_state.shape)


def solution(mesh):
    return jax.shard_map(
        on_device,
        mesh=mesh,
        in_specs=(P(None, None, "gx", "gy"), P(), P(), P(), P(), P(), P(), P()),
        out_specs=P(None, None, "gx", "gy"),
        check_vma=False,
    )
```
